32 devices in a mesh: dp: 8 (over z, y), head: 4 (over x, core).
Axes of the slice: x: 2, y: 2, z: 4, core: 2. Of those that a mesh axis runs over, the one named last changes fastest.
Arguments:
- tokens: bfloat16 [32, 197, 768], P('dp'), may hold values from -6 to 6
- ln1_gain: bfloat16 [768], P('dp'), may hold values from 0.25 to 1.75
- ln1_shift: bfloat16 [768], P('dp'), may hold values from -3 to 3
- w_qkv: bfloat16 [768, 3, 768], P('dp', None, 'head'), may hold values from -0.21875 to 0.21875
- w_proj: bfloat16 [768, 768], P('head', 'dp'), may hold values from -1.75 to 1.75
- mix_pre: float32 [12, 12], P('head'), may hold values from -1.75 to 1.75
- mix_post: float32 [12, 12], P('head'), may hold values from -1.75 to 1.75
- ln2_gain: bfloat16 [768], P('dp'), may hold values from 0.25 to 1.75
- ln2_shift: bfloat16 [768], P('dp'), may hold values from -3 to 3
- w_up: bfloat16 [768, 3072], P('dp', 'head'), may hold values from -0.21875 to 0.21875
- conv_kernel: float32 [7, 7, 3072], P(None, None, 'head'), may hold values from -0.875 to 0.875
- w_down: bfloat16 [3072, 768], P('head', 'dp'), may hold values from -0.109375 to 0.109375
- out_grad: bfloat16 [32, 197, 768], P('dp'), may hold values from -6 to 6
Outputs:
- output: bfloat16 [32, 197, 768], P('dp')
- input_grad: bfloat16 [32, 197, 768], P('dp')
- ln1_gain_grad: float32 [768], P('dp')
- ln1_shift_grad: float32 [768], P('dp')
- w_qkv_grad: float32 [768, 3, 768], P('dp', None, 'head')
- w_proj_grad: float32 [768, 768], P('head', 'dp')
- mix_pre_grad: float32 [12, 12], P('head')
- mix_post_grad: float32 [12, 12], P('head')
- ln2_gain_grad: float32 [768], P('dp')
- ln2_shift_grad: float32 [768], P('dp')
- w_up_grad: float32 [768, 3072], P('dp', 'head')
- conv_kernel_grad: float32 [7, 7, 3072], P(None, None, 'head')
- w_down_grad: float32 [3072, 768], P('head', 'dp')
The draws below stay inside these ranges and needn't reach their ends.
All inputs are finite; a program needn't handle non-finite values.
Results may differ from the reference program's by a relative error of at most 0.023.
Values may be sent and summed in bfloat16 or wider, within the bound.
A program may use at most 256 MiB of HBM per device.

```python
import math
import jax
import jax.numpy as jnp
from jax import lax

D = 768
HEADS = 12
HEAD_DIM = 64
FF = 3072
GRID = 14
KSIZE = 7
SEQ = 197
IMAGES = 32


def strengthened(array, stream_key, source, target, shards_of, factor):
    def block_of(position):
        return (jnp.arange(array.shape[position]) // (array.shape[position] // shards_of)).reshape((-1,) + (1,) * (array.ndim - 1 - position))

    one_side = jax.random.permutation(stream_key, shards_of)[block_of(target)]
    second = (block_of(target) + shards_of // 2) % shards_of
    return jnp.where((block_of(source) == one_side) | (block_of(source) == second), factor * array, array)


def steps_of(own_key, extent, cuts, smallest, high):
    factor_of = 1.0
    for axis_at, shards_of in cuts:
        draws = jax.random.uniform(jax.random.fold_in(jax.random.fold_in(own_key, 6), axis_at), (shards_of,), jnp.float32, smallest / len(cuts), high / len(cuts))
        factor_of = factor_of * jnp.repeat(jnp.exp(draws), extent[axis_at] // shards_of).reshape((-1,) + (1,) * (len(extent) - 1 - axis_at))
    return factor_of


def noise(own_key, dims, deviation, limit, pieces=(), kind=jnp.bfloat16):
    values = deviation * jax.random.normal(own_key, dims, jnp.float32)
    if pieces:
        values = values * steps_of(own_key, dims, pieces, -0.22, 0.18)
    return jnp.clip(values, -limit, limit).astype(kind)


def bell_draw_with(stream_key, shape, deviation, bound, pieces, heavy, kind=jnp.bfloat16):
    drawn = deviation * jax.random.normal(stream_key, shape, jnp.float32)
    if pieces:
        drawn = drawn * steps_of(stream_key, shape, pieces, -0.22, 0.18)
    return jnp.clip(strengthened(drawn, jax.random.fold_in(stream_key, 3), *heavy), -bound, bound).astype(kind)


def setup_inputs(seed: int = 0) -> dict:
    arg_keys = jax.random.split(jax.random.key(seed), 14)
    return {
        "tokens": bell_draw_with(arg_keys[0], (IMAGES, SEQ, D), 1.0, 6.0, ((0, 8),), (0, 2, 8, 2.0)),
        "ln1_gain": jnp.clip(1.0 + 0.15 * jax.random.normal(arg_keys[1], (D,), jnp.float32), 0.25, 1.75).astype(jnp.bfloat16),
        "ln1_shift": noise(arg_keys[2], (D,), 0.5, 3.0, ((0, 8),)),
        "w_qkv": noise(arg_keys[3], (D, 3, D), D ** -0.5, 0.21875, ((0, 8), (2, 4))),
        "w_proj": noise(arg_keys[4], (D, D), (max(D // 64, 1)) ** -0.5, 1.75, ((0, 4), (1, 8))),
        "mix_pre": noise(arg_keys[5], (HEADS, HEADS), HEADS ** -0.5, 1.75, ((0, 4),), jnp.float32),
        "mix_post": noise(arg_keys[6], (HEADS, HEADS), HEADS ** -0.5, 1.75, ((0, 4),), jnp.float32),
        "ln2_gain": jnp.clip(1.0 + 0.15 * jax.random.normal(arg_keys[7], (D,), jnp.float32), 0.25, 1.75).astype(jnp.bfloat16),
        "ln2_shift": noise(arg_keys[8], (D,), 0.5, 3.0, ((0, 8),)),
        "w_up": noise(arg_keys[9], (D, FF), D ** -0.5, 0.21875, ((0, 8), (1, 4))),
        "conv_kernel": noise(arg_keys[10], (KSIZE, KSIZE, FF), (KSIZE * KSIZE) ** -0.5, 0.875, ((2, 4),), jnp.float32),
        "w_down": noise(arg_keys[11], (FF, D), FF ** -0.5, 0.109375, ((0, 4), (1, 8))),
        "out_grad": bell_draw_with(arg_keys[12], (IMAGES, SEQ, D), 1.0, 6.0, ((0, 8),), (0, 2, 8, 2.0)),
    }


highest = lax.Precision.HIGHEST
epsilon = 1e-06

@jax.custom_vjp
def low(v):
    return lax.optimization_barrier(v.astype(jnp.bfloat16)).astype(jnp.float32)

@jax.custom_vjp
def low_back(v):
    return v

def low_keep(v):
    return (low(v), None)

def low_pass(kept, grad):
    return (grad,)

def back_keep(v):
    return (v, None)

def back_low(kept, grad):
    return (low(grad),)
low.defvjp(low_keep, low_pass)
low_back.defvjp(back_keep, back_low)

def layer_norm(values, gain, shift):
    center = lax.optimization_barrier(jnp.mean(values, axis=-1, keepdims=True))
    centered = values - center
    spread = lax.optimization_barrier(jnp.mean(centered * centered, axis=-1, keepdims=True))
    return centered * lax.rsqrt(spread + epsilon) * gain + shift

def depthwise(activ, kernel):
    images = activ.shape[0]
    channels = activ.shape[2]
    margin = (KSIZE - 1) // 2
    patches = activ[:, 1:, :].reshape(images, GRID, GRID, channels)
    padded = jnp.pad(patches, ((0, 0), (margin, margin), (margin, margin), (0, 0)))
    total = patches
    for vertical in range(KSIZE):
        for lateral in range(KSIZE):
            total = total + padded[:, vertical:vertical + GRID, lateral:lateral + GRID, :] * kernel[vertical, lateral]
    return jnp.concatenate([activ[:, :1, :], total.reshape(images, GRID * GRID, channels)], axis=1)

def forward(tokens, ln1_gain, ln1_shift, w_qkv, w_proj, mix_pre, mix_post, ln2_gain, ln2_shift, w_up, conv_kernel, w_down):
    images = tokens.shape[0]
    scale = HEAD_DIM ** (-0.5)
    normed_one = low(layer_norm(tokens, ln1_gain, ln1_shift))
    qkv = low_back(low(jnp.einsum('ind,dce->ince', normed_one, w_qkv, precision=highest)))
    query = qkv[:, :, 0].reshape(images, SEQ, HEADS, HEAD_DIM)
    keys = qkv[:, :, 1].reshape(images, SEQ, HEADS, HEAD_DIM)
    values = qkv[:, :, 2].reshape(images, SEQ, HEADS, HEAD_DIM)
    scores = low_back(low(jnp.einsum('inhd,imhd->ihnm', query, keys, precision=highest) * scale))
    mixed = jnp.einsum('hg,ignm->ihnm', mix_pre, scores, precision=highest)
    probs = low(jax.nn.softmax(mixed, axis=-1))
    post = low(jnp.einsum('hg,ignm->ihnm', mix_post, probs, precision=highest))
    heads_out = jnp.einsum('ihnm,imhd->inhd', post, values, precision=highest).reshape(images, SEQ, D)
    heads_out = low_back(low(heads_out))
    attention = low_back(jnp.einsum('ine,ed->ind', heads_out, w_proj, precision=highest))
    middle = tokens + attention
    normed_two = low(layer_norm(middle, ln2_gain, ln2_shift))
    hidden = low_back(jnp.einsum('ind,df->inf', normed_two, w_up, precision=highest))
    widened = low(depthwise(jax.nn.gelu(hidden, approximate=False), conv_kernel))
    return middle + jnp.einsum('inf,fd->ind', widened, w_down, precision=highest)

def reference(tokens, ln1_gain, ln1_shift, w_qkv, w_proj, mix_pre, mix_post, ln2_gain, ln2_shift, w_up, conv_kernel, w_down, out_grad):
    params = tuple((param.astype(jnp.float32) for param in (ln1_gain, ln1_shift, w_qkv, w_proj, mix_pre, mix_post, ln2_gain, ln2_shift, w_up, conv_kernel, w_down)))
    images = tokens.shape[0]
    group = math.gcd(images, 16)
    blocks = images // group
    inputs = tokens.astype(jnp.float32).reshape(blocks, group, SEQ, D)
    cotangents = out_grad.astype(jnp.float32).reshape(blocks, group, SEQ, D)

    def accumulate(totals, pair):
        block_in, block_cot = pair
        result, pull = jax.vjp(forward, block_in, *params)
        grads = pull(block_cot)
        totals = tuple((total + grad for total, grad in zip(totals, grads[1:])))
        return (totals, (result.astype(jnp.bfloat16), grads[0].astype(jnp.bfloat16)))
    start = tuple((jnp.zeros(param.shape, jnp.float32) for param in params))
    totals, (results, input_grads) = lax.scan(accumulate, start, (inputs, cotangents))
    output = results.reshape(images, SEQ, D)
    input_grad = input_grads.reshape(images, SEQ, D)
    return (output, input_grad, totals[0], totals[1], totals[2], totals[3], totals[4], totals[5], totals[6], totals[7], totals[8], totals[9], totals[10])
```

```python
import jax
import jax.numpy as jnp
import numpy as np
from jax import lax
from jax.sharding import PartitionSpec as P

highest = lax.Precision.HIGHEST
epsilon = 1e-06
bf16 = jnp.bfloat16
f32 = jnp.float32


def spectrum(grid, ksize):
    margin = ksize // 2
    period = grid + margin
    pairs = [(0, 0)] + [(0, v) for v in range(1, period // 2 + 1)]
    pairs += [(u, v) for u in range(1, period // 2 + 1) for v in range(period)]
    freq = np.array(pairs, np.float64)
    place = np.array([(r, c) for r in range(grid) for c in range(grid)], np.float64)
    lags = np.array([(p - margin, q - margin) for p in range(ksize) for q in range(ksize)], np.float64)
    weight = np.sqrt(np.where(np.arange(len(pairs)) == 0, 1.0, 2.0)) / period
    angle = 2 * np.pi / period * freq @ place.T
    angle_lag = 2 * np.pi / period * freq @ lags.T
    count = len(pairs)
    cos = np.zeros((count + 1, grid * grid + 1))
    sin = np.zeros_like(cos)
    cos[:count, 1:] = weight[:, None] * np.cos(angle)
    sin[:count, 1:] = weight[:, None] * np.sin(angle)
    cos[count, 0] = 1.0
    cos_lag = np.zeros((count + 1, ksize * ksize))
    sin_lag = np.zeros_like(cos_lag)
    cos_lag[:count] = np.cos(angle_lag)
    sin_lag[:count] = np.sin(angle_lag)
    back = np.zeros(count + 1)
    back[:count] = 1.0
    return cos, sin, cos_lag, sin_lag, back


def layer_norm(values, gain, shift):
    center = jnp.mean(values, axis=-1, keepdims=True)
    centered = values - center
    spread = jnp.mean(centered * centered, axis=-1, keepdims=True)
    rs = lax.rsqrt(spread + epsilon)
    xhat = centered * rs
    return xhat * gain + shift, xhat, rs


def norm_back(grad, gain, xhat, rs):
    e = grad * gain
    inner = rs * (
        e
        - jnp.mean(e, axis=-1, keepdims=True)
        - xhat * jnp.mean(e * xhat, axis=-1, keepdims=True)
    )
    return inner, jnp.sum(grad * xhat, axis=(0, 1)), jnp.sum(grad, axis=(0, 1))


def dot(spec, a, b):
    return jnp.einsum(spec, a, b, preferred_element_type=f32)


def plain(
    tokens,
    ln1_gain,
    ln1_shift,
    w_qkv,
    w_proj,
    mix_pre,
    mix_post,
    ln2_gain,
    ln2_shift,
    w_up,
    conv_kernel,
    w_down,
    out_grad,
):
    images, seq, width = tokens.shape
    heads_local, heads = mix_pre.shape
    size = width // heads
    scale = size ** (-0.5)
    ksize = conv_kernel.shape[0]
    units = conv_kernel.shape[2]
    grid = int(round((seq - 1) ** 0.5))
    cos, sin, cos_lag, sin_lag, back = spectrum(grid, ksize)
    fourier = jnp.asarray(np.stack([cos, sin]), bf16)
    lagged = jnp.asarray(np.stack([cos_lag, sin_lag]), f32)
    lagged_back = jnp.asarray(np.stack([cos_lag, sin_lag]) * back[:, None], f32)
    mine = lax.axis_index("head")

    gains = jnp.stack([ln1_gain, ln1_shift, ln2_gain, ln2_shift])
    gains = lax.all_gather(gains, "dp", axis=1, tiled=True).astype(f32)
    gain_one, shift_one, gain_two, shift_two = gains[0], gains[1], gains[2], gains[3]
    qkv_w = lax.all_gather(w_qkv, "dp", axis=0, tiled=True)
    up_w = lax.all_gather(w_up, "dp", axis=0, tiled=True)
    down_w = lax.all_gather(w_down, "dp", axis=1, tiled=True)
    proj_w = lax.all_gather(w_proj, "head", axis=0, tiled=True)
    proj_w = lax.all_gather(proj_w, "dp", axis=1, tiled=True)
    mixes = lax.all_gather(jnp.stack([mix_pre, mix_post]), "head", axis=1, tiled=True)
    pre, post_mix = mixes[0], mixes[1]

    source = tokens.astype(f32)
    normed_one, xhat_one, rs_one = layer_norm(source, gain_one, shift_one)
    normed_one = normed_one.astype(bf16)
    qkv = dot("ind,dce->ince", normed_one, qkv_w).astype(bf16)
    qkv = lax.all_to_all(qkv, "head", split_axis=0, concat_axis=3, tiled=True)
    own = qkv.shape[0]
    query = qkv[:, :, 0].reshape(own, seq, heads, size)
    keys = qkv[:, :, 1].reshape(own, seq, heads, size)
    values = qkv[:, :, 2].reshape(own, seq, heads, size)
    scores = (dot("inhd,imhd->ihnm", query, keys) * scale).astype(bf16)
    mixed = jnp.einsum("hg,ignm->ihnm", pre, scores.astype(f32), precision=highest)
    probs = jax.nn.softmax(mixed, axis=-1)
    probs_low = probs.astype(bf16)
    post = jnp.einsum(
        "hg,ignm->ihnm", post_mix, probs_low.astype(f32), precision=highest
    ).astype(bf16)
    heads_own = dot("ihnm,imhd->inhd", post, values).reshape(own, seq, width).astype(bf16)
    heads_out = lax.all_gather(heads_own, "head", axis=0, tiled=True)
    middle = source + dot("ine,ed->ind", heads_out, proj_w)
    normed_two, xhat_two, rs_two = layer_norm(middle, gain_two, shift_two)
    normed_two = normed_two.astype(bf16)
    hidden = dot("ind,df->inf", normed_two, up_w)
    erf = lax.erf(hidden * (0.5**0.5))
    activ = 0.5 * hidden * (1.0 + erf)
    slope = 0.5 * (1.0 + erf) + hidden * jnp.exp(-0.5 * hidden * hidden) * 0.3989422804014327
    delta = np.zeros((ksize * ksize, 1), np.float32)
    delta[ksize * ksize // 2] = 1.0
    taps = conv_kernel.reshape(ksize * ksize, units)
    filters = jnp.einsum("zkl,lf->zkf", lagged, taps, precision=highest)
    cos_k, sin_k = filters[0] + 1.0, filters[1]
    wave = dot("zkn,inf->zikf", fourier, activ.astype(bf16))
    cos_a, sin_a = wave[0], wave[1]
    filtered = jnp.stack([cos_k * cos_a + sin_k * sin_a, cos_k * sin_a - sin_k * cos_a])
    widened = dot("zkn,zikf->inf", fourier, filtered.astype(bf16)).astype(bf16)
    branch = dot("inf,fd->ind", widened, down_w)
    branch = lax.psum(branch.astype(bf16), "head").astype(f32)
    output = (middle + branch).astype(bf16)

    down_grad = dot("inf,ind->fd", widened, out_grad)
    widened_grad = dot("ind,fd->inf", out_grad, down_w)
    wave_grad = dot("zkn,inf->zikf", fourier, widened_grad.astype(bf16))
    cos_g, sin_g = wave_grad[0], wave_grad[1]
    spread_grad = jnp.stack([cos_k * cos_g - sin_k * sin_g, cos_k * sin_g + sin_k * cos_g])
    activ_grad = dot("zkn,zikf->inf", fourier, spread_grad.astype(bf16))
    hidden_grad = (activ_grad * slope).astype(bf16)
    cross = jnp.stack(
        [
            jnp.sum(cos_a * cos_g + sin_a * sin_g, axis=0),
            jnp.sum(sin_a * cos_g - cos_a * sin_g, axis=0),
        ]
    )
    kernel_grad = jnp.einsum("zkl,zkf->lf", lagged_back, cross, precision=highest)
    up_grad = dot("ind,inf->df", normed_two, hidden_grad)
    two_grad = dot("inf,df->ind", hidden_grad, up_w).astype(bf16)
    two_grad = lax.psum_scatter(two_grad, "head", scatter_dimension=0, tiled=True).astype(f32)

    def pick(array):
        return lax.dynamic_slice_in_dim(array, mine * own, own, 0)

    middle_from, gain_two_grad, shift_two_grad = norm_back(
        two_grad, gain_two, pick(xhat_two), pick(rs_two)
    )
    middle_grad = pick(out_grad).astype(f32) + middle_from
    attention_own = middle_grad.astype(bf16)
    attention_grad = lax.all_gather(attention_own, "head", axis=0, tiled=True)
    local = width // lax.axis_size("head")
    heads_mine = lax.dynamic_slice_in_dim(heads_out, mine * local, local, 2)
    proj_grad = dot("ine,ind->ed", heads_mine, attention_grad)
    heads_grad = dot("ind,ed->ine", attention_own, proj_w).astype(bf16)
    heads_grad = heads_grad.reshape(own, seq, heads, size)
    values_grad = dot("ihnm,inhd->imhd", post, heads_grad)
    post_grad = dot("inhd,imhd->ihnm", heads_grad, values)
    probs_grad = jnp.einsum("hg,ihnm->ignm", post_mix, post_grad, precision=highest)
    mixed_grad = probs * (probs_grad - jnp.sum(probs_grad * probs, axis=-1, keepdims=True))
    scores_grad = jnp.einsum("hg,ihnm->ignm", pre, mixed_grad, precision=highest).astype(bf16)
    post_mix_grad = dot("ihnm,ignm->hg", post_grad.astype(bf16), probs_low)
    pre_mix_grad = dot("ihnm,ignm->hg", mixed_grad.astype(bf16), scores)
    query_grad = dot("ihnm,imhd->inhd", scores_grad, keys) * scale
    keys_grad = dot("ihnm,inhd->imhd", scores_grad, query) * scale
    qkv_grad = jnp.stack([query_grad, keys_grad, values_grad], axis=2)
    qkv_grad = qkv_grad.reshape(own, seq, 3, width).astype(bf16)
    qkv_grad = lax.all_to_all(qkv_grad, "head", split_axis=3, concat_axis=0, tiled=True)
    qkv_weight_grad = dot("ind,ince->dce", normed_one, qkv_grad)
    one_grad = dot("ince,dce->ind", qkv_grad, qkv_w).astype(bf16)
    one_grad = lax.psum_scatter(one_grad, "head", scatter_dimension=0, tiled=True).astype(f32)
    source_grad, gain_one_grad, shift_one_grad = norm_back(
        one_grad, gain_one, pick(xhat_one), pick(rs_one)
    )
    input_own = (middle_grad + source_grad).astype(bf16)
    input_grad = lax.all_gather(input_own, "head", axis=0, tiled=True)

    def share(grad, axis):
        return lax.psum_scatter(
            grad.astype(bf16), "dp", scatter_dimension=axis, tiled=True
        ).astype(f32)

    norm_grads = jnp.stack([gain_one_grad, shift_one_grad, gain_two_grad, shift_two_grad])
    norm_grads = lax.psum(norm_grads, "head")
    norm_grads = lax.psum_scatter(norm_grads, "dp", scatter_dimension=1, tiled=True)
    mix_grads = lax.psum_scatter(
        jnp.stack([pre_mix_grad, post_mix_grad]), "head", scatter_dimension=1, tiled=True
    )
    mix_grads, kernel_grad = lax.psum((mix_grads, kernel_grad), "dp")
    return (
        output,
        input_grad,
        norm_grads[0],
        norm_grads[1],
        share(qkv_weight_grad, 0),
        share(proj_grad, 1),
        mix_grads[0],
        mix_grads[1],
        norm_grads[2],
        norm_grads[3],
        share(up_grad, 0),
        kernel_grad.reshape(ksize, ksize, units),
        share(down_grad, 1),
    )


def solution(mesh):
    in_specs = (
        P("dp", None, None),
        P("dp"),
        P("dp"),
        P("dp", None, "head"),
        P("head", "dp"),
        P("head", None),
        P("head", None),
        P("dp"),
        P("dp"),
        P("dp", "head"),
        P(None, None, "head"),
        P("head", "dp"),
        P("dp", None, None),
    )
    out_specs = (
        P("dp", None, None),
        P("dp", None, None),
        P("dp"),
        P("dp"),
        P("dp", None, "head"),
        P("head", "dp"),
        P("head", None),
        P("head", None),
        P("dp"),
        P("dp"),
        P("dp", "head"),
        P(None, None, "head"),
        P("head", "dp"),
    )
    return jax.shard_map(plain, mesh=mesh, in_specs=in_specs, out_specs=out_specs, check_vma=False)
```

```python
import functools

import jax
import jax.numpy as jnp
import numpy as np
from jax import lax
from jax.experimental import pallas as pl
from jax.experimental.pallas import tpu as pltpu
from jax.sharding import PartitionSpec as P

highest = lax.Precision.HIGHEST
epsilon = 1e-06
bf16 = jnp.bfloat16
f32 = jnp.float32


def spectrum(grid, ksize):
    margin = ksize // 2
    period = grid + margin
    pairs = [(0, 0)] + [(0, v) for v in range(1, period // 2 + 1)]
    pairs += [(u, v) for u in range(1, period // 2 + 1) for v in range(period)]
    freq = np.array(pairs, np.float64)
    place = np.array([(r, c) for r in range(grid) for c in range(grid)], np.float64)
    lags = np.array([(p - margin, q - margin) for p in range(ksize) for q in range(ksize)], np.float64)
    weight = np.sqrt(np.where(np.arange(len(pairs)) == 0, 1.0, 2.0)) / period
    angle = 2 * np.pi / period * freq @ place.T
    angle_lag = 2 * np.pi / period * freq @ lags.T
    count = len(pairs)
    cos = np.zeros((count + 1, grid * grid + 1))
    sin = np.zeros_like(cos)
    cos[:count, 1:] = weight[:, None] * np.cos(angle)
    sin[:count, 1:] = weight[:, None] * np.sin(angle)
    cos[count, 0] = 1.0
    cos_lag = np.zeros((count + 1, ksize * ksize))
    sin_lag = np.zeros_like(cos_lag)
    cos_lag[:count] = np.cos(angle_lag)
    sin_lag[:count] = np.sin(angle_lag)
    back = np.zeros(count + 1)
    back[:count] = 1.0
    return cos, sin, cos_lag, sin_lag, back


def layer_norm(values, gain, shift):
    center = jnp.mean(values, axis=-1, keepdims=True)
    centered = values - center
    spread = jnp.mean(centered * centered, axis=-1, keepdims=True)
    rs = lax.rsqrt(spread + epsilon)
    xhat = centered * rs
    return xhat * gain + shift, xhat, rs


def norm_back(grad, gain, xhat, rs):
    e = grad * gain
    inner = rs * (
        e
        - jnp.mean(e, axis=-1, keepdims=True)
        - xhat * jnp.mean(e * xhat, axis=-1, keepdims=True)
    )
    return inner, jnp.sum(grad * xhat, axis=(0, 1)), jnp.sum(grad, axis=(0, 1))


def dot(spec, a, b):
    return jnp.einsum(spec, a, b, preferred_element_type=f32)


MESH = pl.DeviceIdType.MESH


def remote(src, dst, send, recv, device):
    return pltpu.make_async_remote_copy(
        src_ref=src,
        dst_ref=dst,
        send_sem=send,
        recv_sem=recv,
        device_id=device,
        device_id_type=MESH,
    )


class Place:
    def __init__(self, dp, head):
        self.dp, self.head = dp, head
        self.lines = dp // 2
        self.d, self.s = lax.axis_index("dp"), lax.axis_index("head")
        self.z, self.y = self.d // 2, self.d % 2
        self.x, self.c = self.s // 2, self.s % 2

    def z_next(self, k):
        return (self.z + k) % self.lines

    def head_next(self, k):
        return (self.s + k) % self.head

    def dp_next(self, k):
        return (self.d + k) % self.dp

    def greet(self):
        barrier = pltpu.get_barrier_semaphore()
        for k in range(1, self.head):
            pl.semaphore_signal(
                barrier, inc=1, device_id=(self.d, self.head_next(k)), device_id_type=MESH
            )
        for k in range(1, self.dp):
            pl.semaphore_signal(
                barrier, inc=1, device_id=(self.dp_next(k), self.s), device_id_type=MESH
            )
        pl.semaphore_wait(barrier, self.head - 1 + self.dp - 1)


class Scatter:
    def __init__(self, at, src, from_y, to_z, from_z, sems):
        self.at, self.src = at, src
        self.from_y, self.to_z, self.from_z = from_y, to_z, from_z
        self.y_send, self.y_recv, self.z_send, self.z_recv = sems
        self.rows = src.shape[0] // at.dp

    def block(self, z, y):
        return self.src.at[pl.ds(pl.multiple_of((z * 2 + y) * self.rows, self.rows), self.rows)]

    def y_copy(self, k):
        at = self.at
        return remote(
            self.block(at.z_next(k), 1 - at.y),
            self.from_y.at[k],
            self.y_send.at[k],
            self.y_recv.at[k],
            (at.z * 2 + 1 - at.y, at.s),
        )

    def z_copy(self, k):
        at = self.at
        return remote(
            self.to_z.at[k - 1],
            self.from_z.at[k - 1],
            self.z_send.at[k - 1],
            self.z_recv.at[k - 1],
            (at.z_next(k) * 2 + at.y, at.s),
        )

    def start(self):
        for k in (*range(1, self.at.lines), 0):
            self.y_copy(k).start()

    def middle(self, k):
        at = self.at
        self.y_copy(k).wait_recv()
        self.to_z[k - 1] = (
            self.block(at.z_next(k), at.y)[...].astype(f32) + self.from_y[k].astype(f32)
        ).astype(bf16)
        self.z_copy(k).start()

    def finish(self, out):
        at = self.at
        self.y_copy(0).wait_recv()
        total = self.block(at.z, at.y)[...].astype(f32) + self.from_y[0].astype(f32)
        for k in range(1, at.lines):
            self.z_copy(k).wait_recv()
            total = total + self.from_z[k - 1].astype(f32)
        out[...] = total

    def drain(self):
        for k in range(self.at.lines):
            self.y_copy(k).wait_send()
        for k in range(1, self.at.lines):
            self.z_copy(k).wait_send()


class Exchange:
    def __init__(self, at, axis, slots, sems):
        self.at, self.axis, self.slots = at, axis, slots
        self.send, self.recv = sems
        self.count = at.dp if axis == "dp" else at.head
        self.me = at.d if axis == "dp" else at.s

    def peer(self, k):
        return (self.me + k) % self.count

    def copy(self, k, block):
        at = self.at
        device = (self.peer(k), at.s) if self.axis == "dp" else (at.d, self.peer(k))
        return remote(
            block, self.slots.at[self.me], self.send.at[k - 1], self.recv.at[k - 1], device
        )

    def start(self, block_for):
        for k in range(1, self.count):
            self.copy(k, block_for(self.peer(k))).start()

    def wait(self, block_for):
        for k in range(1, self.count):
            self.copy(k, block_for(self.peer(k))).wait_recv()

    def drain(self, block_for):
        for k in range(1, self.count):
            self.copy(k, block_for(self.peer(k))).wait_send()

    def total(self):
        total = self.slots[0]
        for k in range(1, self.count):
            total = total + self.slots[k]
        return total


def tail_kernel(dp, head, count, *refs):
    grads, (taps, small) = refs[:count], refs[count : count + 2]
    refs = refs[count + 2 :]
    outs, (taps_out, small_out) = refs[:count], refs[count : count + 2]
    refs = refs[count + 2 :]
    scratch = [refs[i * 7 : i * 7 + 7] for i in range(count)]
    refs = refs[count * 7 :]
    (taps_slots, taps_sum, small_head, small_sum, small_dp) = refs[:5]
    tr_s, tr_r, tg_s, tg_r, sh_s, sh_r, sd_s, sd_r = refs[5:]
    at = Place(dp, head)
    at.greet()
    scatters = [Scatter(at, g, *s[:3], s[3:]) for g, s in zip(grads, scratch)]

    def tap_rows(d):
        return taps.at[pl.ds(pl.multiple_of(d * 8, 8), 8)]

    taps_in = Exchange(at, "dp", taps_slots, (tr_s, tr_r))
    taps_back = Exchange(at, "dp", taps_sum, (tg_s, tg_r))
    heads = Exchange(at, "head", small_head, (sh_s, sh_r))
    everyone = Exchange(at, "dp", small_dp, (sd_s, sd_r))
    heads.start(lambda s: small.at[s])
    taps_in.start(tap_rows)
    for scatter in scatters:
        scatter.start()
    small_head[at.s] = small[at.s]
    taps_slots[at.d] = tap_rows(at.d)[...]
    heads.wait(lambda s: small.at[s])
    small_dp[at.d] = heads.total()
    everyone.start(lambda d: small_dp.at[at.d])
    taps_in.wait(tap_rows)
    taps_sum[at.d] = taps_in.total()
    taps_back.start(lambda d: taps_sum.at[at.d])
    for scatter in scatters:
        for k in range(1, at.lines):
            scatter.middle(k)
    everyone.wait(lambda d: small_dp.at[at.d])
    small_out[...] = everyone.total()
    taps_back.wait(lambda d: taps_sum.at[at.d])
    taps_out[...] = taps_sum[...]
    for scatter, out in zip(scatters, outs):
        scatter.finish(out)
    for scatter in scatters:
        scatter.drain()
    heads.drain(lambda s: small.at[s])
    everyone.drain(lambda d: small_dp.at[at.d])
    taps_in.drain(tap_rows)
    taps_back.drain(lambda d: taps_sum.at[at.d])


def tail_call(dp, head, grads, taps, small):
    dma = pltpu.SemaphoreType.DMA
    lines = dp // 2
    scratch = []
    for grad in grads:
        block = (grad.shape[0] // dp, grad.shape[1])
        scratch += [
            pltpu.VMEM((lines, *block), bf16),
            pltpu.VMEM((lines - 1, *block), bf16),
            pltpu.VMEM((lines - 1, *block), bf16),
            dma((lines,)),
            dma((lines,)),
            dma((lines - 1,)),
            dma((lines - 1,)),
        ]
    eight = (8, taps.shape[1])
    tiny = small.shape[1:]
    scratch += [
        pltpu.VMEM((dp, *eight), f32),
        pltpu.VMEM((dp, *eight), f32),
        pltpu.VMEM((head, *tiny), f32),
        pltpu.VMEM(tiny, f32),
        pltpu.VMEM((dp, *tiny), f32),
    ]
    scratch += [dma((dp - 1,))] * 4 + [dma((head - 1,))] * 2 + [dma((dp - 1,))] * 2
    out_shape = [jax.ShapeDtypeStruct((g.shape[0] // dp, g.shape[1]), f32) for g in grads]
    out_shape += [jax.ShapeDtypeStruct((dp, *eight), f32), jax.ShapeDtypeStruct(tiny, f32)]
    vmem = pl.BlockSpec(memory_space=pltpu.VMEM)
    return pl.pallas_call(
        functools.partial(tail_kernel, dp, head, len(grads)),
        out_shape=out_shape,
        in_specs=[vmem] * (len(grads) + 2),
        out_specs=[vmem] * len(out_shape),
        scratch_shapes=scratch,
        compiler_params=pltpu.CompilerParams(
            collective_id=0, has_side_effects=True, vmem_limit_bytes=56 * 2**20
        ),
    )(*grads, taps, small)


def plain(
    fused,
    tokens,
    ln1_gain,
    ln1_shift,
    w_qkv,
    w_proj,
    mix_pre,
    mix_post,
    ln2_gain,
    ln2_shift,
    w_up,
    conv_kernel,
    w_down,
    out_grad,
):
    images, seq, width = tokens.shape
    heads_local, heads = mix_pre.shape
    size = width // heads
    scale = size ** (-0.5)
    ksize = conv_kernel.shape[0]
    units = conv_kernel.shape[2]
    grid = int(round((seq - 1) ** 0.5))
    cos, sin, cos_lag, sin_lag, back = spectrum(grid, ksize)
    fourier = jnp.asarray(np.stack([cos, sin]), bf16)
    lagged = jnp.asarray(np.stack([cos_lag, sin_lag]), f32)
    lagged_back = jnp.asarray(np.stack([cos_lag, sin_lag]) * back[:, None], f32)
    mine = lax.axis_index("head")

    gains = jnp.stack([ln1_gain, ln1_shift, ln2_gain, ln2_shift])
    gains = lax.all_gather(gains, "dp", axis=1, tiled=True).astype(f32)
    gain_one, shift_one, gain_two, shift_two = gains[0], gains[1], gains[2], gains[3]
    qkv_w = lax.all_gather(w_qkv, "dp", axis=0, tiled=True)
    up_w = lax.all_gather(w_up, "dp", axis=0, tiled=True)
    down_w = lax.all_gather(w_down, "dp", axis=1, tiled=True)
    proj_w = lax.all_gather(w_proj, "head", axis=0, tiled=True)
    proj_w = lax.all_gather(proj_w, "dp", axis=1, tiled=True)
    mixes = lax.all_gather(jnp.stack([mix_pre, mix_post]), "head", axis=1, tiled=True)
    pre, post_mix = mixes[0], mixes[1]

    source = tokens.astype(f32)
    normed_one, xhat_one, rs_one = layer_norm(source, gain_one, shift_one)
    normed_one = normed_one.astype(bf16)
    qkv = dot("ind,dce->ince", normed_one, qkv_w).astype(bf16)
    qkv = lax.all_to_all(qkv, "head", split_axis=0, concat_axis=3, tiled=True)
    own = qkv.shape[0]
    query = qkv[:, :, 0].reshape(own, seq, heads, size)
    keys = qkv[:, :, 1].reshape(own, seq, heads, size)
    values = qkv[:, :, 2].reshape(own, seq, heads, size)
    scores = (dot("inhd,imhd->ihnm", query, keys) * scale).astype(bf16)
    mixed = jnp.einsum("hg,ignm->ihnm", pre, scores.astype(f32), precision=highest)
    probs = jax.nn.softmax(mixed, axis=-1)
    probs_low = probs.astype(bf16)
    post = jnp.einsum(
        "hg,ignm->ihnm", post_mix, probs_low.astype(f32), precision=highest
    ).astype(bf16)
    heads_own = dot("ihnm,imhd->inhd", post, values).reshape(own, seq, width).astype(bf16)
    heads_out = lax.all_gather(heads_own, "head", axis=0, tiled=True)
    middle = source + dot("ine,ed->ind", heads_out, proj_w)
    normed_two, xhat_two, rs_two = layer_norm(middle, gain_two, shift_two)
    normed_two = normed_two.astype(bf16)
    hidden = dot("ind,df->inf", normed_two, up_w)
    erf = lax.erf(hidden * (0.5**0.5))
    activ = 0.5 * hidden * (1.0 + erf)
    slope = 0.5 * (1.0 + erf) + hidden * jnp.exp(-0.5 * hidden * hidden) * 0.3989422804014327
    delta = np.zeros((ksize * ksize, 1), np.float32)
    delta[ksize * ksize // 2] = 1.0
    taps = conv_kernel.reshape(ksize * ksize, units)
    filters = jnp.einsum("zkl,lf->zkf", lagged, taps, precision=highest)
    cos_k, sin_k = filters[0] + 1.0, filters[1]
    wave = dot("zkn,inf->zikf", fourier, activ.astype(bf16))
    cos_a, sin_a = wave[0], wave[1]
    filtered = jnp.stack([cos_k * cos_a + sin_k * sin_a, cos_k * sin_a - sin_k * cos_a])
    widened = dot("zkn,zikf->inf", fourier, filtered.astype(bf16)).astype(bf16)
    branch = dot("inf,fd->ind", widened, down_w)
    branch = lax.psum(branch.astype(bf16), "head").astype(f32)
    output = (middle + branch).astype(bf16)

    down_grad = dot("inf,ind->fd", widened, out_grad)
    widened_grad = dot("ind,fd->inf", out_grad, down_w)
    wave_grad = dot("zkn,inf->zikf", fourier, widened_grad.astype(bf16))
    cos_g, sin_g = wave_grad[0], wave_grad[1]
    spread_grad = jnp.stack([cos_k * cos_g - sin_k * sin_g, cos_k * sin_g + sin_k * cos_g])
    activ_grad = dot("zkn,zikf->inf", fourier, spread_grad.astype(bf16))
    hidden_grad = (activ_grad * slope).astype(bf16)
    cross = jnp.stack(
        [
            jnp.sum(cos_a * cos_g + sin_a * sin_g, axis=0),
            jnp.sum(sin_a * cos_g - cos_a * sin_g, axis=0),
        ]
    )
    kernel_grad = jnp.einsum("zkl,zkf->lf", lagged_back, cross, precision=highest)
    up_grad = dot("ind,inf->df", normed_two, hidden_grad)
    two_grad = dot("inf,df->ind", hidden_grad, up_w).astype(bf16)
    two_grad = lax.psum_scatter(two_grad, "head", scatter_dimension=0, tiled=True).astype(f32)

    def pick(array):
        return lax.dynamic_slice_in_dim(array, mine * own, own, 0)

    middle_from, gain_two_grad, shift_two_grad = norm_back(
        two_grad, gain_two, pick(xhat_two), pick(rs_two)
    )
    middle_grad = pick(out_grad).astype(f32) + middle_from
    attention_own = middle_grad.astype(bf16)
    attention_grad = lax.all_gather(attention_own, "head", axis=0, tiled=True)
    local = width // lax.axis_size("head")
    heads_mine = lax.dynamic_slice_in_dim(heads_out, mine * local, local, 2)
    proj_grad = dot("ine,ind->ed", heads_mine, attention_grad)
    heads_grad = dot("ind,ed->ine", attention_own, proj_w).astype(bf16)
    heads_grad = heads_grad.reshape(own, seq, heads, size)
    values_grad = dot("ihnm,inhd->imhd", post, heads_grad)
    post_grad = dot("inhd,imhd->ihnm", heads_grad, values)
    probs_grad = jnp.einsum("hg,ihnm->ignm", post_mix, post_grad, precision=highest)
    mixed_grad = probs * (probs_grad - jnp.sum(probs_grad * probs, axis=-1, keepdims=True))
    scores_grad = jnp.einsum("hg,ihnm->ignm", pre, mixed_grad, precision=highest).astype(bf16)
    post_mix_grad = dot("ihnm,ignm->hg", post_grad.astype(bf16), probs_low)
    pre_mix_grad = dot("ihnm,ignm->hg", mixed_grad.astype(bf16), scores)
    query_grad = dot("ihnm,imhd->inhd", scores_grad, keys) * scale
    keys_grad = dot("ihnm,inhd->imhd", scores_grad, query) * scale
    qkv_grad = jnp.stack([query_grad, keys_grad, values_grad], axis=2)
    qkv_grad = qkv_grad.reshape(own, seq, 3, width).astype(bf16)
    qkv_grad = lax.all_to_all(qkv_grad, "head", split_axis=3, concat_axis=0, tiled=True)
    qkv_weight_grad = dot("ind,ince->dce", normed_one, qkv_grad)
    one_grad = dot("ince,dce->ind", qkv_grad, qkv_w).astype(bf16)
    one_grad = lax.psum_scatter(one_grad, "head", scatter_dimension=0, tiled=True).astype(f32)
    source_grad, gain_one_grad, shift_one_grad = norm_back(
        one_grad, gain_one, pick(xhat_one), pick(rs_one)
    )
    input_own = (middle_grad + source_grad).astype(bf16)
    input_grad = lax.all_gather(input_own, "head", axis=0, tiled=True)

    if fused:
        dp, head = lax.axis_size("dp"), lax.axis_size("head")
        norm_grads = jnp.stack([gain_one_grad, shift_one_grad, gain_two_grad, shift_two_grad])
        mix_grads = jnp.stack([pre_mix_grad, post_mix_grad], axis=1).reshape(head, heads_local, 2, heads)
        small = jnp.zeros((head, 8, width + 256), f32)
        small = small.at[:, :4, :width].set(norm_grads[None])
        small = small.at[:, :heads_local, width : width + heads].set(mix_grads[:, :, 0])
        small = small.at[:, :heads_local, width + 128 : width + 128 + heads].set(mix_grads[:, :, 1])
        taps_grad = jnp.pad(kernel_grad, ((0, dp * 8 - ksize * ksize), (0, 0)))
        grads = [
            up_grad.astype(bf16),
            down_grad.T.astype(bf16),
            jnp.pad(qkv_weight_grad.reshape(width, -1), ((0, 0), (0, 64))).astype(bf16),
            jnp.pad(proj_grad.T, ((0, 0), (0, 64))).astype(bf16),
        ]
        up_g, down_g, qkv_g, proj_g, taps_g, small_g = tail_call(dp, head, grads, taps_grad, small)
        rows = width // dp
        norms = lax.dynamic_slice(small_g, (0, lax.axis_index("dp") * rows), (4, rows))
        return (
            output,
            input_grad,
            norms[0],
            norms[1],
            qkv_g[:, : 3 * local].reshape(rows, 3, local),
            proj_g[:, :local].T,
            small_g[:heads_local, width : width + heads],
            small_g[:heads_local, width + 128 : width + 128 + heads],
            norms[2],
            norms[3],
            up_g,
            taps_g.reshape(dp * 8, units)[: ksize * ksize].reshape(ksize, ksize, units),
            down_g.T,
        )

    def share(grad, axis):
        return lax.psum_scatter(
            grad.astype(bf16), "dp", scatter_dimension=axis, tiled=True
        ).astype(f32)

    norm_grads = jnp.stack([gain_one_grad, shift_one_grad, gain_two_grad, shift_two_grad])
    norm_grads = lax.psum(norm_grads, "head")
    norm_grads = lax.psum_scatter(norm_grads, "dp", scatter_dimension=1, tiled=True)
    mix_grads = lax.psum_scatter(
        jnp.stack([pre_mix_grad, post_mix_grad]), "head", scatter_dimension=1, tiled=True
    )
    mix_grads, kernel_grad = lax.psum((mix_grads, kernel_grad), "dp")
    return (
        output,
        input_grad,
        norm_grads[0],
        norm_grads[1],
        share(qkv_weight_grad, 0),
        share(proj_grad, 1),
        mix_grads[0],
        mix_grads[1],
        norm_grads[2],
        norm_grads[3],
        share(up_grad, 0),
        kernel_grad.reshape(ksize, ksize, units),
        share(down_grad, 1),
    )


def solution(mesh):
    in_specs = (
        P("dp", None, None),
        P("dp"),
        P("dp"),
        P("dp", None, "head"),
        P("head", "dp"),
        P("head", None),
        P("head", None),
        P("dp"),
        P("dp"),
        P("dp", "head"),
        P(None, None, "head"),
        P("head", "dp"),
        P("dp", None, None),
    )
    out_specs = (
        P("dp", None, None),
        P("dp", None, None),
        P("dp"),
        P("dp"),
        P("dp", None, "head"),
        P("head", "dp"),
        P("head", None),
        P("head", None),
        P("dp"),
        P("dp"),
        P("dp", "head"),
        P(None, None, "head"),
        P("head", "dp"),
    )
    fused = mesh.shape["dp"] == 8 and mesh.shape["head"] == 4
    return jax.shard_map(functools.partial(plain, fused), mesh=mesh, in_specs=in_specs, out_specs=out_specs, check_vma=False)
```

```python
import functools
import types

import jax
import jax.numpy as jnp
import numpy as np
from jax import lax
from jax.experimental import pallas as pl
from jax.experimental.pallas import tpu as pltpu
from jax.sharding import PartitionSpec as P

highest = lax.Precision.HIGHEST
epsilon = 1e-06
bf16 = jnp.bfloat16
f32 = jnp.float32


def spectrum(grid, ksize):
    margin = ksize // 2
    period = grid + margin
    pairs = [(0, 0)] + [(0, v) for v in range(1, period // 2 + 1)]
    pairs += [(u, v) for u in range(1, period // 2 + 1) for v in range(period)]
    freq = np.array(pairs, np.float64)
    place = np.array([(r, c) for r in range(grid) for c in range(grid)], np.float64)
    lags = np.array([(p - margin, q - margin) for p in range(ksize) for q in range(ksize)], np.float64)
    weight = np.sqrt(np.where(np.arange(len(pairs)) == 0, 1.0, 2.0)) / period
    angle = 2 * np.pi / period * freq @ place.T
    angle_lag = 2 * np.pi / period * freq @ lags.T
    count = len(pairs)
    cos = np.zeros((count + 1, grid * grid + 1))
    sin = np.zeros_like(cos)
    cos[:count, 1:] = weight[:, None] * np.cos(angle)
    sin[:count, 1:] = weight[:, None] * np.sin(angle)
    cos[count, 0] = 1.0
    cos_lag = np.zeros((count + 1, ksize * ksize))
    sin_lag = np.zeros_like(cos_lag)
    cos_lag[:count] = np.cos(angle_lag)
    sin_lag[:count] = np.sin(angle_lag)
    back = np.zeros(count + 1)
    back[:count] = 1.0
    return cos, sin, cos_lag, sin_lag, back


def layer_norm(values, gain, shift):
    center = jnp.mean(values, axis=-1, keepdims=True)
    centered = values - center
    spread = jnp.mean(centered * centered, axis=-1, keepdims=True)
    rs = lax.rsqrt(spread + epsilon)
    xhat = centered * rs
    return xhat * gain + shift, xhat, rs


def norm_back(grad, gain, xhat, rs):
    e = grad * gain
    inner = rs * (
        e
        - jnp.mean(e, axis=-1, keepdims=True)
        - xhat * jnp.mean(e * xhat, axis=-1, keepdims=True)
    )
    return inner, jnp.sum(grad * xhat, axis=(0, 1)), jnp.sum(grad, axis=(0, 1))


def dot(spec, a, b):
    return jnp.einsum(spec, a, b, preferred_element_type=f32)


def plain(
    tokens,
    ln1_gain,
    ln1_shift,
    w_qkv,
    w_proj,
    mix_pre,
    mix_post,
    ln2_gain,
    ln2_shift,
    w_up,
    conv_kernel,
    w_down,
    out_grad,
):
    images, seq, width = tokens.shape
    heads_local, heads = mix_pre.shape
    size = width // heads
    scale = size ** (-0.5)
    ksize = conv_kernel.shape[0]
    units = conv_kernel.shape[2]
    grid = int(round((seq - 1) ** 0.5))
    cos, sin, cos_lag, sin_lag, back = spectrum(grid, ksize)
    fourier = jnp.asarray(np.stack([cos, sin]), bf16)
    lagged = jnp.asarray(np.stack([cos_lag, sin_lag]), f32)
    lagged_back = jnp.asarray(np.stack([cos_lag, sin_lag]) * back[:, None], f32)
    mine = lax.axis_index("head")

    gains = jnp.stack([ln1_gain, ln1_shift, ln2_gain, ln2_shift])
    gains = lax.all_gather(gains, "dp", axis=1, tiled=True).astype(f32)
    gain_one, shift_one, gain_two, shift_two = gains[0], gains[1], gains[2], gains[3]
    qkv_w = lax.all_gather(w_qkv, "dp", axis=0, tiled=True)
    up_w = lax.all_gather(w_up, "dp", axis=0, tiled=True)
    down_w = lax.all_gather(w_down, "dp", axis=1, tiled=True)
    proj_w = lax.all_gather(w_proj, "head", axis=0, tiled=True)
    proj_w = lax.all_gather(proj_w, "dp", axis=1, tiled=True)
    mixes = lax.all_gather(jnp.stack([mix_pre, mix_post]), "head", axis=1, tiled=True)
    pre, post_mix = mixes[0], mixes[1]

    source = tokens.astype(f32)
    normed_one, xhat_one, rs_one = layer_norm(source, gain_one, shift_one)
    normed_one = normed_one.astype(bf16)
    qkv = dot("ind,dce->ince", normed_one, qkv_w).astype(bf16)
    qkv = lax.all_to_all(qkv, "head", split_axis=0, concat_axis=3, tiled=True)
    own = qkv.shape[0]
    query = qkv[:, :, 0].reshape(own, seq, heads, size)
    keys = qkv[:, :, 1].reshape(own, seq, heads, size)
    values = qkv[:, :, 2].reshape(own, seq, heads, size)
    scores = (dot("inhd,imhd->ihnm", query, keys) * scale).astype(bf16)
    mixed = jnp.einsum("hg,ignm->ihnm", pre, scores.astype(f32), precision=highest)
    probs = jax.nn.softmax(mixed, axis=-1)
    probs_low = probs.astype(bf16)
    post = jnp.einsum(
        "hg,ignm->ihnm", post_mix, probs_low.astype(f32), precision=highest
    ).astype(bf16)
    heads_own = dot("ihnm,imhd->inhd", post, values).reshape(own, seq, width).astype(bf16)
    heads_out = lax.all_gather(heads_own, "head", axis=0, tiled=True)
    middle = source + dot("ine,ed->ind", heads_out, proj_w)
    normed_two, xhat_two, rs_two = layer_norm(middle, gain_two, shift_two)
    normed_two = normed_two.astype(bf16)
    hidden = dot("ind,df->inf", normed_two, up_w)
    erf = lax.erf(hidden * (0.5**0.5))
    activ = 0.5 * hidden * (1.0 + erf)
    slope = 0.5 * (1.0 + erf) + hidden * jnp.exp(-0.5 * hidden * hidden) * 0.3989422804014327
    delta = np.zeros((ksize * ksize, 1), np.float32)
    delta[ksize * ksize // 2] = 1.0
    taps = conv_kernel.reshape(ksize * ksize, units)
    filters = jnp.einsum("zkl,lf->zkf", lagged, taps, precision=highest)
    cos_k, sin_k = filters[0] + 1.0, filters[1]
    wave = dot("zkn,inf->zikf", fourier, activ.astype(bf16))
    cos_a, sin_a = wave[0], wave[1]
    filtered = jnp.stack([cos_k * cos_a + sin_k * sin_a, cos_k * sin_a - sin_k * cos_a])
    widened = dot("zkn,zikf->inf", fourier, filtered.astype(bf16)).astype(bf16)
    branch = dot("inf,fd->ind", widened, down_w)
    branch = lax.psum(branch.astype(bf16), "head").astype(f32)
    output = (middle + branch).astype(bf16)

    down_grad = dot("inf,ind->fd", widened, out_grad)
    widened_grad = dot("ind,fd->inf", out_grad, down_w)
    wave_grad = dot("zkn,inf->zikf", fourier, widened_grad.astype(bf16))
    cos_g, sin_g = wave_grad[0], wave_grad[1]
    spread_grad = jnp.stack([cos_k * cos_g - sin_k * sin_g, cos_k * sin_g + sin_k * cos_g])
    activ_grad = dot("zkn,zikf->inf", fourier, spread_grad.astype(bf16))
    hidden_grad = (activ_grad * slope).astype(bf16)
    cross = jnp.stack(
        [
            jnp.sum(cos_a * cos_g + sin_a * sin_g, axis=0),
            jnp.sum(sin_a * cos_g - cos_a * sin_g, axis=0),
        ]
    )
    kernel_grad = jnp.einsum("zkl,zkf->lf", lagged_back, cross, precision=highest)
    up_grad = dot("ind,inf->df", normed_two, hidden_grad)
    two_grad = dot("inf,df->ind", hidden_grad, up_w).astype(bf16)
    two_grad = lax.psum_scatter(two_grad, "head", scatter_dimension=0, tiled=True).astype(f32)

    def pick(array):
        return lax.dynamic_slice_in_dim(array, mine * own, own, 0)

    middle_from, gain_two_grad, shift_two_grad = norm_back(
        two_grad, gain_two, pick(xhat_two), pick(rs_two)
    )
    middle_grad = pick(out_grad).astype(f32) + middle_from
    attention_own = middle_grad.astype(bf16)
    attention_grad = lax.all_gather(attention_own, "head", axis=0, tiled=True)
    local = width // lax.axis_size("head")
    heads_mine = lax.dynamic_slice_in_dim(heads_out, mine * local, local, 2)
    proj_grad = dot("ine,ind->ed", heads_mine, attention_grad)
    heads_grad = dot("ind,ed->ine", attention_own, proj_w).astype(bf16)
    heads_grad = heads_grad.reshape(own, seq, heads, size)
    values_grad = dot("ihnm,inhd->imhd", post, heads_grad)
    post_grad = dot("inhd,imhd->ihnm", heads_grad, values)
    probs_grad = jnp.einsum("hg,ihnm->ignm", post_mix, post_grad, precision=highest)
    mixed_grad = probs * (probs_grad - jnp.sum(probs_grad * probs, axis=-1, keepdims=True))
    scores_grad = jnp.einsum("hg,ihnm->ignm", pre, mixed_grad, precision=highest).astype(bf16)
    post_mix_grad = dot("ihnm,ignm->hg", post_grad.astype(bf16), probs_low)
    pre_mix_grad = dot("ihnm,ignm->hg", mixed_grad.astype(bf16), scores)
    query_grad = dot("ihnm,imhd->inhd", scores_grad, keys) * scale
    keys_grad = dot("ihnm,inhd->imhd", scores_grad, query) * scale
    qkv_grad = jnp.stack([query_grad, keys_grad, values_grad], axis=2)
    qkv_grad = qkv_grad.reshape(own, seq, 3, width).astype(bf16)
    qkv_grad = lax.all_to_all(qkv_grad, "head", split_axis=3, concat_axis=0, tiled=True)
    qkv_weight_grad = dot("ind,ince->dce", normed_one, qkv_grad)
    one_grad = dot("ince,dce->ind", qkv_grad, qkv_w).astype(bf16)
    one_grad = lax.psum_scatter(one_grad, "head", scatter_dimension=0, tiled=True).astype(f32)
    source_grad, gain_one_grad, shift_one_grad = norm_back(
        one_grad, gain_one, pick(xhat_one), pick(rs_one)
    )
    input_own = (middle_grad + source_grad).astype(bf16)
    input_grad = lax.all_gather(input_own, "head", axis=0, tiled=True)

    def share(grad, axis):
        return lax.psum_scatter(
            grad.astype(bf16), "dp", scatter_dimension=axis, tiled=True
        ).astype(f32)

    norm_grads = jnp.stack([gain_one_grad, shift_one_grad, gain_two_grad, shift_two_grad])
    norm_grads = lax.psum(norm_grads, "head")
    norm_grads = lax.psum_scatter(norm_grads, "dp", scatter_dimension=1, tiled=True)
    mix_grads = lax.psum_scatter(
        jnp.stack([pre_mix_grad, post_mix_grad]), "head", scatter_dimension=1, tiled=True
    )
    mix_grads, kernel_grad = lax.psum((mix_grads, kernel_grad), "dp")
    return (
        output,
        input_grad,
        norm_grads[0],
        norm_grads[1],
        share(qkv_weight_grad, 0),
        share(proj_grad, 1),
        mix_grads[0],
        mix_grads[1],
        norm_grads[2],
        norm_grads[3],
        share(up_grad, 0),
        kernel_grad.reshape(ksize, ksize, units),
        share(down_grad, 1),
    )


MESH = pl.DeviceIdType.MESH
NT = (((1,), (1,)), ((), ()))


def mm(a, b):
    return jnp.dot(a, b, preferred_element_type=f32)


def mm_nt(a, b):
    return lax.dot_general(a, b, NT, preferred_element_type=f32)


def exact(a, b):
    return jnp.dot(a, b, preferred_element_type=f32, precision=highest)


def split(a):
    high = a.astype(bf16)
    return high, (a - high.astype(f32)).astype(bf16)


def remote(src, dst, send, recv, device):
    return pltpu.make_async_remote_copy(
        src_ref=src,
        dst_ref=dst,
        send_sem=send,
        recv_sem=recv,
        device_id=device,
        device_id_type=MESH,
    )


class Place:
    def __init__(self, dp, head):
        self.dp, self.head = dp, head
        self.lines = dp // 2
        self.d, self.s = lax.axis_index("dp"), lax.axis_index("head")
        self.z, self.y = self.d // 2, self.d % 2
        self.x, self.c = self.s // 2, self.s % 2
        self.mate = self.x * 2 + 1 - self.c
        self.across = (1 - self.x) * 2 + self.c
        self.corner = (1 - self.x) * 2 + 1 - self.c

    def near(self, j):
        return ((self.x + j // 2) % 2) * 2 + (self.c + j % 2) % 2

    def z_next(self, k):
        return (self.z + k) % self.lines

    def z_prev(self, k):
        return (self.z + self.lines - k) % self.lines

    def head_next(self, k):
        return (self.s + k) % self.head

    def dp_next(self, k):
        return (self.d + k) % self.dp

    def call(self):
        barrier = pltpu.get_barrier_semaphore()
        for k in range(1, self.head):
            pl.semaphore_signal(
                barrier, inc=1, device_id=(self.d, self.head_next(k)), device_id_type=MESH
            )
        for k in range(1, self.dp):
            pl.semaphore_signal(
                barrier, inc=1, device_id=(self.dp_next(k), self.s), device_id_type=MESH
            )

    def answer(self):
        pl.semaphore_wait(pltpu.get_barrier_semaphore(), self.head - 1 + self.dp - 1)


def rows_of(ref, index, count):
    return ref.at[pl.ds(pl.multiple_of(index * count, count), count)]


class Gather:
    def __init__(self, at, buf, sems, wide):
        self.at, self.wide = at, wide
        self.groups = buf
        self.buf = buf.at[at.s] if wide else buf
        self.rows = self.buf.shape[0] // at.dp
        self.sems = sems

    def block(self, k, other, buf=None):
        at = self.at
        y = 1 - at.y if other else at.y
        return rows_of(self.buf if buf is None else buf, at.z_prev(k) * 2 + y, self.rows)

    def z_copy(self, k):
        at, (send, recv) = self.at, self.sems[0]
        ref = self.block(0, False)
        return remote(ref, ref, send.at[k - 1], recv.at[k - 1], (at.z_next(k) * 2 + at.y, at.s))

    def y_copy(self, k):
        at, (send, recv) = self.at, self.sems[1]
        ref = self.block(k, False)
        return remote(ref, ref, send.at[k], recv.at[k], (at.z * 2 + 1 - at.y, at.s))

    def x_copy(self, b):
        at, (send, recv) = self.at, self.sems[2]
        ref = self.block(b % at.lines, b >= at.lines)
        return remote(ref, ref, send.at[b], recv.at[b], (at.d, at.across))

    def mate_copy(self, b, far):
        at, (send, recv) = self.at, self.sems[3]
        ref = self.block(
            b % at.lines, b >= at.lines, self.groups.at[at.across if far else at.s]
        )
        slot = b + at.dp if far else b
        return remote(ref, ref, send.at[slot], recv.at[slot], (at.d, at.mate))

    def on(self, b):
        if self.wide:
            self.x_copy(b).start()
            self.mate_copy(b, False).start()

    def begin(self):
        for k in range(1, self.at.lines):
            self.z_copy(k).start()
        self.y_copy(0).start()
        self.on(0)

    def from_z(self, k):
        self.z_copy(k).wait_recv()
        self.y_copy(k).start()
        self.on(k)

    def from_y(self, k):
        self.y_copy(k).wait_recv()
        self.on(k + self.at.lines)

    def from_x(self, b):
        self.x_copy(b).wait_recv()
        self.mate_copy(b, True).start()

    def from_mate(self, far):
        for b in range(self.at.dp):
            self.mate_copy(b, far).wait_recv()

    def drain(self):
        for k in range(1, self.at.lines):
            self.z_copy(k).wait_send()
        for k in range(self.at.lines):
            self.y_copy(k).wait_send()
        if self.wide:
            for b in range(self.at.dp):
                self.x_copy(b).wait_send()
                self.mate_copy(b, False).wait_send()
                self.mate_copy(b, True).wait_send()


class Share:
    def __init__(self, at, buf, sems):
        self.at, self.buf = at, buf
        self.send, self.recv = sems

    def copy(self, which):
        at = self.at
        ref = self.buf.at[at.across if which == 2 else at.s]
        to = at.across if which == 1 else at.mate
        return remote(ref, ref, self.send.at[which], self.recv.at[which], (at.d, to))

    def start(self):
        self.copy(1).start()
        self.copy(0).start()

    def wait_mate(self):
        self.copy(0).wait_recv()

    def forward(self):
        self.copy(1).wait_recv()
        self.copy(2).start()

    def wait_corner(self):
        self.copy(2).wait_recv()

    def drain(self):
        for which in range(3):
            self.copy(which).wait_send()


class Fold:
    def __init__(self, at, parts, near, far, sems):
        self.at, self.parts, self.near, self.far = at, parts, near, far
        self.send, self.recv = sems

    def mate_copy(self, which):
        at = self.at
        src = self.parts.at[at.corner if which else at.mate]
        return remote(
            src, self.near.at[which], self.send.at[which], self.recv.at[which], (at.d, at.mate)
        )

    def x_copy(self):
        at = self.at
        return remote(
            self.parts.at[at.across], self.far, self.send.at[2], self.recv.at[2], (at.d, at.across)
        )

    def middle(self):
        at = self.at
        self.mate_copy(1).wait_recv()
        self.parts[at.across] = (
            self.parts[at.across].astype(f32) + self.near[1].astype(f32)
        ).astype(bf16)
        self.x_copy().start()

    def wait(self):
        self.mate_copy(0).wait_recv()
        self.x_copy().wait_recv()

    def total(self, rows):
        return (
            self.parts[self.at.s, rows, :].astype(f32)
            + self.near[0, rows, :].astype(f32)
            + self.far[rows, :].astype(f32)
        )

    def drain(self):
        self.mate_copy(0).wait_send()
        self.mate_copy(1).wait_send()
        self.x_copy().wait_send()


class Scatter:
    def __init__(self, at, src, from_y, from_z, sems):
        self.at, self.src, self.from_y, self.from_z = at, src, from_y, from_z
        (self.y_send, self.y_recv), (self.z_send, self.z_recv) = sems
        self.rows = src.shape[0] // at.dp

    def block(self, z, y):
        return rows_of(self.src, z * 2 + y, self.rows)

    def y_copy(self, k):
        at = self.at
        return remote(
            self.block(at.z_next(k), 1 - at.y),
            self.from_y.at[k],
            self.y_send.at[k],
            self.y_recv.at[k],
            (at.z * 2 + 1 - at.y, at.s),
        )

    def z_copy(self, k):
        at = self.at
        return remote(
            self.block(at.z_next(k), at.y),
            self.from_z.at[k - 1],
            self.z_send.at[k - 1],
            self.z_recv.at[k - 1],
            (at.z_next(k) * 2 + at.y, at.s),
        )

    def start(self):
        for k in (*range(1, self.at.lines), 0):
            self.y_copy(k).start()

    def middle(self, k):
        at = self.at
        self.y_copy(k).wait_recv()
        ref = self.block(at.z_next(k), at.y)
        ref[...] = (ref[...].astype(f32) + self.from_y[k].astype(f32)).astype(bf16)
        self.z_copy(k).start()

    def finish(self):
        at = self.at
        self.y_copy(0).wait_recv()
        total = self.block(at.z, at.y)[...].astype(f32) + self.from_y[0].astype(f32)
        for k in range(1, at.lines):
            self.z_copy(k).wait_recv()
            total = total + self.from_z[k - 1].astype(f32)
        return total

    def drain(self):
        for k in range(self.at.lines):
            self.y_copy(k).wait_send()
        for k in range(1, self.at.lines):
            self.z_copy(k).wait_send()


class Exchange:
    def __init__(self, at, axis, slots, sems, block_for):
        self.at, self.axis, self.slots, self.block_for = at, axis, slots, block_for
        self.send, self.recv = sems
        self.count = at.dp if axis == "dp" else at.head
        self.me = at.d if axis == "dp" else at.s

    def copy(self, k):
        at = self.at
        peer = (self.me + k) % self.count
        device = (peer, at.s) if self.axis == "dp" else (at.d, peer)
        return remote(
            self.block_for(peer),
            self.slots.at[self.me],
            self.send.at[k - 1],
            self.recv.at[k - 1],
            device,
        )

    def start(self):
        for k in range(1, self.count):
            self.copy(k).start()

    def wait(self):
        for k in range(1, self.count):
            self.copy(k).wait_recv()

    def drain(self):
        for k in range(1, self.count):
            self.copy(k).wait_send()

    def total(self):
        total = self.slots[0]
        for k in range(1, self.count):
            total = total + self.slots[k]
        return total


def norm_rows(x):
    center = jnp.mean(x, axis=-1, keepdims=True)
    centered = x - center
    spread = jnp.mean(centered * centered, axis=-1, keepdims=True)
    rs = lax.rsqrt(spread + epsilon)
    return centered * rs, rs


def norm_back_rows(grad, gain, xhat, rs):
    e = grad * gain
    return rs * (
        e
        - jnp.mean(e, axis=-1, keepdims=True)
        - xhat * jnp.mean(e * xhat, axis=-1, keepdims=True)
    )


def fold_rows(a):
    return jnp.sum(a.reshape(a.shape[0] // 8, 8, a.shape[1]), axis=0)


def block_kernel(sizes, names_in, names_out, names_scratch, *refs):
    seq, dp, head, scale = sizes
    n_in, n_out = len(names_in), len(names_out)
    i = types.SimpleNamespace(**dict(zip(names_in, refs[:n_in])))
    o = types.SimpleNamespace(**dict(zip(names_out, refs[n_in : n_in + n_out])))
    b = types.SimpleNamespace(**dict(zip(names_scratch, refs[n_in + n_out :])))
    at = Place(dp, head)
    images, padded, width = b.tok.shape
    b.bp, b.dq = b.actg, b.act
    b.dk, b.mg = b.fi.at[:padded], b.wave.at[:padded]
    chunks = padded // 16
    wide = b.k.shape[0]
    slots = b.sc.shape[0]
    pairs = slots // 2
    share = i.wq.shape[0]
    units = b.wu.shape[1]
    bins = b.filt.shape[0] // 2

    def chunk(j):
        return pl.ds(pl.multiple_of(j * 16, 16), 16)

    def tile(p):
        return pl.ds(pl.multiple_of(p * 128, 128), 128)

    def loop(n, body, unroll=1):
        def step(j, carry):
            body(j)
            return carry

        lax.fori_loop(0, n, step, 0, unroll=unroll)

    at.call()
    own_rows = pl.ds(pl.multiple_of(at.d * share, share), share)
    b.wq[at.s, own_rows, :] = i.wq[...]
    b.wp_raw[at.s, own_rows, :] = i.wp[...]
    b.wu[own_rows, :] = i.wu[...]
    b.wd[own_rows, :] = i.wd[...]
    b.gains[at.d] = i.gains[...]
    b.mixes[at.s] = i.mixes[...]
    at.answer()

    gains = Exchange(at, "dp", b.gains, (b.ga_s, b.ga_r), lambda d: i.gains)
    mixes = Exchange(at, "head", b.mixes, (b.mi_s, b.mi_r), lambda s: i.mixes)
    gq = Gather(at, b.wq, ((b.qz_s, b.qz_r), (b.qy_s, b.qy_r), (b.qx_s, b.qx_r), (b.qm_s, b.qm_r)), True)
    gp = Gather(at, b.wp_raw, ((b.pz_s, b.pz_r), (b.py_s, b.py_r), (b.px_s, b.px_r), (b.pm_s, b.pm_r)), True)
    gu = Gather(at, b.wu, ((b.uz_s, b.uz_r), (b.uy_s, b.uy_r)), False)
    gd = Gather(at, b.wd, ((b.dz_s, b.dz_r), (b.dy_s, b.dy_r)), False)
    ho = Share(at, b.ho, (b.ho_s, b.ho_r))
    ag = Share(at, b.ag, (b.ag_s, b.ag_r))
    out = Share(at, o.output, (b.ou_s, b.ou_r))
    inp = Share(at, o.input, (b.in_s, b.in_r))
    fold_two = Fold(at, b.np, b.np_near, b.np_far, (b.np_s, b.np_r))
    fold_out = Fold(at, b.bp, b.bp_near, b.bp_far, (b.bp_s, b.bp_r))
    sc_up = Scatter(at, b.g_up, b.up_y, b.up_z, ((b.uy2_s, b.uy2_r), (b.uz2_s, b.uz2_r)))
    sc_down = Scatter(at, b.g_down, b.down_y, b.down_z, ((b.dy2_s, b.dy2_r), (b.dz2_s, b.dz2_r)))
    sc_qkv = Scatter(at, b.g_qkv, b.qkv_y, b.qkv_z, ((b.qy2_s, b.qy2_r), (b.qz2_s, b.qz2_r)))
    sc_proj = Scatter(at, b.g_proj, b.proj_y, b.proj_z, ((b.py2_s, b.py2_r), (b.pz2_s, b.pz2_r)))
    turn = Exchange(at, "head", b.turned, (b.tu_s, b.tu_r), lambda s: b.turn.at[s])
    taps_in = Exchange(at, "dp", b.taps_slots, (b.ti_s, b.ti_r), lambda d: rows_of(b.taps, d, 8))
    taps_back = Exchange(at, "dp", o.taps, (b.tb_s, b.tb_r), lambda d: o.taps.at[at.d])
    small_head = Exchange(at, "head", b.small_slots, (b.sh_s, b.sh_r), lambda s: b.small.at[s])
    small_dp = Exchange(at, "dp", b.small_dp, (b.sd_s, b.sd_r), lambda d: b.small_dp.at[at.d])

    gains.start()
    mixes.start()
    gq.begin()

    whole = seq // 16 * 16
    for src, dst in ((i.tokens, b.tok), (i.out_grad, b.og)):
        for image in range(images):
            dst[image, :whole, :] = src[image, :whole, :]
            if seq > whole:
                b.edge[...] = jnp.zeros_like(b.edge)
                b.edge[: seq - whole, :] = src[image, whole:, :].astype(f32)
                dst[image, whole:, :] = b.edge[...].astype(bf16)

    b.filt[...] = exact(i.lag[...], i.taps[...])
    b.filt[:bins, :] += 1.0
    b.cross[...] = jnp.zeros_like(b.cross)
    b.mix_one[...] = jnp.zeros_like(b.mix_one)
    b.mix_two[...] = jnp.zeros_like(b.mix_two)
    b.k[padded:, :] = jnp.zeros((wide - padded, width), bf16)
    b.v[padded:, :] = jnp.zeros((wide - padded, width), bf16)

    gains.wait()
    spread = mm(b.gains[...].reshape(dp * 8, 128).astype(bf16), i.comb[...])
    row = lax.broadcasted_iota(jnp.int32, spread.shape, 0)
    lane = lax.broadcasted_iota(jnp.int32, spread.shape, 1)
    first = (row >> 3) * share
    here = (lane >= first) & (lane < first + share)
    for r in range(4):
        b.norms[r : r + 1, :] = jnp.sum(
            jnp.where(here & ((row & 7) == r), spread, 0.0), axis=0, keepdims=True
        )

    def norm_one(image):
        def body(j):
            xhat, _ = norm_rows(b.tok[image, chunk(j), :].astype(f32))
            b.n1[image, chunk(j), :] = (xhat * b.norms[0:1, :] + b.norms[1:2, :]).astype(bf16)

        loop(chunks, body, chunks)

    norm_one(at.s)
    for k in range(1, at.lines):
        gq.from_z(k)
    gp.begin()
    gd.begin()
    gu.begin()

    mixes.wait()
    diagonal = i.diagonal[...]
    for part, piece in enumerate(split(b.mixes[...].reshape(head * 8, 128))):
        for which, pick in enumerate((i.pick_pre, i.pick_post)):
            picked = mm(pick[...], piece).astype(bf16)
            b.kron[which, part] = (mm_nt(picked, i.place[...]) * diagonal).astype(bf16)
            b.kron_t[which, part] = (mm_nt(i.place[...], picked) * diagonal).astype(bf16)

    for k in range(at.lines):
        gq.from_y(k)
    loop(images - 1, lambda j: norm_one(at.head_next(j + 1)))
    for k in range(1, at.lines):
        gp.from_z(k)

    lo = (lax.broadcasted_iota(jnp.int32, (1, 128), 1) < 64).astype(f32)
    low_half = (lax.broadcasted_iota(jnp.int32, (padded, 128), 1)) < 64
    lo_b, hi_b = lo.astype(bf16), (1.0 - lo).astype(bf16)

    def project(g):
        t = mm(b.n1[at.s], b.wq[g])
        b.q[:, tile(g)] = (t[:, :128] * scale).astype(bf16)
        b.k[:padded, tile(g)] = t[:, 128:256].astype(bf16)
        b.v[:padded, tile(g)] = t[:, 256:384].astype(bf16)
        b.third_qk[g] = t[:, 384:512]
        b.third_v[g] = t[:, 512:640]

    project(at.s)
    for k in range(at.lines):
        gp.from_y(k)
    gq.from_mate(False)
    project(at.mate)
    for block in range(dp):
        gq.from_x(block)
    project(at.across)
    gq.from_mate(True)
    project(at.corner)
    for p in range(head // 2):
        one, two = b.third_qk[2 * p], b.third_qk[2 * p + 1]
        third = pl.ds((head + p) * 128, 128)
        b.q[:, third] = (jnp.where(low_half, one, pltpu.roll(two, 64, 1)) * scale).astype(bf16)
        b.k[:padded, third] = jnp.where(low_half, pltpu.roll(one, 64, 1), two).astype(bf16)
        b.v[:padded, third] = jnp.where(
            low_half, b.third_v[2 * p], pltpu.roll(b.third_v[2 * p + 1], 64, 1)
        ).astype(bf16)

    def score(p):
        q, k = b.q[:, tile(p)], b.k[:, tile(p)]
        b.sc[2 * p] = mm_nt(q * lo_b, k).astype(bf16)
        b.sc[2 * p + 1] = mm_nt(q * hi_b, k).astype(bf16)

    loop(pairs, score)

    def mixed(table, which, block):
        return mm(table[which, 0], block) + mm(table[which, 1], block)

    def slab(ref, j):
        return ref[:, chunk(j), :].reshape(slots * 16, wide)

    def put(ref, j, value):
        ref[:, chunk(j), :] = value.reshape(slots, 16, wide)

    beyond = lax.broadcasted_iota(jnp.int32, (slots * 16, wide), 1) >= seq

    def soften(j):
        logits = jnp.where(beyond, -1e30, mixed(b.kron, 0, slab(b.sc, j)))
        top = jnp.max(logits, axis=-1, keepdims=True)
        power = jnp.exp(logits - top)
        probs = power / jnp.sum(power, axis=-1, keepdims=True)
        put(b.pr, j, probs)
        put(b.post, j, mixed(b.kron, 1, probs.astype(bf16)).astype(bf16))
        for k in range(1, at.lines):

            @pl.when(j == 4 * k - 2)
            def _():
                gd.from_z(k)
                gu.from_z(k)

    loop(chunks, soften)

    def gather_heads(p):
        v = b.v[:, tile(p)]
        b.ho[at.s, :, tile(p)] = (mm(b.post[2 * p], v * lo_b) + mm(b.post[2 * p + 1], v * hi_b)).astype(bf16)

    loop(pairs, gather_heads)
    ho.start()

    for block in range(dp):
        gp.from_x(block)
    gp.from_mate(False)
    gp.from_mate(True)
    low_rows = lax.broadcasted_iota(jnp.int32, (width, 128), 1) < 64
    for g in range(head):
        b.wp[:, g * 128 : (g + 1) * 128] = b.wp_raw[g, :, :128]
    for p in range(head // 2):
        one, two = b.wp_raw[2 * p, :, 128:].astype(f32), b.wp_raw[2 * p + 1, :, 128:].astype(f32)
        b.wp[:, (head + p) * 128 : (head + p + 1) * 128] = jnp.where(
            low_rows, one, pltpu.roll(two, 64, 1)
        ).astype(bf16)

    for k in range(at.lines):
        gd.from_y(k)

    def conv_back(image):
        b.act[...] = mm(b.og[image], b.wd[...]).astype(bf16)
        b.wave[...] = mm(i.fourier[...], b.act[...])

        def body(j):
            cos, sin = chunk(j), pl.ds(pl.multiple_of(bins + j * 16, 16), 16)
            cos_g, sin_g = b.wave[cos, :], b.wave[sin, :]
            cos_k, sin_k = b.filt[cos, :], b.filt[sin, :]
            b.gf[image, cos, :] = cos_g.astype(bf16)
            b.gf[image, sin, :] = sin_g.astype(bf16)
            b.fi[cos, :] = (cos_k * cos_g - sin_k * sin_g).astype(bf16)
            b.fi[sin, :] = (cos_k * sin_g + sin_k * cos_g).astype(bf16)

        loop(bins // 16, body)
        b.actg[image] = mm(i.fourier_t[...], b.fi[...]).astype(bf16)

    loop(images, conv_back)
    for k in range(at.lines):
        gu.from_y(k)

    def up(j):
        image = at.near(j)

        @pl.when(j == 1)
        def _():
            ho.wait_mate()

        @pl.when(j == 2)
        def _():
            ho.forward()

        @pl.when(j == 3)
        def _():
            ho.wait_corner()

        b.hid[...] = mm_nt(b.ho[image], b.wp[...])

        def norm_two(r):
            middle = b.tok[image, chunk(r), :].astype(f32) + b.hid[chunk(r), :]
            b.mid[image, chunk(r), :] = middle
            xhat, _ = norm_rows(middle)
            b.n2[image, chunk(r), :] = (xhat * b.norms[2:3, :] + b.norms[3:4, :]).astype(bf16)

        loop(chunks, norm_two, chunks)
        b.hid[...] = mm(b.n2[image], b.wu[...])

        def gelu(r):
            h = b.hid[chunk(r), :]
            cdf = 0.5 * (1.0 + lax.erf(h * (0.5**0.5)))
            slope = cdf + h * jnp.exp(-0.5 * h * h) * 0.3989422804014327
            b.wid[image, chunk(r), :] = (h * cdf).astype(bf16)
            b.hg[image, chunk(r), :] = (b.actg[image, chunk(r), :].astype(f32) * slope).astype(bf16)

        loop(chunks, gelu)
        b.np[image] = mm_nt(b.hg[image], b.wu[...]).astype(bf16)

        @pl.when(j == 1)
        def _():
            fold_two.mate_copy(0).start()

        @pl.when(j == 3)
        def _():
            fold_two.mate_copy(1).start()

    loop(images, up)
    fold_two.middle()

    def down(j):
        image = at.near(j)
        b.wave[...] = mm(i.fourier[...], b.wid[image])

        def body(r):
            cos, sin = chunk(r), pl.ds(pl.multiple_of(bins + r * 16, 16), 16)
            cos_a, sin_a = b.wave[cos, :], b.wave[sin, :]
            cos_k, sin_k = b.filt[cos, :], b.filt[sin, :]
            cos_g, sin_g = b.gf[image, cos, :].astype(f32), b.gf[image, sin, :].astype(f32)
            b.fi[cos, :] = (cos_k * cos_a + sin_k * sin_a).astype(bf16)
            b.fi[sin, :] = (cos_k * sin_a - sin_k * cos_a).astype(bf16)
            b.cross[cos, :] += cos_a * cos_g + sin_a * sin_g
            b.cross[sin, :] += sin_a * cos_g - cos_a * sin_g

        loop(bins // 16, body)
        b.wid[image] = mm(i.fourier_t[...], b.fi[...]).astype(bf16)
        b.bp[image] = mm_nt(b.wid[image], b.wd[...]).astype(bf16)

        @pl.when(j == 1)
        def _():
            fold_out.mate_copy(0).start()

        @pl.when(j == 3)
        def _():
            fold_out.mate_copy(1).start()

    loop(images, down)

    def flip(src):
        def body(r):
            lanes = pl.ds(pl.multiple_of(r * 256, 256), 256)
            block = src[:, :, lanes].reshape(images * padded, 256)
            b.flip[lanes, :] = mm_nt(i.eye[...], block).astype(bf16)

        loop(width // 256, body)

    def weight_grad(dst, right):
        def body(r):
            rows = pl.ds(pl.multiple_of(r * 256, 256), 256)
            dst[rows, :] = mm(b.flip[rows, :], right()).astype(bf16)

        loop(width // 256, body)

    def flat(ref):
        return ref[...].reshape(images * padded, ref.shape[2])

    flip(b.og)
    weight_grad(b.g_down, lambda: flat(b.wid))
    sc_down.start()
    flip(b.n2)
    weight_grad(b.g_up, lambda: flat(b.hg))
    sc_up.start()

    fold_two.wait()

    def back_two(j, carry):
        gain_sum, shift_sum = carry
        grad = fold_two.total(chunk(j))
        xhat, rs = norm_rows(b.mid[at.s, chunk(j), :])
        inner = norm_back_rows(grad, b.norms[2:3, :], xhat, rs)
        total = b.og[at.s, chunk(j), :].astype(f32) + inner
        b.mg[chunk(j), :] = total
        b.ag[at.s, chunk(j), :] = total.astype(bf16)
        return gain_sum + fold_rows(grad * xhat), shift_sum + fold_rows(grad)

    zero = jnp.zeros((8, width), f32)
    gain_sum, shift_sum = lax.fori_loop(0, chunks, back_two, (zero, zero), unroll=True)
    b.sums[2:3, :] = jnp.sum(gain_sum, axis=0, keepdims=True)
    b.sums[3:4, :] = jnp.sum(shift_sum, axis=0, keepdims=True)
    ag.start()
    fold_out.middle()

    b.hgr[...] = mm(b.ag[at.s], b.wp[...]).astype(bf16)

    def flip_one(src, dst):
        def body(r):
            lanes = pl.ds(pl.multiple_of(r * 256, 256), 256)
            dst[lanes, :] = mm_nt(i.eye[...], src[:, lanes]).astype(bf16)

        loop(width // 256, body)

    flip_one(b.hgr, b.hgr_t)
    flip_one(b.q, b.q_t)

    def back_post(p):
        g, v = b.hgr[:, tile(p)], b.v[:, tile(p)]
        for half, mask in enumerate((lo_b, hi_b)):
            b.pg[2 * p + half] = mm_nt(g * mask, v).astype(bf16)
            rows = pl.ds(pl.multiple_of(p * 128 + half * 64, 64), 64)
            b.dv_t[rows, :] = mm(b.hgr_t[rows, :], b.post[2 * p + half]).astype(bf16)

    loop(pairs, back_post)

    for k in range(1, at.lines):
        sc_down.middle(k)

    def back_soften(j):
        grad = slab(b.pg, j)
        probs = slab(b.pr, j)
        b.mix_two[...] += mm_nt(grad, probs.astype(bf16))
        probs_grad = mixed(b.kron_t, 1, grad)
        inner = jnp.sum(probs_grad * probs, axis=-1, keepdims=True)
        mixed_grad = (probs * (probs_grad - inner)).astype(bf16)
        b.mix_one[...] += mm_nt(mixed_grad, slab(b.sc, j))
        put(b.pg, j, mixed(b.kron_t, 0, mixed_grad).astype(bf16))

    loop(chunks, back_soften)

    def back_score(p):
        k = b.k[:, tile(p)]
        b.dq[:, tile(p)] = (
            (mm(b.pg[2 * p], k * lo_b) + mm(b.pg[2 * p + 1], k * hi_b)) * scale
        ).astype(bf16)
        for half in range(2):
            rows = pl.ds(pl.multiple_of(p * 128 + half * 64, 64), 64)
            b.dk_t[rows, :] = mm(b.q_t[rows, :], b.pg[2 * p + half]).astype(bf16)

    loop(pairs, back_score)

    def unflip(src, dst):
        def body(r):
            lanes = pl.ds(pl.multiple_of(r * 256, 256), 256)
            dst[:, lanes] = mm_nt(i.eye[:padded, :], src[lanes, :]).astype(bf16)

        loop(width // 256, body)

    unflip(b.dk_t, b.dk)
    unflip(b.dv_t, b.dv)
    for g in range(head):
        third = pl.ds((head + g // 2) * 128, 128)
        own = pl.ds(g * 128, 128)
        b.turn[g, :, 0:128] = b.dq[:, own]
        b.turn[g, :, 128:256] = b.dk[:, own]
        b.turn[g, :, 256:384] = b.dv[:, own]
        q3, k3, v3 = (ref[:, third].astype(f32) for ref in (b.dq, b.dk, b.dv))
        if g % 2:
            q3, v3 = pltpu.roll(q3, 64, 1), pltpu.roll(v3, 64, 1)
        else:
            k3 = pltpu.roll(k3, 64, 1)
        b.turn[g, :, 384:512] = jnp.where(low_half, q3, k3).astype(bf16)
        b.turn[g, :, 512:640] = jnp.where(low_half, v3, 0.0).astype(bf16)
    turn.start()
    b.turned[at.s] = b.turn[at.s]

    b.hid[...] = mm_nt(b.turn[0], b.wq[0])
    for g in range(1, head):
        b.hid[...] += mm_nt(b.turn[g], b.wq[g])

    def back_one(j, carry):
        gain_sum, shift_sum = carry
        grad = b.hid[chunk(j), :]
        xhat, rs = norm_rows(b.tok[at.s, chunk(j), :].astype(f32))
        inner = norm_back_rows(grad, b.norms[0:1, :], xhat, rs)
        o.input[at.s, chunk(j), :] = (b.mg[chunk(j), :] + inner).astype(bf16)
        return gain_sum + fold_rows(grad * xhat), shift_sum + fold_rows(grad)

    gain_sum, shift_sum = lax.fori_loop(0, chunks, back_one, (zero, zero), unroll=True)
    b.sums[0:1, :] = jnp.sum(gain_sum, axis=0, keepdims=True)
    b.sums[1:2, :] = jnp.sum(shift_sum, axis=0, keepdims=True)

    blocks = jnp.zeros((head * 8, 128), f32)
    for table, pick in ((b.mix_one, i.pick_pre_t), (b.mix_two, i.pick_post_t)):
        blocks += exact(exact(pick[...], table[...] * diagonal), i.place_f[...])
    blocks = blocks.reshape(head, 8, 128)
    b.sums[4:8, :] = jnp.zeros((4, width), f32)
    for g in range(head):
        b.small[g, :, :width] = b.sums[...]
        b.small[g, :, width:] = blocks[g]
    small_head.start()
    b.small_slots[at.s] = b.small[at.s]

    turn.wait()
    flip(b.n1)
    weight_grad(b.g_qkv, lambda: flat(b.turned))
    sc_qkv.start()
    inp.start()
    for k in range(1, at.lines):
        sc_up.middle(k)

    small_head.wait()
    b.small_dp[at.d] = small_head.total()
    small_dp.start()
    b.taps[...] = exact(i.lag_back[...], b.cross[...])
    taps_in.start()
    b.taps_slots[at.d] = rows_of(b.taps, at.d, 8)[...]

    ag.wait_mate()
    ag.forward()
    ag.wait_corner()
    flip(b.ag)

    def heads_mine():
        third = tile(head + at.s // 2)
        return jnp.concatenate(
            [
                b.ho[:, :, tile(at.s)].reshape(images * padded, 128),
                b.ho[:, :, third].reshape(images * padded, 128),
            ],
            axis=1,
        )

    weight_grad(b.g_proj, heads_mine)
    sc_proj.start()

    fold_out.wait()

    def finish_output(j):
        o.output[at.s, chunk(j), :] = (b.mid[at.s, chunk(j), :] + fold_out.total(chunk(j))).astype(bf16)

    loop(chunks, finish_output)
    out.start()
    taps_in.wait()
    o.taps[at.d] = taps_in.total()
    taps_back.start()
    for k in range(1, at.lines):
        sc_qkv.middle(k)
    for k in range(1, at.lines):
        sc_proj.middle(k)
    inp.forward()
    out.forward()
    o.down[...] = sc_down.finish()
    o.up[...] = sc_up.finish()
    small_dp.wait()
    o.small[...] = small_dp.total()
    o.qkv[...] = sc_qkv.finish()
    o.proj[...] = sc_proj.finish()
    taps_back.wait()
    for group in (inp, out):
        group.wait_mate()
        group.wait_corner()
    for item in (
        gains, mixes, gq, gp, gu, gd, ho, ag, out, inp, fold_two, fold_out, sc_up, sc_down, sc_qkv, sc_proj,
        turn, taps_in, taps_back, small_head, small_dp,
    ):
        item.drain()


def tables(seq, dp, head, heads, grid, ksize, share):
    cos, sin, cos_lag, sin_lag, back = spectrum(grid, ksize)
    used = cos.shape[0]
    bins = -(-used // 16) * 16
    padded = -(-seq // 16) * 16
    fourier = np.zeros((2 * bins, padded))
    fourier[:used, :seq] = cos
    fourier[bins : bins + used, :seq] = sin
    taps = ksize * ksize
    lag = np.zeros((2 * bins, -(-taps // 8) * 8))
    lag[:used, :taps] = cos_lag
    lag[bins : bins + used, :taps] = sin_lag
    lag_back = np.zeros((dp * 8, 2 * bins))
    lag_back[:taps, :used] = (cos_lag * back[:, None]).T
    lag_back[:taps, bins : bins + used] = (sin_lag * back[:, None]).T
    comb = (np.arange(share * dp)[None, :] % share == np.arange(128)[:, None]) & (
        np.arange(128)[:, None] < share
    )
    group = heads // head
    slot = [group * g + l for g in range(head) for l in range(2)] + [group * g + 2 for g in range(head)]
    wide = heads * 16
    pick = np.zeros((2, wide, head * 8))
    place = np.zeros((wide, 128))
    for p, h in enumerate(slot):
        for row in range(16):
            for which in range(2):
                pick[which, p * 16 + row, (h // group) * 8 + which * 4 + h % group] = 1.0
            place[p * 16 + row, h] = 1.0
    diagonal = (np.arange(wide)[:, None] % 16) == (np.arange(wide)[None, :] % 16)
    return {
        "fourier": jnp.asarray(fourier, bf16),
        "fourier_t": jnp.asarray(fourier.T, bf16),
        "lag": jnp.asarray(lag, f32),
        "lag_back": jnp.asarray(lag_back, f32),
        "comb": jnp.asarray(comb, bf16),
        "pick_pre": jnp.asarray(pick[0], bf16),
        "pick_post": jnp.asarray(pick[1], bf16),
        "pick_pre_t": jnp.asarray(pick[0].T, f32),
        "pick_post_t": jnp.asarray(pick[1].T, f32),
        "place": jnp.asarray(place, bf16),
        "place_f": jnp.asarray(place, f32),
        "diagonal": jnp.asarray(diagonal, f32),
        "eye": jnp.asarray(np.eye(256), bf16),
    }


def whole_block(
    tokens,
    ln1_gain,
    ln1_shift,
    w_qkv,
    w_proj,
    mix_pre,
    mix_post,
    ln2_gain,
    ln2_shift,
    w_up,
    conv_kernel,
    w_down,
    out_grad,
):
    images, seq, width = tokens.shape
    dp, head = lax.axis_size("dp"), lax.axis_size("head")
    local_heads, heads = mix_pre.shape
    size = width // heads
    local = local_heads * size
    share = w_qkv.shape[0]
    ksize, units = conv_kernel.shape[0], conv_kernel.shape[2]
    grid = int(round((seq - 1) ** 0.5))
    padded = -(-seq // 16) * 16
    wide = -(-seq // 128) * 128
    lines = dp // 2
    const = tables(seq, dp, head, heads, grid, ksize, share)
    bins = const["fourier"].shape[0] // 2

    gains = jnp.stack([ln1_gain, ln1_shift, ln2_gain, ln2_shift]).astype(f32)
    gains = jnp.pad(gains, ((0, 4), (0, 128 - share)))
    mixes = jnp.pad(
        jnp.stack([mix_pre, mix_post]), ((0, 0), (0, 4 - local_heads), (0, 128 - heads))
    ).reshape(8, 128)
    two = 2 * size
    wq = jnp.concatenate(
        [
            w_qkv[:, :, :two].reshape(share, 3 * two),
            w_qkv[:, :, two:].reshape(share, 3 * size),
            jnp.zeros((share, size), bf16),
        ],
        axis=1,
    )
    wp = jnp.pad(w_proj.T, ((0, 0), (0, 256 - local)))
    taps = conv_kernel.reshape(ksize * ksize, units)
    taps = jnp.pad(taps, ((0, const["lag"].shape[1] - ksize * ksize), (0, 0)))
    inputs = {
        "tokens": tokens,
        "out_grad": out_grad,
        "gains": gains,
        "mixes": mixes,
        "wq": wq,
        "wp": wp,
        "wu": w_up,
        "wd": w_down.T,
        "taps": taps,
        **const,
    }
    lanes = wq.shape[1]
    outputs = {
        "output": ((images, padded, width), bf16),
        "input": ((images, padded, width), bf16),
        "qkv": ((share, lanes), f32),
        "proj": ((share, 256), f32),
        "up": ((share, units), f32),
        "down": ((share, units), f32),
        "taps": ((dp, 8, units), f32),
        "small": ((8, width + 128), f32),
    }
    one, every = (padded, width), (images, padded, width)
    square = (heads, padded, wide)
    table = (heads * 16, heads * 16)
    scratch = {
        "tok": (every, bf16),
        "og": (every, bf16),
        "edge": ((16, width), f32),
        "wq": ((head, width, lanes), bf16),
        "wp_raw": ((head, width, 256), bf16),
        "wp": ((width, width), bf16),
        "wu": ((width, units), bf16),
        "wd": ((width, units), bf16),
        "gains": ((dp, 8, 128), f32),
        "mixes": ((head, 8, 128), f32),
        "norms": ((8, width), f32),
        "filt": ((2 * bins, units), f32),
        "cross": ((2 * bins, units), f32),
        "wave": ((2 * bins, units), f32),
        "fi": ((2 * bins, units), bf16),
        "gf": ((images, 2 * bins, units), bf16),
        "actg": ((images, padded, units), bf16),
        "act": ((padded, units), bf16),
        "n1": (every, bf16),
        "n2": (every, bf16),
        "mid": (every, f32),
        "hid": (one, f32),
        "wid": ((images, padded, units), bf16),
        "hg": ((images, padded, units), bf16),
        "np": (every, bf16),
        "np_near": ((2, *one), bf16),
        "np_far": (one, bf16),
        "bp_near": ((2, *one), bf16),
        "bp_far": (one, bf16),
        "flip": ((width, images * padded), bf16),
        "q": (one, bf16),
        "k": ((wide, width), bf16),
        "v": ((wide, width), bf16),
        "third_qk": ((head, padded, 128), f32),
        "third_v": ((head, padded, 128), f32),
        "kron": ((2, 2, *table), bf16),
        "kron_t": ((2, 2, *table), bf16),
        "mix_one": (table, f32),
        "mix_two": (table, f32),
        "sc": (square, bf16),
        "pr": (square, f32),
        "post": (square, bf16),
        "pg": (square, bf16),
        "ho": (every, bf16),
        "ag": (every, bf16),
        "hgr": (one, bf16),
        "hgr_t": ((width, padded), bf16),
        "q_t": ((width, padded), bf16),
        "dv_t": ((width, wide), bf16),
        "dk_t": ((width, wide), bf16),
        "dv": (one, bf16),
        "turn": ((head, padded, lanes), bf16),
        "turned": ((head, padded, lanes), bf16),
        "sums": ((8, width), f32),
        "small": ((head, 8, width + 128), f32),
        "small_slots": ((head, 8, width + 128), f32),
        "small_dp": ((dp, 8, width + 128), f32),
        "taps": ((dp * 8, units), f32),
        "taps_slots": ((dp, 8, units), f32),
    }
    for name, columns in (("up", units), ("down", units), ("qkv", lanes), ("proj", 256)):
        scratch["g_" + name] = ((width, columns), bf16)
        scratch[name + "_y"] = ((lines, share, columns), bf16)
        scratch[name + "_z"] = ((lines - 1, share, columns), bf16)
    sems = {"ga": dp - 1, "mi": head - 1, "ho": 3, "ag": 3, "ou": 3, "in": 3, "np": 3, "bp": 3}
    sems |= {"tu": head - 1, "ti": dp - 1, "tb": dp - 1, "sh": head - 1, "sd": dp - 1}
    for name in "qpud":
        sems |= {name + "z": lines - 1, name + "y": lines}
        sems |= {name + "y2": lines, name + "z2": lines - 1}
    for name in "qp":
        sems |= {name + "x": dp, name + "m": 2 * dp}
    shapes = {name: pltpu.VMEM(*spec) for name, spec in scratch.items()}
    for name, number in sems.items():
        shapes[name + "_s"] = pltpu.SemaphoreType.DMA((number,))
        shapes[name + "_r"] = pltpu.SemaphoreType.DMA((number,))
    vmem = pl.BlockSpec(memory_space=pltpu.VMEM)
    results = pl.pallas_call(
        functools.partial(
            block_kernel,
            (seq, dp, head, size ** (-0.5)),
            tuple(inputs),
            tuple(outputs),
            tuple(shapes),
        ),
        out_shape=[jax.ShapeDtypeStruct(*spec) for spec in outputs.values()],
        in_specs=[vmem] * len(inputs),
        out_specs=[vmem] * len(outputs),
        scratch_shapes=list(shapes.values()),
        compiler_params=pltpu.CompilerParams(
            collective_id=0, has_side_effects=True, vmem_limit_bytes=64 * 2**20
        ),
    )(*inputs.values())
    r = dict(zip(outputs, results))
    norms = lax.dynamic_slice(r["small"], (0, lax.axis_index("dp") * share), (4, share))
    odd = lax.axis_index("head") % 2 == 1
    third = jnp.where(odd, r["proj"][:, two + size :], r["proj"][:, two : two + size])
    qkv = jnp.concatenate(
        [
            r["qkv"][:, : 3 * two].reshape(share, 3, two),
            r["qkv"][:, 3 * two : 3 * (two + size)].reshape(share, 3, size),
        ],
        axis=2,
    )
    small = r["small"][:, width:]
    return (
        r["output"][:, :seq],
        r["input"][:, :seq],
        norms[0],
        norms[1],
        qkv,
        jnp.concatenate([r["proj"][:, :two], third], axis=1).T,
        small[:local_heads, :heads],
        small[4 : 4 + local_heads, :heads],
        norms[2],
        norms[3],
        r["up"],
        r["taps"].reshape(dp * 8, units)[: ksize * ksize].reshape(ksize, ksize, units),
        r["down"].T,
    )


def solution(mesh):
    in_specs = (
        P("dp", None, None),
        P("dp"),
        P("dp"),
        P("dp", None, "head"),
        P("head", "dp"),
        P("head", None),
        P("head", None),
        P("dp"),
        P("dp"),
        P("dp", "head"),
        P(None, None, "head"),
        P("head", "dp"),
        P("dp", None, None),
    )
    out_specs = (
        P("dp", None, None),
        P("dp", None, None),
        P("dp"),
        P("dp"),
        P("dp", None, "head"),
        P("head", "dp"),
        P("head", None),
        P("head", None),
        P("dp"),
        P("dp"),
        P("dp", "head"),
        P(None, None, "head"),
        P("head", "dp"),
    )
    dp, head = mesh.shape["dp"], mesh.shape["head"]

    def shards(*args):
        tokens, w_qkv, mix_pre = args[0], args[3], args[5]
        fits = head == 4 and dp % 2 == 0 and w_qkv.shape[0] % 32 == 0 and w_qkv.shape[0] <= 128
        fits = fits and dp * 8 >= args[10].shape[0] ** 2 and tokens.shape[0] == head
        fits = fits and mix_pre.shape[0] == 3 and tokens.shape[2] == 64 * mix_pre.shape[1]
        return (whole_block if fits else plain)(*args)

    return jax.shard_map(shards, mesh=mesh, in_specs=in_specs, out_specs=out_specs, check_vma=False)
```

```python
import functools
import types

import jax
import jax.numpy as jnp
import numpy as np
from jax import lax
from jax.experimental import pallas as pl
from jax.experimental.pallas import tpu as pltpu
from jax.sharding import PartitionSpec as P

highest = lax.Precision.HIGHEST
epsilon = 1e-06
bf16 = jnp.bfloat16
f32 = jnp.float32


def spectrum(grid, ksize):
    margin = ksize // 2
    period = grid + margin
    pairs = [(0, 0)] + [(0, v) for v in range(1, period // 2 + 1)]
    pairs += [(u, v) for u in range(1, period // 2 + 1) for v in range(period)]
    freq = np.array(pairs, np.float64)
    place = np.array([(r, c) for r in range(grid) for c in range(grid)], np.float64)
    lags = np.array([(p - margin, q - margin) for p in range(ksize) for q in range(ksize)], np.float64)
    weight = np.sqrt(np.where(np.arange(len(pairs)) == 0, 1.0, 2.0)) / period
    angle = 2 * np.pi / period * freq @ place.T
    angle_lag = 2 * np.pi / period * freq @ lags.T
    count = len(pairs)
    cos = np.zeros((count + 1, grid * grid + 1))
    sin = np.zeros_like(cos)
    cos[:count, 1:] = weight[:, None] * np.cos(angle)
    sin[:count, 1:] = weight[:, None] * np.sin(angle)
    cos[count, 0] = 1.0
    cos_lag = np.zeros((count + 1, ksize * ksize))
    sin_lag = np.zeros_like(cos_lag)
    cos_lag[:count] = np.cos(angle_lag)
    sin_lag[:count] = np.sin(angle_lag)
    back = np.zeros(count + 1)
    back[:count] = 1.0
    return cos, sin, cos_lag, sin_lag, back


def layer_norm(values, gain, shift):
    center = jnp.mean(values, axis=-1, keepdims=True)
    centered = values - center
    spread = jnp.mean(centered * centered, axis=-1, keepdims=True)
    rs = lax.rsqrt(spread + epsilon)
    xhat = centered * rs
    return xhat * gain + shift, xhat, rs


def norm_back(grad, gain, xhat, rs):
    e = grad * gain
    inner = rs * (
        e
        - jnp.mean(e, axis=-1, keepdims=True)
        - xhat * jnp.mean(e * xhat, axis=-1, keepdims=True)
    )
    return inner, jnp.sum(grad * xhat, axis=(0, 1)), jnp.sum(grad, axis=(0, 1))


def dot(spec, a, b):
    return jnp.einsum(spec, a, b, preferred_element_type=f32)


def plain(
    tokens,
    ln1_gain,
    ln1_shift,
    w_qkv,
    w_proj,
    mix_pre,
    mix_post,
    ln2_gain,
    ln2_shift,
    w_up,
    conv_kernel,
    w_down,
    out_grad,
):
    images, seq, width = tokens.shape
    heads_local, heads = mix_pre.shape
    size = width // heads
    scale = size ** (-0.5)
    ksize = conv_kernel.shape[0]
    units = conv_kernel.shape[2]
    grid = int(round((seq - 1) ** 0.5))
    cos, sin, cos_lag, sin_lag, back = spectrum(grid, ksize)
    fourier = jnp.asarray(np.stack([cos, sin]), bf16)
    lagged = jnp.asarray(np.stack([cos_lag, sin_lag]), f32)
    lagged_back = jnp.asarray(np.stack([cos_lag, sin_lag]) * back[:, None], f32)
    mine = lax.axis_index("head")

    gains = jnp.stack([ln1_gain, ln1_shift, ln2_gain, ln2_shift])
    gains = lax.all_gather(gains, "dp", axis=1, tiled=True).astype(f32)
    gain_one, shift_one, gain_two, shift_two = gains[0], gains[1], gains[2], gains[3]
    qkv_w = lax.all_gather(w_qkv, "dp", axis=0, tiled=True)
    up_w = lax.all_gather(w_up, "dp", axis=0, tiled=True)
    down_w = lax.all_gather(w_down, "dp", axis=1, tiled=True)
    proj_w = lax.all_gather(w_proj, "head", axis=0, tiled=True)
    proj_w = lax.all_gather(proj_w, "dp", axis=1, tiled=True)
    mixes = lax.all_gather(jnp.stack([mix_pre, mix_post]), "head", axis=1, tiled=True)
    pre, post_mix = mixes[0], mixes[1]

    source = tokens.astype(f32)
    normed_one, xhat_one, rs_one = layer_norm(source, gain_one, shift_one)
    normed_one = normed_one.astype(bf16)
    qkv = dot("ind,dce->ince", normed_one, qkv_w).astype(bf16)
    qkv = lax.all_to_all(qkv, "head", split_axis=0, concat_axis=3, tiled=True)
    own = qkv.shape[0]
    query = qkv[:, :, 0].reshape(own, seq, heads, size)
    keys = qkv[:, :, 1].reshape(own, seq, heads, size)
    values = qkv[:, :, 2].reshape(own, seq, heads, size)
    scores = (dot("inhd,imhd->ihnm", query, keys) * scale).astype(bf16)
    mixed = jnp.einsum("hg,ignm->ihnm", pre, scores.astype(f32), precision=highest)
    probs = jax.nn.softmax(mixed, axis=-1)
    probs_low = probs.astype(bf16)
    post = jnp.einsum(
        "hg,ignm->ihnm", post_mix, probs_low.astype(f32), precision=highest
    ).astype(bf16)
    heads_own = dot("ihnm,imhd->inhd", post, values).reshape(own, seq, width).astype(bf16)
    heads_out = lax.all_gather(heads_own, "head", axis=0, tiled=True)
    middle = source + dot("ine,ed->ind", heads_out, proj_w)
    normed_two, xhat_two, rs_two = layer_norm(middle, gain_two, shift_two)
    normed_two = normed_two.astype(bf16)
    hidden = dot("ind,df->inf", normed_two, up_w)
    erf = lax.erf(hidden * (0.5**0.5))
    activ = 0.5 * hidden * (1.0 + erf)
    slope = 0.5 * (1.0 + erf) + hidden * jnp.exp(-0.5 * hidden * hidden) * 0.3989422804014327
    delta = np.zeros((ksize * ksize, 1), np.float32)
    delta[ksize * ksize // 2] = 1.0
    taps = conv_kernel.reshape(ksize * ksize, units)
    filters = jnp.einsum("zkl,lf->zkf", lagged, taps, precision=highest)
    cos_k, sin_k = filters[0] + 1.0, filters[1]
    wave = dot("zkn,inf->zikf", fourier, activ.astype(bf16))
    cos_a, sin_a = wave[0], wave[1]
    filtered = jnp.stack([cos_k * cos_a + sin_k * sin_a, cos_k * sin_a - sin_k * cos_a])
    widened = dot("zkn,zikf->inf", fourier, filtered.astype(bf16)).astype(bf16)
    branch = dot("inf,fd->ind", widened, down_w)
    branch = lax.psum(branch.astype(bf16), "head").astype(f32)
    output = (middle + branch).astype(bf16)

    down_grad = dot("inf,ind->fd", widened, out_grad)
    widened_grad = dot("ind,fd->inf", out_grad, down_w)
    wave_grad = dot("zkn,inf->zikf", fourier, widened_grad.astype(bf16))
    cos_g, sin_g = wave_grad[0], wave_grad[1]
    spread_grad = jnp.stack([cos_k * cos_g - sin_k * sin_g, cos_k * sin_g + sin_k * cos_g])
    activ_grad = dot("zkn,zikf->inf", fourier, spread_grad.astype(bf16))
    hidden_grad = (activ_grad * slope).astype(bf16)
    cross = jnp.stack(
        [
            jnp.sum(cos_a * cos_g + sin_a * sin_g, axis=0),
            jnp.sum(sin_a * cos_g - cos_a * sin_g, axis=0),
        ]
    )
    kernel_grad = jnp.einsum("zkl,zkf->lf", lagged_back, cross, precision=highest)
    up_grad = dot("ind,inf->df", normed_two, hidden_grad)
    two_grad = dot("inf,df->ind", hidden_grad, up_w).astype(bf16)
    two_grad = lax.psum_scatter(two_grad, "head", scatter_dimension=0, tiled=True).astype(f32)

    def pick(array):
        return lax.dynamic_slice_in_dim(array, mine * own, own, 0)

    middle_from, gain_two_grad, shift_two_grad = norm_back(
        two_grad, gain_two, pick(xhat_two), pick(rs_two)
    )
    middle_grad = pick(out_grad).astype(f32) + middle_from
    attention_own = middle_grad.astype(bf16)
    attention_grad = lax.all_gather(attention_own, "head", axis=0, tiled=True)
    local = width // lax.axis_size("head")
    heads_mine = lax.dynamic_slice_in_dim(heads_out, mine * local, local, 2)
    proj_grad = dot("ine,ind->ed", heads_mine, attention_grad)
    heads_grad = dot("ind,ed->ine", attention_own, proj_w).astype(bf16)
    heads_grad = heads_grad.reshape(own, seq, heads, size)
    values_grad = dot("ihnm,inhd->imhd", post, heads_grad)
    post_grad = dot("inhd,imhd->ihnm", heads_grad, values)
    probs_grad = jnp.einsum("hg,ihnm->ignm", post_mix, post_grad, precision=highest)
    mixed_grad = probs * (probs_grad - jnp.sum(probs_grad * probs, axis=-1, keepdims=True))
    scores_grad = jnp.einsum("hg,ihnm->ignm", pre, mixed_grad, precision=highest).astype(bf16)
    post_mix_grad = dot("ihnm,ignm->hg", post_grad.astype(bf16), probs_low)
    pre_mix_grad = dot("ihnm,ignm->hg", mixed_grad.astype(bf16), scores)
    query_grad = dot("ihnm,imhd->inhd", scores_grad, keys) * scale
    keys_grad = dot("ihnm,inhd->imhd", scores_grad, query) * scale
    qkv_grad = jnp.stack([query_grad, keys_grad, values_grad], axis=2)
    qkv_grad = qkv_grad.reshape(own, seq, 3, width).astype(bf16)
    qkv_grad = lax.all_to_all(qkv_grad, "head", split_axis=3, concat_axis=0, tiled=True)
    qkv_weight_grad = dot("ind,ince->dce", normed_one, qkv_grad)
    one_grad = dot("ince,dce->ind", qkv_grad, qkv_w).astype(bf16)
    one_grad = lax.psum_scatter(one_grad, "head", scatter_dimension=0, tiled=True).astype(f32)
    source_grad, gain_one_grad, shift_one_grad = norm_back(
        one_grad, gain_one, pick(xhat_one), pick(rs_one)
    )
    input_own = (middle_grad + source_grad).astype(bf16)
    input_grad = lax.all_gather(input_own, "head", axis=0, tiled=True)

    def share(grad, axis):
        return lax.psum_scatter(
            grad.astype(bf16), "dp", scatter_dimension=axis, tiled=True
        ).astype(f32)

    norm_grads = jnp.stack([gain_one_grad, shift_one_grad, gain_two_grad, shift_two_grad])
    norm_grads = lax.psum(norm_grads, "head")
    norm_grads = lax.psum_scatter(norm_grads, "dp", scatter_dimension=1, tiled=True)
    mix_grads = lax.psum_scatter(
        jnp.stack([pre_mix_grad, post_mix_grad]), "head", scatter_dimension=1, tiled=True
    )
    mix_grads, kernel_grad = lax.psum((mix_grads, kernel_grad), "dp")
    return (
        output,
        input_grad,
        norm_grads[0],
        norm_grads[1],
        share(qkv_weight_grad, 0),
        share(proj_grad, 1),
        mix_grads[0],
        mix_grads[1],
        norm_grads[2],
        norm_grads[3],
        share(up_grad, 0),
        kernel_grad.reshape(ksize, ksize, units),
        share(down_grad, 1),
    )


MESH = pl.DeviceIdType.MESH
NT = (((1,), (1,)), ((), ()))


def mm(a, b):
    return jnp.dot(a, b, preferred_element_type=f32)


def mm_nt(a, b):
    return lax.dot_general(a, b, NT, preferred_element_type=f32)


def exact(a, b):
    return jnp.dot(a, b, preferred_element_type=f32, precision=highest)


def split(a):
    high = a.astype(bf16)
    return high, (a - high.astype(f32)).astype(bf16)


def remote(src, dst, send, recv, device):
    return pltpu.make_async_remote_copy(
        src_ref=src,
        dst_ref=dst,
        send_sem=send,
        recv_sem=recv,
        device_id=device,
        device_id_type=MESH,
    )


class Place:
    def __init__(self, dp, head):
        self.dp, self.head = dp, head
        self.lines = dp // 2
        self.d, self.s = lax.axis_index("dp"), lax.axis_index("head")
        self.z, self.y = self.d // 2, self.d % 2
        self.x, self.c = self.s // 2, self.s % 2
        self.mate = self.x * 2 + 1 - self.c
        self.across = (1 - self.x) * 2 + self.c
        self.corner = (1 - self.x) * 2 + 1 - self.c

    def near(self, j):
        return ((self.x + j // 2) % 2) * 2 + (self.c + j % 2) % 2

    def z_next(self, k):
        return (self.z + k) % self.lines

    def z_prev(self, k):
        return (self.z + self.lines - k) % self.lines

    def head_next(self, k):
        return (self.s + k) % self.head

    def dp_next(self, k):
        return (self.d + k) % self.dp

    def call(self):
        barrier = pltpu.get_barrier_semaphore()
        for k in range(1, self.head):
            pl.semaphore_signal(
                barrier, inc=1, device_id=(self.d, self.head_next(k)), device_id_type=MESH
            )
        for k in range(1, self.dp):
            pl.semaphore_signal(
                barrier, inc=1, device_id=(self.dp_next(k), self.s), device_id_type=MESH
            )

    def answer(self):
        pl.semaphore_wait(pltpu.get_barrier_semaphore(), self.head - 1 + self.dp - 1)


def rows_of(ref, index, count):
    return ref.at[pl.ds(pl.multiple_of(index * count, count), count)]


class Gather:
    def __init__(self, at, buf, sems, wide):
        self.at, self.wide = at, wide
        self.groups = buf
        self.buf = buf.at[at.s] if wide else buf
        self.rows = self.buf.shape[0] // at.dp
        self.sems = sems

    def block(self, k, other, buf=None):
        at = self.at
        y = 1 - at.y if other else at.y
        return rows_of(self.buf if buf is None else buf, at.z_prev(k) * 2 + y, self.rows)

    def z_copy(self, k):
        at, (send, recv) = self.at, self.sems[0]
        ref = self.block(0, False)
        return remote(ref, ref, send.at[k - 1], recv.at[k - 1], (at.z_next(k) * 2 + at.y, at.s))

    def y_copy(self, k):
        at, (send, recv) = self.at, self.sems[1]
        ref = self.block(k, False)
        return remote(ref, ref, send.at[k], recv.at[k], (at.z * 2 + 1 - at.y, at.s))

    def x_copy(self, b):
        at, (send, recv) = self.at, self.sems[2]
        ref = self.block(b % at.lines, b >= at.lines)
        return remote(ref, ref, send.at[b], recv.at[b], (at.d, at.across))

    def mate_copy(self, b, far):
        at, (send, recv) = self.at, self.sems[3]
        ref = self.block(
            b % at.lines, b >= at.lines, self.groups.at[at.across if far else at.s]
        )
        slot = b + at.dp if far else b
        return remote(ref, ref, send.at[slot], recv.at[slot], (at.d, at.mate))

    def on(self, b):
        if self.wide:
            self.x_copy(b).start()
            self.mate_copy(b, False).start()

    def begin(self):
        for k in sorted(range(1, self.at.lines), key=lambda k: min(k, self.at.lines - k)):
            self.z_copy(k).start()

    def over_y(self):
        self.y_copy(0).start()

    def from_z(self, k):
        self.z_copy(k).wait_recv()
        self.y_copy(k).start()

    def from_y(self, k):
        self.y_copy(k).wait_recv()

    def from_x(self, b):
        self.x_copy(b).wait_recv()
        self.mate_copy(b, True).start()

    def from_mate(self, far):
        for b in range(self.at.dp):
            self.mate_copy(b, far).wait_recv()

    def drain(self):
        for k in range(1, self.at.lines):
            self.z_copy(k).wait_send()
        for k in range(self.at.lines):
            self.y_copy(k).wait_send()
        if self.wide:
            for b in range(self.at.dp):
                self.x_copy(b).wait_send()
                self.mate_copy(b, False).wait_send()
                self.mate_copy(b, True).wait_send()


class Line:
    def __init__(self, at, buf, sems, wide):
        self.at, self.wide = at, wide
        self.groups = buf
        self.buf = buf.at[at.s] if wide else buf
        self.rows = self.buf.shape[0] // at.dp
        self.sems = sems

    def near(self, hops, body):
        at = self.at
        if hops == 0:
            body(at.z)
        else:
            pl.when(at.z >= hops)(lambda: body(at.z - hops))
            pl.when(at.z + hops < at.lines)(lambda: body(at.z + hops))

    def index(self, z, other):
        return z * 2 + (1 - self.at.y if other else self.at.y)

    def block(self, z, other, buf=None):
        return rows_of(self.buf if buf is None else buf, self.index(z, other), self.rows)

    def z_copy(self, up, hops):
        at, (send, recv) = self.at, self.sems[0]
        ref = self.block(at.z - hops if up else at.z + hops, False)
        slot = hops if up else at.lines - 1 + hops
        to = at.z + 1 if up else at.z - 1
        return remote(ref, ref, send.at[slot], recv.at[slot], (to * 2 + at.y, at.s))

    def pass_on(self, up, hops):
        at = self.at
        if up:
            there = (at.z >= hops) & (at.z < at.lines - 1)
        else:
            there = (at.z + hops < at.lines) & (at.z > 0)
        return pl.when(there)

    def y_copy(self, z):
        at, (send, recv) = self.at, self.sems[1]
        ref = self.block(z, False)
        return remote(ref, ref, send.at[z], recv.at[z], (at.z * 2 + 1 - at.y, at.s))

    def x_copy(self, z, other):
        at, (send, recv) = self.at, self.sems[2]
        ref, slot = self.block(z, other), self.index(z, other)
        return remote(ref, ref, send.at[slot], recv.at[slot], (at.d, at.across))

    def mate_copy(self, z, other, far):
        at, (send, recv) = self.at, self.sems[3]
        ref = self.block(z, other, self.groups.at[at.across if far else at.s])
        slot = self.index(z, other) + (at.dp if far else 0)
        return remote(ref, ref, send.at[slot], recv.at[slot], (at.d, at.mate))

    def begin(self):
        for up in (True, False):
            self.pass_on(up, 0)(lambda: self.z_copy(up, 0).start())

    def over_y(self):
        self.y_copy(self.at.z).start()

    def from_z(self, hops):
        at = self.at
        for up in (True, False):

            @pl.when(at.z >= hops if up else at.z + hops < at.lines)
            def _():
                source = at.z - hops if up else at.z + hops
                self.z_copy(up, hops - 1).wait_recv()
                if hops < at.lines - 1:
                    self.pass_on(up, hops)(lambda: self.z_copy(up, hops).start())
                self.y_copy(source).start()

    def on(self, hops, other):
        def body(z):
            self.x_copy(z, other).start()
            self.mate_copy(z, other, False).start()

        self.near(hops, body)

    def from_y(self, hops):
        self.near(hops, lambda z: self.y_copy(z).wait_recv())

    def from_x(self, hops, other):
        def body(z):
            self.x_copy(z, other).wait_recv()
            self.mate_copy(z, other, True).start()

        self.near(hops, body)

    def from_mate(self, far):
        for z in range(self.at.lines):
            for other in (False, True):
                self.mate_copy(z, other, far).wait_recv()

    def drain(self):
        at = self.at
        for hops in range(at.lines - 1):
            for up in (True, False):
                self.pass_on(up, hops)(lambda: self.z_copy(up, hops).wait_send())
        for z in range(at.lines):
            self.y_copy(z).wait_send()
            if self.wide:
                for other in (False, True):
                    self.x_copy(z, other).wait_send()
                    self.mate_copy(z, other, False).wait_send()
                    self.mate_copy(z, other, True).wait_send()


class Share:
    def __init__(self, at, buf, sems):
        self.at, self.buf = at, buf
        self.send, self.recv = sems

    def copy(self, which):
        at = self.at
        ref = self.buf.at[at.across if which == 2 else at.s]
        to = at.across if which == 1 else at.mate
        return remote(ref, ref, self.send.at[which], self.recv.at[which], (at.d, to))

    def start(self):
        self.copy(1).start()
        self.copy(0).start()

    def wait_mate(self):
        self.copy(0).wait_recv()

    def forward(self):
        self.copy(1).wait_recv()
        self.copy(2).start()

    def wait_corner(self):
        self.copy(2).wait_recv()

    def drain(self):
        for which in range(3):
            self.copy(which).wait_send()


class Fold:
    def __init__(self, at, parts, near, far, sems):
        self.at, self.parts, self.near, self.far = at, parts, near, far
        self.send, self.recv = sems

    def mate_copy(self, which):
        at = self.at
        src = self.parts.at[at.corner if which else at.mate]
        return remote(
            src, self.near.at[which], self.send.at[which], self.recv.at[which], (at.d, at.mate)
        )

    def x_copy(self):
        at = self.at
        return remote(
            self.parts.at[at.across], self.far, self.send.at[2], self.recv.at[2], (at.d, at.across)
        )

    def middle(self):
        at = self.at
        self.mate_copy(1).wait_recv()
        self.parts[at.across] = (
            self.parts[at.across].astype(f32) + self.near[1].astype(f32)
        ).astype(bf16)
        self.x_copy().start()

    def wait(self):
        self.mate_copy(0).wait_recv()
        self.x_copy().wait_recv()

    def total(self, rows):
        return (
            self.parts[self.at.s, rows, :].astype(f32)
            + self.near[0, rows, :].astype(f32)
            + self.far[rows, :].astype(f32)
        )

    def drain(self):
        self.mate_copy(0).wait_send()
        self.mate_copy(1).wait_send()
        self.x_copy().wait_send()


class Scatter:
    def __init__(self, at, src, from_y, from_z, sems):
        self.at, self.src, self.from_y, self.from_z = at, src, from_y, from_z
        (self.y_send, self.y_recv), (self.z_send, self.z_recv) = sems
        self.rows = src.shape[0] // at.dp

    def block(self, z, y):
        return rows_of(self.src, z * 2 + y, self.rows)

    def y_copy(self, k):
        at = self.at
        return remote(
            self.block(at.z_next(k), 1 - at.y),
            self.from_y.at[k],
            self.y_send.at[k],
            self.y_recv.at[k],
            (at.z * 2 + 1 - at.y, at.s),
        )

    def z_copy(self, k):
        at = self.at
        return remote(
            self.block(at.z_next(k), at.y),
            self.from_z.at[k - 1],
            self.z_send.at[k - 1],
            self.z_recv.at[k - 1],
            (at.z_next(k) * 2 + at.y, at.s),
        )

    def start(self):
        for k in (*range(1, self.at.lines), 0):
            self.y_copy(k).start()

    def middle(self, k):
        at = self.at
        self.y_copy(k).wait_recv()
        ref = self.block(at.z_next(k), at.y)
        ref[...] = (ref[...].astype(f32) + self.from_y[k].astype(f32)).astype(bf16)
        self.z_copy(k).start()

    def finish(self):
        at = self.at
        self.y_copy(0).wait_recv()
        total = self.block(at.z, at.y)[...].astype(f32) + self.from_y[0].astype(f32)
        for k in range(1, at.lines):
            self.z_copy(k).wait_recv()
            total = total + self.from_z[k - 1].astype(f32)
        return total

    def drain(self):
        for k in range(self.at.lines):
            self.y_copy(k).wait_send()
        for k in range(1, self.at.lines):
            self.z_copy(k).wait_send()


class Exchange:
    def __init__(self, at, axis, slots, sems, block_for):
        self.at, self.axis, self.slots, self.block_for = at, axis, slots, block_for
        self.send, self.recv = sems
        self.count = at.dp if axis == "dp" else at.head
        self.me = at.d if axis == "dp" else at.s

    def copy(self, k):
        at = self.at
        peer = (self.me + k) % self.count
        device = (peer, at.s) if self.axis == "dp" else (at.d, peer)
        return remote(
            self.block_for(peer),
            self.slots.at[self.me],
            self.send.at[k - 1],
            self.recv.at[k - 1],
            device,
        )

    def start(self):
        for k in range(1, self.count):
            self.copy(k).start()

    def wait(self):
        for k in range(1, self.count):
            self.copy(k).wait_recv()

    def drain(self):
        for k in range(1, self.count):
            self.copy(k).wait_send()

    def total(self):
        total = self.slots[0]
        for k in range(1, self.count):
            total = total + self.slots[k]
        return total


def norm_rows(x):
    center = jnp.mean(x, axis=-1, keepdims=True)
    centered = x - center
    spread = jnp.mean(centered * centered, axis=-1, keepdims=True)
    rs = lax.rsqrt(spread + epsilon)
    return centered * rs, rs


def norm_back_rows(grad, gain, xhat, rs):
    e = grad * gain
    return rs * (
        e
        - jnp.mean(e, axis=-1, keepdims=True)
        - xhat * jnp.mean(e * xhat, axis=-1, keepdims=True)
    )


def fold_rows(a):
    return jnp.sum(a.reshape(a.shape[0] // 8, 8, a.shape[1]), axis=0)


def block_kernel(sizes, names_in, names_out, names_scratch, *refs):
    seq, dp, head, scale = sizes
    n_in, n_out = len(names_in), len(names_out)
    i = types.SimpleNamespace(**dict(zip(names_in, refs[:n_in])))
    o = types.SimpleNamespace(**dict(zip(names_out, refs[n_in : n_in + n_out])))
    b = types.SimpleNamespace(**dict(zip(names_scratch, refs[n_in + n_out :])))
    at = Place(dp, head)
    images, padded, width = b.tok.shape
    b.bp, b.dq = b.actg, b.act.at[0]
    b.dk, b.mg = b.fi.at[:padded], b.wave.at[:padded]
    b.inp, b.out = b.n1, b.n2
    hops = range(1, at.lines)
    share = i.w_up.shape[0]
    own_rows = pl.ds(pl.multiple_of(at.d * share, share), share)
    loads = [
        pltpu.make_async_copy(src, dst, b.loads.at[n])
        for n, (src, dst) in enumerate(
            (
                (i.w_down, b.wd.at[own_rows]),
                (i.w_up, b.wu.at[own_rows]),
                (i.tokens, b.raw.at[0]),
                (i.out_grad, b.raw.at[1]),
            )
        )
    ]
    chunks = padded // 16
    wide = b.k.shape[0]
    slots = b.sc.shape[0]
    pairs = slots // 2
    units = b.wu.shape[1]
    bins = b.filt.shape[0] // 2

    def span(j, size):
        return pl.ds(j * size if isinstance(j, int) else pl.multiple_of(j * size, size), size)

    def chunk(j):
        return span(j, 16)

    def tile(p):
        return span(p, 128)

    def each(steps, body):
        for j in range(steps) if isinstance(steps, int) else steps:
            body(j)

    def flip_block(a):
        return mm_nt(i.eye[: a.shape[1], : a.shape[1]], a)

    def halves(low, high):
        return (mm(low, i.eye[:64, :128]) + mm(high, i.eye[64:128, :128])).astype(bf16)

    at.call()
    for load in loads:
        load.start()
    w_q, w_k, w_v = i.w_qkv[0], i.w_qkv[1], i.w_qkv[2]
    b.wqk[at.s, own_rows, 0:128] = w_q[:, :128]
    b.wqk[at.s, own_rows, 128:256] = w_k[:, :128]
    b.wqk[at.s, own_rows, 256:384] = halves(w_q[:, 128:], w_k[:, 128:])
    own_gains, own_mixes = b.gains.at[at.d], b.mixes.at[at.s]
    own_gains[...] = jnp.zeros((8, 128), f32)
    own_mixes[...] = jnp.zeros((8, 128), f32)
    for r, gain in enumerate((i.ln1_gain, i.ln1_shift, i.ln2_gain, i.ln2_shift)):
        own_gains[r : r + 1, :share] = gain[...].astype(f32)
    local_heads, heads = i.mix_pre.shape
    own_mixes[:local_heads, :heads] = i.mix_pre[...]
    own_mixes[4 : 4 + local_heads, :heads] = i.mix_post[...]
    at.answer()

    gains = Exchange(at, "dp", b.gains, (b.ga_s, b.ga_r), lambda d: own_gains)
    mixes = Exchange(at, "head", b.mixes, (b.mi_s, b.mi_r), lambda s: own_mixes)
    gq = Gather(at, b.wqk, ((b.qz_s, b.qz_r), (b.qy_s, b.qy_r), (b.qx_s, b.qx_r), (b.qm_s, b.qm_r)), True)
    gv = Line(at, b.wv, ((b.vz_s, b.vz_r), (b.vy_s, b.vy_r), (b.vx_s, b.vx_r), (b.vm_s, b.vm_r)), True)
    gp = Line(at, b.wp_two, ((b.pz_s, b.pz_r), (b.py_s, b.py_r), (b.px_s, b.px_r), (b.pm_s, b.pm_r)), True)
    gu = Line(at, b.wu, ((b.uz_s, b.uz_r), (b.uy_s, b.uy_r)), False)
    gd = Line(at, b.wd, ((b.dz_s, b.dz_r), (b.dy_s, b.dy_r)), False)
    ho = Share(at, b.ho, (b.ho_s, b.ho_r))
    ag = Share(at, b.ag, (b.ag_s, b.ag_r))
    out = Share(at, b.out, (b.ou_s, b.ou_r))
    inp = Share(at, b.inp, (b.in_s, b.in_r))
    fold_two = Fold(at, b.np, b.np_near, b.np_far, (b.np_s, b.np_r))
    fold_out = Fold(at, b.bp, b.bp_near, b.bp_far, (b.bp_s, b.bp_r))
    sc_up = Scatter(at, b.g_up, b.up_y, b.up_z, ((b.uy2_s, b.uy2_r), (b.uz2_s, b.uz2_r)))
    sc_down = Scatter(at, b.g_down, b.down_y, b.down_z, ((b.dy2_s, b.dy2_r), (b.dz2_s, b.dz2_r)))
    sc_qk = Scatter(at, b.g_qk, b.qk_y, b.qk_z, ((b.qy2_s, b.qy2_r), (b.qz2_s, b.qz2_r)))
    sc_pv = Scatter(at, b.g_pv, b.pv_y, b.pv_z, ((b.py2_s, b.py2_r), (b.pz2_s, b.pz2_r)))
    turn_v = Exchange(at, "head", b.turned_v, (b.tv_s, b.tv_r), lambda s: b.turn_v.at[s])
    turn = Exchange(at, "head", b.turned, (b.tu_s, b.tu_r), lambda s: b.turn.at[s])
    taps_in = Exchange(at, "dp", b.taps_slots, (b.ti_s, b.ti_r), lambda d: rows_of(b.taps, d, 8))
    taps_back = Exchange(at, "dp", b.taps_all, (b.tb_s, b.tb_r), lambda d: b.taps_all.at[at.d])
    small_head = Exchange(at, "head", b.small_slots, (b.sh_s, b.sh_r), lambda s: b.small.at[s])
    small_dp = Exchange(at, "dp", b.small_dp, (b.sd_s, b.sd_r), lambda d: b.small_dp.at[at.d])

    order = sorted(range(1, at.lines), key=lambda k: min(k, at.lines - k))
    sides, late = order[:-1], order[-1]
    passed = (0, *sides, at.lines, late, *(at.lines + k for k in order))
    gains.start()
    mixes.start()
    gq.begin()
    gq.over_y()
    gq.on(0)
    p_t = flip_block(i.w_proj[...]).astype(bf16)
    b.wv[at.s, own_rows, 0:128] = w_v[:, :128]
    b.wv[at.s, own_rows, 128:256] = halves(w_v[:, 128:], p_t[:, 128:])
    b.wp_two[at.s, own_rows, :] = p_t[:, :128]
    gv.begin()
    gv.over_y()
    gp.begin()
    gp.over_y()
    loads[0].wait()
    gd.begin()
    gd.over_y()
    loads[1].wait()
    gu.begin()

    for which, dst in enumerate((b.tok, b.og)):
        loads[2 + which].wait()
        for r in range(chunks):
            n = min(16, seq - r * 16)
            rows = b.raw[which, r * 16 : r * 16 + n].reshape(n * images, width)
            apart = mm(i.deal[:, : n * images], rows).astype(bf16)
            dst[:, chunk(r), :] = apart.reshape(images, 16, width)

    gains.wait()
    spread = mm(b.gains[...].reshape(dp * 8, 128).astype(bf16), i.comb[...])
    row = lax.broadcasted_iota(jnp.int32, spread.shape, 0)
    lane = lax.broadcasted_iota(jnp.int32, spread.shape, 1)
    first = (row >> 3) * share
    here = (lane >= first) & (lane < first + share)
    for r in range(4):
        b.norms[r : r + 1, :] = jnp.sum(
            jnp.where(here & ((row & 7) == r), spread, 0.0), axis=0, keepdims=True
        )

    def norm_one(image):
        def body(j):
            xhat, _ = norm_rows(b.tok[image, chunk(j), :].astype(f32))
            b.n1[image, chunk(j), :] = (xhat * b.norms[0:1, :] + b.norms[1:2, :]).astype(bf16)

        each(chunks, body)

    for k in sides:
        gq.from_z(k)
        gq.on(k)
    gq.from_y(0)
    gq.on(at.lines)
    norm_one(at.s)
    gq.from_z(late)
    gq.on(late)
    for k in sides:
        gq.from_y(k)
        gq.on(at.lines + k)
    gu.over_y()
    gv.from_z(1)
    gp.from_z(1)

    mixes.wait()
    diagonal = i.diagonal[...]
    for part, piece in enumerate(split(b.mixes[...].reshape(head * 8, 128))):
        for which, pick in enumerate((i.pick_pre, i.pick_post)):
            picked = mm(pick[...], piece).astype(bf16)
            b.kron[which, part] = (mm_nt(picked, i.place[...]) * diagonal).astype(bf16)
            b.kron_t[which, part] = (mm_nt(i.place[...], picked) * diagonal).astype(bf16)

    gv.from_z(2)
    gd.from_z(1)
    gq.from_y(late)
    gq.on(at.lines + late)
    gp.from_z(2)
    gv.on(0, False)
    gv.on(1, False)
    gv.from_y(0)
    gv.on(0, True)
    gv.on(2, False)

    ksize = i.taps.shape[0]
    b.edge[...] = jnp.zeros_like(b.edge)
    for p in range(ksize):
        b.edge[p * ksize : (p + 1) * ksize, :] = i.taps[p]
    b.filt[...] = exact(i.lag[...], b.edge[...])
    b.filt[:bins, :] += 1.0
    b.cross[...] = jnp.zeros_like(b.cross)
    b.mix_one[...] = jnp.zeros_like(b.mix_one)
    b.mix_two[...] = jnp.zeros_like(b.mix_two)
    b.k[padded:, :] = jnp.zeros((wide - padded, width), bf16)
    b.v[padded:, :] = jnp.zeros((wide - padded, width), bf16)

    lo = (lax.broadcasted_iota(jnp.int32, (1, 128), 1) < 64).astype(f32)
    low_half = lax.broadcasted_iota(jnp.int32, (padded, 128), 1) < 64
    lo_b, hi_b = lo.astype(bf16), (1.0 - lo).astype(bf16)

    def project(g):
        t = mm(b.n1[at.s], b.wqk[g])
        b.q[:, tile(g)] = (t[:, :128] * scale).astype(bf16)
        b.k[:padded, tile(g)] = t[:, 128:256].astype(bf16)
        b.third_qk[g] = t[:, 256:]

    def project_v(g):
        t = mm(b.n1[at.s], b.wv[g])
        b.v[:padded, tile(g)] = t[:, :128].astype(bf16)
        b.third_v[g] = t[:, 128:]

    project(at.s)
    gv.from_z(3)
    gv.from_y(1)
    gv.on(1, True)
    gv.on(3, False)
    gu.from_z(1)
    gp.from_z(3)
    gq.from_mate(False)
    project(at.mate)
    for block in passed:
        gq.from_x(block)
    gd.from_z(2)
    gv.from_y(2)
    gv.on(2, True)
    project(at.across)
    gq.from_mate(True)
    project(at.corner)
    for p in range(head // 2):
        one, two = b.third_qk[2 * p], b.third_qk[2 * p + 1]
        third = tile(head + p)
        b.q[:, third] = (jnp.where(low_half, one, pltpu.roll(two, 64, 1)) * scale).astype(bf16)
        b.k[:padded, third] = jnp.where(low_half, pltpu.roll(one, 64, 1), two).astype(bf16)

    def score(p):
        q, k = b.q[:, tile(p)], b.k[:, tile(p)]
        b.sc[2 * p] = mm_nt(q * lo_b, k).astype(bf16)
        b.sc[2 * p + 1] = mm_nt(q * hi_b, k).astype(bf16)

    each(pairs, score)
    gv.from_y(3)
    gv.on(3, True)
    for k in range(4):
        gp.on(k, False)
    for k in range(4):
        gp.from_y(k)
        gp.on(k, True)
    gu.from_z(2)

    def mixed(table, which, block):
        return mm(table[which, 0], block) + mm(table[which, 1], block)

    def slab(ref, j):
        return ref[:, chunk(j), :].reshape(slots * 16, wide)

    def put(ref, j, value):
        ref[:, chunk(j), :] = value.reshape(slots, 16, wide)

    def soften(j):
        beyond = lax.broadcasted_iota(jnp.int32, (slots * 16, wide), 1) >= seq
        logits = jnp.where(beyond, -1e30, mixed(b.kron, 0, slab(b.sc, j)))
        top = jnp.max(logits, axis=-1, keepdims=True)
        power = jnp.exp(logits - top)
        probs = power / jnp.sum(power, axis=-1, keepdims=True)
        put(b.pr, j, probs)
        put(b.post, j, mixed(b.kron, 1, probs.astype(bf16)).astype(bf16))

    each(chunks, soften)
    gd.from_z(3)
    for k, other in ((0, False), (1, False), (0, True), (2, False), (1, True), (3, False), (2, True), (3, True)):
        gv.from_x(k, other)
    project_v(at.s)
    gv.from_mate(False)
    project_v(at.mate)
    project_v(at.across)
    gv.from_mate(True)
    project_v(at.corner)
    for p in range(head // 2):
        b.v[:padded, tile(head + p)] = jnp.where(
            low_half, b.third_v[2 * p], pltpu.roll(b.third_v[2 * p + 1], 64, 1)
        ).astype(bf16)

    def gather_heads(p):
        v = b.v[:, tile(p)]
        b.ho[at.s, :, tile(p)] = (mm(b.post[2 * p], v * lo_b) + mm(b.post[2 * p + 1], v * hi_b)).astype(bf16)

    each(pairs, gather_heads)
    ho.start()
    gu.from_z(3)

    def flip(src, dst):
        for r in range(width // 256):
            lanes = span(r, 256)
            block = src[:, :, lanes].reshape(images * padded, 256)
            dst[lanes, :] = mm_nt(i.eye[...], block).astype(bf16)

    def weight_grad(dst, left, right):
        for r in range(width // 256):
            rows = span(r, 256)
            dst[rows, :] = mm(left[rows, :], right()).astype(bf16)

    def flat(ref):
        return ref[...].reshape(images * padded, ref.shape[2])

    for k in range(1, images):
        norm_one(at.head_next(k))
    flip(b.og, b.og_t)

    for other in (False, True):
        for k in range(4):
            gp.from_x(k, other)
    gp.from_mate(False)
    gp.from_mate(True)
    low_rows = lax.broadcasted_iota(jnp.int32, (width, 128), 1) < 64
    for g in range(head):
        b.wp[:, tile(g)] = b.wp_two[g]
    for p in range(head // 2):
        one, two = b.wv[2 * p, :, 128:].astype(f32), b.wv[2 * p + 1, :, 128:].astype(f32)
        b.wp[:, tile(head + p)] = jnp.where(low_rows, pltpu.roll(one, 64, 1), two).astype(bf16)

    def chip_images(step):
        return 2 * ((at.x + step) % 2)

    def two(ref, step):
        return ref[pl.ds(chip_images(step), 2)].reshape(2 * padded, ref.shape[2])

    def rows_in_two(step, body):
        for half in range(2):
            for r in range(chunks):
                body(chip_images(step) + half, chunk(r), chunk(half * chunks + r))

    def bins_of(body):
        for j in range(bins // 16):
            body(span(j, 16), pl.ds(bins + j * 16, 16))

    def conv_back(step):
        b.act[...] = mm(two(b.og, step), b.wd[...]).astype(bf16).reshape(2, padded, units)
        for half in range(2):
            image = chip_images(step) + half
            b.wave[...] = mm(i.fourier[...], b.act[half])

            def body(cos, sin):
                cos_g, sin_g = b.wave[cos, :], b.wave[sin, :]
                cos_k, sin_k = b.filt[cos, :], b.filt[sin, :]
                b.gf[image, cos, :] = cos_g.astype(bf16)
                b.gf[image, sin, :] = sin_g.astype(bf16)
                b.fi[cos, :] = (cos_k * cos_g - sin_k * sin_g).astype(bf16)
                b.fi[sin, :] = (cos_k * sin_g + sin_k * cos_g).astype(bf16)

            bins_of(body)
            b.actg[image] = mm(i.fourier_t[...], b.fi[...]).astype(bf16)

    def up(step):
        b.hid[...] = mm_nt(two(b.ho, step), b.wp[...])

        def norm_two(image, rows, both):
            middle = b.tok[image, rows, :].astype(f32) + b.hid[both, :]
            b.mid[jnp.minimum(jnp.abs(image - at.s), 1), rows, :] = middle
            xhat, _ = norm_rows(middle)
            b.n2[image, rows, :] = (xhat * b.norms[2:3, :] + b.norms[3:4, :]).astype(bf16)

        rows_in_two(step, norm_two)
        b.hid[...] = mm(two(b.n2, step), b.wu[...])

        def gelu(image, rows, both):
            h = b.hid[both, :]
            cdf = 0.5 * (1.0 + lax.erf(h * (0.5**0.5)))
            slope = cdf + h * jnp.exp(-0.5 * h * h) * 0.3989422804014327
            b.wid[image, rows, :] = (h * cdf).astype(bf16)
            b.hg[image, rows, :] = (b.actg[image, rows, :].astype(f32) * slope).astype(bf16)

        rows_in_two(step, gelu)
        b.np[pl.ds(chip_images(step), 2)] = (
            mm_nt(two(b.hg, step), b.wu[...]).astype(bf16).reshape(2, padded, width)
        )

    for k in range(at.lines):
        gd.from_y(k)
    conv_back(1)
    ho.forward()
    conv_back(0)
    for k in range(at.lines):
        gu.from_y(k)
    ho.wait_corner()
    up(1)
    fold_two.mate_copy(1).start()
    ho.wait_mate()
    up(0)
    fold_two.mate_copy(0).start()
    fold_two.middle()
    flip(b.n2, b.flip)
    weight_grad(b.g_up, b.flip, lambda: flat(b.hg))
    sc_up.start()

    def down(step):
        for half in range(2):
            image = chip_images(step) + half
            b.wave[...] = mm(i.fourier[...], b.wid[image])

            def body(cos, sin):
                cos_a, sin_a = b.wave[cos, :], b.wave[sin, :]
                cos_k, sin_k = b.filt[cos, :], b.filt[sin, :]
                cos_g, sin_g = b.gf[image, cos, :].astype(f32), b.gf[image, sin, :].astype(f32)
                b.fi[cos, :] = (cos_k * cos_a + sin_k * sin_a).astype(bf16)
                b.fi[sin, :] = (cos_k * sin_a - sin_k * cos_a).astype(bf16)
                b.cross[cos, :] += cos_a * cos_g + sin_a * sin_g
                b.cross[sin, :] += sin_a * cos_g - cos_a * sin_g

            bins_of(body)
            b.wid[image] = mm(i.fourier_t[...], b.fi[...]).astype(bf16)
        b.bp[pl.ds(chip_images(step), 2)] = (
            mm_nt(two(b.wid, step), b.wd[...]).astype(bf16).reshape(2, padded, width)
        )

    down(1)
    fold_out.mate_copy(1).start()
    down(0)
    fold_out.mate_copy(0).start()
    weight_grad(b.g_down, b.og_t, lambda: flat(b.wid))
    sc_down.start()
    fold_out.middle()
    b.taps[...] = exact(i.lag_back[...], b.cross[...])
    taps_in.start()
    b.taps_slots[at.d] = rows_of(b.taps, at.d, 8)[...]
    sc_up.middle(1)
    flip(b.n1, b.flip)

    fold_two.wait()
    zero = jnp.zeros((8, width), f32)
    gain_sum, shift_sum = zero, zero
    for j in range(chunks):
        grad = fold_two.total(chunk(j))
        xhat, rs = norm_rows(b.mid[0, chunk(j), :])
        inner = norm_back_rows(grad, b.norms[2:3, :], xhat, rs)
        total = b.og[at.s, chunk(j), :].astype(f32) + inner
        b.mg[chunk(j), :] = total
        b.ag[at.s, chunk(j), :] = total.astype(bf16)
        gain_sum += fold_rows(grad * xhat)
        shift_sum += fold_rows(grad)
    b.sums[2:3, :] = jnp.sum(gain_sum, axis=0, keepdims=True)
    b.sums[3:4, :] = jnp.sum(shift_sum, axis=0, keepdims=True)
    ag.start()

    b.hgr[...] = mm(b.ag[at.s], b.wp[...]).astype(bf16)

    def flip_one(src, dst):
        for r in range(width // 256):
            dst[span(r, 256), :] = mm_nt(i.eye[...], src[:, span(r, 256)]).astype(bf16)

    flip_one(b.hgr, b.hgr_t)
    flip_one(b.q, b.q_t)

    def back_post(p):
        g, v = b.hgr[:, tile(p)], b.v[:, tile(p)]
        for half, mask in enumerate((lo_b, hi_b)):
            b.pg[2 * p + half] = mm_nt(g * mask, v).astype(bf16)
            rows = span(2 * p + half, 64)
            b.dv_t[rows, :] = mm(b.hgr_t[rows, :], b.post[2 * p + half]).astype(bf16)

    each(pairs, back_post)

    def unflip(src, dst):
        for r in range(width // 256):
            dst[:, span(r, 256)] = mm_nt(i.eye[:padded, :], src[span(r, 256), :]).astype(bf16)

    unflip(b.dv_t, b.dv)
    for g in range(head):
        b.turn_v[g, :, 0:128] = b.dv[:, tile(g)]
        v3 = b.dv[:, tile(head + g // 2)].astype(f32)
        if g % 2:
            v3 = pltpu.roll(v3, 64, 1)
        b.turn_v[g, :, 128:256] = jnp.where(low_half, v3, 0.0).astype(bf16)
    turn_v.start()
    b.turned_v[at.s] = b.turn_v[at.s]
    sc_up.middle(2)

    def back_soften(j):
        grad = slab(b.pg, j)
        probs = slab(b.pr, j)
        b.mix_two[...] += mm_nt(grad, probs.astype(bf16))
        probs_grad = mixed(b.kron_t, 1, grad)
        inner = jnp.sum(probs_grad * probs, axis=-1, keepdims=True)
        mixed_grad = (probs * (probs_grad - inner)).astype(bf16)
        b.mix_one[...] += mm_nt(mixed_grad, slab(b.sc, j))
        put(b.pg, j, mixed(b.kron_t, 0, mixed_grad).astype(bf16))

    each(chunks, back_soften)

    def back_score(p):
        k = b.k[:, tile(p)]
        b.dq[:, tile(p)] = (
            (mm(b.pg[2 * p], k * lo_b) + mm(b.pg[2 * p + 1], k * hi_b)) * scale
        ).astype(bf16)
        for half in range(2):
            rows = span(2 * p + half, 64)
            b.dk_t[rows, :] = mm(b.q_t[rows, :], b.pg[2 * p + half]).astype(bf16)

    each(pairs, back_score)
    unflip(b.dk_t, b.dk)
    for g in range(head):
        b.turn[g, :, 0:128] = b.dq[:, tile(g)]
        b.turn[g, :, 128:256] = b.dk[:, tile(g)]
        third = tile(head + g // 2)
        q3, k3 = b.dq[:, third].astype(f32), b.dk[:, third].astype(f32)
        if g % 2:
            q3 = pltpu.roll(q3, 64, 1)
        else:
            k3 = pltpu.roll(k3, 64, 1)
        b.turn[g, :, 256:384] = jnp.where(low_half, q3, k3).astype(bf16)
    turn.start()
    b.turned[at.s] = b.turn[at.s]
    for k in range(3, at.lines):
        sc_up.middle(k)
    ag.forward()

    for g in range(head):
        part = mm_nt(b.turn[g], b.wqk[g]) + mm_nt(b.turn_v[g], b.wv[g])
        if g:
            b.hid[:padded, :] += part
        else:
            b.hid[:padded, :] = part
    gain_sum, shift_sum = zero, zero
    for j in range(chunks):
        grad = b.hid[chunk(j), :]
        xhat, rs = norm_rows(b.tok[at.s, chunk(j), :].astype(f32))
        inner = norm_back_rows(grad, b.norms[0:1, :], xhat, rs)
        b.inp[at.s, chunk(j), :] = (b.mg[chunk(j), :] + inner).astype(bf16)
        gain_sum += fold_rows(grad * xhat)
        shift_sum += fold_rows(grad)
    b.sums[0:1, :] = jnp.sum(gain_sum, axis=0, keepdims=True)
    b.sums[1:2, :] = jnp.sum(shift_sum, axis=0, keepdims=True)

    blocks = jnp.zeros((head * 8, 128), f32)
    for table, pick in ((b.mix_one, i.pick_pre_t), (b.mix_two, i.pick_post_t)):
        blocks += exact(exact(pick[...], table[...] * diagonal), i.place_f[...])
    blocks = blocks.reshape(head, 8, 128)
    b.sums[4:8, :] = jnp.zeros((4, width), f32)
    for g in range(head):
        b.small[g, :, :width] = b.sums[...]
        b.small[g, :, width:] = blocks[g]
    small_head.start()
    b.small_slots[at.s] = b.small[at.s]
    sc_down.middle(1)
    turn_v.wait()
    inp.start()

    ag.wait_mate()
    ag.wait_corner()
    flip(b.ag, b.og_t)

    def heads_mine():
        return jnp.concatenate(
            [
                b.ho[:, :, tile(at.s)].reshape(images * padded, 128),
                b.ho[:, :, tile(head + at.s // 2)].reshape(images * padded, 128),
            ],
            axis=1,
        )

    for r in range(width // 256):
        rows = span(r, 256)
        proj = mm(b.og_t[rows, :], heads_mine())
        values = mm(b.flip[rows, :], flat(b.turned_v))
        third = pltpu.roll(proj[:, 128:], 64 * (1 - at.c), 1)
        low = lax.broadcasted_iota(jnp.int32, third.shape, 1) < 64
        b.g_pv[rows, 0:128] = values[:, :128].astype(bf16)
        b.g_pv[rows, 128:256] = jnp.where(low, values[:, 128:], third).astype(bf16)
        b.g_pv[rows, 256:384] = proj[:, :128].astype(bf16)
    sc_pv.start()
    for k in range(2, at.lines):
        sc_down.middle(k)
    turn.wait()
    weight_grad(b.g_qk, b.flip, lambda: flat(b.turned))
    sc_qk.start()
    small_head.wait()
    b.small_dp[at.d] = small_head.total()
    small_dp.start()
    taps_in.wait()
    b.taps_all[at.d] = taps_in.total()
    taps_back.start()
    sc_pv.middle(1)
    fold_out.wait()
    for j in range(chunks):
        b.out[at.s, chunk(j), :] = (b.mid[0, chunk(j), :] + fold_out.total(chunk(j))).astype(bf16)
    out.start()
    for k in range(2, at.lines):
        sc_pv.middle(k)
    o.w_up[...] = sc_up.finish()
    for k in range(1, at.lines):
        sc_qk.middle(k)
    o.w_down[...] = sc_down.finish()
    inp.forward()
    small_dp.wait()
    small = small_dp.total()
    o.mixes[...] = small[:, width:]
    columns = lax.broadcasted_iota(jnp.int32, (8, width), 1)
    mine = (columns >= at.d * share) & (columns < (at.d + 1) * share)
    o.norms[...] = exact(jnp.where(mine, small[:, :width], 0.0), i.comb_t[...])
    out.forward()
    pv = sc_pv.finish()

    def turned_over(a):
        return lax.dot_general(
            i.eye_f[: a.shape[1], : a.shape[1]], a, NT, preferred_element_type=f32, precision=highest
        )

    o.w_v[:, 0:128] = pv[:, :128]
    o.w_v[:, 128:] = pv[:, 128:192]
    o.w_proj[:128, :] = turned_over(pv[:, 256:])
    o.w_proj[128:, :] = turned_over(pv[:, 128:256])[64:, :]
    taps_back.wait()
    o.taps[...] = b.taps_all[...]
    out.wait_mate()
    out.wait_corner()
    save_out = pltpu.make_async_copy(b.out, o.output, b.loads.at[0])
    save_out.start()
    inp.wait_mate()
    inp.wait_corner()
    save_inp = pltpu.make_async_copy(b.inp, o.input, b.loads.at[1])
    save_inp.start()
    o.qk[...] = sc_qk.finish()
    save_out.wait()
    save_inp.wait()
    for item in (
        gains, mixes, gq, gv, gp, gu, gd, ho, ag, out, inp, fold_two, fold_out, sc_up, sc_down, sc_qk, sc_pv,
        turn, turn_v, taps_in, taps_back, small_head, small_dp,
    ):
        item.drain()


def finish_kernel(sizes, *refs):
    local_heads, heads, share = sizes
    (output, inputs, qk, w_v, w_proj, up, down, norms, mixes, taps, deal_t) = refs[:11]
    (o_output, o_input, o_one_g, o_one_s, o_qkv, o_proj, o_pre, o_post, o_two_g, o_two_s, o_up, o_taps, o_down) = refs[11:]
    images, rows, width = output.shape
    for src, dst in ((output, o_output), (inputs, o_input)):
        for r in range(rows // 16):
            some = pl.ds(r * 16, 16)
            mixed = mm(deal_t[...], src[:, some, :].reshape(images * 16, width))
            dst[some] = mixed.astype(bf16).reshape(16, images, width)

    @pl.when(pl.program_id(0) == 0)
    def _():
        thirds = qk[:, 256:]
        o_qkv[0, :, 0:128] = qk[:, 0:128]
        o_qkv[0, :, 128:] = thirds[:, :64]
        o_qkv[1, :, 0:128] = qk[:, 128:256]
        o_qkv[1, :, 128:] = pltpu.roll(thirds, 64, 1)[:, :64]
        o_qkv[2] = w_v[...]
        o_proj[...] = w_proj[...]
        o_up[...] = up[...]
        o_down[...] = down[...]
        o_pre[...] = mixes[:local_heads, :heads]
        o_post[...] = mixes[4 : 4 + local_heads, :heads]
        for r, ref in enumerate((o_one_g, o_one_s, o_two_g, o_two_s)):
            ref[...] = norms[r : r + 1, :share]
        ksize = o_taps.shape[0]
        every = taps[...].reshape(taps.shape[0] * taps.shape[1], taps.shape[2])
        for p in range(ksize):
            o_taps[p] = every[p * ksize : (p + 1) * ksize, :]


def tables(seq, dp, head, heads, grid, ksize, share):
    cos, sin, cos_lag, sin_lag, back = spectrum(grid, ksize)
    used = cos.shape[0]
    bins = -(-used // 16) * 16
    padded = -(-seq // 16) * 16
    fourier = np.zeros((2 * bins, padded))
    fourier[:used, :seq] = cos
    fourier[bins : bins + used, :seq] = sin
    taps = ksize * ksize
    lag = np.zeros((2 * bins, -(-taps // 8) * 8))
    lag[:used, :taps] = cos_lag
    lag[bins : bins + used, :taps] = sin_lag
    lag_back = np.zeros((dp * 8, 2 * bins))
    lag_back[:taps, :used] = (cos_lag * back[:, None]).T
    lag_back[:taps, bins : bins + used] = (sin_lag * back[:, None]).T
    comb = (np.arange(share * dp)[None, :] % share == np.arange(128)[:, None]) & (
        np.arange(128)[:, None] < share
    )
    group = heads // head
    slot = [group * g + l for g in range(head) for l in range(2)] + [group * g + 2 for g in range(head)]
    wide = heads * 16
    pick = np.zeros((2, wide, head * 8))
    place = np.zeros((wide, 128))
    for p, h in enumerate(slot):
        for row in range(16):
            for which in range(2):
                pick[which, p * 16 + row, (h // group) * 8 + which * 4 + h % group] = 1.0
            place[p * 16 + row, h] = 1.0
    deal = np.zeros((16 * head, 16 * head))
    for token in range(16):
        for image in range(head):
            deal[image * 16 + token, token * head + image] = 1.0
    diagonal = (np.arange(wide)[:, None] % 16) == (np.arange(wide)[None, :] % 16)
    return {
        "fourier": jnp.asarray(fourier, bf16),
        "fourier_t": jnp.asarray(fourier.T, bf16),
        "lag": jnp.asarray(lag, f32),
        "lag_back": jnp.asarray(lag_back, f32),
        "comb": jnp.asarray(comb, bf16),
        "comb_t": jnp.asarray(comb.T, f32),
        "pick_pre": jnp.asarray(pick[0], bf16),
        "pick_post": jnp.asarray(pick[1], bf16),
        "pick_pre_t": jnp.asarray(pick[0].T, f32),
        "pick_post_t": jnp.asarray(pick[1].T, f32),
        "place": jnp.asarray(place, bf16),
        "place_f": jnp.asarray(place, f32),
        "diagonal": jnp.asarray(diagonal, f32),
        "eye": jnp.asarray(np.eye(256), bf16),
        "eye_f": jnp.asarray(np.eye(256), f32),
        "deal": jnp.asarray(deal, bf16),
        "deal_t": jnp.asarray(deal.T, bf16),
    }


def whole_block(
    tokens,
    ln1_gain,
    ln1_shift,
    w_qkv,
    w_proj,
    mix_pre,
    mix_post,
    ln2_gain,
    ln2_shift,
    w_up,
    conv_kernel,
    w_down,
    out_grad,
):
    images, seq, width = tokens.shape
    dp, head = lax.axis_size("dp"), lax.axis_size("head")
    local_heads, heads = mix_pre.shape
    size = width // heads
    local = local_heads * size
    share = w_qkv.shape[0]
    ksize, units = conv_kernel.shape[0], conv_kernel.shape[2]
    grid = int(round((seq - 1) ** 0.5))
    padded = -(-seq // 16) * 16
    wide = -(-seq // 128) * 128
    lines = dp // 2
    const = tables(seq, dp, head, heads, grid, ksize, share)
    bins = const["fourier"].shape[0] // 2

    inputs = {
        "tokens": jnp.transpose(tokens, (1, 0, 2)),
        "out_grad": jnp.transpose(out_grad, (1, 0, 2)),
        "ln1_gain": ln1_gain.reshape(1, share),
        "ln1_shift": ln1_shift.reshape(1, share),
        "ln2_gain": ln2_gain.reshape(1, share),
        "ln2_shift": ln2_shift.reshape(1, share),
        "mix_pre": mix_pre,
        "mix_post": mix_post,
        "w_qkv": jnp.transpose(w_qkv, (1, 0, 2)),
        "w_proj": w_proj,
        "w_up": w_up,
        "w_down": w_down.T,
        "taps": conv_kernel,
        **{name: value for name, value in const.items() if name != "deal_t"},
    }
    outputs = {
        "output": ((images, padded, width), bf16),
        "input": ((images, padded, width), bf16),
        "qk": ((share, 384), f32),
        "w_v": ((share, local), f32),
        "w_proj": ((local, share), f32),
        "w_up": ((share, units), f32),
        "w_down": ((share, units), f32),
        "norms": ((8, 128), f32),
        "mixes": ((8, 128), f32),
        "taps": ((dp, 8, units), f32),
    }
    finals = {
        "output": ((seq, images, width), bf16),
        "input": ((seq, images, width), bf16),
        "ln1_gain": ((1, share), f32),
        "ln1_shift": ((1, share), f32),
        "w_qkv": ((3, share, local), f32),
        "w_proj": ((local, share), f32),
        "mix_pre": ((local_heads, heads), f32),
        "mix_post": ((local_heads, heads), f32),
        "ln2_gain": ((1, share), f32),
        "ln2_shift": ((1, share), f32),
        "w_up": ((share, units), f32),
        "taps": ((ksize, ksize, units), f32),
        "w_down": ((share, units), f32),
    }
    one, every = (padded, width), (images, padded, width)
    square = (heads, padded, wide)
    table = (heads * 16, heads * 16)
    scratch = {
        "tok": (every, bf16),
        "og": (every, bf16),
        "raw": ((2, seq, images, width), bf16),
        "edge": ((const["lag"].shape[1], units), f32),
        "wqk": ((head, width, 384), bf16),
        "wv": ((head, width, 256), bf16),
        "wp_two": ((head, width, 128), bf16),
        "wp": ((width, width), bf16),
        "wu": ((width, units), bf16),
        "wd": ((width, units), bf16),
        "gains": ((dp, 8, 128), f32),
        "mixes": ((head, 8, 128), f32),
        "norms": ((8, width), f32),
        "filt": ((2 * bins, units), f32),
        "cross": ((2 * bins, units), f32),
        "wave": ((2 * bins, units), f32),
        "fi": ((2 * bins, units), bf16),
        "gf": ((images, 2 * bins, units), bf16),
        "actg": ((images, padded, units), bf16),
        "act": ((2, padded, units), bf16),
        "n1": (every, bf16),
        "n2": (every, bf16),
        "mid": ((2, *one), f32),
        "hid": ((2 * padded, width), f32),
        "wid": ((images, padded, units), bf16),
        "hg": ((images, padded, units), bf16),
        "np": (every, bf16),
        "np_near": ((2, *one), bf16),
        "np_far": (one, bf16),
        "bp_near": ((2, *one), bf16),
        "bp_far": (one, bf16),
        "flip": ((width, images * padded), bf16),
        "q": (one, bf16),
        "k": ((wide, width), bf16),
        "v": ((wide, width), bf16),
        "third_qk": ((head, padded, 128), f32),
        "third_v": ((head, padded, 128), f32),
        "kron": ((2, 2, *table), bf16),
        "kron_t": ((2, 2, *table), bf16),
        "mix_one": (table, f32),
        "mix_two": (table, f32),
        "sc": (square, bf16),
        "pr": (square, f32),
        "post": (square, bf16),
        "pg": (square, bf16),
        "ho": (every, bf16),
        "ag": (every, bf16),
        "hgr": (one, bf16),
        "hgr_t": ((width, padded), bf16),
        "q_t": ((width, padded), bf16),
        "dv_t": ((width, wide), bf16),
        "dk_t": ((width, wide), bf16),
        "dv": (one, bf16),
        "turn": ((head, padded, 384), bf16),
        "turned": ((head, padded, 384), bf16),
        "turn_v": ((head, padded, 256), bf16),
        "turned_v": ((head, padded, 256), bf16),
        "og_t": ((width, images * padded), bf16),
        "sums": ((8, width), f32),
        "small": ((head, 8, width + 128), f32),
        "small_slots": ((head, 8, width + 128), f32),
        "small_dp": ((dp, 8, width + 128), f32),
        "taps": ((dp * 8, units), f32),
        "taps_slots": ((dp, 8, units), f32),
        "taps_all": ((dp, 8, units), f32),
    }
    for name, columns in (("up", units), ("down", units), ("qk", 384), ("pv", 384)):
        scratch["g_" + name] = ((width, columns), bf16)
        scratch[name + "_y"] = ((lines, share, columns), bf16)
        scratch[name + "_z"] = ((lines - 1, share, columns), bf16)
    sems = {"ga": dp - 1, "mi": head - 1, "ho": 3, "ag": 3, "ou": 3, "in": 3, "np": 3, "bp": 3}
    sems |= {"tv": head - 1, "tu": head - 1, "ti": dp - 1, "tb": dp - 1, "sh": head - 1, "sd": dp - 1}
    for name in "qvpud":
        sems |= {name + "z": (1 if name == "q" else 2) * (lines - 1), name + "y": lines}
        sems |= {name + "y2": lines, name + "z2": lines - 1}
    for name in "qvp":
        sems |= {name + "x": dp, name + "m": 2 * dp}
    shapes = {name: pltpu.VMEM(*spec) for name, spec in scratch.items()}
    for name, number in sems.items():
        shapes[name + "_s"] = pltpu.SemaphoreType.DMA((number,))
        shapes[name + "_r"] = pltpu.SemaphoreType.DMA((number,))
    shapes["loads"] = pltpu.SemaphoreType.DMA((4,))
    vmem = pl.BlockSpec(memory_space=pltpu.VMEM)
    left = pl.BlockSpec(memory_space=pl.ANY)
    results = pl.pallas_call(
        functools.partial(
            block_kernel,
            (seq, dp, head, size ** (-0.5)),
            tuple(inputs),
            tuple(outputs),
            tuple(shapes),
        ),
        out_shape=[jax.ShapeDtypeStruct(*spec) for spec in outputs.values()],
        in_specs=[left if n in ("tokens", "out_grad", "w_up", "w_down") else vmem for n in inputs],
        out_specs=[left if n in ("output", "input") else vmem for n in outputs],
        scratch_shapes=list(shapes.values()),
        compiler_params=pltpu.CompilerParams(
            collective_id=0, has_side_effects=True, vmem_limit_bytes=64 * 2**20
        ),
    )(*inputs.values())
    r = dict(zip(outputs, results))

    def kept(shape):
        return pl.BlockSpec(shape, lambda j: (0,) * len(shape))

    parts = [*r.values(), const["deal_t"]]
    step = -(-padded // (16 * 2)) * 16
    by_rows = pl.BlockSpec((images, step, width), lambda j: (0, j, 0))
    by_tokens = pl.BlockSpec((step, images, width), lambda j: (j, 0, 0))
    results = pl.pallas_call(
        functools.partial(finish_kernel, (local_heads, heads, share)),
        grid=(-(-padded // step),),
        out_shape=[jax.ShapeDtypeStruct(*spec) for spec in finals.values()],
        in_specs=[by_rows] * 2 + [kept(part.shape) for part in parts[2:]],
        out_specs=[by_tokens] * 2 + [kept(spec[0]) for spec in list(finals.values())[2:]],
    )(*parts)
    r = dict(zip(finals, results))
    for name in ("output", "input", "w_qkv"):
        r[name] = jnp.transpose(r[name], (1, 0, 2))
    for name in ("ln1_gain", "ln1_shift", "ln2_gain", "ln2_shift"):
        r[name] = r[name].reshape(share)
    r["w_down"] = r["w_down"].T
    return tuple(r.values())


def solution(mesh):
    in_specs = (
        P("dp", None, None),
        P("dp"),
        P("dp"),
        P("dp", None, "head"),
        P("head", "dp"),
        P("head", None),
        P("head", None),
        P("dp"),
        P("dp"),
        P("dp", "head"),
        P(None, None, "head"),
        P("head", "dp"),
        P("dp", None, None),
    )
    out_specs = (
        P("dp", None, None),
        P("dp", None, None),
        P("dp"),
        P("dp"),
        P("dp", None, "head"),
        P("head", "dp"),
        P("head", None),
        P("head", None),
        P("dp"),
        P("dp"),
        P("dp", "head"),
        P(None, None, "head"),
        P("head", "dp"),
    )
    dp, head = mesh.shape["dp"], mesh.shape["head"]

    def shards(*args):
        tokens, w_qkv, mix_pre = args[0], args[3], args[5]
        fits = head == 4 and dp % 2 == 0 and w_qkv.shape[0] % 32 == 0 and w_qkv.shape[0] <= 128
        fits = fits and dp * 8 >= args[10].shape[0] ** 2 and tokens.shape[0] == head
        fits = fits and mix_pre.shape[0] == 3 and tokens.shape[2] == 64 * mix_pre.shape[1]
        return (whole_block if fits else plain)(*args)

    return jax.shard_map(shards, mesh=mesh, in_specs=in_specs, out_specs=out_specs, check_vma=False)
```

```python
import functools
import types

import jax
import jax.numpy as jnp
import numpy as np
from jax import lax
from jax.experimental import pallas as pl
from jax.experimental.pallas import tpu as pltpu
from jax.sharding import PartitionSpec as P

highest = lax.Precision.HIGHEST
epsilon = 1e-06
bf16 = jnp.bfloat16
f32 = jnp.float32


def spectrum(grid, ksize):
    margin = ksize // 2
    period = grid + margin
    pairs = [(0, 0)] + [(0, v) for v in range(1, period // 2 + 1)]
    pairs += [(u, v) for u in range(1, period // 2 + 1) for v in range(period)]
    freq = np.array(pairs, np.float64)
    place = np.array([(r, c) for r in range(grid) for c in range(grid)], np.float64)
    lags = np.array([(p - margin, q - margin) for p in range(ksize) for q in range(ksize)], np.float64)
    weight = np.sqrt(np.where(np.arange(len(pairs)) == 0, 1.0, 2.0)) / period
    angle = 2 * np.pi / period * freq @ place.T
    angle_lag = 2 * np.pi / period * freq @ lags.T
    count = len(pairs)
    cos = np.zeros((count + 1, grid * grid + 1))
    sin = np.zeros_like(cos)
    cos[:count, 1:] = weight[:, None] * np.cos(angle)
    sin[:count, 1:] = weight[:, None] * np.sin(angle)
    cos[count, 0] = 1.0
    cos_lag = np.zeros((count + 1, ksize * ksize))
    sin_lag = np.zeros_like(cos_lag)
    cos_lag[:count] = np.cos(angle_lag)
    sin_lag[:count] = np.sin(angle_lag)
    back = np.zeros(count + 1)
    back[:count] = 1.0
    return cos, sin, cos_lag, sin_lag, back


def layer_norm(values, gain, shift):
    center = jnp.mean(values, axis=-1, keepdims=True)
    centered = values - center
    spread = jnp.mean(centered * centered, axis=-1, keepdims=True)
    rs = lax.rsqrt(spread + epsilon)
    xhat = centered * rs
    return xhat * gain + shift, xhat, rs


def norm_back(grad, gain, xhat, rs):
    e = grad * gain
    inner = rs * (
        e
        - jnp.mean(e, axis=-1, keepdims=True)
        - xhat * jnp.mean(e * xhat, axis=-1, keepdims=True)
    )
    return inner, jnp.sum(grad * xhat, axis=(0, 1)), jnp.sum(grad, axis=(0, 1))


def dot(spec, a, b):
    return jnp.einsum(spec, a, b, preferred_element_type=f32)


def plain(
    tokens,
    ln1_gain,
    ln1_shift,
    w_qkv,
    w_proj,
    mix_pre,
    mix_post,
    ln2_gain,
    ln2_shift,
    w_up,
    conv_kernel,
    w_down,
    out_grad,
):
    images, seq, width = tokens.shape
    heads_local, heads = mix_pre.shape
    size = width // heads
    scale = size ** (-0.5)
    ksize = conv_kernel.shape[0]
    units = conv_kernel.shape[2]
    grid = int(round((seq - 1) ** 0.5))
    cos, sin, cos_lag, sin_lag, back = spectrum(grid, ksize)
    fourier = jnp.asarray(np.stack([cos, sin]), bf16)
    lagged = jnp.asarray(np.stack([cos_lag, sin_lag]), f32)
    lagged_back = jnp.asarray(np.stack([cos_lag, sin_lag]) * back[:, None], f32)
    mine = lax.axis_index("head")

    gains = jnp.stack([ln1_gain, ln1_shift, ln2_gain, ln2_shift])
    gains = lax.all_gather(gains, "dp", axis=1, tiled=True).astype(f32)
    gain_one, shift_one, gain_two, shift_two = gains[0], gains[1], gains[2], gains[3]
    qkv_w = lax.all_gather(w_qkv, "dp", axis=0, tiled=True)
    up_w = lax.all_gather(w_up, "dp", axis=0, tiled=True)
    down_w = lax.all_gather(w_down, "dp", axis=1, tiled=True)
    proj_w = lax.all_gather(w_proj, "head", axis=0, tiled=True)
    proj_w = lax.all_gather(proj_w, "dp", axis=1, tiled=True)
    mixes = lax.all_gather(jnp.stack([mix_pre, mix_post]), "head", axis=1, tiled=True)
    pre, post_mix = mixes[0], mixes[1]

    source = tokens.astype(f32)
    normed_one, xhat_one, rs_one = layer_norm(source, gain_one, shift_one)
    normed_one = normed_one.astype(bf16)
    qkv = dot("ind,dce->ince", normed_one, qkv_w).astype(bf16)
    qkv = lax.all_to_all(qkv, "head", split_axis=0, concat_axis=3, tiled=True)
    own = qkv.shape[0]
    query = qkv[:, :, 0].reshape(own, seq, heads, size)
    keys = qkv[:, :, 1].reshape(own, seq, heads, size)
    values = qkv[:, :, 2].reshape(own, seq, heads, size)
    scores = (dot("inhd,imhd->ihnm", query, keys) * scale).astype(bf16)
    mixed = jnp.einsum("hg,ignm->ihnm", pre, scores.astype(f32), precision=highest)
    probs = jax.nn.softmax(mixed, axis=-1)
    probs_low = probs.astype(bf16)
    post = jnp.einsum(
        "hg,ignm->ihnm", post_mix, probs_low.astype(f32), precision=highest
    ).astype(bf16)
    heads_own = dot("ihnm,imhd->inhd", post, values).reshape(own, seq, width).astype(bf16)
    heads_out = lax.all_gather(heads_own, "head", axis=0, tiled=True)
    middle = source + dot("ine,ed->ind", heads_out, proj_w)
    normed_two, xhat_two, rs_two = layer_norm(middle, gain_two, shift_two)
    normed_two = normed_two.astype(bf16)
    hidden = dot("ind,df->inf", normed_two, up_w)
    erf = lax.erf(hidden * (0.5**0.5))
    activ = 0.5 * hidden * (1.0 + erf)
    slope = 0.5 * (1.0 + erf) + hidden * jnp.exp(-0.5 * hidden * hidden) * 0.3989422804014327
    delta = np.zeros((ksize * ksize, 1), np.float32)
    delta[ksize * ksize // 2] = 1.0
    taps = conv_kernel.reshape(ksize * ksize, units)
    filters = jnp.einsum("zkl,lf->zkf", lagged, taps, precision=highest)
    cos_k, sin_k = filters[0] + 1.0, filters[1]
    wave = dot("zkn,inf->zikf", fourier, activ.astype(bf16))
    cos_a, sin_a = wave[0], wave[1]
    filtered = jnp.stack([cos_k * cos_a + sin_k * sin_a, cos_k * sin_a - sin_k * cos_a])
    widened = dot("zkn,zikf->inf", fourier, filtered.astype(bf16)).astype(bf16)
    branch = dot("inf,fd->ind", widened, down_w)
    branch = lax.psum(branch.astype(bf16), "head").astype(f32)
    output = (middle + branch).astype(bf16)

    down_grad = dot("inf,ind->fd", widened, out_grad)
    widened_grad = dot("ind,fd->inf", out_grad, down_w)
    wave_grad = dot("zkn,inf->zikf", fourier, widened_grad.astype(bf16))
    cos_g, sin_g = wave_grad[0], wave_grad[1]
    spread_grad = jnp.stack([cos_k * cos_g - sin_k * sin_g, cos_k * sin_g + sin_k * cos_g])
    activ_grad = dot("zkn,zikf->inf", fourier, spread_grad.astype(bf16))
    hidden_grad = (activ_grad * slope).astype(bf16)
    cross = jnp.stack(
        [
            jnp.sum(cos_a * cos_g + sin_a * sin_g, axis=0),
            jnp.sum(sin_a * cos_g - cos_a * sin_g, axis=0),
        ]
    )
    kernel_grad = jnp.einsum("zkl,zkf->lf", lagged_back, cross, precision=highest)
    up_grad = dot("ind,inf->df", normed_two, hidden_grad)
    two_grad = dot("inf,df->ind", hidden_grad, up_w).astype(bf16)
    two_grad = lax.psum_scatter(two_grad, "head", scatter_dimension=0, tiled=True).astype(f32)

    def pick(array):
        return lax.dynamic_slice_in_dim(array, mine * own, own, 0)

    middle_from, gain_two_grad, shift_two_grad = norm_back(
        two_grad, gain_two, pick(xhat_two), pick(rs_two)
    )
    middle_grad = pick(out_grad).astype(f32) + middle_from
    attention_own = middle_grad.astype(bf16)
    attention_grad = lax.all_gather(attention_own, "head", axis=0, tiled=True)
    local = width // lax.axis_size("head")
    heads_mine = lax.dynamic_slice_in_dim(heads_out, mine * local, local, 2)
    proj_grad = dot("ine,ind->ed", heads_mine, attention_grad)
    heads_grad = dot("ind,ed->ine", attention_own, proj_w).astype(bf16)
    heads_grad = heads_grad.reshape(own, seq, heads, size)
    values_grad = dot("ihnm,inhd->imhd", post, heads_grad)
    post_grad = dot("inhd,imhd->ihnm", heads_grad, values)
    probs_grad = jnp.einsum("hg,ihnm->ignm", post_mix, post_grad, precision=highest)
    mixed_grad = probs * (probs_grad - jnp.sum(probs_grad * probs, axis=-1, keepdims=True))
    scores_grad = jnp.einsum("hg,ihnm->ignm", pre, mixed_grad, precision=highest).astype(bf16)
    post_mix_grad = dot("ihnm,ignm->hg", post_grad.astype(bf16), probs_low)
    pre_mix_grad = dot("ihnm,ignm->hg", mixed_grad.astype(bf16), scores)
    query_grad = dot("ihnm,imhd->inhd", scores_grad, keys) * scale
    keys_grad = dot("ihnm,inhd->imhd", scores_grad, query) * scale
    qkv_grad = jnp.stack([query_grad, keys_grad, values_grad], axis=2)
    qkv_grad = qkv_grad.reshape(own, seq, 3, width).astype(bf16)
    qkv_grad = lax.all_to_all(qkv_grad, "head", split_axis=3, concat_axis=0, tiled=True)
    qkv_weight_grad = dot("ind,ince->dce", normed_one, qkv_grad)
    one_grad = dot("ince,dce->ind", qkv_grad, qkv_w).astype(bf16)
    one_grad = lax.psum_scatter(one_grad, "head", scatter_dimension=0, tiled=True).astype(f32)
    source_grad, gain_one_grad, shift_one_grad = norm_back(
        one_grad, gain_one, pick(xhat_one), pick(rs_one)
    )
    input_own = (middle_grad + source_grad).astype(bf16)
    input_grad = lax.all_gather(input_own, "head", axis=0, tiled=True)

    def share(grad, axis):
        return lax.psum_scatter(
            grad.astype(bf16), "dp", scatter_dimension=axis, tiled=True
        ).astype(f32)

    norm_grads = jnp.stack([gain_one_grad, shift_one_grad, gain_two_grad, shift_two_grad])
    norm_grads = lax.psum(norm_grads, "head")
    norm_grads = lax.psum_scatter(norm_grads, "dp", scatter_dimension=1, tiled=True)
    mix_grads = lax.psum_scatter(
        jnp.stack([pre_mix_grad, post_mix_grad]), "head", scatter_dimension=1, tiled=True
    )
    mix_grads, kernel_grad = lax.psum((mix_grads, kernel_grad), "dp")
    return (
        output,
        input_grad,
        norm_grads[0],
        norm_grads[1],
        share(qkv_weight_grad, 0),
        share(proj_grad, 1),
        mix_grads[0],
        mix_grads[1],
        norm_grads[2],
        norm_grads[3],
        share(up_grad, 0),
        kernel_grad.reshape(ksize, ksize, units),
        share(down_grad, 1),
    )


MESH = pl.DeviceIdType.MESH
NT = (((1,), (1,)), ((), ()))


def mm(a, b):
    return jnp.dot(a, b, preferred_element_type=f32)


def mm_nt(a, b):
    return lax.dot_general(a, b, NT, preferred_element_type=f32)


def exact(a, b):
    return jnp.dot(a, b, preferred_element_type=f32, precision=highest)


def split(a):
    high = a.astype(bf16)
    return high, (a - high.astype(f32)).astype(bf16)


def remote(src, dst, send, recv, device):
    return pltpu.make_async_remote_copy(
        src_ref=src,
        dst_ref=dst,
        send_sem=send,
        recv_sem=recv,
        device_id=device,
        device_id_type=MESH,
    )


class Place:
    def __init__(self, dp, head):
        self.dp, self.head = dp, head
        self.lines = dp // 2
        self.d, self.s = lax.axis_index("dp"), lax.axis_index("head")
        self.z, self.y = self.d // 2, self.d % 2
        self.x, self.c = self.s // 2, self.s % 2
        self.mate = self.x * 2 + 1 - self.c
        self.across = (1 - self.x) * 2 + self.c
        self.corner = (1 - self.x) * 2 + 1 - self.c

    def near(self, j):
        return ((self.x + j // 2) % 2) * 2 + (self.c + j % 2) % 2

    def z_next(self, k):
        return (self.z + k) % self.lines

    def z_prev(self, k):
        return (self.z + self.lines - k) % self.lines

    def head_next(self, k):
        return (self.s + k) % self.head

    def dp_next(self, k):
        return (self.d + k) % self.dp

    def call(self):
        barrier = pltpu.get_barrier_semaphore()

        def tell(d, s):
            pl.semaphore_signal(barrier, inc=1, device_id=(d, s), device_id_type=MESH)

        tell(self.d, self.mate)
        tell(self.d, self.across)
        tell(self.z * 2 + 1 - self.y, self.s)
        pl.when(self.z > 0)(lambda: tell((self.z - 1) * 2 + self.y, self.s))
        pl.when(self.z < self.lines - 1)(lambda: tell((self.z + 1) * 2 + self.y, self.s))

    def answer(self):
        inner = (self.z > 0) & (self.z < self.lines - 1)
        pl.semaphore_wait(pltpu.get_barrier_semaphore(), jnp.where(inner, 5, 4))


def rows_of(ref, index, count):
    return ref.at[pl.ds(pl.multiple_of(index * count, count), count)]


class Line:
    def __init__(self, at, buf, sems, wide):
        self.at, self.wide = at, wide
        self.groups = buf
        self.buf = buf.at[at.s] if wide else buf
        self.rows = self.buf.shape[0] // at.dp
        self.sems = sems

    def near(self, hops, body):
        at = self.at
        if hops == 0:
            body(at.z)
        else:
            pl.when(at.z >= hops)(lambda: body(at.z - hops))
            pl.when(at.z + hops < at.lines)(lambda: body(at.z + hops))

    def index(self, z, other):
        return z * 2 + (1 - self.at.y if other else self.at.y)

    def block(self, z, other, buf=None):
        return rows_of(self.buf if buf is None else buf, self.index(z, other), self.rows)

    def z_copy(self, up, hops):
        at, (send, recv) = self.at, self.sems[0]
        ref = self.block(at.z - hops if up else at.z + hops, False)
        slot = hops if up else at.lines - 1 + hops
        to = at.z + 1 if up else at.z - 1
        return remote(ref, ref, send.at[slot], recv.at[slot], (to * 2 + at.y, at.s))

    def pass_on(self, up, hops):
        at = self.at
        if up:
            there = (at.z >= hops) & (at.z < at.lines - 1)
        else:
            there = (at.z + hops < at.lines) & (at.z > 0)
        return pl.when(there)

    def y_copy(self, z):
        at, (send, recv) = self.at, self.sems[1]
        ref = self.block(z, False)
        return remote(ref, ref, send.at[z], recv.at[z], (at.z * 2 + 1 - at.y, at.s))

    def x_copy(self, z, other):
        at, (send, recv) = self.at, self.sems[2]
        ref, slot = self.block(z, other), self.index(z, other)
        return remote(ref, ref, send.at[slot], recv.at[slot], (at.d, at.across))

    def mate_copy(self, z, other, far):
        at, (send, recv) = self.at, self.sems[3]
        ref = self.block(z, other, self.groups.at[at.across if far else at.s])
        slot = self.index(z, other) + (at.dp if far else 0)
        return remote(ref, ref, send.at[slot], recv.at[slot], (at.d, at.mate))

    def begin(self):
        for up in (True, False):
            self.pass_on(up, 0)(lambda: self.z_copy(up, 0).start())

    def over_y(self):
        self.y_copy(self.at.z).start()

    def from_z(self, hops):
        at = self.at
        for up in (True, False):

            @pl.when(at.z >= hops if up else at.z + hops < at.lines)
            def _():
                source = at.z - hops if up else at.z + hops
                self.z_copy(up, hops - 1).wait_recv()
                if hops < at.lines - 1:
                    self.pass_on(up, hops)(lambda: self.z_copy(up, hops).start())
                self.y_copy(source).start()

    def on(self, hops, other):
        def body(z):
            self.x_copy(z, other).start()
            self.mate_copy(z, other, False).start()

        self.near(hops, body)

    def from_y(self, hops):
        self.near(hops, lambda z: self.y_copy(z).wait_recv())

    def from_x(self, hops, other):
        def body(z):
            self.x_copy(z, other).wait_recv()
            self.mate_copy(z, other, True).start()

        self.near(hops, body)

    def from_mate(self, far):
        for z in range(self.at.lines):
            for other in (False, True):
                self.mate_copy(z, other, far).wait_recv()

    def drain(self):
        at = self.at
        for hops in range(at.lines - 1):
            for up in (True, False):
                self.pass_on(up, hops)(lambda: self.z_copy(up, hops).wait_send())
        for z in range(at.lines):
            self.y_copy(z).wait_send()
            if self.wide:
                for other in (False, True):
                    self.x_copy(z, other).wait_send()
                    self.mate_copy(z, other, False).wait_send()
                    self.mate_copy(z, other, True).wait_send()


class Rows(Line):
    def both(self, z):
        return rows_of(self.buf, z, 2 * self.rows)

    def z_copy(self, up, hops):
        at, (send, recv) = self.at, self.sems[0]
        ref = self.both(at.z - hops if up else at.z + hops)
        slot = hops if up else at.lines - 1 + hops
        to = at.z + 1 if up else at.z - 1
        return remote(ref, ref, send.at[slot], recv.at[slot], (to * 2 + at.y, at.s))

    def from_y(self):
        self.y_copy(self.at.z).wait_recv()
        self.begin()

    def from_z(self, hops):
        at = self.at
        for up in (True, False):

            @pl.when(at.z >= hops if up else at.z + hops < at.lines)
            def _():
                self.z_copy(up, hops - 1).wait_recv()
                if hops < at.lines - 1:
                    self.pass_on(up, hops)(lambda: self.z_copy(up, hops).start())

    def drain(self):
        at = self.at
        self.y_copy(at.z).wait_send()
        for hops in range(at.lines - 1):
            for up in (True, False):
                self.pass_on(up, hops)(lambda: self.z_copy(up, hops).wait_send())


class Share:
    def __init__(self, at, buf, sems):
        self.at, self.buf = at, buf
        self.send, self.recv = sems

    def copy(self, which):
        at = self.at
        ref = self.buf.at[at.across if which == 2 else at.s]
        to = at.across if which == 1 else at.mate
        return remote(ref, ref, self.send.at[which], self.recv.at[which], (at.d, to))

    def start(self):
        self.copy(1).start()
        self.copy(0).start()

    def wait_mate(self):
        self.copy(0).wait_recv()

    def forward(self):
        self.copy(1).wait_recv()
        self.copy(2).start()

    def wait_corner(self):
        self.copy(2).wait_recv()

    def drain(self):
        for which in range(3):
            self.copy(which).wait_send()


class Fold:
    def __init__(self, at, parts, near, far, sems):
        self.at, self.parts, self.near, self.far = at, parts, near, far
        self.send, self.recv = sems

    def mate_copy(self, which):
        at = self.at
        src = self.parts.at[at.corner if which else at.mate]
        return remote(
            src, self.near.at[which], self.send.at[which], self.recv.at[which], (at.d, at.mate)
        )

    def x_copy(self):
        at = self.at
        return remote(
            self.parts.at[at.across], self.far, self.send.at[2], self.recv.at[2], (at.d, at.across)
        )

    def middle(self):
        at = self.at
        self.mate_copy(1).wait_recv()
        self.parts[at.across] = (
            self.parts[at.across].astype(f32) + self.near[1].astype(f32)
        ).astype(bf16)
        self.x_copy().start()

    def wait(self):
        self.mate_copy(0).wait_recv()
        self.x_copy().wait_recv()

    def total(self, rows):
        return (
            self.parts[self.at.s, rows, :].astype(f32)
            + self.near[0, rows, :].astype(f32)
            + self.far[rows, :].astype(f32)
        )

    def drain(self):
        self.mate_copy(0).wait_send()
        self.mate_copy(1).wait_send()
        self.x_copy().wait_send()


class Scatter:
    def __init__(self, at, src, from_y, from_z, sems):
        self.at, self.src, self.from_y, self.from_z = at, src, from_y, from_z
        (self.y_send, self.y_recv), (self.z_send, self.z_recv) = sems
        self.rows = src.shape[0] // at.dp

    def block(self, z, y):
        return rows_of(self.src, z * 2 + y, self.rows)

    def y_copy(self, k):
        at = self.at
        return remote(
            self.block(at.z_next(k), 1 - at.y),
            self.from_y.at[k],
            self.y_send.at[k],
            self.y_recv.at[k],
            (at.z * 2 + 1 - at.y, at.s),
        )

    def z_copy(self, k):
        at = self.at
        return remote(
            self.block(at.z_next(k), at.y),
            self.from_z.at[k - 1],
            self.z_send.at[k - 1],
            self.z_recv.at[k - 1],
            (at.z_next(k) * 2 + at.y, at.s),
        )

    def start(self):
        for k in (*range(1, self.at.lines), 0):
            self.y_copy(k).start()

    def middle(self, k):
        at = self.at
        self.y_copy(k).wait_recv()
        ref = self.block(at.z_next(k), at.y)
        ref[...] = (ref[...].astype(f32) + self.from_y[k].astype(f32)).astype(bf16)
        self.z_copy(k).start()

    def finish(self):
        at = self.at
        self.y_copy(0).wait_recv()
        total = self.block(at.z, at.y)[...].astype(f32) + self.from_y[0].astype(f32)
        for k in range(1, at.lines):
            self.z_copy(k).wait_recv()
            total = total + self.from_z[k - 1].astype(f32)
        return total

    def drain(self):
        for k in range(self.at.lines):
            self.y_copy(k).wait_send()
        for k in range(1, self.at.lines):
            self.z_copy(k).wait_send()


class Halves(Scatter):
    def partner(self, k):
        z = self.at.z
        return (3 - z, z + 1 - 2 * (z % 2), (z + 2) % 4, z)[k]

    def y_copy(self, k):
        at = self.at
        return remote(
            self.block(self.partner(k), 1 - at.y),
            self.from_y.at[k],
            self.y_send.at[k],
            self.y_recv.at[k],
            (at.z * 2 + 1 - at.y, at.s),
        )

    def z_copy(self, k):
        at = self.at
        return remote(
            self.block(self.partner(k), at.y),
            self.from_z.at[k],
            self.z_send.at[k],
            self.z_recv.at[k],
            (self.partner(max(k, 1)) * 2 + at.y, at.s),
        )

    def start(self):
        for k in range(4):
            self.y_copy(k).start()

    def middle(self, k):
        at, k = self.at, k - 1
        self.y_copy(k).wait_recv()
        ref = self.block(self.partner(k), at.y)
        total = ref[...].astype(f32) + self.from_y[k].astype(f32)
        if k == 2:
            self.z_copy(0).wait_recv()
            total = total + self.from_z[0].astype(f32)
        ref[...] = total.astype(bf16)
        self.z_copy(k).start()

    def finish(self):
        at = self.at
        self.y_copy(3).wait_recv()
        total = self.block(at.z, at.y)[...].astype(f32) + self.from_y[3].astype(f32)
        for k in (1, 2):
            self.z_copy(k).wait_recv()
            total = total + self.from_z[k].astype(f32)
        return total

    def drain(self):
        for k in range(4):
            self.y_copy(k).wait_send()
        for k in range(3):
            self.z_copy(k).wait_send()


class Exchange:
    def __init__(self, at, axis, slots, sems, block_for):
        self.at, self.axis, self.slots, self.block_for = at, axis, slots, block_for
        self.send, self.recv = sems
        self.count = at.dp if axis == "dp" else at.head
        self.me = at.d if axis == "dp" else at.s

    def copy(self, k):
        at = self.at
        peer = (self.me + k) % self.count
        device = (peer, at.s) if self.axis == "dp" else (at.d, peer)
        return remote(
            self.block_for(peer),
            self.slots.at[self.me],
            self.send.at[k - 1],
            self.recv.at[k - 1],
            device,
        )

    def start(self):
        for k in range(1, self.count):
            self.copy(k).start()

    def wait(self):
        for k in range(1, self.count):
            self.copy(k).wait_recv()

    def drain(self):
        for k in range(1, self.count):
            self.copy(k).wait_send()

    def total(self):
        total = self.slots[0]
        for k in range(1, self.count):
            total = total + self.slots[k]
        return total


class Doubling:
    def __init__(self, at, held, slots, sems, partners):
        self.at, self.held, self.slots, self.partners = at, held, slots, partners
        self.send, self.recv = sems

    def copy(self, k):
        return remote(
            self.held.at[k], self.slots.at[k], self.send.at[k], self.recv.at[k], self.partners[k]
        )

    def start(self):
        self.copy(0).start()

    def step(self, k):
        self.copy(k).wait_recv()
        total = self.held[k].astype(f32) + self.slots[k].astype(f32)
        if k + 1 == len(self.partners):
            return total
        self.held[k + 1] = total.astype(self.held.dtype)
        self.copy(k + 1).start()

    def drain(self):
        for k in range(len(self.partners)):
            self.copy(k).wait_send()


def norm_rows(x):
    center = jnp.mean(x, axis=-1, keepdims=True)
    centered = x - center
    spread = jnp.mean(centered * centered, axis=-1, keepdims=True)
    rs = lax.rsqrt(spread + epsilon)
    return centered * rs, rs


def norm_back_rows(grad, gain, xhat, rs):
    e = grad * gain
    return rs * (
        e
        - jnp.mean(e, axis=-1, keepdims=True)
        - xhat * jnp.mean(e * xhat, axis=-1, keepdims=True)
    )


def fold_rows(a):
    return jnp.sum(a.reshape(a.shape[0] // 8, 8, a.shape[1]), axis=0)


def block_kernel(sizes, names_in, names_out, names_scratch, *refs):
    seq, dp, head, scale = sizes
    n_in, n_out = len(names_in), len(names_out)
    i = types.SimpleNamespace(**dict(zip(names_in, refs[:n_in])))
    o = types.SimpleNamespace(**dict(zip(names_out, refs[n_in : n_in + n_out])))
    b = types.SimpleNamespace(**dict(zip(names_scratch, refs[n_in + n_out :])))
    at = Place(dp, head)
    images, padded, width = b.tok.shape
    b.bp, b.dq = b.actg, b.act.at[0]
    b.dk, b.mg = b.fi.at[:padded], b.wave.at[:padded]
    b.inp, b.out = b.n1, b.n2
    hops = range(1, at.lines)
    share = i.w_up.shape[0]
    own_rows = pl.ds(pl.multiple_of(at.d * share, share), share)
    loads = [
        pltpu.make_async_copy(src, dst, b.loads.at[n])
        for n, (src, dst) in enumerate(
            (
                (i.w_down, b.wd.at[own_rows]),
                (i.w_up, b.wu.at[own_rows]),
                (i.tokens, b.raw.at[0]),
                (i.out_grad, b.raw.at[1]),
            )
        )
    ]
    chunks = padded // 16
    wide = b.k.shape[0]
    slots = b.sc.shape[0]
    pairs = slots // 2
    units = b.wu.shape[1]
    bins = b.filt.shape[0] // 2

    def span(j, size):
        return pl.ds(j * size if isinstance(j, int) else pl.multiple_of(j * size, size), size)

    def chunk(j):
        return span(j, 16)

    def tile(p):
        return span(p, 128)

    def each(steps, body):
        for j in range(steps) if isinstance(steps, int) else steps:
            body(j)

    def flip_block(a):
        return mm_nt(i.eye[: a.shape[1], : a.shape[1]], a)

    def halves(low, high):
        return (mm(low, i.eye[:64, :128]) + mm(high, i.eye[64:128, :128])).astype(bf16)

    at.call()
    for load in loads:
        load.start()
    w_q, w_k, w_v = i.w_qkv[0], i.w_qkv[1], i.w_qkv[2]
    b.wqk[at.s, own_rows, 0:128] = w_q[:, :128]
    b.wqk[at.s, own_rows, 128:256] = w_k[:, :128]
    b.wqk[at.s, own_rows, 256:384] = halves(w_q[:, 128:], w_k[:, 128:])
    own_gains, own_mixes = rows_of(b.gains, at.d, 8), b.mixes.at[at.s]
    own_gains[...] = jnp.zeros((8, 128), f32)
    own_mixes[...] = jnp.zeros((8, 128), f32)
    for r, gain in enumerate((i.ln1_gain, i.ln1_shift, i.ln2_gain, i.ln2_shift)):
        own_gains[r : r + 1, :share] = gain[...].astype(f32)
    local_heads, heads = i.mix_pre.shape
    own_mixes[:local_heads, :heads] = i.mix_pre[...]
    own_mixes[4 : 4 + local_heads, :heads] = i.mix_post[...]
    p_t = flip_block(i.w_proj[...]).astype(bf16)
    b.wv[at.s, own_rows, 0:128] = w_v[:, :128]
    b.wv[at.s, own_rows, 128:256] = halves(w_v[:, 128:], p_t[:, 128:])
    b.wp_two[at.s, own_rows, :] = p_t[:, :128]

    ksize = i.taps.shape[0]
    b.edge[...] = jnp.zeros_like(b.edge)
    for p in range(ksize):
        b.edge[p * ksize : (p + 1) * ksize, :] = i.taps[p]
    b.filt[...] = exact(i.lag[...], b.edge[...])
    b.filt[:bins, :] += 1.0
    b.cross[...] = jnp.zeros_like(b.cross)
    b.mix_one[...] = jnp.zeros_like(b.mix_one)
    b.mix_two[...] = jnp.zeros_like(b.mix_two)
    b.k[padded:, :] = jnp.zeros((wide - padded, width), bf16)
    b.v[padded:, :] = jnp.zeros((wide - padded, width), bf16)

    for which, dst in enumerate((b.tok, b.og)):
        loads[2 + which].wait()
        for r in range(chunks):
            n = min(16, seq - r * 16)
            rows = b.raw[which, r * 16 : r * 16 + n].reshape(n * images, width)
            apart = mm(i.deal[:, : n * images], rows).astype(bf16)
            dst[:, chunk(r), :] = apart.reshape(images, 16, width)

    loads[0].wait()
    loads[1].wait()
    at.answer()

    def line(kind, buf, name, wide):
        sems = [(getattr(b, name + part + "_s"), getattr(b, name + part + "_r")) for part in ("zyxm" if wide else "zy")]
        return kind(at, buf, sems, wide)

    gains = line(Line, b.gains, "g", False)
    mixes = Share(at, b.mixes, (b.mi_s, b.mi_r))
    gq = line(Line, b.wqk, "q", True)
    gv = line(Line, b.wv, "v", True)
    gp = line(Line, b.wp_two, "p", True)
    cut = units // 3 * 2
    gu = line(Line, b.wu.at[:, :cut], "u", False)
    gr = line(Rows, b.wu.at[:, cut:], "r", False)
    gd = line(Line, b.wd, "d", False)
    ho = Share(at, b.ho, (b.ho_s, b.ho_r))
    ag = Share(at, b.ag, (b.ag_s, b.ag_r))
    out = Share(at, b.out, (b.ou_s, b.ou_r))
    inp = Share(at, b.inp, (b.in_s, b.in_r))
    fold_two = Fold(at, b.np, b.np_near, b.np_far, (b.np_s, b.np_r))
    fold_out = Fold(at, b.bp, b.bp_near, b.bp_far, (b.bp_s, b.bp_r))
    sc_up = Halves(at, b.g_up, b.up_y, b.up_z, ((b.uy2_s, b.uy2_r), (b.uz2_s, b.uz2_r)))
    sc_down = Halves(at, b.g_down, b.down_y, b.down_z, ((b.dy2_s, b.dy2_r), (b.dz2_s, b.dz2_r)))
    sc_qk = Scatter(at, b.g_qk, b.qk_y, b.qk_z, ((b.qy2_s, b.qy2_r), (b.qz2_s, b.qz2_r)))
    sc_pv = Scatter(at, b.g_pv, b.pv_y, b.pv_z, ((b.py2_s, b.py2_r), (b.pz2_s, b.pz2_r)))
    sc_v = Scatter(at, b.g_v, b.v_y, b.v_z, ((b.vy2_s, b.vy2_r), (b.vz2_s, b.vz2_r)))
    turn_v = Exchange(at, "head", b.turned_v, (b.tv_s, b.tv_r), lambda s: b.turn_v.at[s])
    turn = Exchange(at, "head", b.turned, (b.tu_s, b.tu_r), lambda s: b.turn.at[s])
    over_dp = (
        ((at.z + 1 - 2 * (at.z % 2)) * 2 + at.y, at.s),
        ((at.z + 2) % 4 * 2 + at.y, at.s),
        (at.z * 2 + 1 - at.y, at.s),
    )
    taps = Doubling(at, b.taps, b.taps_in, (b.ta_s, b.ta_r), over_dp)
    small = Doubling(
        at, b.small, b.small_in, (b.sm_s, b.sm_r), ((at.d, at.across), (at.d, at.mate), *over_dp)
    )

    passed = ((0, False), (1, False), (0, True), (2, False), (1, True), (3, False), (2, True), (3, True))
    gq.begin()
    gq.over_y()
    gq.on(0, False)
    gains.begin()
    gains.over_y()
    mixes.start()
    gv.begin()
    gv.over_y()
    gv.on(0, False)
    gp.begin()
    gp.over_y()
    gp.on(0, False)
    gr.over_y()

    def norm_one(image):
        def body(j):
            xhat, _ = norm_rows(b.tok[image, chunk(j), :].astype(f32))
            b.n1[image, chunk(j), :] = (xhat * b.norms[0:1, :] + b.norms[1:2, :]).astype(bf16)

        each(chunks, body)

    gains.from_z(1)
    gq.from_z(1)
    gq.on(1, False)
    gq.from_y(0)
    gq.on(0, True)
    gv.from_z(1)
    gp.from_z(1)
    gains.from_z(2)
    mixes.forward()
    gq.from_z(2)
    gq.on(2, False)
    gq.from_y(1)
    gq.on(1, True)
    gv.from_z(2)
    gp.from_z(2)
    gd.begin()
    gd.over_y()
    gu.begin()
    gu.over_y()
    gains.from_z(3)
    gq.from_z(3)
    gq.on(3, False)
    gr.from_y()
    gq.from_y(2)
    gq.on(2, True)
    gv.on(1, False)
    gv.from_y(0)
    gv.on(0, True)
    for k in range(at.lines):
        gains.from_y(k)
    spread = mm(b.gains[...].astype(bf16), i.comb[...])
    row = lax.broadcasted_iota(jnp.int32, spread.shape, 0)
    lane = lax.broadcasted_iota(jnp.int32, spread.shape, 1)
    first = (row >> 3) * share
    here = (lane >= first) & (lane < first + share)
    for r in range(4):
        b.norms[r : r + 1, :] = jnp.sum(
            jnp.where(here & ((row & 7) == r), spread, 0.0), axis=0, keepdims=True
        )
    norm_one(at.s)
    gv.from_z(3)
    gp.from_z(3)

    mixes.wait_mate()
    mixes.wait_corner()
    diagonal = i.diagonal[...]
    for part, piece in enumerate(split(b.mixes[...].reshape(head * 8, 128))):
        for which, pick in enumerate((i.pick_pre, i.pick_post)):
            picked = mm(pick[...], piece).astype(bf16)
            b.kron[which, part] = (mm_nt(picked, i.place[...]) * diagonal).astype(bf16)
            b.kron_t[which, part] = (mm_nt(i.place[...], picked) * diagonal).astype(bf16)

    gd.from_z(1)
    gq.from_y(3)
    gq.on(3, True)
    gv.on(2, False)
    gv.from_y(1)
    gv.on(1, True)
    gv.on(3, False)

    lo = (lax.broadcasted_iota(jnp.int32, (1, 128), 1) < 64).astype(f32)
    low_half = lax.broadcasted_iota(jnp.int32, (padded, 128), 1) < 64
    lo_b, hi_b = lo.astype(bf16), (1.0 - lo).astype(bf16)

    def project(g):
        t = mm(b.n1[at.s], b.wqk[g])
        b.q[:, tile(g)] = (t[:, :128] * scale).astype(bf16)
        b.k[:padded, tile(g)] = t[:, 128:256].astype(bf16)
        b.third_qk[g] = t[:, 256:]

    def project_v(g):
        t = mm(b.n1[at.s], b.wv[g])
        b.v[:padded, tile(g)] = t[:, :128].astype(bf16)
        b.third_v[g] = t[:, 128:]

    project(at.s)
    gv.from_y(2)
    gv.on(2, True)
    gq.from_mate(False)
    project(at.mate)
    gu.from_z(1)
    for block in passed:
        gq.from_x(*block)
    project(at.across)
    gv.from_y(3)
    gv.on(3, True)
    gq.from_mate(True)
    project(at.corner)
    for p in range(head // 2):
        one, two = b.third_qk[2 * p], b.third_qk[2 * p + 1]
        third = tile(head + p)
        b.q[:, third] = (jnp.where(low_half, one, pltpu.roll(two, 64, 1)) * scale).astype(bf16)
        b.k[:padded, third] = jnp.where(low_half, pltpu.roll(one, 64, 1), two).astype(bf16)

    def score(p):
        q, k = b.q[:, tile(p)], b.k[:, tile(p)]
        b.sc[2 * p] = mm_nt(q * lo_b, k).astype(bf16)
        b.sc[2 * p + 1] = mm_nt(q * hi_b, k).astype(bf16)

    each(pairs, score)
    gr.from_z(1)
    for block in passed[1:]:
        if block[1]:
            gp.from_y(block[0])
        gp.on(*block)
    gd.from_z(2)

    def mixed(table, which, block):
        return mm(table[which, 0], block) + mm(table[which, 1], block)

    def slab(ref, j):
        return ref[:, chunk(j), :].reshape(slots * 16, wide)

    def put(ref, j, value):
        ref[:, chunk(j), :] = value.reshape(slots, 16, wide)

    def soften(j):
        beyond = lax.broadcasted_iota(jnp.int32, (slots * 16, wide), 1) >= seq
        logits = jnp.where(beyond, -1e30, mixed(b.kron, 0, slab(b.sc, j)))
        top = jnp.max(logits, axis=-1, keepdims=True)
        power = jnp.exp(logits - top)
        probs = power / jnp.sum(power, axis=-1, keepdims=True)
        put(b.pr, j, probs)
        put(b.post, j, mixed(b.kron, 1, probs.astype(bf16)).astype(bf16))

    each(chunks, soften)
    gu.from_z(2)
    for block in passed:
        gv.from_x(*block)
    project_v(at.s)
    gv.from_mate(False)
    project_v(at.mate)
    project_v(at.across)
    gv.from_mate(True)
    project_v(at.corner)
    for p in range(head // 2):
        b.v[:padded, tile(head + p)] = jnp.where(
            low_half, b.third_v[2 * p], pltpu.roll(b.third_v[2 * p + 1], 64, 1)
        ).astype(bf16)

    def gather_heads(p):
        v = b.v[:, tile(p)]
        b.ho[at.s, :, tile(p)] = (mm(b.post[2 * p], v * lo_b) + mm(b.post[2 * p + 1], v * hi_b)).astype(bf16)

    each(pairs, gather_heads)
    ho.start()
    gr.from_z(2)
    gd.from_z(3)
    gu.from_z(3)

    def flip(src, dst):
        for r in range(width // 256):
            lanes = span(r, 256)
            block = src[:, :, lanes].reshape(images * padded, 256)
            dst[lanes, :] = mm_nt(i.eye[...], block).astype(bf16)

    def weight_grad(dst, left, right):
        for r in range(width // 256):
            rows = span(r, 256)
            dst[rows, :] = mm(left[rows, :], right()).astype(bf16)

    def flat(ref):
        return ref[...].reshape(images * padded, ref.shape[2])

    for k in range(1, images):
        norm_one(at.head_next(k))
    flip(b.og, b.og_t)

    for block in passed:
        gp.from_x(*block)
    gp.from_mate(False)
    gp.from_mate(True)
    low_rows = lax.broadcasted_iota(jnp.int32, (width, 128), 1) < 64
    for g in range(head):
        b.wp[:, tile(g)] = b.wp_two[g]
    for p in range(head // 2):
        one, two = b.wv[2 * p, :, 128:].astype(f32), b.wv[2 * p + 1, :, 128:].astype(f32)
        b.wp[:, tile(head + p)] = jnp.where(low_rows, pltpu.roll(one, 64, 1), two).astype(bf16)

    def chip_images(step):
        return 2 * ((at.x + step) % 2)

    def two(ref, step):
        return ref[pl.ds(chip_images(step), 2)].reshape(2 * padded, ref.shape[2])

    def rows_in_two(step, body):
        for half in range(2):
            for r in range(chunks):
                body(chip_images(step) + half, chunk(r), chunk(half * chunks + r))

    def bins_of(body):
        for j in range(bins // 16):
            body(span(j, 16), pl.ds(bins + j * 16, 16))

    def conv_back(step):
        b.act[...] = mm(two(b.og, step), b.wd[...]).astype(bf16).reshape(2, padded, units)
        for half in range(2):
            image = chip_images(step) + half
            b.wave[...] = mm(i.fourier[...], b.act[half])

            def body(cos, sin):
                cos_g, sin_g = b.wave[cos, :], b.wave[sin, :]
                cos_k, sin_k = b.filt[cos, :], b.filt[sin, :]
                b.gf[image, cos, :] = cos_g.astype(bf16)
                b.gf[image, sin, :] = sin_g.astype(bf16)
                b.fi[cos, :] = (cos_k * cos_g - sin_k * sin_g).astype(bf16)
                b.fi[sin, :] = (cos_k * sin_g + sin_k * cos_g).astype(bf16)

            bins_of(body)
            b.actg[image] = mm(i.fourier_t[...], b.fi[...]).astype(bf16)

    def up(step, between):
        b.hid[...] = mm_nt(two(b.ho, step), b.wp[...])

        def norm_two(image, rows, both):
            middle = b.tok[image, rows, :].astype(f32) + b.hid[both, :]
            b.mid[jnp.minimum(jnp.abs(image - at.s), 1), rows, :] = middle
            xhat, _ = norm_rows(middle)
            b.n2[image, rows, :] = (xhat * b.norms[2:3, :] + b.norms[3:4, :]).astype(bf16)

        rows_in_two(step, norm_two)
        between()
        b.hid[...] = mm(two(b.n2, step), b.wu[...])

        def gelu(image, rows, both):
            h = b.hid[both, :]
            cdf = 0.5 * (1.0 + lax.erf(h * (0.5**0.5)))
            slope = cdf + h * jnp.exp(-0.5 * h * h) * 0.3989422804014327
            b.wid[image, rows, :] = (h * cdf).astype(bf16)
            b.hg[image, rows, :] = (b.actg[image, rows, :].astype(f32) * slope).astype(bf16)

        rows_in_two(step, gelu)
        b.np[pl.ds(chip_images(step), 2)] = (
            mm_nt(two(b.hg, step), b.wu[...]).astype(bf16).reshape(2, padded, width)
        )

    for k in range(at.lines):
        gd.from_y(k)
    conv_back(1)
    ho.forward()
    conv_back(0)
    gr.from_z(3)
    for k in range(at.lines):
        gu.from_y(k)
    ho.wait_corner()
    up(1, lambda: None)
    fold_two.mate_copy(1).start()
    ho.wait_mate()
    up(0, fold_two.middle)
    fold_two.mate_copy(0).start()
    flip(b.n2, b.flip)
    weight_grad(b.g_up, b.flip, lambda: flat(b.hg))
    sc_up.start()

    def down(step):
        for half in range(2):
            image = chip_images(step) + half
            b.wave[...] = mm(i.fourier[...], b.wid[image])

            def body(cos, sin):
                cos_a, sin_a = b.wave[cos, :], b.wave[sin, :]
                cos_k, sin_k = b.filt[cos, :], b.filt[sin, :]
                cos_g, sin_g = b.gf[image, cos, :].astype(f32), b.gf[image, sin, :].astype(f32)
                b.fi[cos, :] = (cos_k * cos_a + sin_k * sin_a).astype(bf16)
                b.fi[sin, :] = (cos_k * sin_a - sin_k * cos_a).astype(bf16)
                b.cross[cos, :] += cos_a * cos_g + sin_a * sin_g
                b.cross[sin, :] += sin_a * cos_g - cos_a * sin_g

            bins_of(body)
            b.wid[image] = mm(i.fourier_t[...], b.fi[...]).astype(bf16)
        b.bp[pl.ds(chip_images(step), 2)] = (
            mm_nt(two(b.wid, step), b.wd[...]).astype(bf16).reshape(2, padded, width)
        )

    down(1)
    fold_out.mate_copy(1).start()
    down(0)
    fold_out.mate_copy(0).start()
    fold_out.middle()
    weight_grad(b.g_down, b.og_t, lambda: flat(b.wid))
    sc_down.start()
    b.taps[0] = exact(i.lag_back[...], b.cross[...]).astype(bf16)
    taps.start()
    sc_up.middle(1)
    flip(b.n1, b.flip)

    fold_two.wait()
    zero = jnp.zeros((8, width), f32)
    gain_sum, shift_sum = zero, zero
    for j in range(chunks):
        grad = fold_two.total(chunk(j))
        xhat, rs = norm_rows(b.mid[0, chunk(j), :])
        inner = norm_back_rows(grad, b.norms[2:3, :], xhat, rs)
        total = b.og[at.s, chunk(j), :].astype(f32) + inner
        b.mg[chunk(j), :] = total
        b.ag[at.s, chunk(j), :] = total.astype(bf16)
        gain_sum += fold_rows(grad * xhat)
        shift_sum += fold_rows(grad)
    b.sums[2:3, :] = jnp.sum(gain_sum, axis=0, keepdims=True)
    b.sums[3:4, :] = jnp.sum(shift_sum, axis=0, keepdims=True)

    b.hgr[...] = mm(b.ag[at.s], b.wp[...]).astype(bf16)

    def flip_one(src, dst):
        for r in range(width // 256):
            dst[span(r, 256), :] = mm_nt(i.eye[...], src[:, span(r, 256)]).astype(bf16)

    flip_one(b.hgr, b.hgr_t)
    flip_one(b.q, b.q_t)

    def back_post(p):
        g, v = b.hgr[:, tile(p)], b.v[:, tile(p)]
        for half, mask in enumerate((lo_b, hi_b)):
            b.pg[2 * p + half] = mm_nt(g * mask, v).astype(bf16)
            rows = span(2 * p + half, 64)
            b.dv_t[rows, :] = mm(b.hgr_t[rows, :], b.post[2 * p + half]).astype(bf16)

    each(pairs, back_post)

    def unflip(src, dst):
        for r in range(width // 256):
            dst[:, span(r, 256)] = mm_nt(i.eye[:padded, :], src[span(r, 256), :]).astype(bf16)

    unflip(b.dv_t, b.dv)
    for g in range(head):
        b.turn_v[g, :, 0:128] = b.dv[:, tile(g)]
        v3 = b.dv[:, tile(head + g // 2)].astype(f32)
        if g % 2:
            v3 = pltpu.roll(v3, 64, 1)
        b.turn_v[g, :, 128:256] = jnp.where(low_half, v3, 0.0).astype(bf16)
    turn_v.start()
    b.turned_v[at.s] = b.turn_v[at.s]
    sc_up.middle(2)

    def back_soften(j):
        grad = slab(b.pg, j)
        probs = slab(b.pr, j)
        b.mix_two[...] += mm_nt(grad, probs.astype(bf16))
        probs_grad = mixed(b.kron_t, 1, grad)
        inner = jnp.sum(probs_grad * probs, axis=-1, keepdims=True)
        mixed_grad = (probs * (probs_grad - inner)).astype(bf16)
        b.mix_one[...] += mm_nt(mixed_grad, slab(b.sc, j))
        put(b.pg, j, mixed(b.kron_t, 0, mixed_grad).astype(bf16))

    each(chunks, back_soften)

    def back_score(p):
        k = b.k[:, tile(p)]
        b.dq[:, tile(p)] = (
            (mm(b.pg[2 * p], k * lo_b) + mm(b.pg[2 * p + 1], k * hi_b)) * scale
        ).astype(bf16)
        for half in range(2):
            rows = span(2 * p + half, 64)
            b.dk_t[rows, :] = mm(b.q_t[rows, :], b.pg[2 * p + half]).astype(bf16)

    each(pairs, back_score)
    unflip(b.dk_t, b.dk)
    for g in range(head):
        b.turn[g, :, 0:128] = b.dq[:, tile(g)]
        b.turn[g, :, 128:256] = b.dk[:, tile(g)]
        third = tile(head + g // 2)
        q3, k3 = b.dq[:, third].astype(f32), b.dk[:, third].astype(f32)
        if g % 2:
            q3 = pltpu.roll(q3, 64, 1)
        else:
            k3 = pltpu.roll(k3, 64, 1)
        b.turn[g, :, 256:384] = jnp.where(low_half, q3, k3).astype(bf16)
    turn.start()
    b.turned[at.s] = b.turn[at.s]
    for k in range(3, at.lines):
        sc_up.middle(k)

    for g in range(head):
        part = mm_nt(b.turn[g], b.wqk[g]) + mm_nt(b.turn_v[g], b.wv[g])
        if g:
            b.hid[:padded, :] += part
        else:
            b.hid[:padded, :] = part
    gain_sum, shift_sum = zero, zero
    for j in range(chunks):
        grad = b.hid[chunk(j), :]
        xhat, rs = norm_rows(b.tok[at.s, chunk(j), :].astype(f32))
        inner = norm_back_rows(grad, b.norms[0:1, :], xhat, rs)
        b.inp[at.s, chunk(j), :] = (b.mg[chunk(j), :] + inner).astype(bf16)
        gain_sum += fold_rows(grad * xhat)
        shift_sum += fold_rows(grad)
    b.sums[0:1, :] = jnp.sum(gain_sum, axis=0, keepdims=True)
    b.sums[1:2, :] = jnp.sum(shift_sum, axis=0, keepdims=True)

    blocks = jnp.zeros((head * 8, 128), f32)
    for table, pick in ((b.mix_one, i.pick_pre_t), (b.mix_two, i.pick_post_t)):
        blocks += exact(exact(pick[...], table[...] * diagonal), i.place_f[...])
    b.sums[4:8, :] = jnp.zeros((4, width), f32)
    b.small[0, :, :width] = b.sums[...]
    for g in range(head):
        b.small[0, :, width + g * 128 : width + (g + 1) * 128] = blocks[g * 8 : (g + 1) * 8]
    small.start()
    ag.start()
    taps.step(0)
    sc_down.middle(1)

    turn_v.wait()
    inp.start()
    for r in range(width // 256):
        rows = span(r, 256)
        values = mm(b.flip[rows, :], flat(b.turned_v))
        b.g_v[rows, :] = values[:, :128].astype(bf16)
        b.g_pv[rows, 0:128] = values[:, 128:].astype(bf16)
    sc_v.start()
    fold_out.wait()
    for j in range(chunks):
        b.out[at.s, chunk(j), :] = (b.mid[0, chunk(j), :] + fold_out.total(chunk(j))).astype(bf16)
    out.start()
    taps.step(1)
    sc_down.middle(2)
    turn.wait()
    weight_grad(b.g_qk, b.flip, lambda: flat(b.turned))
    sc_qk.start()
    sc_down.middle(3)
    small.step(0)
    small.step(1)
    ag.forward()
    for k in range(1, at.lines):
        sc_v.middle(k)
    ag.wait_mate()
    ag.wait_corner()
    small.step(2)
    flip(b.ag, b.og_t)
    mine = tile(at.s)
    third_tile = tile(head + at.s // 2)
    for r in range(width // 256):
        rows = span(r, 256)
        left = b.og_t[rows, :]
        proj = mm(left, b.ho[:, :, mine].reshape(images * padded, 128))
        third = pltpu.roll(mm(left, b.ho[:, :, third_tile].reshape(images * padded, 128)), 64 * (1 - at.c), 1)
        low = lax.broadcasted_iota(jnp.int32, third.shape, 1) < 64
        b.g_pv[rows, 0:128] = jnp.where(low, b.g_pv[rows, 0:128].astype(f32), third).astype(bf16)
        b.g_pv[rows, 128:256] = proj.astype(bf16)
    sc_pv.start()
    for k in range(1, at.lines):
        sc_qk.middle(k)
    small.step(3)
    o.w_up[...] = sc_up.finish()
    for k in range(1, at.lines):
        sc_pv.middle(k)
    o.taps[...] = taps.step(2)
    o.w_down[...] = sc_down.finish()
    inp.forward()
    small_total = small.step(4)
    o.mixes[...] = jnp.zeros((8, 128), f32)
    for g in range(head):

        @pl.when(at.s == g)
        def _():
            o.mixes[...] = small_total[:, width + g * 128 : width + (g + 1) * 128]

    columns = lax.broadcasted_iota(jnp.int32, (8, width), 1)
    own = (columns >= at.d * share) & (columns < (at.d + 1) * share)
    o.norms[...] = exact(jnp.where(own, small_total[:, :width], 0.0), i.comb_t[...])
    out.forward()
    def turned_over(a):
        return lax.dot_general(
            i.eye_f[: a.shape[1], : a.shape[1]], a, NT, preferred_element_type=f32, precision=highest
        )

    o.w_v[:, 0:128] = sc_v.finish()
    out.wait_mate()
    out.wait_corner()
    save_out = pltpu.make_async_copy(b.out, o.output, b.loads.at[0])
    save_out.start()
    inp.wait_mate()
    inp.wait_corner()
    save_inp = pltpu.make_async_copy(b.inp, o.input, b.loads.at[1])
    save_inp.start()
    o.qk[...] = sc_qk.finish()
    pv = sc_pv.finish()
    o.w_v[:, 128:] = pv[:, :64]
    o.w_proj[:128, :] = turned_over(pv[:, 128:])
    o.w_proj[128:, :] = turned_over(pv[:, :128])[64:, :]
    save_out.wait()
    save_inp.wait()
    for item in (
        gains, mixes, gq, gv, gp, gu, gr, gd, ho, ag, out, inp, fold_two, fold_out, sc_up, sc_down, sc_qk, sc_pv, sc_v,
        turn, turn_v, taps, small,
    ):
        item.drain()


def finish_kernel(sizes, *refs):
    local_heads, heads, share = sizes
    (output, inputs, qk, w_v, w_proj, up, down, norms, mixes, taps, deal_t) = refs[:11]
    (o_output, o_input, o_one_g, o_one_s, o_qkv, o_proj, o_pre, o_post, o_two_g, o_two_s, o_up, o_taps, o_down) = refs[11:]
    images, rows, width = output.shape
    for src, dst in ((output, o_output), (inputs, o_input)):
        for r in range(rows // 16):
            some = pl.ds(r * 16, 16)
            mixed = mm(deal_t[...], src[:, some, :].reshape(images * 16, width))
            dst[some] = mixed.astype(bf16).reshape(16, images, width)

    @pl.when(pl.program_id(0) == 0)
    def _():
        thirds = qk[:, 256:]
        o_qkv[0, :, 0:128] = qk[:, 0:128]
        o_qkv[0, :, 128:] = thirds[:, :64]
        o_qkv[1, :, 0:128] = qk[:, 128:256]
        o_qkv[1, :, 128:] = pltpu.roll(thirds, 64, 1)[:, :64]
        o_qkv[2] = w_v[...]
        o_proj[...] = w_proj[...]
        o_up[...] = up[...]
        o_down[...] = down[...]
        o_pre[...] = mixes[:local_heads, :heads]
        o_post[...] = mixes[4 : 4 + local_heads, :heads]
        for r, ref in enumerate((o_one_g, o_one_s, o_two_g, o_two_s)):
            ref[...] = norms[r : r + 1, :share]
        ksize = o_taps.shape[0]
        for p in range(ksize):
            o_taps[p] = taps[p * ksize : (p + 1) * ksize, :]


def tables(seq, dp, head, heads, grid, ksize, share):
    cos, sin, cos_lag, sin_lag, back = spectrum(grid, ksize)
    used = cos.shape[0]
    bins = -(-used // 16) * 16
    padded = -(-seq // 16) * 16
    fourier = np.zeros((2 * bins, padded))
    fourier[:used, :seq] = cos
    fourier[bins : bins + used, :seq] = sin
    taps = ksize * ksize
    lag = np.zeros((2 * bins, -(-taps // 8) * 8))
    lag[:used, :taps] = cos_lag
    lag[bins : bins + used, :taps] = sin_lag
    lag_back = np.zeros((-(-taps // 16) * 16, 2 * bins))
    lag_back[:taps, :used] = (cos_lag * back[:, None]).T
    lag_back[:taps, bins : bins + used] = (sin_lag * back[:, None]).T
    comb = (np.arange(share * dp)[None, :] % share == np.arange(128)[:, None]) & (
        np.arange(128)[:, None] < share
    )
    group = heads // head
    slot = [group * g + l for g in range(head) for l in range(2)] + [group * g + 2 for g in range(head)]
    wide = heads * 16
    pick = np.zeros((2, wide, head * 8))
    place = np.zeros((wide, 128))
    for p, h in enumerate(slot):
        for row in range(16):
            for which in range(2):
                pick[which, p * 16 + row, (h // group) * 8 + which * 4 + h % group] = 1.0
            place[p * 16 + row, h] = 1.0
    deal = np.zeros((16 * head, 16 * head))
    for token in range(16):
        for image in range(head):
            deal[image * 16 + token, token * head + image] = 1.0
    diagonal = (np.arange(wide)[:, None] % 16) == (np.arange(wide)[None, :] % 16)
    return {
        "fourier": jnp.asarray(fourier, bf16),
        "fourier_t": jnp.asarray(fourier.T, bf16),
        "lag": jnp.asarray(lag, f32),
        "lag_back": jnp.asarray(lag_back, f32),
        "comb": jnp.asarray(comb, bf16),
        "comb_t": jnp.asarray(comb.T, f32),
        "pick_pre": jnp.asarray(pick[0], bf16),
        "pick_post": jnp.asarray(pick[1], bf16),
        "pick_pre_t": jnp.asarray(pick[0].T, f32),
        "pick_post_t": jnp.asarray(pick[1].T, f32),
        "place": jnp.asarray(place, bf16),
        "place_f": jnp.asarray(place, f32),
        "diagonal": jnp.asarray(diagonal, f32),
        "eye": jnp.asarray(np.eye(256), bf16),
        "eye_f": jnp.asarray(np.eye(256), f32),
        "deal": jnp.asarray(deal, bf16),
        "deal_t": jnp.asarray(deal.T, bf16),
    }


def whole_block(
    tokens,
    ln1_gain,
    ln1_shift,
    w_qkv,
    w_proj,
    mix_pre,
    mix_post,
    ln2_gain,
    ln2_shift,
    w_up,
    conv_kernel,
    w_down,
    out_grad,
):
    images, seq, width = tokens.shape
    dp, head = lax.axis_size("dp"), lax.axis_size("head")
    local_heads, heads = mix_pre.shape
    size = width // heads
    local = local_heads * size
    share = w_qkv.shape[0]
    ksize, units = conv_kernel.shape[0], conv_kernel.shape[2]
    grid = int(round((seq - 1) ** 0.5))
    padded = -(-seq // 16) * 16
    wide = -(-seq // 128) * 128
    lines = dp // 2
    const = tables(seq, dp, head, heads, grid, ksize, share)
    bins = const["fourier"].shape[0] // 2
    taps = const["lag_back"].shape[0]

    inputs = {
        "tokens": jnp.transpose(tokens, (1, 0, 2)),
        "out_grad": jnp.transpose(out_grad, (1, 0, 2)),
        "ln1_gain": ln1_gain.reshape(1, share),
        "ln1_shift": ln1_shift.reshape(1, share),
        "ln2_gain": ln2_gain.reshape(1, share),
        "ln2_shift": ln2_shift.reshape(1, share),
        "mix_pre": mix_pre,
        "mix_post": mix_post,
        "w_qkv": jnp.transpose(w_qkv, (1, 0, 2)),
        "w_proj": w_proj,
        "w_up": w_up,
        "w_down": w_down.T,
        "taps": conv_kernel,
        **{name: value for name, value in const.items() if name != "deal_t"},
    }
    outputs = {
        "output": ((images, padded, width), bf16),
        "input": ((images, padded, width), bf16),
        "qk": ((share, 384), f32),
        "w_v": ((share, local), f32),
        "w_proj": ((local, share), f32),
        "w_up": ((share, units), f32),
        "w_down": ((share, units), f32),
        "norms": ((8, 128), f32),
        "mixes": ((8, 128), f32),
        "taps": ((taps, units), f32),
    }
    finals = {
        "output": ((seq, images, width), bf16),
        "input": ((seq, images, width), bf16),
        "ln1_gain": ((1, share), f32),
        "ln1_shift": ((1, share), f32),
        "w_qkv": ((3, share, local), f32),
        "w_proj": ((local, share), f32),
        "mix_pre": ((local_heads, heads), f32),
        "mix_post": ((local_heads, heads), f32),
        "ln2_gain": ((1, share), f32),
        "ln2_shift": ((1, share), f32),
        "w_up": ((share, units), f32),
        "taps": ((ksize, ksize, units), f32),
        "w_down": ((share, units), f32),
    }
    one, every = (padded, width), (images, padded, width)
    square = (heads, padded, wide)
    table = (heads * 16, heads * 16)
    scratch = {
        "tok": (every, bf16),
        "og": (every, bf16),
        "raw": ((2, seq, images, width), bf16),
        "edge": ((const["lag"].shape[1], units), f32),
        "wqk": ((head, width, 384), bf16),
        "wv": ((head, width, 256), bf16),
        "wp_two": ((head, width, 128), bf16),
        "wp": ((width, width), bf16),
        "wu": ((width, units), bf16),
        "wd": ((width, units), bf16),
        "gains": ((dp * 8, 128), f32),
        "mixes": ((head, 8, 128), f32),
        "norms": ((8, width), f32),
        "filt": ((2 * bins, units), f32),
        "cross": ((2 * bins, units), f32),
        "wave": ((2 * bins, units), f32),
        "fi": ((2 * bins, units), bf16),
        "gf": ((images, 2 * bins, units), bf16),
        "actg": ((images, padded, units), bf16),
        "act": ((2, padded, units), bf16),
        "n1": (every, bf16),
        "n2": (every, bf16),
        "mid": ((2, *one), f32),
        "hid": ((2 * padded, width), f32),
        "wid": ((images, padded, units), bf16),
        "hg": ((images, padded, units), bf16),
        "np": (every, bf16),
        "np_near": ((2, *one), bf16),
        "np_far": (one, bf16),
        "bp_near": ((2, *one), bf16),
        "bp_far": (one, bf16),
        "flip": ((width, images * padded), bf16),
        "q": (one, bf16),
        "k": ((wide, width), bf16),
        "v": ((wide, width), bf16),
        "third_qk": ((head, padded, 128), f32),
        "third_v": ((head, padded, 128), f32),
        "kron": ((2, 2, *table), bf16),
        "kron_t": ((2, 2, *table), bf16),
        "mix_one": (table, f32),
        "mix_two": (table, f32),
        "sc": (square, bf16),
        "pr": (square, f32),
        "post": (square, bf16),
        "pg": (square, bf16),
        "ho": (every, bf16),
        "ag": (every, bf16),
        "hgr": (one, bf16),
        "hgr_t": ((width, padded), bf16),
        "q_t": ((width, padded), bf16),
        "dv_t": ((width, wide), bf16),
        "dk_t": ((width, wide), bf16),
        "dv": (one, bf16),
        "turn": ((head, padded, 384), bf16),
        "turned": ((head, padded, 384), bf16),
        "turn_v": ((head, padded, 256), bf16),
        "turned_v": ((head, padded, 256), bf16),
        "og_t": ((width, images * padded), bf16),
        "sums": ((8, width), f32),
        "small": ((5, 8, width + head * 128), f32),
        "small_in": ((5, 8, width + head * 128), f32),
        "taps": ((3, taps, units), bf16),
        "taps_in": ((3, taps, units), bf16),
    }
    for name, columns in (("up", units), ("down", units), ("qk", 384), ("pv", 256), ("v", 128)):
        scratch["g_" + name] = ((width, columns), bf16)
        scratch[name + "_y"] = ((lines, share, columns), bf16)
        scratch[name + "_z"] = ((lines - 1, share, columns), bf16)
    sems = {"mi": 3, "ho": 3, "ag": 3, "ou": 3, "in": 3, "np": 3, "bp": 3}
    sems |= {"tv": head - 1, "tu": head - 1, "ta": 3, "sm": 5}
    for name in "gqvpurd":
        sems |= {name + "z": 2 * (lines - 1), name + "y": lines}
    for name in "qvpud":
        sems |= {name + "y2": lines, name + "z2": lines - 1}
    for name in "qvp":
        sems |= {name + "x": dp, name + "m": 2 * dp}
    shapes = {name: pltpu.VMEM(*spec) for name, spec in scratch.items()}
    for name, number in sems.items():
        shapes[name + "_s"] = pltpu.SemaphoreType.DMA((number,))
        shapes[name + "_r"] = pltpu.SemaphoreType.DMA((number,))
    shapes["loads"] = pltpu.SemaphoreType.DMA((4,))
    vmem = pl.BlockSpec(memory_space=pltpu.VMEM)
    left = pl.BlockSpec(memory_space=pl.ANY)
    results = pl.pallas_call(
        functools.partial(
            block_kernel,
            (seq, dp, head, size ** (-0.5)),
            tuple(inputs),
            tuple(outputs),
            tuple(shapes),
        ),
        out_shape=[jax.ShapeDtypeStruct(*spec) for spec in outputs.values()],
        in_specs=[left if n in ("tokens", "out_grad", "w_up", "w_down") else vmem for n in inputs],
        out_specs=[left if n in ("output", "input") else vmem for n in outputs],
        scratch_shapes=list(shapes.values()),
        compiler_params=pltpu.CompilerParams(
            collective_id=0, has_side_effects=True, vmem_limit_bytes=64 * 2**20
        ),
    )(*inputs.values())
    r = dict(zip(outputs, results))

    def kept(shape):
        return pl.BlockSpec(shape, lambda j: (0,) * len(shape))

    parts = [*r.values(), const["deal_t"]]
    step = -(-padded // (32)) * 16
    by_rows = pl.BlockSpec((images, step, width), lambda j: (0, j, 0))
    by_tokens = pl.BlockSpec((step, images, width), lambda j: (j, 0, 0))
    results = pl.pallas_call(
        functools.partial(finish_kernel, (local_heads, heads, share)),
        grid=(-(-padded // step),),
        out_shape=[jax.ShapeDtypeStruct(*spec) for spec in finals.values()],
        in_specs=[by_rows] * 2 + [kept(part.shape) for part in parts[2:]],
        out_specs=[by_tokens] * 2 + [kept(spec[0]) for spec in list(finals.values())[2:]],
    )(*parts)
    r = dict(zip(finals, results))
    for name in ("output", "input", "w_qkv"):
        r[name] = jnp.transpose(r[name], (1, 0, 2))
    for name in ("ln1_gain", "ln1_shift", "ln2_gain", "ln2_shift"):
        r[name] = r[name].reshape(share)
    r["w_down"] = r["w_down"].T
    return tuple(r.values())


def solution(mesh):
    in_specs = (
        P("dp", None, None),
        P("dp"),
        P("dp"),
        P("dp", None, "head"),
        P("head", "dp"),
        P("head", None),
        P("head", None),
        P("dp"),
        P("dp"),
        P("dp", "head"),
        P(None, None, "head"),
        P("head", "dp"),
        P("dp", None, None),
    )
    out_specs = (
        P("dp", None, None),
        P("dp", None, None),
        P("dp"),
        P("dp"),
        P("dp", None, "head"),
        P("head", "dp"),
        P("head", None),
        P("head", None),
        P("dp"),
        P("dp"),
        P("dp", "head"),
        P(None, None, "head"),
        P("head", "dp"),
    )
    dp, head = mesh.shape["dp"], mesh.shape["head"]

    def shards(*args):
        tokens, w_qkv, mix_pre = args[0], args[3], args[5]
        fits = head == 4 and dp == 8 and w_qkv.shape[0] % 32 == 0 and w_qkv.shape[0] <= 128
        fits = fits and tokens.shape[0] == head
        fits = fits and mix_pre.shape[0] == 3 and tokens.shape[2] == 64 * mix_pre.shape[1]
        return (whole_block if fits else plain)(*args)

    return jax.shard_map(shards, mesh=mesh, in_specs=in_specs, out_specs=out_specs, check_vma=False)
```

```python
import functools
import types

import jax
import jax.numpy as jnp
import numpy as np
from jax import lax
from jax.experimental import pallas as pl
from jax.experimental.pallas import tpu as pltpu
from jax.sharding import PartitionSpec as P

highest = lax.Precision.HIGHEST
epsilon = 1e-06
bf16 = jnp.bfloat16
f32 = jnp.float32


def spectrum(grid, ksize):
    margin = ksize // 2
    period = grid + margin
    pairs = [(0, 0)] + [(0, v) for v in range(1, period // 2 + 1)]
    pairs += [(u, v) for u in range(1, period // 2 + 1) for v in range(period)]
    freq = np.array(pairs, np.float64)
    place = np.array([(r, c) for r in range(grid) for c in range(grid)], np.float64)
    lags = np.array([(p - margin, q - margin) for p in range(ksize) for q in range(ksize)], np.float64)
    weight = np.sqrt(np.where(np.arange(len(pairs)) == 0, 1.0, 2.0)) / period
    angle = 2 * np.pi / period * freq @ place.T
    angle_lag = 2 * np.pi / period * freq @ lags.T
    count = len(pairs)
    cos = np.zeros((count + 1, grid * grid + 1))
    sin = np.zeros_like(cos)
    cos[:count, 1:] = weight[:, None] * np.cos(angle)
    sin[:count, 1:] = weight[:, None] * np.sin(angle)
    cos[count, 0] = 1.0
    cos_lag = np.zeros((count + 1, ksize * ksize))
    sin_lag = np.zeros_like(cos_lag)
    cos_lag[:count] = np.cos(angle_lag)
    sin_lag[:count] = np.sin(angle_lag)
    back = np.zeros(count + 1)
    back[:count] = 1.0
    return cos, sin, cos_lag, sin_lag, back


def layer_norm(values, gain, shift):
    center = jnp.mean(values, axis=-1, keepdims=True)
    centered = values - center
    spread = jnp.mean(centered * centered, axis=-1, keepdims=True)
    rs = lax.rsqrt(spread + epsilon)
    xhat = centered * rs
    return xhat * gain + shift, xhat, rs


def norm_back(grad, gain, xhat, rs):
    e = grad * gain
    inner = rs * (
        e
        - jnp.mean(e, axis=-1, keepdims=True)
        - xhat * jnp.mean(e * xhat, axis=-1, keepdims=True)
    )
    return inner, jnp.sum(grad * xhat, axis=(0, 1)), jnp.sum(grad, axis=(0, 1))


def dot(spec, a, b):
    return jnp.einsum(spec, a, b, preferred_element_type=f32)


def plain(
    tokens,
    ln1_gain,
    ln1_shift,
    w_qkv,
    w_proj,
    mix_pre,
    mix_post,
    ln2_gain,
    ln2_shift,
    w_up,
    conv_kernel,
    w_down,
    out_grad,
):
    images, seq, width = tokens.shape
    heads_local, heads = mix_pre.shape
    size = width // heads
    scale = size ** (-0.5)
    ksize = conv_kernel.shape[0]
    units = conv_kernel.shape[2]
    grid = int(round((seq - 1) ** 0.5))
    cos, sin, cos_lag, sin_lag, back = spectrum(grid, ksize)
    fourier = jnp.asarray(np.stack([cos, sin]), bf16)
    lagged = jnp.asarray(np.stack([cos_lag, sin_lag]), f32)
    lagged_back = jnp.asarray(np.stack([cos_lag, sin_lag]) * back[:, None], f32)
    mine = lax.axis_index("head")

    gains = jnp.stack([ln1_gain, ln1_shift, ln2_gain, ln2_shift])
    gains = lax.all_gather(gains, "dp", axis=1, tiled=True).astype(f32)
    gain_one, shift_one, gain_two, shift_two = gains[0], gains[1], gains[2], gains[3]
    qkv_w = lax.all_gather(w_qkv, "dp", axis=0, tiled=True)
    up_w = lax.all_gather(w_up, "dp", axis=0, tiled=True)
    down_w = lax.all_gather(w_down, "dp", axis=1, tiled=True)
    proj_w = lax.all_gather(w_proj, "head", axis=0, tiled=True)
    proj_w = lax.all_gather(proj_w, "dp", axis=1, tiled=True)
    mixes = lax.all_gather(jnp.stack([mix_pre, mix_post]), "head", axis=1, tiled=True)
    pre, post_mix = mixes[0], mixes[1]

    source = tokens.astype(f32)
    normed_one, xhat_one, rs_one = layer_norm(source, gain_one, shift_one)
    normed_one = normed_one.astype(bf16)
    qkv = dot("ind,dce->ince", normed_one, qkv_w).astype(bf16)
    qkv = lax.all_to_all(qkv, "head", split_axis=0, concat_axis=3, tiled=True)
    own = qkv.shape[0]
    query = qkv[:, :, 0].reshape(own, seq, heads, size)
    keys = qkv[:, :, 1].reshape(own, seq, heads, size)
    values = qkv[:, :, 2].reshape(own, seq, heads, size)
    scores = (dot("inhd,imhd->ihnm", query, keys) * scale).astype(bf16)
    mixed = jnp.einsum("hg,ignm->ihnm", pre, scores.astype(f32), precision=highest)
    probs = jax.nn.softmax(mixed, axis=-1)
    probs_low = probs.astype(bf16)
    post = jnp.einsum(
        "hg,ignm->ihnm", post_mix, probs_low.astype(f32), precision=highest
    ).astype(bf16)
    heads_own = dot("ihnm,imhd->inhd", post, values).reshape(own, seq, width).astype(bf16)
    heads_out = lax.all_gather(heads_own, "head", axis=0, tiled=True)
    middle = source + dot("ine,ed->ind", heads_out, proj_w)
    normed_two, xhat_two, rs_two = layer_norm(middle, gain_two, shift_two)
    normed_two = normed_two.astype(bf16)
    hidden = dot("ind,df->inf", normed_two, up_w)
    erf = lax.erf(hidden * (0.5**0.5))
    activ = 0.5 * hidden * (1.0 + erf)
    slope = 0.5 * (1.0 + erf) + hidden * jnp.exp(-0.5 * hidden * hidden) * 0.3989422804014327
    delta = np.zeros((ksize * ksize, 1), np.float32)
    delta[ksize * ksize // 2] = 1.0
    taps = conv_kernel.reshape(ksize * ksize, units)
    filters = jnp.einsum("zkl,lf->zkf", lagged, taps, precision=highest)
    cos_k, sin_k = filters[0] + 1.0, filters[1]
    wave = dot("zkn,inf->zikf", fourier, activ.astype(bf16))
    cos_a, sin_a = wave[0], wave[1]
    filtered = jnp.stack([cos_k * cos_a + sin_k * sin_a, cos_k * sin_a - sin_k * cos_a])
    widened = dot("zkn,zikf->inf", fourier, filtered.astype(bf16)).astype(bf16)
    branch = dot("inf,fd->ind", widened, down_w)
    branch = lax.psum(branch.astype(bf16), "head").astype(f32)
    output = (middle + branch).astype(bf16)

    down_grad = dot("inf,ind->fd", widened, out_grad)
    widened_grad = dot("ind,fd->inf", out_grad, down_w)
    wave_grad = dot("zkn,inf->zikf", fourier, widened_grad.astype(bf16))
    cos_g, sin_g = wave_grad[0], wave_grad[1]
    spread_grad = jnp.stack([cos_k * cos_g - sin_k * sin_g, cos_k * sin_g + sin_k * cos_g])
    activ_grad = dot("zkn,zikf->inf", fourier, spread_grad.astype(bf16))
    hidden_grad = (activ_grad * slope).astype(bf16)
    cross = jnp.stack(
        [
            jnp.sum(cos_a * cos_g + sin_a * sin_g, axis=0),
            jnp.sum(sin_a * cos_g - cos_a * sin_g, axis=0),
        ]
    )
    kernel_grad = jnp.einsum("zkl,zkf->lf", lagged_back, cross, precision=highest)
    up_grad = dot("ind,inf->df", normed_two, hidden_grad)
    two_grad = dot("inf,df->ind", hidden_grad, up_w).astype(bf16)
    two_grad = lax.psum_scatter(two_grad, "head", scatter_dimension=0, tiled=True).astype(f32)

    def pick(array):
        return lax.dynamic_slice_in_dim(array, mine * own, own, 0)

    middle_from, gain_two_grad, shift_two_grad = norm_back(
        two_grad, gain_two, pick(xhat_two), pick(rs_two)
    )
    middle_grad = pick(out_grad).astype(f32) + middle_from
    attention_own = middle_grad.astype(bf16)
    attention_grad = lax.all_gather(attention_own, "head", axis=0, tiled=True)
    local = width // lax.axis_size("head")
    heads_mine = lax.dynamic_slice_in_dim(heads_out, mine * local, local, 2)
    proj_grad = dot("ine,ind->ed", heads_mine, attention_grad)
    heads_grad = dot("ind,ed->ine", attention_own, proj_w).astype(bf16)
    heads_grad = heads_grad.reshape(own, seq, heads, size)
    values_grad = dot("ihnm,inhd->imhd", post, heads_grad)
    post_grad = dot("inhd,imhd->ihnm", heads_grad, values)
    probs_grad = jnp.einsum("hg,ihnm->ignm", post_mix, post_grad, precision=highest)
    mixed_grad = probs * (probs_grad - jnp.sum(probs_grad * probs, axis=-1, keepdims=True))
    scores_grad = jnp.einsum("hg,ihnm->ignm", pre, mixed_grad, precision=highest).astype(bf16)
    post_mix_grad = dot("ihnm,ignm->hg", post_grad.astype(bf16), probs_low)
    pre_mix_grad = dot("ihnm,ignm->hg", mixed_grad.astype(bf16), scores)
    query_grad = dot("ihnm,imhd->inhd", scores_grad, keys) * scale
    keys_grad = dot("ihnm,inhd->imhd", scores_grad, query) * scale
    qkv_grad = jnp.stack([query_grad, keys_grad, values_grad], axis=2)
    qkv_grad = qkv_grad.reshape(own, seq, 3, width).astype(bf16)
    qkv_grad = lax.all_to_all(qkv_grad, "head", split_axis=3, concat_axis=0, tiled=True)
    qkv_weight_grad = dot("ind,ince->dce", normed_one, qkv_grad)
    one_grad = dot("ince,dce->ind", qkv_grad, qkv_w).astype(bf16)
    one_grad = lax.psum_scatter(one_grad, "head", scatter_dimension=0, tiled=True).astype(f32)
    source_grad, gain_one_grad, shift_one_grad = norm_back(
        one_grad, gain_one, pick(xhat_one), pick(rs_one)
    )
    input_own = (middle_grad + source_grad).astype(bf16)
    input_grad = lax.all_gather(input_own, "head", axis=0, tiled=True)

    def share(grad, axis):
        return lax.psum_scatter(
            grad.astype(bf16), "dp", scatter_dimension=axis, tiled=True
        ).astype(f32)

    norm_grads = jnp.stack([gain_one_grad, shift_one_grad, gain_two_grad, shift_two_grad])
    norm_grads = lax.psum(norm_grads, "head")
    norm_grads = lax.psum_scatter(norm_grads, "dp", scatter_dimension=1, tiled=True)
    mix_grads = lax.psum_scatter(
        jnp.stack([pre_mix_grad, post_mix_grad]), "head", scatter_dimension=1, tiled=True
    )
    mix_grads, kernel_grad = lax.psum((mix_grads, kernel_grad), "dp")
    return (
        output,
        input_grad,
        norm_grads[0],
        norm_grads[1],
        share(qkv_weight_grad, 0),
        share(proj_grad, 1),
        mix_grads[0],
        mix_grads[1],
        norm_grads[2],
        norm_grads[3],
        share(up_grad, 0),
        kernel_grad.reshape(ksize, ksize, units),
        share(down_grad, 1),
    )


MESH = pl.DeviceIdType.MESH
NT = (((1,), (1,)), ((), ()))


def mm(a, b):
    return jnp.dot(a, b, preferred_element_type=f32)


def mm_nt(a, b):
    return lax.dot_general(a, b, NT, preferred_element_type=f32)


def exact(a, b):
    return jnp.dot(a, b, preferred_element_type=f32, precision=highest)


def split(a):
    high = a.astype(bf16)
    return high, (a - high.astype(f32)).astype(bf16)


def remote(src, dst, send, recv, device):
    return pltpu.make_async_remote_copy(
        src_ref=src,
        dst_ref=dst,
        send_sem=send,
        recv_sem=recv,
        device_id=device,
        device_id_type=MESH,
    )


class Place:
    def __init__(self, dp, head):
        self.dp, self.head = dp, head
        self.lines = dp // 2
        self.d, self.s = lax.axis_index("dp"), lax.axis_index("head")
        self.z, self.y = self.d // 2, self.d % 2
        self.x, self.c = self.s // 2, self.s % 2
        self.mate = self.x * 2 + 1 - self.c
        self.across = (1 - self.x) * 2 + self.c
        self.corner = (1 - self.x) * 2 + 1 - self.c

    def near(self, j):
        return ((self.x + j // 2) % 2) * 2 + (self.c + j % 2) % 2

    def z_next(self, k):
        return (self.z + k) % self.lines

    def z_prev(self, k):
        return (self.z + self.lines - k) % self.lines

    def head_next(self, k):
        return (self.s + k) % self.head

    def dp_next(self, k):
        return (self.d + k) % self.dp

    def call(self):
        barrier = pltpu.get_barrier_semaphore()

        def tell(d, s):
            pl.semaphore_signal(barrier, inc=1, device_id=(d, s), device_id_type=MESH)

        tell(self.d, self.mate)
        tell(self.d, self.across)
        tell(self.z * 2 + 1 - self.y, self.s)
        pl.when(self.z > 0)(lambda: tell((self.z - 1) * 2 + self.y, self.s))
        pl.when(self.z < self.lines - 1)(lambda: tell((self.z + 1) * 2 + self.y, self.s))

    def answer(self):
        inner = (self.z > 0) & (self.z < self.lines - 1)
        pl.semaphore_wait(pltpu.get_barrier_semaphore(), jnp.where(inner, 5, 4))


def rows_of(ref, index, count):
    return ref.at[pl.ds(pl.multiple_of(index * count, count), count)]


class Line:
    def __init__(self, at, buf, sems, wide):
        self.at, self.wide = at, wide
        self.groups = buf
        self.buf = buf.at[at.s] if wide else buf
        self.rows = self.buf.shape[0] // at.dp
        self.sems = sems

    def near(self, hops, body):
        at = self.at
        if hops == 0:
            body(at.z)
        else:
            pl.when(at.z >= hops)(lambda: body(at.z - hops))
            pl.when(at.z + hops < at.lines)(lambda: body(at.z + hops))

    def index(self, z, other):
        return z * 2 + (1 - self.at.y if other else self.at.y)

    def block(self, z, other, buf=None):
        return rows_of(self.buf if buf is None else buf, self.index(z, other), self.rows)

    def z_copy(self, up, hops):
        at, (send, recv) = self.at, self.sems[0]
        ref = self.block(at.z - hops if up else at.z + hops, False)
        slot = hops if up else at.lines - 1 + hops
        to = at.z + 1 if up else at.z - 1
        return remote(ref, ref, send.at[slot], recv.at[slot], (to * 2 + at.y, at.s))

    def pass_on(self, up, hops):
        at = self.at
        if up:
            there = (at.z >= hops) & (at.z < at.lines - 1)
        else:
            there = (at.z + hops < at.lines) & (at.z > 0)
        return pl.when(there)

    def y_copy(self, z):
        at, (send, recv) = self.at, self.sems[1]
        ref = self.block(z, False)
        return remote(ref, ref, send.at[z], recv.at[z], (at.z * 2 + 1 - at.y, at.s))

    def x_copy(self, z, other):
        at, (send, recv) = self.at, self.sems[2]
        ref, slot = self.block(z, other), self.index(z, other)
        return remote(ref, ref, send.at[slot], recv.at[slot], (at.d, at.across))

    def mate_copy(self, z, other, far):
        at, (send, recv) = self.at, self.sems[3]
        ref = self.block(z, other, self.groups.at[at.across if far else at.s])
        slot = self.index(z, other) + (at.dp if far else 0)
        return remote(ref, ref, send.at[slot], recv.at[slot], (at.d, at.mate))

    def begin(self):
        for up in (True, False):
            self.pass_on(up, 0)(lambda: self.z_copy(up, 0).start())

    def over_y(self):
        self.y_copy(self.at.z).start()

    def from_z(self, hops):
        at = self.at
        for up in (True, False):

            @pl.when(at.z >= hops if up else at.z + hops < at.lines)
            def _():
                source = at.z - hops if up else at.z + hops
                self.z_copy(up, hops - 1).wait_recv()
                if hops < at.lines - 1:
                    self.pass_on(up, hops)(lambda: self.z_copy(up, hops).start())
                self.y_copy(source).start()

    def on(self, hops, other):
        def body(z):
            self.x_copy(z, other).start()
            self.mate_copy(z, other, False).start()

        self.near(hops, body)

    def from_y(self, hops):
        self.near(hops, lambda z: self.y_copy(z).wait_recv())

    def from_x(self, hops, other):
        def body(z):
            self.x_copy(z, other).wait_recv()
            self.mate_copy(z, other, True).start()

        self.near(hops, body)

    def from_mate(self, far):
        for z in range(self.at.lines):
            for other in (False, True):
                self.mate_copy(z, other, far).wait_recv()

    def drain(self):
        at = self.at
        for hops in range(at.lines - 1):
            for up in (True, False):
                self.pass_on(up, hops)(lambda: self.z_copy(up, hops).wait_send())
        for z in range(at.lines):
            self.y_copy(z).wait_send()
            if self.wide:
                for other in (False, True):
                    self.x_copy(z, other).wait_send()
                    self.mate_copy(z, other, False).wait_send()
                    self.mate_copy(z, other, True).wait_send()


class Rows(Line):
    def both(self, z):
        return rows_of(self.buf, z, 2 * self.rows)

    def z_copy(self, up, hops):
        at, (send, recv) = self.at, self.sems[0]
        ref = self.both(at.z - hops if up else at.z + hops)
        slot = hops if up else at.lines - 1 + hops
        to = at.z + 1 if up else at.z - 1
        return remote(ref, ref, send.at[slot], recv.at[slot], (to * 2 + at.y, at.s))

    def from_y(self):
        self.y_copy(self.at.z).wait_recv()
        self.begin()

    def from_z(self, hops):
        at = self.at
        for up in (True, False):

            @pl.when(at.z >= hops if up else at.z + hops < at.lines)
            def _():
                self.z_copy(up, hops - 1).wait_recv()
                if hops < at.lines - 1:
                    self.pass_on(up, hops)(lambda: self.z_copy(up, hops).start())

    def drain(self):
        at = self.at
        self.y_copy(at.z).wait_send()
        for hops in range(at.lines - 1):
            for up in (True, False):
                self.pass_on(up, hops)(lambda: self.z_copy(up, hops).wait_send())


class Share:
    def __init__(self, at, buf, sems):
        self.at, self.buf = at, buf
        self.send, self.recv = sems

    def copy(self, which):
        at = self.at
        ref = self.buf.at[at.across if which == 2 else at.s]
        to = at.across if which == 1 else at.mate
        return remote(ref, ref, self.send.at[which], self.recv.at[which], (at.d, to))

    def start(self):
        self.copy(1).start()
        self.copy(0).start()

    def wait_mate(self):
        self.copy(0).wait_recv()

    def forward(self):
        self.copy(1).wait_recv()
        self.copy(2).start()

    def wait_corner(self):
        self.copy(2).wait_recv()

    def drain(self):
        for which in range(3):
            self.copy(which).wait_send()


class Fold:
    def __init__(self, at, parts, near, far, sems):
        self.at, self.parts, self.near, self.far = at, parts, near, far
        self.send, self.recv = sems

    def mate_copy(self, which):
        at = self.at
        src = self.parts.at[at.corner if which else at.mate]
        return remote(
            src, self.near.at[which], self.send.at[which], self.recv.at[which], (at.d, at.mate)
        )

    def x_copy(self):
        at = self.at
        return remote(
            self.parts.at[at.across], self.far, self.send.at[2], self.recv.at[2], (at.d, at.across)
        )

    def middle(self):
        at = self.at
        self.mate_copy(1).wait_recv()
        self.parts[at.across] = (
            self.parts[at.across].astype(f32) + self.near[1].astype(f32)
        ).astype(bf16)
        self.x_copy().start()

    def wait(self):
        self.mate_copy(0).wait_recv()
        self.x_copy().wait_recv()

    def total(self, rows):
        return (
            self.parts[self.at.s, rows, :].astype(f32)
            + self.near[0, rows, :].astype(f32)
            + self.far[rows, :].astype(f32)
        )

    def drain(self):
        self.mate_copy(0).wait_send()
        self.mate_copy(1).wait_send()
        self.x_copy().wait_send()


class Scatter:
    def __init__(self, at, src, from_y, from_z, sems):
        self.at, self.src, self.from_y, self.from_z = at, src, from_y, from_z
        (self.y_send, self.y_recv), (self.z_send, self.z_recv) = sems
        self.rows = src.shape[0] // at.dp

    def block(self, z, y):
        return rows_of(self.src, z * 2 + y, self.rows)

    def y_copy(self, k):
        at = self.at
        return remote(
            self.block(at.z_next(k), 1 - at.y),
            self.from_y.at[k],
            self.y_send.at[k],
            self.y_recv.at[k],
            (at.z * 2 + 1 - at.y, at.s),
        )

    def z_copy(self, k):
        at = self.at
        return remote(
            self.block(at.z_next(k), at.y),
            self.from_z.at[k - 1],
            self.z_send.at[k - 1],
            self.z_recv.at[k - 1],
            (at.z_next(k) * 2 + at.y, at.s),
        )

    def start(self):
        for k in (*range(1, self.at.lines), 0):
            self.y_copy(k).start()

    def middle(self, k):
        at = self.at
        self.y_copy(k).wait_recv()
        ref = self.block(at.z_next(k), at.y)
        ref[...] = (ref[...].astype(f32) + self.from_y[k].astype(f32)).astype(bf16)
        self.z_copy(k).start()

    def finish(self):
        at = self.at
        self.y_copy(0).wait_recv()
        total = self.block(at.z, at.y)[...].astype(f32) + self.from_y[0].astype(f32)
        for k in range(1, at.lines):
            self.z_copy(k).wait_recv()
            total = total + self.from_z[k - 1].astype(f32)
        return total

    def drain(self):
        for k in range(self.at.lines):
            self.y_copy(k).wait_send()
        for k in range(1, self.at.lines):
            self.z_copy(k).wait_send()


class Halves(Scatter):
    def partner(self, k):
        z = self.at.z
        return (3 - z, z + 1 - 2 * (z % 2), (z + 2) % 4, z)[k]

    def y_copy(self, k):
        at = self.at
        return remote(
            self.block(self.partner(k), 1 - at.y),
            self.from_y.at[k],
            self.y_send.at[k],
            self.y_recv.at[k],
            (at.z * 2 + 1 - at.y, at.s),
        )

    def z_copy(self, k):
        at = self.at
        return remote(
            self.block(self.partner(k), at.y),
            self.from_z.at[k],
            self.z_send.at[k],
            self.z_recv.at[k],
            (self.partner(max(k, 1)) * 2 + at.y, at.s),
        )

    def start(self):
        for k in range(4):
            self.y_copy(k).start()

    def middle(self, k):
        at, k = self.at, k - 1
        self.y_copy(k).wait_recv()
        ref = self.block(self.partner(k), at.y)
        total = ref[...].astype(f32) + self.from_y[k].astype(f32)
        if k == 2:
            self.z_copy(0).wait_recv()
            total = total + self.from_z[0].astype(f32)
        ref[...] = total.astype(bf16)
        self.z_copy(k).start()

    def finish(self):
        at = self.at
        self.y_copy(3).wait_recv()
        total = self.block(at.z, at.y)[...].astype(f32) + self.from_y[3].astype(f32)
        for k in (1, 2):
            self.z_copy(k).wait_recv()
            total = total + self.from_z[k].astype(f32)
        return total

    def drain(self):
        for k in range(4):
            self.y_copy(k).wait_send()
        for k in range(3):
            self.z_copy(k).wait_send()


class Exchange:
    def __init__(self, at, axis, slots, sems, block_for):
        self.at, self.axis, self.slots, self.block_for = at, axis, slots, block_for
        self.send, self.recv = sems
        self.count = at.dp if axis == "dp" else at.head
        self.me = at.d if axis == "dp" else at.s

    def copy(self, k):
        at = self.at
        peer = (self.me + k) % self.count
        device = (peer, at.s) if self.axis == "dp" else (at.d, peer)
        return remote(
            self.block_for(peer),
            self.slots.at[self.me],
            self.send.at[k - 1],
            self.recv.at[k - 1],
            device,
        )

    def start(self):
        for k in range(1, self.count):
            self.copy(k).start()

    def wait(self):
        for k in range(1, self.count):
            self.copy(k).wait_recv()

    def drain(self):
        for k in range(1, self.count):
            self.copy(k).wait_send()

    def total(self):
        total = self.slots[0]
        for k in range(1, self.count):
            total = total + self.slots[k]
        return total


class Doubling:
    def __init__(self, at, held, slots, sems, partners):
        self.at, self.held, self.slots, self.partners = at, held, slots, partners
        self.send, self.recv = sems

    def copy(self, k):
        return remote(
            self.held.at[k], self.slots.at[k], self.send.at[k], self.recv.at[k], self.partners[k]
        )

    def start(self):
        self.copy(0).start()

    def step(self, k):
        self.copy(k).wait_recv()
        total = self.held[k].astype(f32) + self.slots[k].astype(f32)
        if k + 1 == len(self.partners):
            return total
        self.held[k + 1] = total.astype(self.held.dtype)
        self.copy(k + 1).start()

    def drain(self):
        for k in range(len(self.partners)):
            self.copy(k).wait_send()


def norm_rows(x):
    center = jnp.mean(x, axis=-1, keepdims=True)
    centered = x - center
    spread = jnp.mean(centered * centered, axis=-1, keepdims=True)
    rs = lax.rsqrt(spread + epsilon)
    return centered * rs, rs


def norm_back_rows(grad, gain, xhat, rs):
    e = grad * gain
    return rs * (
        e
        - jnp.mean(e, axis=-1, keepdims=True)
        - xhat * jnp.mean(e * xhat, axis=-1, keepdims=True)
    )


def fold_rows(a):
    return jnp.sum(a.reshape(a.shape[0] // 8, 8, a.shape[1]), axis=0)


def block_kernel(sizes, names_in, names_out, names_scratch, *refs):
    seq, dp, head, scale = sizes
    n_in, n_out = len(names_in), len(names_out)
    i = types.SimpleNamespace(**dict(zip(names_in, refs[:n_in])))
    o = types.SimpleNamespace(**dict(zip(names_out, refs[n_in : n_in + n_out])))
    b = types.SimpleNamespace(**dict(zip(names_scratch, refs[n_in + n_out :])))
    at = Place(dp, head)
    images, padded, width = b.tok.shape
    b.bp, b.dq = b.actg, b.act.at[0]
    b.dk, b.mg = b.fi.at[:padded], b.wave.at[:padded]
    b.inp, b.out = b.n1, b.n2
    hops = range(1, at.lines)
    share = i.w_up.shape[0]
    own_rows = pl.ds(pl.multiple_of(at.d * share, share), share)
    loads = [
        pltpu.make_async_copy(src, dst, b.loads.at[n])
        for n, (src, dst) in enumerate(
            (
                (i.w_down, b.wd.at[own_rows]),
                (i.w_up, b.wu.at[own_rows]),
                (i.tokens, b.raw.at[0]),
                (i.out_grad, b.raw.at[1]),
            )
        )
    ]
    chunks = padded // 16
    wide = b.k.shape[0]
    slots = b.sc.shape[0]
    pairs = slots // 2
    units = b.wu.shape[1]
    bins = b.filt.shape[0] // 2

    def span(j, size):
        return pl.ds(j * size if isinstance(j, int) else pl.multiple_of(j * size, size), size)

    def chunk(j):
        return span(j, 16)

    def tile(p):
        return span(p, 128)

    def twice(body):
        def step(k, carry):
            body(1 - k)
            return carry

        lax.fori_loop(0, 2, step, 0)

    def each(steps, body):
        for j in range(steps) if isinstance(steps, int) else steps:
            body(j)

    def flip_block(a):
        return mm_nt(i.eye[: a.shape[1], : a.shape[1]], a)

    def halves(low, high):
        return (mm(low, i.eye[:64, :128]) + mm(high, i.eye[64:128, :128])).astype(bf16)

    at.call()
    for load in loads:
        load.start()
    w_q, w_k, w_v = i.w_qkv[0], i.w_qkv[1], i.w_qkv[2]
    b.wqk[at.s, own_rows, 0:128] = w_q[:, :128]
    b.wqk[at.s, own_rows, 128:256] = w_k[:, :128]
    b.wqk[at.s, own_rows, 256:384] = halves(w_q[:, 128:], w_k[:, 128:])
    own_gains, own_mixes = rows_of(b.gains, at.d, 8), b.mixes.at[at.s]
    own_gains[...] = jnp.zeros((8, 128), f32)
    own_mixes[...] = jnp.zeros((8, 128), f32)
    for r, gain in enumerate((i.ln1_gain, i.ln1_shift, i.ln2_gain, i.ln2_shift)):
        own_gains[r : r + 1, :share] = gain[...].astype(f32)
    local_heads, heads = i.mix_pre.shape
    own_mixes[:local_heads, :heads] = i.mix_pre[...]
    own_mixes[4 : 4 + local_heads, :heads] = i.mix_post[...]
    p_t = flip_block(i.w_proj[...]).astype(bf16)
    b.wv[at.s, own_rows, 0:128] = w_v[:, :128]
    b.wv[at.s, own_rows, 128:256] = halves(w_v[:, 128:], p_t[:, 128:])
    b.wp_two[at.s, own_rows, :] = p_t[:, :128]

    at.answer()
    loads[0].wait()
    loads[1].wait()

    def line(kind, buf, name, wide):
        sems = [(getattr(b, name + part + "_s"), getattr(b, name + part + "_r")) for part in ("zyxm" if wide else "zy")]
        return kind(at, buf, sems, wide)

    gains = line(Line, b.gains, "g", False)
    mixes = Share(at, b.mixes, (b.mi_s, b.mi_r))
    gq = line(Line, b.wqk, "q", True)
    gv = line(Line, b.wv, "v", True)
    gp = line(Line, b.wp_two, "p", True)
    cut = units // 3 * 2
    gu = line(Line, b.wu.at[:, :cut], "u", False)
    gr = line(Rows, b.wu.at[:, cut:], "r", False)
    gd = line(Line, b.wd, "d", False)
    ho = Share(at, b.ho, (b.ho_s, b.ho_r))
    ag = Share(at, b.ag, (b.ag_s, b.ag_r))
    out = Share(at, b.out, (b.ou_s, b.ou_r))
    inp = Share(at, b.inp, (b.in_s, b.in_r))
    fold_two = Fold(at, b.np, b.np_near, b.np_far, (b.np_s, b.np_r))
    fold_out = Fold(at, b.bp, b.bp_near, b.bp_far, (b.bp_s, b.bp_r))
    sc_up = Halves(at, b.g_up, b.up_y, b.up_z, ((b.uy2_s, b.uy2_r), (b.uz2_s, b.uz2_r)))
    sc_down = Halves(at, b.g_down, b.down_y, b.down_z, ((b.dy2_s, b.dy2_r), (b.dz2_s, b.dz2_r)))
    sc_qk = Scatter(at, b.g_qk, b.qk_y, b.qk_z, ((b.qy2_s, b.qy2_r), (b.qz2_s, b.qz2_r)))
    sc_pv = Scatter(at, b.g_pv, b.pv_y, b.pv_z, ((b.py2_s, b.py2_r), (b.pz2_s, b.pz2_r)))
    sc_v = Scatter(at, b.g_v, b.v_y, b.v_z, ((b.vy2_s, b.vy2_r), (b.vz2_s, b.vz2_r)))
    turn_v = Exchange(at, "head", b.turned_v, (b.tv_s, b.tv_r), lambda s: b.turn_v.at[s])
    turn = Exchange(at, "head", b.turned, (b.tu_s, b.tu_r), lambda s: b.turn.at[s])
    over_dp = (
        ((at.z + 1 - 2 * (at.z % 2)) * 2 + at.y, at.s),
        ((at.z + 2) % 4 * 2 + at.y, at.s),
        (at.z * 2 + 1 - at.y, at.s),
    )
    taps = Doubling(at, b.taps, b.taps_in, (b.ta_s, b.ta_r), over_dp)
    small = Doubling(
        at, b.small, b.small_in, (b.sm_s, b.sm_r), ((at.d, at.across), (at.d, at.mate), *over_dp)
    )

    passed = ((0, False), (1, False), (0, True), (2, False), (1, True), (3, False), (2, True), (3, True))
    gq.begin()
    gq.over_y()
    gq.on(0, False)
    gains.begin()
    gains.over_y()
    mixes.start()
    gv.begin()
    gv.over_y()
    gv.on(0, False)
    gp.begin()
    gp.over_y()
    gp.on(0, False)
    gr.over_y()

    def norm_one(image):
        def body(j):
            xhat, _ = norm_rows(b.tok[image, chunk(j), :].astype(f32))
            b.n1[image, chunk(j), :] = (xhat * b.norms[0:1, :] + b.norms[1:2, :]).astype(bf16)

        each(chunks, body)

    ksize = i.taps.shape[0]
    b.edge[...] = jnp.zeros_like(b.edge)
    for p in range(ksize):
        b.edge[p * ksize : (p + 1) * ksize, :] = i.taps[p]
    b.filt[...] = exact(i.lag[...], b.edge[...])
    b.filt[:bins, :] += 1.0
    b.cross[...] = jnp.zeros_like(b.cross)
    b.mix_one[...] = jnp.zeros_like(b.mix_one)
    b.mix_two[...] = jnp.zeros_like(b.mix_two)
    b.k[padded:, :] = jnp.zeros((wide - padded, width), bf16)
    b.v[padded:, :] = jnp.zeros((wide - padded, width), bf16)

    for which, dst in enumerate((b.tok, b.og)):
        loads[2 + which].wait()
        for r in range(chunks):
            n = min(16, seq - r * 16)
            rows = b.raw[which, r * 16 : r * 16 + n].reshape(n * images, width)
            apart = mm(i.deal[:, : n * images], rows).astype(bf16)
            dst[:, chunk(r), :] = apart.reshape(images, 16, width)

    gains.from_z(1)
    gq.from_z(1)
    gq.on(1, False)
    gq.from_y(0)
    gq.on(0, True)
    gv.from_z(1)
    gp.from_z(1)
    gains.from_z(2)
    mixes.forward()
    gq.from_z(2)
    gq.on(2, False)
    gq.from_y(1)
    gq.on(1, True)
    gv.from_z(2)
    gp.from_z(2)
    gd.begin()
    gd.over_y()
    gu.begin()
    gu.over_y()
    gains.from_z(3)
    gq.from_z(3)
    gq.on(3, False)
    gr.from_y()
    gq.from_y(2)
    gq.on(2, True)
    gv.on(1, False)
    gv.from_y(0)
    gv.on(0, True)
    for k in range(at.lines):
        gains.from_y(k)
    spread = mm(b.gains[...].astype(bf16), i.comb[...])
    row = lax.broadcasted_iota(jnp.int32, spread.shape, 0)
    lane = lax.broadcasted_iota(jnp.int32, spread.shape, 1)
    first = (row >> 3) * share
    here = (lane >= first) & (lane < first + share)
    for r in range(4):
        b.norms[r : r + 1, :] = jnp.sum(
            jnp.where(here & ((row & 7) == r), spread, 0.0), axis=0, keepdims=True
        )
    norm_one(at.s)
    gv.from_z(3)
    gp.from_z(3)

    mixes.wait_mate()
    mixes.wait_corner()
    diagonal = i.diagonal[...]
    for part, piece in enumerate(split(b.mixes[...].reshape(head * 8, 128))):
        for which, pick in enumerate((i.pick_pre, i.pick_post)):
            picked = mm(pick[...], piece).astype(bf16)
            b.kron[which, part] = (mm_nt(picked, i.place[...]) * diagonal).astype(bf16)
            b.kron_t[which, part] = (mm_nt(i.place[...], picked) * diagonal).astype(bf16)

    gd.from_z(1)
    gq.from_y(3)
    gq.on(3, True)
    gv.on(2, False)
    gv.from_y(1)
    gv.on(1, True)
    gv.on(3, False)

    lo = (lax.broadcasted_iota(jnp.int32, (1, 128), 1) < 64).astype(f32)
    low_half = lax.broadcasted_iota(jnp.int32, (padded, 128), 1) < 64
    lo_b, hi_b = lo.astype(bf16), (1.0 - lo).astype(bf16)

    def project(g):
        t = mm(b.n1[at.s], b.wqk[g])
        b.q[:, tile(g)] = (t[:, :128] * scale).astype(bf16)
        b.k[:padded, tile(g)] = t[:, 128:256].astype(bf16)
        b.third_qk[g] = t[:, 256:]

    def project_v(g):
        t = mm(b.n1[at.s], b.wv[g])
        b.v[:padded, tile(g)] = t[:, :128].astype(bf16)
        b.third_v[g] = t[:, 128:]

    project(at.s)
    gv.from_y(2)
    gv.on(2, True)
    gq.from_mate(False)
    project(at.mate)
    gu.from_z(1)
    for block in passed:
        gq.from_x(*block)
    project(at.across)
    gv.from_y(3)
    gv.on(3, True)
    gq.from_mate(True)
    project(at.corner)
    for p in range(head // 2):
        one, two = b.third_qk[2 * p], b.third_qk[2 * p + 1]
        third = tile(head + p)
        b.q[:, third] = (jnp.where(low_half, one, pltpu.roll(two, 64, 1)) * scale).astype(bf16)
        b.k[:padded, third] = jnp.where(low_half, pltpu.roll(one, 64, 1), two).astype(bf16)

    def score(p):
        q, k = b.q[:, tile(p)], b.k[:, tile(p)]
        b.sc[2 * p] = mm_nt(q * lo_b, k).astype(bf16)
        b.sc[2 * p + 1] = mm_nt(q * hi_b, k).astype(bf16)

    each(pairs, score)
    gr.from_z(1)
    for block in passed[1:]:
        if block[1]:
            gp.from_y(block[0])
        gp.on(*block)
    gd.from_z(2)

    def mixed(table, which, block):
        return mm(table[which, 0], block) + mm(table[which, 1], block)

    def slab(ref, j):
        return ref[:, chunk(j), :].reshape(slots * 16, wide)

    def put(ref, j, value):
        ref[:, chunk(j), :] = value.reshape(slots, 16, wide)

    def soften(j):
        beyond = lax.broadcasted_iota(jnp.int32, (slots * 16, wide), 1) >= seq
        logits = jnp.where(beyond, -1e30, mixed(b.kron, 0, slab(b.sc, j)))
        top = jnp.max(logits, axis=-1, keepdims=True)
        power = jnp.exp(logits - top)
        probs = power / jnp.sum(power, axis=-1, keepdims=True)
        put(b.pr, j, probs)
        put(b.post, j, mixed(b.kron, 1, probs.astype(bf16)).astype(bf16))

    each(chunks, soften)
    gu.from_z(2)
    for block in passed:
        gv.from_x(*block)
    project_v(at.s)
    gv.from_mate(False)
    project_v(at.mate)
    project_v(at.across)
    gv.from_mate(True)
    project_v(at.corner)
    for p in range(head // 2):
        b.v[:padded, tile(head + p)] = jnp.where(
            low_half, b.third_v[2 * p], pltpu.roll(b.third_v[2 * p + 1], 64, 1)
        ).astype(bf16)

    def gather_heads(p):
        v = b.v[:, tile(p)]
        b.ho[at.s, :, tile(p)] = (mm(b.post[2 * p], v * lo_b) + mm(b.post[2 * p + 1], v * hi_b)).astype(bf16)

    each(pairs, gather_heads)
    ho.start()
    gr.from_z(2)
    gd.from_z(3)
    gu.from_z(3)

    def flip(src, dst):
        for r in range(width // 256):
            lanes = span(r, 256)
            block = src[:, :, lanes].reshape(images * padded, 256)
            dst[lanes, :] = mm_nt(i.eye[...], block).astype(bf16)

    def weight_grad(dst, left, right):
        for r in range(width // 256):
            rows = span(r, 256)
            dst[rows, :] = mm(left[rows, :], right()).astype(bf16)

    def flat(ref):
        return ref[...].reshape(images * padded, ref.shape[2])

    lax.fori_loop(1, images, lambda k, carry: (norm_one(at.head_next(k)), carry)[1], 0)
    flip(b.og, b.og_t)

    for block in passed:
        gp.from_x(*block)
    gp.from_mate(False)
    gp.from_mate(True)
    low_rows = lax.broadcasted_iota(jnp.int32, (width, 128), 1) < 64
    for g in range(head):
        b.wp[:, tile(g)] = b.wp_two[g]
    for p in range(head // 2):
        one, two = b.wv[2 * p, :, 128:].astype(f32), b.wv[2 * p + 1, :, 128:].astype(f32)
        b.wp[:, tile(head + p)] = jnp.where(low_rows, pltpu.roll(one, 64, 1), two).astype(bf16)

    def chip_images(step):
        return 2 * ((at.x + step) % 2)

    def two(ref, step):
        return ref[pl.ds(chip_images(step), 2)].reshape(2 * padded, ref.shape[2])

    def rows_in_two(step, body):
        for half in range(2):
            for r in range(chunks):
                body(chip_images(step) + half, chunk(r), chunk(half * chunks + r))

    def bins_of(body):
        for j in range(bins // 16):
            body(span(j, 16), pl.ds(bins + j * 16, 16))

    def conv_back(step):
        b.act[...] = mm(two(b.og, step), b.wd[...]).astype(bf16).reshape(2, padded, units)
        for half in range(2):
            image = chip_images(step) + half
            b.wave[...] = mm(i.fourier[...], b.act[half])

            def body(cos, sin):
                cos_g, sin_g = b.wave[cos, :], b.wave[sin, :]
                cos_k, sin_k = b.filt[cos, :], b.filt[sin, :]
                b.gf[image, cos, :] = cos_g.astype(bf16)
                b.gf[image, sin, :] = sin_g.astype(bf16)
                b.fi[cos, :] = (cos_k * cos_g - sin_k * sin_g).astype(bf16)
                b.fi[sin, :] = (cos_k * sin_g + sin_k * cos_g).astype(bf16)

            bins_of(body)
            b.actg[image] = mm(i.fourier_t[...], b.fi[...]).astype(bf16)

    def up(step, between):
        b.hid[...] = mm_nt(two(b.ho, step), b.wp[...])

        def norm_two(image, rows, both):
            middle = b.tok[image, rows, :].astype(f32) + b.hid[both, :]
            b.mid[jnp.minimum(jnp.abs(image - at.s), 1), rows, :] = middle
            xhat, _ = norm_rows(middle)
            b.n2[image, rows, :] = (xhat * b.norms[2:3, :] + b.norms[3:4, :]).astype(bf16)

        rows_in_two(step, norm_two)
        between()
        b.hid[...] = mm(two(b.n2, step), b.wu[...])

        def gelu(image, rows, both):
            h = b.hid[both, :]
            cdf = 0.5 * (1.0 + lax.erf(h * (0.5**0.5)))
            slope = cdf + h * jnp.exp(-0.5 * h * h) * 0.3989422804014327
            b.wid[image, rows, :] = (h * cdf).astype(bf16)
            b.hg[image, rows, :] = (b.actg[image, rows, :].astype(f32) * slope).astype(bf16)

        rows_in_two(step, gelu)
        b.np[pl.ds(chip_images(step), 2)] = (
            mm_nt(two(b.hg, step), b.wu[...]).astype(bf16).reshape(2, padded, width)
        )

    for k in range(at.lines):
        gd.from_y(k)

    def backward_part(step):
        conv_back(step)
        pl.when(step == 1)(ho.forward)

    def forward_part(step):
        pl.when(step == 0)(ho.wait_mate)
        up(step, lambda: pl.when(step == 0)(fold_two.middle))
        pl.when(step == 1)(lambda: fold_two.mate_copy(1).start())
        pl.when(step == 0)(lambda: fold_two.mate_copy(0).start())

    twice(backward_part)
    gr.from_z(3)
    for k in range(at.lines):
        gu.from_y(k)
    ho.wait_corner()
    twice(forward_part)
    flip(b.n2, b.flip)
    weight_grad(b.g_up, b.flip, lambda: flat(b.hg))
    sc_up.start()

    def down(step, between):
        for half in range(2):
            image = chip_images(step) + half
            if half:
                between()
            b.wave[...] = mm(i.fourier[...], b.wid[image])

            def body(cos, sin):
                cos_a, sin_a = b.wave[cos, :], b.wave[sin, :]
                cos_k, sin_k = b.filt[cos, :], b.filt[sin, :]
                cos_g, sin_g = b.gf[image, cos, :].astype(f32), b.gf[image, sin, :].astype(f32)
                b.fi[cos, :] = (cos_k * cos_a + sin_k * sin_a).astype(bf16)
                b.fi[sin, :] = (cos_k * sin_a - sin_k * cos_a).astype(bf16)
                b.cross[cos, :] += cos_a * cos_g + sin_a * sin_g
                b.cross[sin, :] += sin_a * cos_g - cos_a * sin_g

            bins_of(body)
            b.wid[image] = mm(i.fourier_t[...], b.fi[...]).astype(bf16)
        b.bp[pl.ds(chip_images(step), 2)] = (
            mm_nt(two(b.wid, step), b.wd[...]).astype(bf16).reshape(2, padded, width)
        )

    def down_part(step):
        down(step, lambda: pl.when(step == 0)(fold_out.middle))
        pl.when(step == 1)(lambda: fold_out.mate_copy(1).start())
        pl.when(step == 0)(lambda: fold_out.mate_copy(0).start())

    twice(down_part)
    weight_grad(b.g_down, b.og_t, lambda: flat(b.wid))
    sc_down.start()
    b.taps[0] = exact(i.lag_back[...], b.cross[...]).astype(bf16)
    taps.start()
    sc_up.middle(1)
    flip(b.n1, b.flip)

    fold_two.wait()
    zero = jnp.zeros((8, width), f32)
    gain_sum, shift_sum = zero, zero
    for j in range(chunks):
        grad = fold_two.total(chunk(j))
        xhat, rs = norm_rows(b.mid[0, chunk(j), :])
        inner = norm_back_rows(grad, b.norms[2:3, :], xhat, rs)
        total = b.og[at.s, chunk(j), :].astype(f32) + inner
        b.mg[chunk(j), :] = total
        b.ag[at.s, chunk(j), :] = total.astype(bf16)
        gain_sum += fold_rows(grad * xhat)
        shift_sum += fold_rows(grad)
    b.sums[2:3, :] = jnp.sum(gain_sum, axis=0, keepdims=True)
    b.sums[3:4, :] = jnp.sum(shift_sum, axis=0, keepdims=True)

    b.hgr[...] = mm(b.ag[at.s], b.wp[...]).astype(bf16)

    def flip_one(src, dst):
        for r in range(width // 256):
            dst[span(r, 256), :] = mm_nt(i.eye[...], src[:, span(r, 256)]).astype(bf16)

    flip_one(b.hgr, b.hgr_t)
    flip_one(b.q, b.q_t)

    def back_post(p):
        g, v = b.hgr[:, tile(p)], b.v[:, tile(p)]
        for half, mask in enumerate((lo_b, hi_b)):
            b.pg[2 * p + half] = mm_nt(g * mask, v).astype(bf16)
            rows = span(2 * p + half, 64)
            b.dv_t[rows, :] = mm(b.hgr_t[rows, :], b.post[2 * p + half]).astype(bf16)

    each(pairs, back_post)

    def unflip(src, dst):
        for r in range(width // 256):
            dst[:, span(r, 256)] = mm_nt(i.eye[:padded, :], src[span(r, 256), :]).astype(bf16)

    unflip(b.dv_t, b.dv)
    for g in range(head):
        b.turn_v[g, :, 0:128] = b.dv[:, tile(g)]
        v3 = b.dv[:, tile(head + g // 2)].astype(f32)
        if g % 2:
            v3 = pltpu.roll(v3, 64, 1)
        b.turn_v[g, :, 128:256] = jnp.where(low_half, v3, 0.0).astype(bf16)
    turn_v.start()
    b.turned_v[at.s] = b.turn_v[at.s]
    sc_up.middle(2)

    def back_soften(j):
        grad = slab(b.pg, j)
        probs = slab(b.pr, j)
        b.mix_two[...] += mm_nt(grad, probs.astype(bf16))
        probs_grad = mixed(b.kron_t, 1, grad)
        inner = jnp.sum(probs_grad * probs, axis=-1, keepdims=True)
        mixed_grad = (probs * (probs_grad - inner)).astype(bf16)
        b.mix_one[...] += mm_nt(mixed_grad, slab(b.sc, j))
        put(b.pg, j, mixed(b.kron_t, 0, mixed_grad).astype(bf16))

    each(chunks, back_soften)

    def back_score(p):
        k = b.k[:, tile(p)]
        b.dq[:, tile(p)] = (
            (mm(b.pg[2 * p], k * lo_b) + mm(b.pg[2 * p + 1], k * hi_b)) * scale
        ).astype(bf16)
        for half in range(2):
            rows = span(2 * p + half, 64)
            b.dk_t[rows, :] = mm(b.q_t[rows, :], b.pg[2 * p + half]).astype(bf16)

    each(pairs, back_score)
    unflip(b.dk_t, b.dk)
    for g in range(head):
        b.turn[g, :, 0:128] = b.dq[:, tile(g)]
        b.turn[g, :, 128:256] = b.dk[:, tile(g)]
        third = tile(head + g // 2)
        q3, k3 = b.dq[:, third].astype(f32), b.dk[:, third].astype(f32)
        if g % 2:
            q3 = pltpu.roll(q3, 64, 1)
        else:
            k3 = pltpu.roll(k3, 64, 1)
        b.turn[g, :, 256:384] = jnp.where(low_half, q3, k3).astype(bf16)
    turn.start()
    b.turned[at.s] = b.turn[at.s]
    for k in range(3, at.lines):
        sc_up.middle(k)

    for g in range(head):
        part = mm_nt(b.turn[g], b.wqk[g]) + mm_nt(b.turn_v[g], b.wv[g])
        if g:
            b.hid[:padded, :] += part
        else:
            b.hid[:padded, :] = part
    gain_sum, shift_sum = zero, zero
    for j in range(chunks):
        grad = b.hid[chunk(j), :]
        xhat, rs = norm_rows(b.tok[at.s, chunk(j), :].astype(f32))
        inner = norm_back_rows(grad, b.norms[0:1, :], xhat, rs)
        b.inp[at.s, chunk(j), :] = (b.mg[chunk(j), :] + inner).astype(bf16)
        gain_sum += fold_rows(grad * xhat)
        shift_sum += fold_rows(grad)
    b.sums[0:1, :] = jnp.sum(gain_sum, axis=0, keepdims=True)
    b.sums[1:2, :] = jnp.sum(shift_sum, axis=0, keepdims=True)

    blocks = jnp.zeros((head * 8, 128), f32)
    for table, pick in ((b.mix_one, i.pick_pre_t), (b.mix_two, i.pick_post_t)):
        blocks += exact(exact(pick[...], table[...] * diagonal), i.place_f[...])
    b.sums[4:8, :] = jnp.zeros((4, width), f32)
    b.small[0, :, :width] = b.sums[...]
    for g in range(head):
        b.small[0, :, width + g * 128 : width + (g + 1) * 128] = blocks[g * 8 : (g + 1) * 8]
    small.start()
    ag.start()
    taps.step(0)
    sc_down.middle(1)

    turn_v.wait()
    inp.start()
    for r in range(width // 256):
        rows = span(r, 256)
        values = mm(b.flip[rows, :], flat(b.turned_v))
        b.g_v[rows, :] = values[:, :128].astype(bf16)
        b.g_pv[rows, 0:128] = values[:, 128:].astype(bf16)
    sc_v.start()
    fold_out.wait()
    for j in range(chunks):
        b.out[at.s, chunk(j), :] = (b.mid[0, chunk(j), :] + fold_out.total(chunk(j))).astype(bf16)
    out.start()
    taps.step(1)
    sc_down.middle(2)
    turn.wait()
    weight_grad(b.g_qk, b.flip, lambda: flat(b.turned))
    sc_qk.start()
    sc_down.middle(3)
    small.step(0)
    small.step(1)
    ag.forward()
    for k in range(1, at.lines):
        sc_v.middle(k)
    ag.wait_mate()
    ag.wait_corner()
    flip(b.ag, b.og_t)
    mine = tile(at.s)
    third_tile = tile(head + at.s // 2)
    for r in range(width // 256):
        rows = span(r, 256)
        left = b.og_t[rows, :]
        proj = mm(left, b.ho[:, :, mine].reshape(images * padded, 128))
        third = pltpu.roll(mm(left, b.ho[:, :, third_tile].reshape(images * padded, 128)), 64 * (1 - at.c), 1)
        low = lax.broadcasted_iota(jnp.int32, third.shape, 1) < 64
        b.g_pv[rows, 0:128] = jnp.where(low, b.g_pv[rows, 0:128].astype(f32), third).astype(bf16)
        b.g_pv[rows, 128:256] = proj.astype(bf16)
    sc_pv.start()
    small.step(2)
    for k in range(1, at.lines):
        sc_qk.middle(k)
    small.step(3)
    o.w_up[...] = sc_up.finish()
    for k in range(1, at.lines):
        sc_pv.middle(k)
    o.taps[...] = taps.step(2)
    o.w_down[...] = sc_down.finish()
    inp.forward()
    small_total = small.step(4)
    o.mixes[...] = jnp.zeros((8, 128), f32)
    for g in range(head):

        @pl.when(at.s == g)
        def _():
            o.mixes[...] = small_total[:, width + g * 128 : width + (g + 1) * 128]

    columns = lax.broadcasted_iota(jnp.int32, (8, width), 1)
    own = (columns >= at.d * share) & (columns < (at.d + 1) * share)
    o.norms[...] = exact(jnp.where(own, small_total[:, :width], 0.0), i.comb_t[...])
    out.forward()
    def turned_over(a):
        return lax.dot_general(
            i.eye_f[: a.shape[1], : a.shape[1]], a, NT, preferred_element_type=f32, precision=highest
        )

    o.w_v[:, 0:128] = sc_v.finish()
    out.wait_mate()
    out.wait_corner()
    save_out = pltpu.make_async_copy(b.out, o.output, b.loads.at[0])
    save_out.start()
    inp.wait_mate()
    inp.wait_corner()
    save_inp = pltpu.make_async_copy(b.inp, o.input, b.loads.at[1])
    save_inp.start()
    o.qk[...] = sc_qk.finish()
    pv = sc_pv.finish()
    o.w_v[:, 128:] = pv[:, :64]
    o.w_proj[:128, :] = turned_over(pv[:, 128:])
    o.w_proj[128:, :] = turned_over(pv[:, :128])[64:, :]
    save_out.wait()
    save_inp.wait()
    for item in (
        gains, mixes, gq, gv, gp, gu, gr, gd, ho, ag, out, inp, fold_two, fold_out, sc_up, sc_down, sc_qk, sc_pv, sc_v,
        turn, turn_v, taps, small,
    ):
        item.drain()


def finish_kernel(sizes, *refs):
    local_heads, heads, share = sizes
    (output, inputs, qk, w_v, w_proj, up, down, norms, mixes, taps, deal_t) = refs[:11]
    (o_output, o_input, o_one_g, o_one_s, o_qkv, o_proj, o_pre, o_post, o_two_g, o_two_s, o_up, o_taps, o_down) = refs[11:]
    images, rows, width = output.shape
    for src, dst in ((output, o_output), (inputs, o_input)):
        for r in range(rows // 16):
            some = pl.ds(r * 16, 16)
            mixed = mm(deal_t[...], src[:, some, :].reshape(images * 16, width))
            dst[some] = mixed.astype(bf16).reshape(16, images, width)

    @pl.when(pl.program_id(0) == 0)
    def _():
        thirds = qk[:, 256:]
        o_qkv[0, :, 0:128] = qk[:, 0:128]
        o_qkv[0, :, 128:] = thirds[:, :64]
        o_qkv[1, :, 0:128] = qk[:, 128:256]
        o_qkv[1, :, 128:] = pltpu.roll(thirds, 64, 1)[:, :64]
        o_qkv[2] = w_v[...]
        o_proj[...] = w_proj[...]
        o_up[...] = up[...]
        o_down[...] = down[...]
        o_pre[...] = mixes[:local_heads, :heads]
        o_post[...] = mixes[4 : 4 + local_heads, :heads]
        for r, ref in enumerate((o_one_g, o_one_s, o_two_g, o_two_s)):
            ref[...] = norms[r : r + 1, :share]
        ksize = o_taps.shape[0]
        for p in range(ksize):
            o_taps[p] = taps[p * ksize : (p + 1) * ksize, :]


def tables(seq, dp, head, heads, grid, ksize, share):
    cos, sin, cos_lag, sin_lag, back = spectrum(grid, ksize)
    used = cos.shape[0]
    bins = -(-used // 16) * 16
    padded = -(-seq // 16) * 16
    fourier = np.zeros((2 * bins, padded))
    fourier[:used, :seq] = cos
    fourier[bins : bins + used, :seq] = sin
    taps = ksize * ksize
    lag = np.zeros((2 * bins, -(-taps // 8) * 8))
    lag[:used, :taps] = cos_lag
    lag[bins : bins + used, :taps] = sin_lag
    lag_back = np.zeros((-(-taps // 16) * 16, 2 * bins))
    lag_back[:taps, :used] = (cos_lag * back[:, None]).T
    lag_back[:taps, bins : bins + used] = (sin_lag * back[:, None]).T
    comb = (np.arange(share * dp)[None, :] % share == np.arange(128)[:, None]) & (
        np.arange(128)[:, None] < share
    )
    group = heads // head
    slot = [group * g + l for g in range(head) for l in range(2)] + [group * g + 2 for g in range(head)]
    wide = heads * 16
    pick = np.zeros((2, wide, head * 8))
    place = np.zeros((wide, 128))
    for p, h in enumerate(slot):
        for row in range(16):
            for which in range(2):
                pick[which, p * 16 + row, (h // group) * 8 + which * 4 + h % group] = 1.0
            place[p * 16 + row, h] = 1.0
    deal = np.zeros((16 * head, 16 * head))
    for token in range(16):
        for image in range(head):
            deal[image * 16 + token, token * head + image] = 1.0
    diagonal = (np.arange(wide)[:, None] % 16) == (np.arange(wide)[None, :] % 16)
    return {
        "fourier": jnp.asarray(fourier, bf16),
        "fourier_t": jnp.asarray(fourier.T, bf16),
        "lag": jnp.asarray(lag, f32),
        "lag_back": jnp.asarray(lag_back, f32),
        "comb": jnp.asarray(comb, bf16),
        "comb_t": jnp.asarray(comb.T, f32),
        "pick_pre": jnp.asarray(pick[0], bf16),
        "pick_post": jnp.asarray(pick[1], bf16),
        "pick_pre_t": jnp.asarray(pick[0].T, f32),
        "pick_post_t": jnp.asarray(pick[1].T, f32),
        "place": jnp.asarray(place, bf16),
        "place_f": jnp.asarray(place, f32),
        "diagonal": jnp.asarray(diagonal, f32),
        "eye": jnp.asarray(np.eye(256), bf16),
        "eye_f": jnp.asarray(np.eye(256), f32),
        "deal": jnp.asarray(deal, bf16),
        "deal_t": jnp.asarray(deal.T, bf16),
    }


def whole_block(
    tokens,
    ln1_gain,
    ln1_shift,
    w_qkv,
    w_proj,
    mix_pre,
    mix_post,
    ln2_gain,
    ln2_shift,
    w_up,
    conv_kernel,
    w_down,
    out_grad,
):
    images, seq, width = tokens.shape
    dp, head = lax.axis_size("dp"), lax.axis_size("head")
    local_heads, heads = mix_pre.shape
    size = width // heads
    local = local_heads * size
    share = w_qkv.shape[0]
    ksize, units = conv_kernel.shape[0], conv_kernel.shape[2]
    grid = int(round((seq - 1) ** 0.5))
    padded = -(-seq // 16) * 16
    wide = -(-seq // 128) * 128
    lines = dp // 2
    const = tables(seq, dp, head, heads, grid, ksize, share)
    bins = const["fourier"].shape[0] // 2
    taps = const["lag_back"].shape[0]

    inputs = {
        "tokens": jnp.transpose(tokens, (1, 0, 2)),
        "out_grad": jnp.transpose(out_grad, (1, 0, 2)),
        "ln1_gain": ln1_gain.reshape(1, share),
        "ln1_shift": ln1_shift.reshape(1, share),
        "ln2_gain": ln2_gain.reshape(1, share),
        "ln2_shift": ln2_shift.reshape(1, share),
        "mix_pre": mix_pre,
        "mix_post": mix_post,
        "w_qkv": jnp.transpose(w_qkv, (1, 0, 2)),
        "w_proj": w_proj,
        "w_up": w_up,
        "w_down": w_down.T,
        "taps": conv_kernel,
        **{name: value for name, value in const.items() if name != "deal_t"},
    }
    outputs = {
        "output": ((images, padded, width), bf16),
        "input": ((images, padded, width), bf16),
        "qk": ((share, 384), f32),
        "w_v": ((share, local), f32),
        "w_proj": ((local, share), f32),
        "w_up": ((share, units), f32),
        "w_down": ((share, units), f32),
        "norms": ((8, 128), f32),
        "mixes": ((8, 128), f32),
        "taps": ((taps, units), f32),
    }
    finals = {
        "output": ((seq, images, width), bf16),
        "input": ((seq, images, width), bf16),
        "ln1_gain": ((1, share), f32),
        "ln1_shift": ((1, share), f32),
        "w_qkv": ((3, share, local), f32),
        "w_proj": ((local, share), f32),
        "mix_pre": ((local_heads, heads), f32),
        "mix_post": ((local_heads, heads), f32),
        "ln2_gain": ((1, share), f32),
        "ln2_shift": ((1, share), f32),
        "w_up": ((share, units), f32),
        "taps": ((ksize, ksize, units), f32),
        "w_down": ((share, units), f32),
    }
    one, every = (padded, width), (images, padded, width)
    square = (heads, padded, wide)
    table = (heads * 16, heads * 16)
    scratch = {
        "tok": (every, bf16),
        "og": (every, bf16),
        "raw": ((2, seq, images, width), bf16),
        "edge": ((const["lag"].shape[1], units), f32),
        "wqk": ((head, width, 384), bf16),
        "wv": ((head, width, 256), bf16),
        "wp_two": ((head, width, 128), bf16),
        "wp": ((width, width), bf16),
        "wu": ((width, units), bf16),
        "wd": ((width, units), bf16),
        "gains": ((dp * 8, 128), f32),
        "mixes": ((head, 8, 128), f32),
        "norms": ((8, width), f32),
        "filt": ((2 * bins, units), f32),
        "cross": ((2 * bins, units), f32),
        "wave": ((2 * bins, units), f32),
        "fi": ((2 * bins, units), bf16),
        "gf": ((images, 2 * bins, units), bf16),
        "actg": ((images, padded, units), bf16),
        "act": ((2, padded, units), bf16),
        "n1": (every, bf16),
        "n2": (every, bf16),
        "mid": ((2, *one), f32),
        "hid": ((2 * padded, width), f32),
        "wid": ((images, padded, units), bf16),
        "hg": ((images, padded, units), bf16),
        "np": (every, bf16),
        "np_near": ((2, *one), bf16),
        "np_far": (one, bf16),
        "bp_near": ((2, *one), bf16),
        "bp_far": (one, bf16),
        "flip": ((width, images * padded), bf16),
        "q": (one, bf16),
        "k": ((wide, width), bf16),
        "v": ((wide, width), bf16),
        "third_qk": ((head, padded, 128), f32),
        "third_v": ((head, padded, 128), f32),
        "kron": ((2, 2, *table), bf16),
        "kron_t": ((2, 2, *table), bf16),
        "mix_one": (table, f32),
        "mix_two": (table, f32),
        "sc": (square, bf16),
        "pr": (square, f32),
        "post": (square, bf16),
        "pg": (square, bf16),
        "ho": (every, bf16),
        "ag": (every, bf16),
        "hgr": (one, bf16),
        "hgr_t": ((width, padded), bf16),
        "q_t": ((width, padded), bf16),
        "dv_t": ((width, wide), bf16),
        "dk_t": ((width, wide), bf16),
        "dv": (one, bf16),
        "turn": ((head, padded, 384), bf16),
        "turned": ((head, padded, 384), bf16),
        "turn_v": ((head, padded, 256), bf16),
        "turned_v": ((head, padded, 256), bf16),
        "og_t": ((width, images * padded), bf16),
        "sums": ((8, width), f32),
        "small": ((5, 8, width + head * 128), f32),
        "small_in": ((5, 8, width + head * 128), f32),
        "taps": ((3, taps, units), bf16),
        "taps_in": ((3, taps, units), bf16),
    }
    for name, columns in (("up", units), ("down", units), ("qk", 384), ("pv", 256), ("v", 128)):
        scratch["g_" + name] = ((width, columns), bf16)
        scratch[name + "_y"] = ((lines, share, columns), bf16)
        scratch[name + "_z"] = ((lines - 1, share, columns), bf16)
    sems = {"mi": 3, "ho": 3, "ag": 3, "ou": 3, "in": 3, "np": 3, "bp": 3}
    sems |= {"tv": head - 1, "tu": head - 1, "ta": 3, "sm": 5}
    for name in "gqvpurd":
        sems |= {name + "z": 2 * (lines - 1), name + "y": lines}
    for name in "qvpud":
        sems |= {name + "y2": lines, name + "z2": lines - 1}
    for name in "qvp":
        sems |= {name + "x": dp, name + "m": 2 * dp}
    shapes = {name: pltpu.VMEM(*spec) for name, spec in scratch.items()}
    for name, number in sems.items():
        shapes[name + "_s"] = pltpu.SemaphoreType.DMA((number,))
        shapes[name + "_r"] = pltpu.SemaphoreType.DMA((number,))
    shapes["loads"] = pltpu.SemaphoreType.DMA((4,))
    vmem = pl.BlockSpec(memory_space=pltpu.VMEM)
    left = pl.BlockSpec(memory_space=pl.ANY)
    results = pl.pallas_call(
        functools.partial(
            block_kernel,
            (seq, dp, head, size ** (-0.5)),
            tuple(inputs),
            tuple(outputs),
            tuple(shapes),
        ),
        out_shape=[jax.ShapeDtypeStruct(*spec) for spec in outputs.values()],
        in_specs=[left if n in ("tokens", "out_grad", "w_up", "w_down") else vmem for n in inputs],
        out_specs=[left if n in ("output", "input") else vmem for n in outputs],
        scratch_shapes=list(shapes.values()),
        compiler_params=pltpu.CompilerParams(
            collective_id=0, has_side_effects=True, vmem_limit_bytes=64 * 2**20
        ),
    )(*inputs.values())
    r = dict(zip(outputs, results))

    def kept(shape):
        return pl.BlockSpec(shape, lambda j: (0,) * len(shape))

    parts = [*r.values(), const["deal_t"]]
    step = -(-padded // (32)) * 16
    by_rows = pl.BlockSpec((images, step, width), lambda j: (0, j, 0))
    by_tokens = pl.BlockSpec((step, images, width), lambda j: (j, 0, 0))
    results = pl.pallas_call(
        functools.partial(finish_kernel, (local_heads, heads, share)),
        grid=(-(-padded // step),),
        out_shape=[jax.ShapeDtypeStruct(*spec) for spec in finals.values()],
        in_specs=[by_rows] * 2 + [kept(part.shape) for part in parts[2:]],
        out_specs=[by_tokens] * 2 + [kept(spec[0]) for spec in list(finals.values())[2:]],
    )(*parts)
    r = dict(zip(finals, results))
    for name in ("output", "input", "w_qkv"):
        r[name] = jnp.transpose(r[name], (1, 0, 2))
    for name in ("ln1_gain", "ln1_shift", "ln2_gain", "ln2_shift"):
        r[name] = r[name].reshape(share)
    r["w_down"] = r["w_down"].T
    return tuple(r.values())


def solution(mesh):
    in_specs = (
        P("dp", None, None),
        P("dp"),
        P("dp"),
        P("dp", None, "head"),
        P("head", "dp"),
        P("head", None),
        P("head", None),
        P("dp"),
        P("dp"),
        P("dp", "head"),
        P(None, None, "head"),
        P("head", "dp"),
        P("dp", None, None),
    )
    out_specs = (
        P("dp", None, None),
        P("dp", None, None),
        P("dp"),
        P("dp"),
        P("dp", None, "head"),
        P("head", "dp"),
        P("head", None),
        P("head", None),
        P("dp"),
        P("dp"),
        P("dp", "head"),
        P(None, None, "head"),
        P("head", "dp"),
    )
    dp, head = mesh.shape["dp"], mesh.shape["head"]

    def shards(*args):
        tokens, w_qkv, mix_pre = args[0], args[3], args[5]
        fits = head == 4 and dp == 8 and w_qkv.shape[0] % 32 == 0 and w_qkv.shape[0] <= 128
        fits = fits and tokens.shape[0] == head
        fits = fits and mix_pre.shape[0] == 3 and tokens.shape[2] == 64 * mix_pre.shape[1]
        return (whole_block if fits else plain)(*args)

    return jax.shard_map(shards, mesh=mesh, in_specs=in_specs, out_specs=out_specs, check_vma=False)
```

```python
import functools
import types

import jax
import jax.numpy as jnp
import numpy as np
from jax import lax
from jax.experimental import pallas as pl
from jax.experimental.pallas import tpu as pltpu
from jax.sharding import PartitionSpec as P

highest = lax.Precision.HIGHEST
epsilon = 1e-06
bf16 = jnp.bfloat16
f32 = jnp.float32


def spectrum(grid, ksize):
    margin = ksize // 2
    period = grid + margin
    pairs = [(0, 0)] + [(0, v) for v in range(1, period // 2 + 1)]
    pairs += [(u, v) for u in range(1, period // 2 + 1) for v in range(period)]
    freq = np.array(pairs, np.float64)
    place = np.array([(r, c) for r in range(grid) for c in range(grid)], np.float64)
    lags = np.array([(p - margin, q - margin) for p in range(ksize) for q in range(ksize)], np.float64)
    weight = np.sqrt(np.where(np.arange(len(pairs)) == 0, 1.0, 2.0)) / period
    angle = 2 * np.pi / period * freq @ place.T
    angle_lag = 2 * np.pi / period * freq @ lags.T
    count = len(pairs)
    cos = np.zeros((count + 1, grid * grid + 1))
    sin = np.zeros_like(cos)
    cos[:count, 1:] = weight[:, None] * np.cos(angle)
    sin[:count, 1:] = weight[:, None] * np.sin(angle)
    cos[count, 0] = 1.0
    cos_lag = np.zeros((count + 1, ksize * ksize))
    sin_lag = np.zeros_like(cos_lag)
    cos_lag[:count] = np.cos(angle_lag)
    sin_lag[:count] = np.sin(angle_lag)
    back = np.zeros(count + 1)
    back[:count] = 1.0
    return cos, sin, cos_lag, sin_lag, back


def layer_norm(values, gain, shift):
    center = jnp.mean(values, axis=-1, keepdims=True)
    centered = values - center
    spread = jnp.mean(centered * centered, axis=-1, keepdims=True)
    rs = lax.rsqrt(spread + epsilon)
    xhat = centered * rs
    return xhat * gain + shift, xhat, rs


def norm_back(grad, gain, xhat, rs):
    e = grad * gain
    inner = rs * (
        e
        - jnp.mean(e, axis=-1, keepdims=True)
        - xhat * jnp.mean(e * xhat, axis=-1, keepdims=True)
    )
    return inner, jnp.sum(grad * xhat, axis=(0, 1)), jnp.sum(grad, axis=(0, 1))


def dot(spec, a, b):
    return jnp.einsum(spec, a, b, preferred_element_type=f32)


def plain(
    tokens,
    ln1_gain,
    ln1_shift,
    w_qkv,
    w_proj,
    mix_pre,
    mix_post,
    ln2_gain,
    ln2_shift,
    w_up,
    conv_kernel,
    w_down,
    out_grad,
):
    images, seq, width = tokens.shape
    heads_local, heads = mix_pre.shape
    size = width // heads
    scale = size ** (-0.5)
    ksize = conv_kernel.shape[0]
    units = conv_kernel.shape[2]
    grid = int(round((seq - 1) ** 0.5))
    cos, sin, cos_lag, sin_lag, back = spectrum(grid, ksize)
    fourier = jnp.asarray(np.stack([cos, sin]), bf16)
    lagged = jnp.asarray(np.stack([cos_lag, sin_lag]), f32)
    lagged_back = jnp.asarray(np.stack([cos_lag, sin_lag]) * back[:, None], f32)
    mine = lax.axis_index("head")

    gains = jnp.stack([ln1_gain, ln1_shift, ln2_gain, ln2_shift])
    gains = lax.all_gather(gains, "dp", axis=1, tiled=True).astype(f32)
    gain_one, shift_one, gain_two, shift_two = gains[0], gains[1], gains[2], gains[3]
    qkv_w = lax.all_gather(w_qkv, "dp", axis=0, tiled=True)
    up_w = lax.all_gather(w_up, "dp", axis=0, tiled=True)
    down_w = lax.all_gather(w_down, "dp", axis=1, tiled=True)
    proj_w = lax.all_gather(w_proj, "head", axis=0, tiled=True)
    proj_w = lax.all_gather(proj_w, "dp", axis=1, tiled=True)
    mixes = lax.all_gather(jnp.stack([mix_pre, mix_post]), "head", axis=1, tiled=True)
    pre, post_mix = mixes[0], mixes[1]

    source = tokens.astype(f32)
    normed_one, xhat_one, rs_one = layer_norm(source, gain_one, shift_one)
    normed_one = normed_one.astype(bf16)
    qkv = dot("ind,dce->ince", normed_one, qkv_w).astype(bf16)
    qkv = lax.all_to_all(qkv, "head", split_axis=0, concat_axis=3, tiled=True)
    own = qkv.shape[0]
    query = qkv[:, :, 0].reshape(own, seq, heads, size)
    keys = qkv[:, :, 1].reshape(own, seq, heads, size)
    values = qkv[:, :, 2].reshape(own, seq, heads, size)
    scores = (dot("inhd,imhd->ihnm", query, keys) * scale).astype(bf16)
    mixed = jnp.einsum("hg,ignm->ihnm", pre, scores.astype(f32), precision=highest)
    probs = jax.nn.softmax(mixed, axis=-1)
    probs_low = probs.astype(bf16)
    post = jnp.einsum(
        "hg,ignm->ihnm", post_mix, probs_low.astype(f32), precision=highest
    ).astype(bf16)
    heads_own = dot("ihnm,imhd->inhd", post, values).reshape(own, seq, width).astype(bf16)
    heads_out = lax.all_gather(heads_own, "head", axis=0, tiled=True)
    middle = source + dot("ine,ed->ind", heads_out, proj_w)
    normed_two, xhat_two, rs_two = layer_norm(middle, gain_two, shift_two)
    normed_two = normed_two.astype(bf16)
    hidden = dot("ind,df->inf", normed_two, up_w)
    erf = lax.erf(hidden * (0.5**0.5))
    activ = 0.5 * hidden * (1.0 + erf)
    slope = 0.5 * (1.0 + erf) + hidden * jnp.exp(-0.5 * hidden * hidden) * 0.3989422804014327
    delta = np.zeros((ksize * ksize, 1), np.float32)
    delta[ksize * ksize // 2] = 1.0
    taps = conv_kernel.reshape(ksize * ksize, units)
    filters = jnp.einsum("zkl,lf->zkf", lagged, taps, precision=highest)
    cos_k, sin_k = filters[0] + 1.0, filters[1]
    wave = dot("zkn,inf->zikf", fourier, activ.astype(bf16))
    cos_a, sin_a = wave[0], wave[1]
    filtered = jnp.stack([cos_k * cos_a + sin_k * sin_a, cos_k * sin_a - sin_k * cos_a])
    widened = dot("zkn,zikf->inf", fourier, filtered.astype(bf16)).astype(bf16)
    branch = dot("inf,fd->ind", widened, down_w)
    branch = lax.psum(branch.astype(bf16), "head").astype(f32)
    output = (middle + branch).astype(bf16)

    down_grad = dot("inf,ind->fd", widened, out_grad)
    widened_grad = dot("ind,fd->inf", out_grad, down_w)
    wave_grad = dot("zkn,inf->zikf", fourier, widened_grad.astype(bf16))
    cos_g, sin_g = wave_grad[0], wave_grad[1]
    spread_grad = jnp.stack([cos_k * cos_g - sin_k * sin_g, cos_k * sin_g + sin_k * cos_g])
    activ_grad = dot("zkn,zikf->inf", fourier, spread_grad.astype(bf16))
    hidden_grad = (activ_grad * slope).astype(bf16)
    cross = jnp.stack(
        [
            jnp.sum(cos_a * cos_g + sin_a * sin_g, axis=0),
            jnp.sum(sin_a * cos_g - cos_a * sin_g, axis=0),
        ]
    )
    kernel_grad = jnp.einsum("zkl,zkf->lf", lagged_back, cross, precision=highest)
    up_grad = dot("ind,inf->df", normed_two, hidden_grad)
    two_grad = dot("inf,df->ind", hidden_grad, up_w).astype(bf16)
    two_grad = lax.psum_scatter(two_grad, "head", scatter_dimension=0, tiled=True).astype(f32)

    def pick(array):
        return lax.dynamic_slice_in_dim(array, mine * own, own, 0)

    middle_from, gain_two_grad, shift_two_grad = norm_back(
        two_grad, gain_two, pick(xhat_two), pick(rs_two)
    )
    middle_grad = pick(out_grad).astype(f32) + middle_from
    attention_own = middle_grad.astype(bf16)
    attention_grad = lax.all_gather(attention_own, "head", axis=0, tiled=True)
    local = width // lax.axis_size("head")
    heads_mine = lax.dynamic_slice_in_dim(heads_out, mine * local, local, 2)
    proj_grad = dot("ine,ind->ed", heads_mine, attention_grad)
    heads_grad = dot("ind,ed->ine", attention_own, proj_w).astype(bf16)
    heads_grad = heads_grad.reshape(own, seq, heads, size)
    values_grad = dot("ihnm,inhd->imhd", post, heads_grad)
    post_grad = dot("inhd,imhd->ihnm", heads_grad, values)
    probs_grad = jnp.einsum("hg,ihnm->ignm", post_mix, post_grad, precision=highest)
    mixed_grad = probs * (probs_grad - jnp.sum(probs_grad * probs, axis=-1, keepdims=True))
    scores_grad = jnp.einsum("hg,ihnm->ignm", pre, mixed_grad, precision=highest).astype(bf16)
    post_mix_grad = dot("ihnm,ignm->hg", post_grad.astype(bf16), probs_low)
    pre_mix_grad = dot("ihnm,ignm->hg", mixed_grad.astype(bf16), scores)
    query_grad = dot("ihnm,imhd->inhd", scores_grad, keys) * scale
    keys_grad = dot("ihnm,inhd->imhd", scores_grad, query) * scale
    qkv_grad = jnp.stack([query_grad, keys_grad, values_grad], axis=2)
    qkv_grad = qkv_grad.reshape(own, seq, 3, width).astype(bf16)
    qkv_grad = lax.all_to_all(qkv_grad, "head", split_axis=3, concat_axis=0, tiled=True)
    qkv_weight_grad = dot("ind,ince->dce", normed_one, qkv_grad)
    one_grad = dot("ince,dce->ind", qkv_grad, qkv_w).astype(bf16)
    one_grad = lax.psum_scatter(one_grad, "head", scatter_dimension=0, tiled=True).astype(f32)
    source_grad, gain_one_grad, shift_one_grad = norm_back(
        one_grad, gain_one, pick(xhat_one), pick(rs_one)
    )
    input_own = (middle_grad + source_grad).astype(bf16)
    input_grad = lax.all_gather(input_own, "head", axis=0, tiled=True)

    def share(grad, axis):
        return lax.psum_scatter(
            grad.astype(bf16), "dp", scatter_dimension=axis, tiled=True
        ).astype(f32)

    norm_grads = jnp.stack([gain_one_grad, shift_one_grad, gain_two_grad, shift_two_grad])
    norm_grads = lax.psum(norm_grads, "head")
    norm_grads = lax.psum_scatter(norm_grads, "dp", scatter_dimension=1, tiled=True)
    mix_grads = lax.psum_scatter(
        jnp.stack([pre_mix_grad, post_mix_grad]), "head", scatter_dimension=1, tiled=True
    )
    mix_grads, kernel_grad = lax.psum((mix_grads, kernel_grad), "dp")
    return (
        output,
        input_grad,
        norm_grads[0],
        norm_grads[1],
        share(qkv_weight_grad, 0),
        share(proj_grad, 1),
        mix_grads[0],
        mix_grads[1],
        norm_grads[2],
        norm_grads[3],
        share(up_grad, 0),
        kernel_grad.reshape(ksize, ksize, units),
        share(down_grad, 1),
    )


MESH = pl.DeviceIdType.MESH
NT = (((1,), (1,)), ((), ()))


def mm(a, b):
    return jnp.dot(a, b, preferred_element_type=f32)


def mm_nt(a, b):
    return lax.dot_general(a, b, NT, preferred_element_type=f32)


def exact(a, b):
    return jnp.dot(a, b, preferred_element_type=f32, precision=highest)


def split(a):
    high = a.astype(bf16)
    return high, (a - high.astype(f32)).astype(bf16)


def remote(src, dst, send, recv, device):
    return pltpu.make_async_remote_copy(
        src_ref=src,
        dst_ref=dst,
        send_sem=send,
        recv_sem=recv,
        device_id=device,
        device_id_type=MESH,
    )


class Place:
    def __init__(self, dp, head):
        self.dp, self.head = dp, head
        self.lines = dp // 2
        self.d, self.s = lax.axis_index("dp"), lax.axis_index("head")
        self.z, self.y = self.d // 2, self.d % 2
        self.x, self.c = self.s // 2, self.s % 2
        self.mate = self.x * 2 + 1 - self.c
        self.across = (1 - self.x) * 2 + self.c
        self.corner = (1 - self.x) * 2 + 1 - self.c

    def near(self, j):
        return ((self.x + j // 2) % 2) * 2 + (self.c + j % 2) % 2

    def z_next(self, k):
        return (self.z + k) % self.lines

    def z_prev(self, k):
        return (self.z + self.lines - k) % self.lines

    def head_next(self, k):
        return (self.s + k) % self.head

    def dp_next(self, k):
        return (self.d + k) % self.dp

    def call(self):
        barrier = pltpu.get_barrier_semaphore()

        def tell(d, s):
            pl.semaphore_signal(barrier, inc=1, device_id=(d, s), device_id_type=MESH)

        tell(self.d, self.mate)
        tell(self.d, self.across)
        tell(self.z * 2 + 1 - self.y, self.s)
        pl.when(self.z > 0)(lambda: tell((self.z - 1) * 2 + self.y, self.s))
        pl.when(self.z < self.lines - 1)(lambda: tell((self.z + 1) * 2 + self.y, self.s))

    def answer(self):
        inner = (self.z > 0) & (self.z < self.lines - 1)
        pl.semaphore_wait(pltpu.get_barrier_semaphore(), jnp.where(inner, 5, 4))


def rows_of(ref, index, count):
    return ref.at[pl.ds(pl.multiple_of(index * count, count), count)]


class Line:
    def __init__(self, at, buf, sems, wide):
        self.at, self.wide = at, wide
        self.groups = buf
        self.buf = buf.at[at.s] if wide else buf
        self.rows = self.buf.shape[0] // at.dp
        self.sems = sems

    def near(self, hops, body):
        at = self.at
        if hops == 0:
            body(at.z)
        else:
            pl.when(at.z >= hops)(lambda: body(at.z - hops))
            pl.when(at.z + hops < at.lines)(lambda: body(at.z + hops))

    def index(self, z, other):
        return z * 2 + (1 - self.at.y if other else self.at.y)

    def block(self, z, other, buf=None):
        return rows_of(self.buf if buf is None else buf, self.index(z, other), self.rows)

    def z_copy(self, up, hops):
        at, (send, recv) = self.at, self.sems[0]
        ref = self.block(at.z - hops if up else at.z + hops, False)
        slot = hops if up else at.lines - 1 + hops
        to = at.z + 1 if up else at.z - 1
        return remote(ref, ref, send.at[slot], recv.at[slot], (to * 2 + at.y, at.s))

    def pass_on(self, up, hops):
        at = self.at
        if up:
            there = (at.z >= hops) & (at.z < at.lines - 1)
        else:
            there = (at.z + hops < at.lines) & (at.z > 0)
        return pl.when(there)

    def y_copy(self, z):
        at, (send, recv) = self.at, self.sems[1]
        ref = self.block(z, False)
        return remote(ref, ref, send.at[z], recv.at[z], (at.z * 2 + 1 - at.y, at.s))

    def x_copy(self, z, other):
        at, (send, recv) = self.at, self.sems[2]
        ref, slot = self.block(z, other), self.index(z, other)
        return remote(ref, ref, send.at[slot], recv.at[slot], (at.d, at.across))

    def mate_copy(self, z, other, far):
        at, (send, recv) = self.at, self.sems[3]
        ref = self.block(z, other, self.groups.at[at.across if far else at.s])
        slot = self.index(z, other) + (at.dp if far else 0)
        return remote(ref, ref, send.at[slot], recv.at[slot], (at.d, at.mate))

    def begin(self):
        for up in (True, False):
            self.pass_on(up, 0)(lambda: self.z_copy(up, 0).start())

    def over_y(self):
        self.y_copy(self.at.z).start()

    def from_z(self, hops):
        at = self.at
        for up in (True, False):

            @pl.when(at.z >= hops if up else at.z + hops < at.lines)
            def _():
                source = at.z - hops if up else at.z + hops
                self.z_copy(up, hops - 1).wait_recv()
                if hops < at.lines - 1:
                    self.pass_on(up, hops)(lambda: self.z_copy(up, hops).start())
                self.y_copy(source).start()

    def on(self, hops, other):
        def body(z):
            self.x_copy(z, other).start()
            self.mate_copy(z, other, False).start()

        self.near(hops, body)

    def from_y(self, hops):
        self.near(hops, lambda z: self.y_copy(z).wait_recv())

    def from_x(self, hops, other):
        def body(z):
            self.x_copy(z, other).wait_recv()
            self.mate_copy(z, other, True).start()

        self.near(hops, body)

    def from_mate(self, far):
        for z in range(self.at.lines):
            for other in (False, True):
                self.mate_copy(z, other, far).wait_recv()

    def drain(self):
        at = self.at
        for hops in range(at.lines - 1):
            for up in (True, False):
                self.pass_on(up, hops)(lambda: self.z_copy(up, hops).wait_send())
        for z in range(at.lines):
            self.y_copy(z).wait_send()
            if self.wide:
                for other in (False, True):
                    self.x_copy(z, other).wait_send()
                    self.mate_copy(z, other, False).wait_send()
                    self.mate_copy(z, other, True).wait_send()


class Rows(Line):
    def both(self, z):
        return rows_of(self.buf, z, 2 * self.rows)

    def z_copy(self, up, hops):
        at, (send, recv) = self.at, self.sems[0]
        ref = self.both(at.z - hops if up else at.z + hops)
        slot = hops if up else at.lines - 1 + hops
        to = at.z + 1 if up else at.z - 1
        return remote(ref, ref, send.at[slot], recv.at[slot], (to * 2 + at.y, at.s))

    def from_y(self):
        self.y_copy(self.at.z).wait_recv()
        self.begin()

    def from_z(self, hops):
        at = self.at
        for up in (True, False):

            @pl.when(at.z >= hops if up else at.z + hops < at.lines)
            def _():
                self.z_copy(up, hops - 1).wait_recv()
                if hops < at.lines - 1:
                    self.pass_on(up, hops)(lambda: self.z_copy(up, hops).start())

    def drain(self):
        at = self.at
        self.y_copy(at.z).wait_send()
        for hops in range(at.lines - 1):
            for up in (True, False):
                self.pass_on(up, hops)(lambda: self.z_copy(up, hops).wait_send())


class Share:
    def __init__(self, at, buf, sems):
        self.at, self.buf = at, buf
        self.send, self.recv = sems

    def copy(self, which):
        at = self.at
        ref = self.buf.at[at.across if which == 2 else at.s]
        to = at.across if which == 1 else at.mate
        return remote(ref, ref, self.send.at[which], self.recv.at[which], (at.d, to))

    def start(self):
        self.copy(1).start()
        self.copy(0).start()

    def wait_mate(self):
        self.copy(0).wait_recv()

    def forward(self):
        self.copy(1).wait_recv()
        self.copy(2).start()

    def wait_corner(self):
        self.copy(2).wait_recv()

    def drain(self):
        for which in range(3):
            self.copy(which).wait_send()


class Fold:
    def __init__(self, at, parts, near, far, sems):
        self.at, self.parts, self.near, self.far = at, parts, near, far
        self.send, self.recv = sems

    def mate_copy(self, which):
        at = self.at
        src = self.parts.at[at.corner if which else at.mate]
        return remote(
            src, self.near.at[which], self.send.at[which], self.recv.at[which], (at.d, at.mate)
        )

    def x_copy(self):
        at = self.at
        return remote(
            self.parts.at[at.across], self.far, self.send.at[2], self.recv.at[2], (at.d, at.across)
        )

    def middle(self):
        at = self.at
        self.mate_copy(1).wait_recv()
        self.parts[at.across] = (
            self.parts[at.across].astype(f32) + self.near[1].astype(f32)
        ).astype(bf16)
        self.x_copy().start()

    def wait(self):
        self.mate_copy(0).wait_recv()
        self.x_copy().wait_recv()

    def total(self, rows):
        return (
            self.parts[self.at.s, rows, :].astype(f32)
            + self.near[0, rows, :].astype(f32)
            + self.far[rows, :].astype(f32)
        )

    def drain(self):
        self.mate_copy(0).wait_send()
        self.mate_copy(1).wait_send()
        self.x_copy().wait_send()


class Scatter:
    def __init__(self, at, src, from_y, from_z, sems):
        self.at, self.src, self.from_y, self.from_z = at, src, from_y, from_z
        (self.y_send, self.y_recv), (self.z_send, self.z_recv) = sems
        self.rows = src.shape[0] // at.dp

    def block(self, z, y):
        return rows_of(self.src, z * 2 + y, self.rows)

    def y_copy(self, k):
        at = self.at
        return remote(
            self.block(at.z_next(k), 1 - at.y),
            self.from_y.at[k],
            self.y_send.at[k],
            self.y_recv.at[k],
            (at.z * 2 + 1 - at.y, at.s),
        )

    def z_copy(self, k):
        at = self.at
        return remote(
            self.block(at.z_next(k), at.y),
            self.from_z.at[k - 1],
            self.z_send.at[k - 1],
            self.z_recv.at[k - 1],
            (at.z_next(k) * 2 + at.y, at.s),
        )

    def start(self):
        for k in (*range(1, self.at.lines), 0):
            self.y_copy(k).start()

    def middle(self, k):
        at = self.at
        self.y_copy(k).wait_recv()
        ref = self.block(at.z_next(k), at.y)
        ref[...] = (ref[...].astype(f32) + self.from_y[k].astype(f32)).astype(bf16)
        self.z_copy(k).start()

    def finish(self):
        at = self.at
        self.y_copy(0).wait_recv()
        total = self.block(at.z, at.y)[...].astype(f32) + self.from_y[0].astype(f32)
        for k in range(1, at.lines):
            self.z_copy(k).wait_recv()
            total = total + self.from_z[k - 1].astype(f32)
        return total

    def drain(self):
        for k in range(self.at.lines):
            self.y_copy(k).wait_send()
        for k in range(1, self.at.lines):
            self.z_copy(k).wait_send()


class Halves(Scatter):
    def partner(self, k):
        z = self.at.z
        return (3 - z, z + 1 - 2 * (z % 2), (z + 2) % 4, z)[k]

    def y_copy(self, k):
        at = self.at
        return remote(
            self.block(self.partner(k), 1 - at.y),
            self.from_y.at[k],
            self.y_send.at[k],
            self.y_recv.at[k],
            (at.z * 2 + 1 - at.y, at.s),
        )

    def z_copy(self, k):
        at = self.at
        return remote(
            self.block(self.partner(k), at.y),
            self.from_z.at[k],
            self.z_send.at[k],
            self.z_recv.at[k],
            (self.partner(max(k, 1)) * 2 + at.y, at.s),
        )

    def start(self):
        for k in range(4):
            self.y_copy(k).start()

    def middle(self, k):
        at, k = self.at, k - 1
        self.y_copy(k).wait_recv()
        ref = self.block(self.partner(k), at.y)
        total = ref[...].astype(f32) + self.from_y[k].astype(f32)
        if k == 2:
            self.z_copy(0).wait_recv()
            total = total + self.from_z[0].astype(f32)
        ref[...] = total.astype(bf16)
        self.z_copy(k).start()

    def finish(self):
        at = self.at
        self.y_copy(3).wait_recv()
        total = self.block(at.z, at.y)[...].astype(f32) + self.from_y[3].astype(f32)
        for k in (1, 2):
            self.z_copy(k).wait_recv()
            total = total + self.from_z[k].astype(f32)
        return total

    def drain(self):
        for k in range(4):
            self.y_copy(k).wait_send()
        for k in range(3):
            self.z_copy(k).wait_send()


class Exchange:
    def __init__(self, at, axis, slots, sems, block_for):
        self.at, self.axis, self.slots, self.block_for = at, axis, slots, block_for
        self.send, self.recv = sems
        self.count = at.dp if axis == "dp" else at.head
        self.me = at.d if axis == "dp" else at.s

    def copy(self, k):
        at = self.at
        peer = (self.me + k) % self.count
        device = (peer, at.s) if self.axis == "dp" else (at.d, peer)
        return remote(
            self.block_for(peer),
            self.slots.at[self.me],
            self.send.at[k - 1],
            self.recv.at[k - 1],
            device,
        )

    def start(self):
        for k in range(1, self.count):
            self.copy(k).start()

    def wait(self):
        for k in range(1, self.count):
            self.copy(k).wait_recv()

    def drain(self):
        for k in range(1, self.count):
            self.copy(k).wait_send()

    def total(self):
        total = self.slots[0]
        for k in range(1, self.count):
            total = total + self.slots[k]
        return total


class Doubling:
    def __init__(self, at, held, slots, sems, partners):
        self.at, self.held, self.slots, self.partners = at, held, slots, partners
        self.send, self.recv = sems

    def copy(self, k):
        return remote(
            self.held.at[k], self.slots.at[k], self.send.at[k], self.recv.at[k], self.partners[k]
        )

    def start(self):
        self.copy(0).start()

    def step(self, k):
        self.copy(k).wait_recv()
        total = self.held[k].astype(f32) + self.slots[k].astype(f32)
        if k + 1 == len(self.partners):
            return total
        self.held[k + 1] = total.astype(self.held.dtype)
        self.copy(k + 1).start()

    def drain(self):
        for k in range(len(self.partners)):
            self.copy(k).wait_send()


def norm_rows(x):
    center = jnp.mean(x, axis=-1, keepdims=True)
    centered = x - center
    spread = jnp.mean(centered * centered, axis=-1, keepdims=True)
    rs = lax.rsqrt(spread + epsilon)
    return centered * rs, rs


def norm_back_rows(grad, gain, xhat, rs):
    e = grad * gain
    return rs * (
        e
        - jnp.mean(e, axis=-1, keepdims=True)
        - xhat * jnp.mean(e * xhat, axis=-1, keepdims=True)
    )


def fold_rows(a):
    return jnp.sum(a.reshape(a.shape[0] // 8, 8, a.shape[1]), axis=0)


def block_kernel(sizes, names_in, names_out, names_scratch, *refs):
    seq, dp, head, scale = sizes
    n_in, n_out = len(names_in), len(names_out)
    i = types.SimpleNamespace(**dict(zip(names_in, refs[:n_in])))
    o = types.SimpleNamespace(**dict(zip(names_out, refs[n_in : n_in + n_out])))
    b = types.SimpleNamespace(**dict(zip(names_scratch, refs[n_in + n_out :])))
    at = Place(dp, head)
    images, padded, width = b.tok.shape
    b.bp, b.dq = b.actg, b.act.at[0]
    b.dk, b.mg = b.fi.at[:padded], b.wave.at[:padded]
    b.inp, b.out = b.n1, b.n2
    hops = range(1, at.lines)
    share = i.w_up.shape[0]
    own_rows = pl.ds(pl.multiple_of(at.d * share, share), share)
    loads = [
        pltpu.make_async_copy(src, dst, b.loads.at[n])
        for n, (src, dst) in enumerate(
            (
                (i.w_down, b.wd.at[own_rows]),
                (i.w_up, b.wu.at[own_rows]),
                (i.tokens, b.raw.at[0]),
                (i.out_grad, b.raw.at[1]),
            )
        )
    ]
    chunks = padded // 16
    wide = b.k.shape[0]
    slots = b.sc.shape[0]
    pairs = slots // 2
    units = b.wu.shape[1]
    bins = b.filt.shape[0] // 2

    def span(j, size):
        return pl.ds(j * size if isinstance(j, int) else pl.multiple_of(j * size, size), size)

    def chunk(j):
        return span(j, 16)

    def tile(p):
        return span(p, 128)

    def twice(body):
        def step(k, carry):
            body(1 - k)
            return carry

        lax.fori_loop(0, 2, step, 0)

    def each(steps, body):
        for j in range(steps) if isinstance(steps, int) else steps:
            body(j)

    def flip_block(a):
        return mm_nt(i.eye[: a.shape[1], : a.shape[1]], a)

    def halves(low, high):
        return (mm(low, i.eye[:64, :128]) + mm(high, i.eye[64:128, :128])).astype(bf16)

    at.call()
    for load in loads:
        load.start()
    w_q, w_k, w_v = i.w_qkv[0], i.w_qkv[1], i.w_qkv[2]
    b.wqk[at.s, own_rows, 0:128] = w_q[:, :128]
    b.wqk[at.s, own_rows, 128:256] = w_k[:, :128]
    b.wqk[at.s, own_rows, 256:384] = halves(w_q[:, 128:], w_k[:, 128:])
    own_gains, own_mixes = rows_of(b.gains, at.d, 8), b.mixes.at[at.s]
    own_gains[...] = jnp.zeros((8, 128), f32)
    own_mixes[...] = jnp.zeros((8, 128), f32)
    for r, gain in enumerate((i.ln1_gain, i.ln1_shift, i.ln2_gain, i.ln2_shift)):
        own_gains[r : r + 1, :share] = gain[...].astype(f32)
    local_heads, heads = i.mix_pre.shape
    own_mixes[:local_heads, :heads] = i.mix_pre[...]
    own_mixes[4 : 4 + local_heads, :heads] = i.mix_post[...]
    p_t = flip_block(i.w_proj[...]).astype(bf16)
    b.wv[at.s, own_rows, 0:128] = w_v[:, :128]
    b.wv[at.s, own_rows, 128:256] = halves(w_v[:, 128:], p_t[:, 128:])
    b.wp_two[at.s, own_rows, :] = p_t[:, :128]

    at.answer()
    loads[0].wait()
    loads[1].wait()

    def line(kind, buf, name, wide):
        sems = [(getattr(b, name + part + "_s"), getattr(b, name + part + "_r")) for part in ("zyxm" if wide else "zy")]
        return kind(at, buf, sems, wide)

    gains = line(Line, b.gains, "g", False)
    mixes = Share(at, b.mixes, (b.mi_s, b.mi_r))
    gq = line(Line, b.wqk, "q", True)
    gv = line(Line, b.wv, "v", True)
    gp = line(Line, b.wp_two, "p", True)
    cut = units // 3 * 2
    gu = line(Line, b.wu.at[:, :cut], "u", False)
    gr = line(Rows, b.wu.at[:, cut:], "r", False)
    gd = line(Line, b.wd, "d", False)
    ho = Share(at, b.ho, (b.ho_s, b.ho_r))
    ag = Share(at, b.ag, (b.ag_s, b.ag_r))
    out = Share(at, b.out, (b.ou_s, b.ou_r))
    inp = Share(at, b.inp, (b.in_s, b.in_r))
    fold_two = Fold(at, b.np, b.np_near, b.np_far, (b.np_s, b.np_r))
    fold_out = Fold(at, b.bp, b.bp_near, b.bp_far, (b.bp_s, b.bp_r))
    sc_up = Halves(at, b.g_up, b.up_y, b.up_z, ((b.uy2_s, b.uy2_r), (b.uz2_s, b.uz2_r)))
    sc_down = Halves(at, b.g_down, b.down_y, b.down_z, ((b.dy2_s, b.dy2_r), (b.dz2_s, b.dz2_r)))
    sc_qk = Scatter(at, b.g_qk, b.qk_y, b.qk_z, ((b.qy2_s, b.qy2_r), (b.qz2_s, b.qz2_r)))
    sc_pv = Scatter(at, b.g_pv, b.pv_y, b.pv_z, ((b.py2_s, b.py2_r), (b.pz2_s, b.pz2_r)))
    sc_v = Scatter(at, b.g_v, b.v_y, b.v_z, ((b.vy2_s, b.vy2_r), (b.vz2_s, b.vz2_r)))
    turn_v = Exchange(at, "head", b.turned_v, (b.tv_s, b.tv_r), lambda s: b.turn_v.at[s, :, pl.ds(0, 128)])
    turn_w = Exchange(at, "head", b.turned_w, (b.tw_s, b.tw_r), lambda s: b.turn_w.at[s])
    turn = Exchange(at, "head", b.turned, (b.tu_s, b.tu_r), lambda s: b.turn.at[s])
    over_dp = (
        ((at.z + 1 - 2 * (at.z % 2)) * 2 + at.y, at.s),
        ((at.z + 2) % 4 * 2 + at.y, at.s),
        (at.z * 2 + 1 - at.y, at.s),
    )
    taps = Doubling(at, b.taps, b.taps_in, (b.ta_s, b.ta_r), over_dp)
    small = Doubling(
        at, b.small, b.small_in, (b.sm_s, b.sm_r), ((at.d, at.across), (at.d, at.mate), *over_dp)
    )

    passed = ((0, False), (1, False), (0, True), (2, False), (1, True), (3, False), (2, True), (3, True))
    gq.begin()
    gq.over_y()
    gq.on(0, False)
    gains.begin()
    gains.over_y()
    mixes.start()
    gv.begin()
    gv.over_y()
    gv.on(0, False)
    gp.begin()
    gp.over_y()
    gp.on(0, False)
    gr.over_y()

    def norm_one(image):
        def body(j):
            xhat, _ = norm_rows(b.tok[image, chunk(j), :].astype(f32))
            b.n1[image, chunk(j), :] = (xhat * b.norms[0:1, :] + b.norms[1:2, :]).astype(bf16)

        each(chunks, body)

    ksize = i.taps.shape[0]
    b.edge[...] = jnp.zeros_like(b.edge)
    for p in range(ksize):
        b.edge[p * ksize : (p + 1) * ksize, :] = i.taps[p]
    b.filt[...] = exact(i.lag[...], b.edge[...])
    b.filt[:bins, :] += 1.0
    b.cross[...] = jnp.zeros_like(b.cross)
    b.mix_one[...] = jnp.zeros_like(b.mix_one)
    b.mix_two[...] = jnp.zeros_like(b.mix_two)
    b.k[padded:, :] = jnp.zeros((wide - padded, width), bf16)
    b.v[padded:, :] = jnp.zeros((wide - padded, width), bf16)

    for which, dst in enumerate((b.tok, b.og)):
        loads[2 + which].wait()
        for r in range(chunks):
            n = min(16, seq - r * 16)
            rows = b.raw[which, r * 16 : r * 16 + n].reshape(n * images, width)
            apart = mm(i.deal[:, : n * images], rows).astype(bf16)
            dst[:, chunk(r), :] = apart.reshape(images, 16, width)

    gains.from_z(1)
    gq.from_z(1)
    gq.on(1, False)
    gq.from_y(0)
    gq.on(0, True)
    gv.from_z(1)
    gp.from_z(1)
    gains.from_z(2)
    mixes.forward()
    gq.from_z(2)
    gq.on(2, False)
    gq.from_y(1)
    gq.on(1, True)
    gv.from_z(2)
    gp.from_z(2)
    gd.begin()
    gu.begin()
    gains.from_z(3)
    gq.from_z(3)
    gq.on(3, False)
    gd.over_y()
    gu.over_y()
    gr.from_y()
    gq.from_y(2)
    gq.on(2, True)
    gv.on(1, False)
    gv.from_y(0)
    gv.on(0, True)
    for k in range(at.lines):
        gains.from_y(k)
    spread = mm(b.gains[...].astype(bf16), i.comb[...])
    row = lax.broadcasted_iota(jnp.int32, spread.shape, 0)
    lane = lax.broadcasted_iota(jnp.int32, spread.shape, 1)
    first = (row >> 3) * share
    here = (lane >= first) & (lane < first + share)
    for r in range(4):
        b.norms[r : r + 1, :] = jnp.sum(
            jnp.where(here & ((row & 7) == r), spread, 0.0), axis=0, keepdims=True
        )
    norm_one(at.s)
    gv.from_z(3)
    gp.from_z(3)

    mixes.wait_mate()
    mixes.wait_corner()
    diagonal = i.diagonal[...]
    for part, piece in enumerate(split(b.mixes[...].reshape(head * 8, 128))):
        for which, pick in enumerate((i.pick_pre, i.pick_post)):
            picked = mm(pick[...], piece).astype(bf16)
            b.kron[which, part] = (mm_nt(picked, i.place[...]) * diagonal).astype(bf16)
            b.kron_t[which, part] = (mm_nt(i.place[...], picked) * diagonal).astype(bf16)

    gd.from_z(1)
    gq.from_y(3)
    gq.on(3, True)
    gv.on(2, False)
    gv.from_y(1)
    gv.on(1, True)
    gv.on(3, False)

    lo = (lax.broadcasted_iota(jnp.int32, (1, 128), 1) < 64).astype(f32)
    low_half = lax.broadcasted_iota(jnp.int32, (padded, 128), 1) < 64
    lo_b, hi_b = lo.astype(bf16), (1.0 - lo).astype(bf16)

    def project(g):
        t = mm(b.n1[at.s], b.wqk[g])
        b.q[:, tile(g)] = (t[:, :128] * scale).astype(bf16)
        b.k[:padded, tile(g)] = t[:, 128:256].astype(bf16)
        b.third_qk[g] = t[:, 256:]

    def project_v(g):
        t = mm(b.n1[at.s], b.wv[g])
        b.v[:padded, tile(g)] = t[:, :128].astype(bf16)
        b.third_v[g] = t[:, 128:]

    project(at.s)
    gv.from_y(2)
    gv.on(2, True)
    gq.from_mate(False)
    project(at.mate)
    gu.from_z(1)
    for block in passed:
        gq.from_x(*block)
    project(at.across)
    gv.from_y(3)
    gv.on(3, True)
    gq.from_mate(True)
    project(at.corner)
    for p in range(head // 2):
        one, two = b.third_qk[2 * p], b.third_qk[2 * p + 1]
        third = tile(head + p)
        b.q[:, third] = (jnp.where(low_half, one, pltpu.roll(two, 64, 1)) * scale).astype(bf16)
        b.k[:padded, third] = jnp.where(low_half, pltpu.roll(one, 64, 1), two).astype(bf16)

    def score(p):
        q, k = b.q[:, tile(p)], b.k[:, tile(p)]
        b.sc[2 * p] = mm_nt(q * lo_b, k).astype(bf16)
        b.sc[2 * p + 1] = mm_nt(q * hi_b, k).astype(bf16)

    each(pairs, score)
    gr.from_z(1)
    for block in passed[1:]:
        if block[1]:
            gp.from_y(block[0])
        gp.on(*block)
    gd.from_z(2)

    def mixed(table, which, block):
        return mm(table[which, 0], block) + mm(table[which, 1], block)

    def slab(ref, j):
        return ref[:, chunk(j), :].reshape(slots * 16, wide)

    def put(ref, j, value):
        ref[:, chunk(j), :] = value.reshape(slots, 16, wide)

    def soften(j):
        beyond = lax.broadcasted_iota(jnp.int32, (slots * 16, wide), 1) >= seq
        logits = jnp.where(beyond, -1e30, mixed(b.kron, 0, slab(b.sc, j)))
        top = jnp.max(logits, axis=-1, keepdims=True)
        power = jnp.exp(logits - top)
        probs = power / jnp.sum(power, axis=-1, keepdims=True)
        put(b.pr, j, probs)
        put(b.post, j, mixed(b.kron, 1, probs.astype(bf16)).astype(bf16))

    each(chunks, soften)
    gu.from_z(2)
    for block in passed:
        gv.from_x(*block)
    project_v(at.s)
    gv.from_mate(False)
    project_v(at.mate)
    project_v(at.across)
    gv.from_mate(True)
    project_v(at.corner)
    for p in range(head // 2):
        b.v[:padded, tile(head + p)] = jnp.where(
            low_half, b.third_v[2 * p], pltpu.roll(b.third_v[2 * p + 1], 64, 1)
        ).astype(bf16)

    def gather_heads(p):
        v = b.v[:, tile(p)]
        b.ho[at.s, :, tile(p)] = (mm(b.post[2 * p], v * lo_b) + mm(b.post[2 * p + 1], v * hi_b)).astype(bf16)

    each(pairs, gather_heads)
    ho.start()
    gr.from_z(2)
    gd.from_z(3)
    gu.from_z(3)

    def flip(src, dst):
        for r in range(width // 256):
            lanes = span(r, 256)
            block = src[:, :, lanes].reshape(images * padded, 256)
            dst[lanes, :] = mm_nt(i.eye[...], block).astype(bf16)

    def weight_grad(dst, left, right):
        for r in range(width // 256):
            rows = span(r, 256)
            dst[rows, :] = mm(left[rows, :], right()).astype(bf16)

    def flat(ref):
        return ref[...].reshape(images * padded, ref.shape[2])

    lax.fori_loop(1, images, lambda k, carry: (norm_one(at.head_next(k)), carry)[1], 0)
    flip(b.og, b.og_t)

    for block in passed:
        gp.from_x(*block)
    gp.from_mate(False)
    gp.from_mate(True)
    low_rows = lax.broadcasted_iota(jnp.int32, (width, 128), 1) < 64
    for g in range(head):
        b.wp[:, tile(g)] = b.wp_two[g]
    for p in range(head // 2):
        one, two = b.wv[2 * p, :, 128:].astype(f32), b.wv[2 * p + 1, :, 128:].astype(f32)
        b.wp[:, tile(head + p)] = jnp.where(low_rows, pltpu.roll(one, 64, 1), two).astype(bf16)

    def chip_images(step):
        return 2 * ((at.x + step) % 2)

    def two(ref, step):
        return ref[pl.ds(chip_images(step), 2)].reshape(2 * padded, ref.shape[2])

    def rows_in_two(step, body):
        for half in range(2):
            for r in range(chunks):
                body(chip_images(step) + half, chunk(r), chunk(half * chunks + r))

    def bins_of(body):
        for j in range(bins // 16):
            body(span(j, 16), pl.ds(bins + j * 16, 16))

    def conv_back(step):
        b.act[...] = mm(two(b.og, step), b.wd[...]).astype(bf16).reshape(2, padded, units)
        for half in range(2):
            image = chip_images(step) + half
            b.wave[...] = mm(i.fourier[...], b.act[half])

            def body(cos, sin):
                cos_g, sin_g = b.wave[cos, :], b.wave[sin, :]
                cos_k, sin_k = b.filt[cos, :], b.filt[sin, :]
                b.gf[image, cos, :] = cos_g.astype(bf16)
                b.gf[image, sin, :] = sin_g.astype(bf16)
                b.fi[cos, :] = (cos_k * cos_g - sin_k * sin_g).astype(bf16)
                b.fi[sin, :] = (cos_k * sin_g + sin_k * cos_g).astype(bf16)

            bins_of(body)
            b.actg[image] = mm(i.fourier_t[...], b.fi[...]).astype(bf16)

    def up(step, between):
        b.hid[...] = mm_nt(two(b.ho, step), b.wp[...])

        def norm_two(image, rows, both):
            middle = b.tok[image, rows, :].astype(f32) + b.hid[both, :]
            b.mid[jnp.minimum(jnp.abs(image - at.s), 1), rows, :] = middle
            xhat, _ = norm_rows(middle)
            b.n2[image, rows, :] = (xhat * b.norms[2:3, :] + b.norms[3:4, :]).astype(bf16)

        rows_in_two(step, norm_two)
        between()
        b.hid[...] = mm(two(b.n2, step), b.wu[...])

        def gelu(image, rows, both):
            h = b.hid[both, :]
            cdf = 0.5 * (1.0 + lax.erf(h * (0.5**0.5)))
            slope = cdf + h * jnp.exp(-0.5 * h * h) * 0.3989422804014327
            b.wid[image, rows, :] = (h * cdf).astype(bf16)
            b.hg[image, rows, :] = (b.actg[image, rows, :].astype(f32) * slope).astype(bf16)

        rows_in_two(step, gelu)
        b.np[pl.ds(chip_images(step), 2)] = (
            mm_nt(two(b.hg, step), b.wu[...]).astype(bf16).reshape(2, padded, width)
        )

    for k in range(at.lines):
        gd.from_y(k)

    def backward_part(step):
        conv_back(step)
        pl.when(step == 1)(ho.forward)

    def forward_part(step):
        pl.when(step == 0)(ho.wait_mate)
        up(step, lambda: pl.when(step == 0)(fold_two.middle))
        pl.when(step == 1)(lambda: fold_two.mate_copy(1).start())
        pl.when(step == 0)(lambda: fold_two.mate_copy(0).start())

    twice(backward_part)
    gr.from_z(3)
    for k in range(at.lines):
        gu.from_y(k)
    ho.wait_corner()
    twice(forward_part)
    flip(b.n2, b.flip)
    weight_grad(b.g_up, b.flip, lambda: flat(b.hg))
    sc_up.start()

    def down(step, between):
        for half in range(2):
            image = chip_images(step) + half
            if half:
                between()
            b.wave[...] = mm(i.fourier[...], b.wid[image])

            def body(cos, sin):
                cos_a, sin_a = b.wave[cos, :], b.wave[sin, :]
                cos_k, sin_k = b.filt[cos, :], b.filt[sin, :]
                cos_g, sin_g = b.gf[image, cos, :].astype(f32), b.gf[image, sin, :].astype(f32)
                b.fi[cos, :] = (cos_k * cos_a + sin_k * sin_a).astype(bf16)
                b.fi[sin, :] = (cos_k * sin_a - sin_k * cos_a).astype(bf16)
                b.cross[cos, :] += cos_a * cos_g + sin_a * sin_g
                b.cross[sin, :] += sin_a * cos_g - cos_a * sin_g

            bins_of(body)
            b.wid[image] = mm(i.fourier_t[...], b.fi[...]).astype(bf16)
        b.bp[pl.ds(chip_images(step), 2)] = (
            mm_nt(two(b.wid, step), b.wd[...]).astype(bf16).reshape(2, padded, width)
        )

    def down_part(step):
        down(step, lambda: pl.when(step == 0)(fold_out.middle))
        pl.when(step == 1)(lambda: fold_out.mate_copy(1).start())
        pl.when(step == 0)(lambda: fold_out.mate_copy(0).start())

    twice(down_part)
    weight_grad(b.g_down, b.og_t, lambda: flat(b.wid))
    sc_down.start()
    b.taps[0] = exact(i.lag_back[...], b.cross[...]).astype(bf16)
    taps.start()
    sc_up.middle(1)
    flip(b.n1, b.flip)

    fold_two.wait()
    zero = jnp.zeros((8, width), f32)
    gain_sum, shift_sum = zero, zero
    for j in range(chunks):
        grad = fold_two.total(chunk(j))
        xhat, rs = norm_rows(b.mid[0, chunk(j), :])
        inner = norm_back_rows(grad, b.norms[2:3, :], xhat, rs)
        total = b.og[at.s, chunk(j), :].astype(f32) + inner
        b.mg[chunk(j), :] = total
        b.ag[at.s, chunk(j), :] = total.astype(bf16)
        gain_sum += fold_rows(grad * xhat)
        shift_sum += fold_rows(grad)
    b.sums[2:3, :] = jnp.sum(gain_sum, axis=0, keepdims=True)
    b.sums[3:4, :] = jnp.sum(shift_sum, axis=0, keepdims=True)

    b.hgr[...] = mm(b.ag[at.s], b.wp[...]).astype(bf16)

    def flip_one(src, dst):
        for r in range(width // 256):
            dst[span(r, 256), :] = mm_nt(i.eye[...], src[:, span(r, 256)]).astype(bf16)

    flip_one(b.hgr, b.hgr_t)
    flip_one(b.q, b.q_t)

    def back_post(p):
        g, v = b.hgr[:, tile(p)], b.v[:, tile(p)]
        for half, mask in enumerate((lo_b, hi_b)):
            b.pg[2 * p + half] = mm_nt(g * mask, v).astype(bf16)
            rows = span(2 * p + half, 64)
            b.dv_t[rows, :] = mm(b.hgr_t[rows, :], b.post[2 * p + half]).astype(bf16)

    each(pairs, back_post)

    def unflip(src, dst):
        for r in range(width // 256):
            dst[:, span(r, 256)] = mm_nt(i.eye[:padded, :], src[span(r, 256), :]).astype(bf16)

    unflip(b.dv_t, b.dv)
    fold_at = b.turn_w.shape[1]
    for g in range(head):
        b.turn_v[g, :, 0:128] = b.dv[:, tile(g)]
        v3 = b.dv[:, tile(head + g // 2)].astype(f32)
        if g % 2:
            v3 = pltpu.roll(v3, 64, 1)
        b.turn_v[g, :, 128:256] = jnp.where(low_half, v3, 0.0).astype(bf16)
        b.turn_w[g] = jnp.where(low_half[:fold_at], v3[:fold_at], pltpu.roll(v3[-fold_at:], 64, 1)).astype(bf16)
    turn_v.start()
    turn_w.start()
    b.turned_v[at.s] = b.turn_v[at.s, :, 0:128]
    b.turned_w[at.s] = b.turn_w[at.s]
    sc_up.middle(2)

    def back_soften(j):
        grad = slab(b.pg, j)
        probs = slab(b.pr, j)
        b.mix_two[...] += mm_nt(grad, probs.astype(bf16))
        probs_grad = mixed(b.kron_t, 1, grad)
        inner = jnp.sum(probs_grad * probs, axis=-1, keepdims=True)
        mixed_grad = (probs * (probs_grad - inner)).astype(bf16)
        b.mix_one[...] += mm_nt(mixed_grad, slab(b.sc, j))
        put(b.pg, j, mixed(b.kron_t, 0, mixed_grad).astype(bf16))

    each(chunks, back_soften)

    def back_score(p):
        k = b.k[:, tile(p)]
        b.dq[:, tile(p)] = (
            (mm(b.pg[2 * p], k * lo_b) + mm(b.pg[2 * p + 1], k * hi_b)) * scale
        ).astype(bf16)
        for half in range(2):
            rows = span(2 * p + half, 64)
            b.dk_t[rows, :] = mm(b.q_t[rows, :], b.pg[2 * p + half]).astype(bf16)

    each(pairs, back_score)
    unflip(b.dk_t, b.dk)
    for g in range(head):
        b.turn[g, :, 0:128] = b.dq[:, tile(g)]
        b.turn[g, :, 128:256] = b.dk[:, tile(g)]
        third = tile(head + g // 2)
        q3, k3 = b.dq[:, third].astype(f32), b.dk[:, third].astype(f32)
        if g % 2:
            q3 = pltpu.roll(q3, 64, 1)
        else:
            k3 = pltpu.roll(k3, 64, 1)
        b.turn[g, :, 256:384] = jnp.where(low_half, q3, k3).astype(bf16)
    turn.start()
    b.turned[at.s] = b.turn[at.s]
    for k in range(3, at.lines):
        sc_up.middle(k)

    for g in range(head):
        part = mm_nt(b.turn[g], b.wqk[g]) + mm_nt(b.turn_v[g], b.wv[g])
        if g:
            b.hid[:padded, :] += part
        else:
            b.hid[:padded, :] = part
    gain_sum, shift_sum = zero, zero
    for j in range(chunks):
        grad = b.hid[chunk(j), :]
        xhat, rs = norm_rows(b.tok[at.s, chunk(j), :].astype(f32))
        inner = norm_back_rows(grad, b.norms[0:1, :], xhat, rs)
        b.inp[at.s, chunk(j), :] = (b.mg[chunk(j), :] + inner).astype(bf16)
        gain_sum += fold_rows(grad * xhat)
        shift_sum += fold_rows(grad)
    b.sums[0:1, :] = jnp.sum(gain_sum, axis=0, keepdims=True)
    b.sums[1:2, :] = jnp.sum(shift_sum, axis=0, keepdims=True)

    blocks = jnp.zeros((head * 8, 128), f32)
    for table, pick in ((b.mix_one, i.pick_pre_t), (b.mix_two, i.pick_post_t)):
        blocks += exact(exact(pick[...], table[...] * diagonal), i.place_f[...])
    b.sums[4:8, :] = jnp.zeros((4, width), f32)
    b.small[0, :, :width] = b.sums[...]
    for g in range(head):
        b.small[0, :, width + g * 128 : width + (g + 1) * 128] = blocks[g * 8 : (g + 1) * 8]
    small.start()
    ag.start()
    taps.step(0)

    turn_v.wait()
    turn_w.wait()
    inp.start()
    kept = []

    def keep(src, dst):
        kept.append(pltpu.make_async_copy(src, dst, b.saves.at[len(kept)]))
        kept[-1].start()

    def keep_image(src, dst, image):
        keep(src.at[image], dst.at[image])

    keep_image(b.inp, o.input, at.s)
    for image in range(images):
        b.thirds[image, :fold_at, :] = b.turned_w[image]
        rest = b.turned_w[image, 2 * fold_at - padded :, :].astype(f32)
        b.thirds[image, fold_at:, :] = pltpu.roll(rest, 64, 1).astype(bf16)
    for r in range(width // 256):
        rows = span(r, 256)
        b.g_v[rows, :] = mm(b.flip[rows, :], flat(b.turned_v)).astype(bf16)
        b.g_pv[rows, 0:128] = mm(b.flip[rows, :], flat(b.thirds)).astype(bf16)
    sc_v.start()
    sc_down.middle(1)
    fold_out.wait()
    for j in range(chunks):
        b.out[at.s, chunk(j), :] = (b.mid[0, chunk(j), :] + fold_out.total(chunk(j))).astype(bf16)
    out.start()
    keep_image(b.out, o.output, at.s)
    sc_down.middle(2)
    for item in (gains, mixes, gq, gv, gp, gu, gr, gd, ho, fold_two, turn_v, turn_w):
        item.drain()
    turn.wait()
    weight_grad(b.g_qk, b.flip, lambda: flat(b.turned))
    sc_qk.start()
    small.step(0)
    small.step(1)
    taps.step(1)
    sc_down.middle(3)
    for k in range(1, at.lines):
        sc_v.middle(k)
    small.step(2)
    ag.forward()
    sc_qk.middle(1)
    ag.wait_mate()
    ag.wait_corner()
    sc_qk.middle(2)
    flip(b.ag, b.og_t)
    mine = tile(at.s)
    third_tile = tile(head + at.s // 2)
    for r in range(width // 256):
        rows = span(r, 256)
        left = b.og_t[rows, :]
        proj = mm(left, b.ho[:, :, mine].reshape(images * padded, 128))
        third = pltpu.roll(mm(left, b.ho[:, :, third_tile].reshape(images * padded, 128)), 64 * (1 - at.c), 1)
        low = lax.broadcasted_iota(jnp.int32, third.shape, 1) < 64
        b.g_pv[rows, 0:128] = jnp.where(low, b.g_pv[rows, 0:128].astype(f32), third).astype(bf16)
        b.g_pv[rows, 128:256] = proj.astype(bf16)
    sc_pv.start()
    sc_qk.middle(3)
    small.step(3)
    b.s_up[...] = sc_up.finish()
    keep(b.s_up, o.w_up)
    for k in range(1, at.lines):
        sc_pv.middle(k)
    o.taps[...] = taps.step(2)
    b.s_down[...] = sc_down.finish()
    keep(b.s_down, o.w_down)
    inp.forward()
    keep_image(b.inp, o.input, at.across)
    inp.wait_mate()
    keep_image(b.inp, o.input, at.mate)
    o.w_v[:, 0:128] = sc_v.finish()
    small_total = small.step(4)
    o.mixes[...] = jnp.zeros((8, 128), f32)
    for g in range(head):

        @pl.when(at.s == g)
        def _():
            o.mixes[...] = small_total[:, width + g * 128 : width + (g + 1) * 128]

    columns = lax.broadcasted_iota(jnp.int32, (8, width), 1)
    own = (columns >= at.d * share) & (columns < (at.d + 1) * share)
    o.norms[...] = exact(jnp.where(own, small_total[:, :width], 0.0), i.comb_t[...])
    inp.wait_corner()
    keep_image(b.inp, o.input, at.corner)
    out.wait_mate()
    keep_image(b.out, o.output, at.mate)
    out.forward()
    keep_image(b.out, o.output, at.across)
    o.qk[...] = sc_qk.finish()
    out.wait_corner()
    keep_image(b.out, o.output, at.corner)
    pv = sc_pv.finish()
    o.w_v[:, 128:] = pv[:, :64]
    o.w_proj[:128, :] = pv[:, 128:].T
    o.w_proj[128:, :] = pv[:, :128].T[64:, :]
    for copy in kept:
        copy.wait()
    for item in (ag, out, inp, fold_out, sc_up, sc_down, sc_qk, sc_pv, sc_v, turn, taps, small):
        item.drain()


def finish_kernel(sizes, *refs):
    local_heads, heads, share = sizes
    (output, inputs, qk, w_v, w_proj, up, down, norms, mixes, taps, deal_t) = refs[:11]
    (o_output, o_input, o_one_g, o_one_s, o_qkv, o_proj, o_pre, o_post, o_two_g, o_two_s, o_up, o_taps, o_down) = refs[11:]
    images, rows, width = output.shape
    for src, dst in ((output, o_output), (inputs, o_input)):
        for r in range(rows // 16):
            some = pl.ds(r * 16, 16)
            mixed = mm(deal_t[...], src[:, some, :].reshape(images * 16, width))
            dst[some] = mixed.astype(bf16).reshape(16, images, width)

    @pl.when(pl.program_id(0) == 0)
    def _():
        thirds = qk[:, 256:]
        o_qkv[0, :, 0:128] = qk[:, 0:128]
        o_qkv[0, :, 128:] = thirds[:, :64]
        o_qkv[1, :, 0:128] = qk[:, 128:256]
        o_qkv[1, :, 128:] = pltpu.roll(thirds, 64, 1)[:, :64]
        o_qkv[2] = w_v[...]
        o_proj[...] = w_proj[...]
        o_up[...] = up[...]
        o_down[...] = down[...]
        o_pre[...] = mixes[:local_heads, :heads]
        o_post[...] = mixes[4 : 4 + local_heads, :heads]
        for r, ref in enumerate((o_one_g, o_one_s, o_two_g, o_two_s)):
            ref[...] = norms[r : r + 1, :share]
        ksize = o_taps.shape[0]
        for p in range(ksize):
            o_taps[p] = taps[p * ksize : (p + 1) * ksize, :]


def tables(seq, dp, head, heads, grid, ksize, share):
    cos, sin, cos_lag, sin_lag, back = spectrum(grid, ksize)
    used = cos.shape[0]
    bins = -(-used // 16) * 16
    padded = -(-seq // 16) * 16
    fourier = np.zeros((2 * bins, padded))
    fourier[:used, :seq] = cos
    fourier[bins : bins + used, :seq] = sin
    taps = ksize * ksize
    lag = np.zeros((2 * bins, -(-taps // 8) * 8))
    lag[:used, :taps] = cos_lag
    lag[bins : bins + used, :taps] = sin_lag
    lag_back = np.zeros((-(-taps // 16) * 16, 2 * bins))
    lag_back[:taps, :used] = (cos_lag * back[:, None]).T
    lag_back[:taps, bins : bins + used] = (sin_lag * back[:, None]).T
    comb = (np.arange(share * dp)[None, :] % share == np.arange(128)[:, None]) & (
        np.arange(128)[:, None] < share
    )
    group = heads // head
    slot = [group * g + l for g in range(head) for l in range(2)] + [group * g + 2 for g in range(head)]
    wide = heads * 16
    pick = np.zeros((2, wide, head * 8))
    place = np.zeros((wide, 128))
    for p, h in enumerate(slot):
        for row in range(16):
            for which in range(2):
                pick[which, p * 16 + row, (h // group) * 8 + which * 4 + h % group] = 1.0
            place[p * 16 + row, h] = 1.0
    deal = np.zeros((16 * head, 16 * head))
    for token in range(16):
        for image in range(head):
            deal[image * 16 + token, token * head + image] = 1.0
    diagonal = (np.arange(wide)[:, None] % 16) == (np.arange(wide)[None, :] % 16)
    return {
        "fourier": jnp.asarray(fourier, bf16),
        "fourier_t": jnp.asarray(fourier.T, bf16),
        "lag": jnp.asarray(lag, f32),
        "lag_back": jnp.asarray(lag_back, f32),
        "comb": jnp.asarray(comb, bf16),
        "comb_t": jnp.asarray(comb.T, f32),
        "pick_pre": jnp.asarray(pick[0], bf16),
        "pick_post": jnp.asarray(pick[1], bf16),
        "pick_pre_t": jnp.asarray(pick[0].T, f32),
        "pick_post_t": jnp.asarray(pick[1].T, f32),
        "place": jnp.asarray(place, bf16),
        "place_f": jnp.asarray(place, f32),
        "diagonal": jnp.asarray(diagonal, f32),
        "eye": jnp.asarray(np.eye(256), bf16),
        "eye_f": jnp.asarray(np.eye(256), f32),
        "deal": jnp.asarray(deal, bf16),
        "deal_t": jnp.asarray(deal.T, bf16),
    }


def whole_block(
    tokens,
    ln1_gain,
    ln1_shift,
    w_qkv,
    w_proj,
    mix_pre,
    mix_post,
    ln2_gain,
    ln2_shift,
    w_up,
    conv_kernel,
    w_down,
    out_grad,
):
    images, seq, width = tokens.shape
    dp, head = lax.axis_size("dp"), lax.axis_size("head")
    local_heads, heads = mix_pre.shape
    size = width // heads
    local = local_heads * size
    share = w_qkv.shape[0]
    ksize, units = conv_kernel.shape[0], conv_kernel.shape[2]
    grid = int(round((seq - 1) ** 0.5))
    padded = -(-seq // 16) * 16
    wide = -(-seq // 128) * 128
    lines = dp // 2
    const = tables(seq, dp, head, heads, grid, ksize, share)
    bins = const["fourier"].shape[0] // 2
    taps = const["lag_back"].shape[0]

    inputs = {
        "tokens": jnp.transpose(tokens, (1, 0, 2)),
        "out_grad": jnp.transpose(out_grad, (1, 0, 2)),
        "ln1_gain": ln1_gain.reshape(1, share),
        "ln1_shift": ln1_shift.reshape(1, share),
        "ln2_gain": ln2_gain.reshape(1, share),
        "ln2_shift": ln2_shift.reshape(1, share),
        "mix_pre": mix_pre,
        "mix_post": mix_post,
        "w_qkv": jnp.transpose(w_qkv, (1, 0, 2)),
        "w_proj": w_proj,
        "w_up": w_up,
        "w_down": w_down.T,
        "taps": conv_kernel,
        **{name: value for name, value in const.items() if name not in ("deal_t", "eye_f")},
    }
    outputs = {
        "output": ((images, padded, width), bf16),
        "input": ((images, padded, width), bf16),
        "qk": ((share, 384), f32),
        "w_v": ((share, local), f32),
        "w_proj": ((local, share), f32),
        "w_up": ((share, units), f32),
        "w_down": ((share, units), f32),
        "norms": ((8, 128), f32),
        "mixes": ((8, 128), f32),
        "taps": ((taps, units), f32),
    }
    finals = {
        "output": ((seq, images, width), bf16),
        "input": ((seq, images, width), bf16),
        "ln1_gain": ((1, share), f32),
        "ln1_shift": ((1, share), f32),
        "w_qkv": ((3, share, local), f32),
        "w_proj": ((local, share), f32),
        "mix_pre": ((local_heads, heads), f32),
        "mix_post": ((local_heads, heads), f32),
        "ln2_gain": ((1, share), f32),
        "ln2_shift": ((1, share), f32),
        "w_up": ((share, units), f32),
        "taps": ((ksize, ksize, units), f32),
        "w_down": ((share, units), f32),
    }
    one, every = (padded, width), (images, padded, width)
    square = (heads, padded, wide)
    table = (heads * 16, heads * 16)
    scratch = {
        "tok": (every, bf16),
        "og": (every, bf16),
        "raw": ((2, seq, images, width), bf16),
        "edge": ((const["lag"].shape[1], units), f32),
        "wqk": ((head, width, 384), bf16),
        "wv": ((head, width, 256), bf16),
        "wp_two": ((head, width, 128), bf16),
        "wp": ((width, width), bf16),
        "wu": ((width, units), bf16),
        "wd": ((width, units), bf16),
        "gains": ((dp * 8, 128), f32),
        "mixes": ((head, 8, 128), f32),
        "norms": ((8, width), f32),
        "filt": ((2 * bins, units), f32),
        "cross": ((2 * bins, units), f32),
        "wave": ((2 * bins, units), f32),
        "fi": ((2 * bins, units), bf16),
        "gf": ((images, 2 * bins, units), bf16),
        "actg": ((images, padded, units), bf16),
        "act": ((2, padded, units), bf16),
        "n1": (every, bf16),
        "n2": (every, bf16),
        "mid": ((2, *one), f32),
        "hid": ((2 * padded, width), f32),
        "wid": ((images, padded, units), bf16),
        "hg": ((images, padded, units), bf16),
        "np": (every, bf16),
        "np_near": ((2, *one), bf16),
        "np_far": (one, bf16),
        "bp_near": ((2, *one), bf16),
        "bp_far": (one, bf16),
        "flip": ((width, images * padded), bf16),
        "q": (one, bf16),
        "k": ((wide, width), bf16),
        "v": ((wide, width), bf16),
        "third_qk": ((head, padded, 128), f32),
        "third_v": ((head, padded, 128), f32),
        "kron": ((2, 2, *table), bf16),
        "kron_t": ((2, 2, *table), bf16),
        "mix_one": (table, f32),
        "mix_two": (table, f32),
        "sc": (square, bf16),
        "pr": (square, f32),
        "post": (square, bf16),
        "pg": (square, bf16),
        "ho": (every, bf16),
        "ag": (every, bf16),
        "hgr": (one, bf16),
        "hgr_t": ((width, padded), bf16),
        "q_t": ((width, padded), bf16),
        "dv_t": ((width, wide), bf16),
        "dk_t": ((width, wide), bf16),
        "dv": (one, bf16),
        "turn": ((head, padded, 384), bf16),
        "turned": ((head, padded, 384), bf16),
        "turn_v": ((head, padded, 256), bf16),
        "turned_v": ((head, padded, 128), bf16),
        "turn_w": ((head, (padded // 16 + 1) // 2 * 16, 128), bf16),
        "turned_w": ((head, (padded // 16 + 1) // 2 * 16, 128), bf16),
        "thirds": ((head, padded, 128), bf16),
        "og_t": ((width, images * padded), bf16),
        "sums": ((8, width), f32),
        "s_up": ((share, units), f32),
        "s_down": ((share, units), f32),
        "small": ((5, 8, width + head * 128), f32),
        "small_in": ((5, 8, width + head * 128), f32),
        "taps": ((3, taps, units), bf16),
        "taps_in": ((3, taps, units), bf16),
    }
    for name, columns in (("up", units), ("down", units), ("qk", 384), ("pv", 256), ("v", 128)):
        scratch["g_" + name] = ((width, columns), bf16)
        scratch[name + "_y"] = ((lines, share, columns), bf16)
        scratch[name + "_z"] = ((lines - 1, share, columns), bf16)
    sems = {"mi": 3, "ho": 3, "ag": 3, "ou": 3, "in": 3, "np": 3, "bp": 3}
    sems |= {"tv": head - 1, "tw": head - 1, "tu": head - 1, "ta": 3, "sm": 5}
    for name in "gqvpurd":
        sems |= {name + "z": 2 * (lines - 1), name + "y": lines}
    for name in "qvpud":
        sems |= {name + "y2": lines, name + "z2": lines - 1}
    for name in "qvp":
        sems |= {name + "x": dp, name + "m": 2 * dp}
    shapes = {name: pltpu.VMEM(*spec) for name, spec in scratch.items()}
    for name, number in sems.items():
        shapes[name + "_s"] = pltpu.SemaphoreType.DMA((number,))
        shapes[name + "_r"] = pltpu.SemaphoreType.DMA((number,))
    shapes["saves"] = pltpu.SemaphoreType.DMA((10,))
    shapes["loads"] = pltpu.SemaphoreType.DMA((4,))
    vmem = pl.BlockSpec(memory_space=pltpu.VMEM)
    left = pl.BlockSpec(memory_space=pl.ANY)
    results = pl.pallas_call(
        functools.partial(
            block_kernel,
            (seq, dp, head, size ** (-0.5)),
            tuple(inputs),
            tuple(outputs),
            tuple(shapes),
        ),
        out_shape=[jax.ShapeDtypeStruct(*spec) for spec in outputs.values()],
        in_specs=[left if n in ("tokens", "out_grad", "w_up", "w_down") else vmem for n in inputs],
        out_specs=[left if n in ("output", "input", "w_up", "w_down") else vmem for n in outputs],
        scratch_shapes=list(shapes.values()),
        compiler_params=pltpu.CompilerParams(
            collective_id=0, has_side_effects=True, vmem_limit_bytes=64 * 2**20
        ),
    )(*inputs.values())
    r = dict(zip(outputs, results))

    def kept(shape):
        return pl.BlockSpec(shape, lambda j: (0,) * len(shape))

    parts = [*r.values(), const["deal_t"]]
    step = -(-padded // (32)) * 16
    by_rows = pl.BlockSpec((images, step, width), lambda j: (0, j, 0))
    by_tokens = pl.BlockSpec((step, images, width), lambda j: (j, 0, 0))
    results = pl.pallas_call(
        functools.partial(finish_kernel, (local_heads, heads, share)),
        grid=(-(-padded // step),),
        out_shape=[jax.ShapeDtypeStruct(*spec) for spec in finals.values()],
        in_specs=[by_rows] * 2 + [kept(part.shape) for part in parts[2:]],
        out_specs=[by_tokens] * 2 + [kept(spec[0]) for spec in list(finals.values())[2:]],
    )(*parts)
    r = dict(zip(finals, results))
    for name in ("output", "input", "w_qkv"):
        r[name] = jnp.transpose(r[name], (1, 0, 2))
    for name in ("ln1_gain", "ln1_shift", "ln2_gain", "ln2_shift"):
        r[name] = r[name].reshape(share)
    r["w_down"] = r["w_down"].T
    return tuple(r.values())


def solution(mesh):
    in_specs = (
        P("dp", None, None),
        P("dp"),
        P("dp"),
        P("dp", None, "head"),
        P("head", "dp"),
        P("head", None),
        P("head", None),
        P("dp"),
        P("dp"),
        P("dp", "head"),
        P(None, None, "head"),
        P("head", "dp"),
        P("dp", None, None),
    )
    out_specs = (
        P("dp", None, None),
        P("dp", None, None),
        P("dp"),
        P("dp"),
        P("dp", None, "head"),
        P("head", "dp"),
        P("head", None),
        P("head", None),
        P("dp"),
        P("dp"),
        P("dp", "head"),
        P(None, None, "head"),
        P("head", "dp"),
    )
    dp, head = mesh.shape["dp"], mesh.shape["head"]

    def shards(*args):
        tokens, w_qkv, mix_pre = args[0], args[3], args[5]
        fits = head == 4 and dp == 8 and w_qkv.shape[0] % 32 == 0 and w_qkv.shape[0] <= 128
        fits = fits and tokens.shape[0] == head
        fits = fits and mix_pre.shape[0] == 3 and tokens.shape[2] == 64 * mix_pre.shape[1]
        return (whole_block if fits else plain)(*args)

    return jax.shard_map(shards, mesh=mesh, in_specs=in_specs, out_specs=out_specs, check_vma=False)
```

```python
import functools
import types

import jax
import jax.numpy as jnp
import numpy as np
from jax import lax
from jax.experimental import pallas as pl
from jax.experimental.pallas import tpu as pltpu
from jax.sharding import PartitionSpec as P

highest = lax.Precision.HIGHEST
epsilon = 1e-06
bf16 = jnp.bfloat16
f32 = jnp.float32


def spectrum(grid, ksize):
    margin = ksize // 2
    period = grid + margin
    pairs = [(0, 0)] + [(0, v) for v in range(1, period // 2 + 1)]
    pairs += [(u, v) for u in range(1, period // 2 + 1) for v in range(period)]
    freq = np.array(pairs, np.float64)
    place = np.array([(r, c) for r in range(grid) for c in range(grid)], np.float64)
    lags = np.array([(p - margin, q - margin) for p in range(ksize) for q in range(ksize)], np.float64)
    weight = np.sqrt(np.where(np.arange(len(pairs)) == 0, 1.0, 2.0)) / period
    angle = 2 * np.pi / period * freq @ place.T
    angle_lag = 2 * np.pi / period * freq @ lags.T
    count = len(pairs)
    cos = np.zeros((count + 1, grid * grid + 1))
    sin = np.zeros_like(cos)
    cos[:count, 1:] = weight[:, None] * np.cos(angle)
    sin[:count, 1:] = weight[:, None] * np.sin(angle)
    cos[count, 0] = 1.0
    cos_lag = np.zeros((count + 1, ksize * ksize))
    sin_lag = np.zeros_like(cos_lag)
    cos_lag[:count] = np.cos(angle_lag)
    sin_lag[:count] = np.sin(angle_lag)
    back = np.zeros(count + 1)
    back[:count] = 1.0
    return cos, sin, cos_lag, sin_lag, back


def layer_norm(values, gain, shift):
    center = jnp.mean(values, axis=-1, keepdims=True)
    centered = values - center
    spread = jnp.mean(centered * centered, axis=-1, keepdims=True)
    rs = lax.rsqrt(spread + epsilon)
    xhat = centered * rs
    return xhat * gain + shift, xhat, rs


def norm_back(grad, gain, xhat, rs):
    e = grad * gain
    inner = rs * (
        e
        - jnp.mean(e, axis=-1, keepdims=True)
        - xhat * jnp.mean(e * xhat, axis=-1, keepdims=True)
    )
    return inner, jnp.sum(grad * xhat, axis=(0, 1)), jnp.sum(grad, axis=(0, 1))


def dot(spec, a, b):
    return jnp.einsum(spec, a, b, preferred_element_type=f32)


def plain(
    tokens,
    ln1_gain,
    ln1_shift,
    w_qkv,
    w_proj,
    mix_pre,
    mix_post,
    ln2_gain,
    ln2_shift,
    w_up,
    conv_kernel,
    w_down,
    out_grad,
):
    images, seq, width = tokens.shape
    heads_local, heads = mix_pre.shape
    size = width // heads
    scale = size ** (-0.5)
    ksize = conv_kernel.shape[0]
    units = conv_kernel.shape[2]
    grid = int(round((seq - 1) ** 0.5))
    cos, sin, cos_lag, sin_lag, back = spectrum(grid, ksize)
    fourier = jnp.asarray(np.stack([cos, sin]), bf16)
    lagged = jnp.asarray(np.stack([cos_lag, sin_lag]), f32)
    lagged_back = jnp.asarray(np.stack([cos_lag, sin_lag]) * back[:, None], f32)
    mine = lax.axis_index("head")

    gains = jnp.stack([ln1_gain, ln1_shift, ln2_gain, ln2_shift])
    gains = lax.all_gather(gains, "dp", axis=1, tiled=True).astype(f32)
    gain_one, shift_one, gain_two, shift_two = gains[0], gains[1], gains[2], gains[3]
    qkv_w = lax.all_gather(w_qkv, "dp", axis=0, tiled=True)
    up_w = lax.all_gather(w_up, "dp", axis=0, tiled=True)
    down_w = lax.all_gather(w_down, "dp", axis=1, tiled=True)
    proj_w = lax.all_gather(w_proj, "head", axis=0, tiled=True)
    proj_w = lax.all_gather(proj_w, "dp", axis=1, tiled=True)
    mixes = lax.all_gather(jnp.stack([mix_pre, mix_post]), "head", axis=1, tiled=True)
    pre, post_mix = mixes[0], mixes[1]

    source = tokens.astype(f32)
    normed_one, xhat_one, rs_one = layer_norm(source, gain_one, shift_one)
    normed_one = normed_one.astype(bf16)
    qkv = dot("ind,dce->ince", normed_one, qkv_w).astype(bf16)
    qkv = lax.all_to_all(qkv, "head", split_axis=0, concat_axis=3, tiled=True)
    own = qkv.shape[0]
    query = qkv[:, :, 0].reshape(own, seq, heads, size)
    keys = qkv[:, :, 1].reshape(own, seq, heads, size)
    values = qkv[:, :, 2].reshape(own, seq, heads, size)
    scores = (dot("inhd,imhd->ihnm", query, keys) * scale).astype(bf16)
    mixed = jnp.einsum("hg,ignm->ihnm", pre, scores.astype(f32), precision=highest)
    probs = jax.nn.softmax(mixed, axis=-1)
    probs_low = probs.astype(bf16)
    post = jnp.einsum(
        "hg,ignm->ihnm", post_mix, probs_low.astype(f32), precision=highest
    ).astype(bf16)
    heads_own = dot("ihnm,imhd->inhd", post, values).reshape(own, seq, width).astype(bf16)
    heads_out = lax.all_gather(heads_own, "head", axis=0, tiled=True)
    middle = source + dot("ine,ed->ind", heads_out, proj_w)
    normed_two, xhat_two, rs_two = layer_norm(middle, gain_two, shift_two)
    normed_two = normed_two.astype(bf16)
    hidden = dot("ind,df->inf", normed_two, up_w)
    erf = lax.erf(hidden * (0.5**0.5))
    activ = 0.5 * hidden * (1.0 + erf)
    slope = 0.5 * (1.0 + erf) + hidden * jnp.exp(-0.5 * hidden * hidden) * 0.3989422804014327
    delta = np.zeros((ksize * ksize, 1), np.float32)
    delta[ksize * ksize // 2] = 1.0
    taps = conv_kernel.reshape(ksize * ksize, units)
    filters = jnp.einsum("zkl,lf->zkf", lagged, taps, precision=highest)
    cos_k, sin_k = filters[0] + 1.0, filters[1]
    wave = dot("zkn,inf->zikf", fourier, activ.astype(bf16))
    cos_a, sin_a = wave[0], wave[1]
    filtered = jnp.stack([cos_k * cos_a + sin_k * sin_a, cos_k * sin_a - sin_k * cos_a])
    widened = dot("zkn,zikf->inf", fourier, filtered.astype(bf16)).astype(bf16)
    branch = dot("inf,fd->ind", widened, down_w)
    branch = lax.psum(branch.astype(bf16), "head").astype(f32)
    output = (middle + branch).astype(bf16)

    down_grad = dot("inf,ind->fd", widened, out_grad)
    widened_grad = dot("ind,fd->inf", out_grad, down_w)
    wave_grad = dot("zkn,inf->zikf", fourier, widened_grad.astype(bf16))
    cos_g, sin_g = wave_grad[0], wave_grad[1]
    spread_grad = jnp.stack([cos_k * cos_g - sin_k * sin_g, cos_k * sin_g + sin_k * cos_g])
    activ_grad = dot("zkn,zikf->inf", fourier, spread_grad.astype(bf16))
    hidden_grad = (activ_grad * slope).astype(bf16)
    cross = jnp.stack(
        [
            jnp.sum(cos_a * cos_g + sin_a * sin_g, axis=0),
            jnp.sum(sin_a * cos_g - cos_a * sin_g, axis=0),
        ]
    )
    kernel_grad = jnp.einsum("zkl,zkf->lf", lagged_back, cross, precision=highest)
    up_grad = dot("ind,inf->df", normed_two, hidden_grad)
    two_grad = dot("inf,df->ind", hidden_grad, up_w).astype(bf16)
    two_grad = lax.psum_scatter(two_grad, "head", scatter_dimension=0, tiled=True).astype(f32)

    def pick(array):
        return lax.dynamic_slice_in_dim(array, mine * own, own, 0)

    middle_from, gain_two_grad, shift_two_grad = norm_back(
        two_grad, gain_two, pick(xhat_two), pick(rs_two)
    )
    middle_grad = pick(out_grad).astype(f32) + middle_from
    attention_own = middle_grad.astype(bf16)
    attention_grad = lax.all_gather(attention_own, "head", axis=0, tiled=True)
    local = width // lax.axis_size("head")
    heads_mine = lax.dynamic_slice_in_dim(heads_out, mine * local, local, 2)
    proj_grad = dot("ine,ind->ed", heads_mine, attention_grad)
    heads_grad = dot("ind,ed->ine", attention_own, proj_w).astype(bf16)
    heads_grad = heads_grad.reshape(own, seq, heads, size)
    values_grad = dot("ihnm,inhd->imhd", post, heads_grad)
    post_grad = dot("inhd,imhd->ihnm", heads_grad, values)
    probs_grad = jnp.einsum("hg,ihnm->ignm", post_mix, post_grad, precision=highest)
    mixed_grad = probs * (probs_grad - jnp.sum(probs_grad * probs, axis=-1, keepdims=True))
    scores_grad = jnp.einsum("hg,ihnm->ignm", pre, mixed_grad, precision=highest).astype(bf16)
    post_mix_grad = dot("ihnm,ignm->hg", post_grad.astype(bf16), probs_low)
    pre_mix_grad = dot("ihnm,ignm->hg", mixed_grad.astype(bf16), scores)
    query_grad = dot("ihnm,imhd->inhd", scores_grad, keys) * scale
    keys_grad = dot("ihnm,inhd->imhd", scores_grad, query) * scale
    qkv_grad = jnp.stack([query_grad, keys_grad, values_grad], axis=2)
    qkv_grad = qkv_grad.reshape(own, seq, 3, width).astype(bf16)
    qkv_grad = lax.all_to_all(qkv_grad, "head", split_axis=3, concat_axis=0, tiled=True)
    qkv_weight_grad = dot("ind,ince->dce", normed_one, qkv_grad)
    one_grad = dot("ince,dce->ind", qkv_grad, qkv_w).astype(bf16)
    one_grad = lax.psum_scatter(one_grad, "head", scatter_dimension=0, tiled=True).astype(f32)
    source_grad, gain_one_grad, shift_one_grad = norm_back(
        one_grad, gain_one, pick(xhat_one), pick(rs_one)
    )
    input_own = (middle_grad + source_grad).astype(bf16)
    input_grad = lax.all_gather(input_own, "head", axis=0, tiled=True)

    def share(grad, axis):
        return lax.psum_scatter(
            grad.astype(bf16), "dp", scatter_dimension=axis, tiled=True
        ).astype(f32)

    norm_grads = jnp.stack([gain_one_grad, shift_one_grad, gain_two_grad, shift_two_grad])
    norm_grads = lax.psum(norm_grads, "head")
    norm_grads = lax.psum_scatter(norm_grads, "dp", scatter_dimension=1, tiled=True)
    mix_grads = lax.psum_scatter(
        jnp.stack([pre_mix_grad, post_mix_grad]), "head", scatter_dimension=1, tiled=True
    )
    mix_grads, kernel_grad = lax.psum((mix_grads, kernel_grad), "dp")
    return (
        output,
        input_grad,
        norm_grads[0],
        norm_grads[1],
        share(qkv_weight_grad, 0),
        share(proj_grad, 1),
        mix_grads[0],
        mix_grads[1],
        norm_grads[2],
        norm_grads[3],
        share(up_grad, 0),
        kernel_grad.reshape(ksize, ksize, units),
        share(down_grad, 1),
    )


MESH = pl.DeviceIdType.MESH
NT = (((1,), (1,)), ((), ()))


def mm(a, b):
    return jnp.dot(a, b, preferred_element_type=f32)


def mm_nt(a, b):
    return lax.dot_general(a, b, NT, preferred_element_type=f32)


def exact(a, b):
    return jnp.dot(a, b, preferred_element_type=f32, precision=highest)


def split(a):
    high = a.astype(bf16)
    return high, (a - high.astype(f32)).astype(bf16)


def remote(src, dst, send, recv, device):
    return pltpu.make_async_remote_copy(
        src_ref=src,
        dst_ref=dst,
        send_sem=send,
        recv_sem=recv,
        device_id=device,
        device_id_type=MESH,
    )


class Place:
    def __init__(self, dp, head):
        self.dp, self.head = dp, head
        self.lines = dp // 2
        self.d, self.s = lax.axis_index("dp"), lax.axis_index("head")
        self.z, self.y = self.d // 2, self.d % 2
        self.x, self.c = self.s // 2, self.s % 2
        self.mate = self.x * 2 + 1 - self.c
        self.across = (1 - self.x) * 2 + self.c
        self.corner = (1 - self.x) * 2 + 1 - self.c

    def near(self, j):
        return ((self.x + j // 2) % 2) * 2 + (self.c + j % 2) % 2

    def z_next(self, k):
        return (self.z + k) % self.lines

    def z_prev(self, k):
        return (self.z + self.lines - k) % self.lines

    def head_next(self, k):
        return (self.s + k) % self.head

    def dp_next(self, k):
        return (self.d + k) % self.dp

    def call(self):
        barrier = pltpu.get_barrier_semaphore()

        def tell(d, s):
            pl.semaphore_signal(barrier, inc=1, device_id=(d, s), device_id_type=MESH)

        tell(self.d, self.mate)
        tell(self.d, self.across)
        tell(self.z * 2 + 1 - self.y, self.s)
        pl.when(self.z > 0)(lambda: tell((self.z - 1) * 2 + self.y, self.s))
        pl.when(self.z < self.lines - 1)(lambda: tell((self.z + 1) * 2 + self.y, self.s))

    def answer(self):
        inner = (self.z > 0) & (self.z < self.lines - 1)
        pl.semaphore_wait(pltpu.get_barrier_semaphore(), jnp.where(inner, 5, 4))


def rows_of(ref, index, count):
    return ref.at[pl.ds(pl.multiple_of(index * count, count), count)]


class Line:
    def __init__(self, at, buf, sems, wide):
        self.at, self.wide = at, wide
        self.groups = buf
        self.buf = buf.at[at.s] if wide else buf
        self.rows = self.buf.shape[0] // at.dp
        self.sems = sems

    def near(self, hops, body):
        at = self.at
        if hops == 0:
            body(at.z)
        else:
            pl.when(at.z >= hops)(lambda: body(at.z - hops))
            pl.when(at.z + hops < at.lines)(lambda: body(at.z + hops))

    def index(self, z, other):
        return z * 2 + (1 - self.at.y if other else self.at.y)

    def block(self, z, other, buf=None):
        return rows_of(self.buf if buf is None else buf, self.index(z, other), self.rows)

    def z_copy(self, up, hops):
        at, (send, recv) = self.at, self.sems[0]
        ref = self.block(at.z - hops if up else at.z + hops, False)
        slot = hops if up else at.lines - 1 + hops
        to = at.z_next(1) if up else at.z_prev(1)
        return remote(ref, ref, send.at[slot], recv.at[slot], (to * 2 + at.y, at.s))

    def pass_on(self, up, hops):
        at = self.at
        if up:
            there = (at.z >= hops) & (at.z < at.lines - 1)
        else:
            there = (at.z + hops < at.lines) & (at.z > 0)
        return pl.when(there)

    def y_copy(self, z):
        at, (send, recv) = self.at, self.sems[1]
        ref = self.block(z, False)
        return remote(ref, ref, send.at[z], recv.at[z], (at.z * 2 + 1 - at.y, at.s))

    def x_copy(self, z, other):
        at, (send, recv) = self.at, self.sems[2]
        ref, slot = self.block(z, other), self.index(z, other)
        return remote(ref, ref, send.at[slot], recv.at[slot], (at.d, at.across))

    def mate_copy(self, z, other, far):
        at, (send, recv) = self.at, self.sems[3]
        ref = self.block(z, other, self.groups.at[at.across if far else at.s])
        slot = self.index(z, other) + (at.dp if far else 0)
        return remote(ref, ref, send.at[slot], recv.at[slot], (at.d, at.mate))

    def begin(self):
        for up in (True, False):
            self.pass_on(up, 0)(lambda: self.z_copy(up, 0).start())

    def over_y(self):
        self.y_copy(self.at.z).start()

    def from_z(self, hops):
        at = self.at
        for up in (True, False):

            @pl.when(at.z >= hops if up else at.z + hops < at.lines)
            def _():
                source = at.z - hops if up else at.z + hops
                self.z_copy(up, hops - 1).wait_recv()
                if hops < at.lines - 1:
                    self.pass_on(up, hops)(lambda: self.z_copy(up, hops).start())
                self.y_copy(source).start()

    def on(self, hops, other):
        def body(z):
            self.x_copy(z, other).start()
            self.mate_copy(z, other, False).start()

        self.near(hops, body)

    def from_y(self, hops):
        self.near(hops, lambda z: self.y_copy(z).wait_recv())

    def from_x(self, hops, other):
        def body(z):
            self.x_copy(z, other).wait_recv()
            self.mate_copy(z, other, True).start()

        self.near(hops, body)

    def from_mate(self, far):
        for z in range(self.at.lines):
            for other in (False, True):
                self.mate_copy(z, other, far).wait_recv()

    def drain(self):
        at = self.at
        for hops in range(at.lines - 1):
            for up in (True, False):
                self.pass_on(up, hops)(lambda: self.z_copy(up, hops).wait_send())
        for z in range(at.lines):
            self.y_copy(z).wait_send()
            if self.wide:
                for other in (False, True):
                    self.x_copy(z, other).wait_send()
                    self.mate_copy(z, other, False).wait_send()
                    self.mate_copy(z, other, True).wait_send()


class Rows(Line):
    def both(self, z):
        return rows_of(self.buf, z, 2 * self.rows)

    def z_copy(self, up, hops):
        at, (send, recv) = self.at, self.sems[0]
        ref = self.both(at.z - hops if up else at.z + hops)
        slot = hops if up else at.lines - 1 + hops
        to = at.z_next(1) if up else at.z_prev(1)
        return remote(ref, ref, send.at[slot], recv.at[slot], (to * 2 + at.y, at.s))

    def from_y(self):
        self.y_copy(self.at.z).wait_recv()
        self.begin()

    def from_z(self, hops):
        at = self.at
        for up in (True, False):

            @pl.when(at.z >= hops if up else at.z + hops < at.lines)
            def _():
                self.z_copy(up, hops - 1).wait_recv()
                if hops < at.lines - 1:
                    self.pass_on(up, hops)(lambda: self.z_copy(up, hops).start())

    def drain(self):
        at = self.at
        self.y_copy(at.z).wait_send()
        for hops in range(at.lines - 1):
            for up in (True, False):
                self.pass_on(up, hops)(lambda: self.z_copy(up, hops).wait_send())


class Share:
    def __init__(self, at, buf, sems):
        self.at, self.buf = at, buf
        self.send, self.recv = sems

    def copy(self, which):
        at = self.at
        ref = self.buf.at[at.across if which == 2 else at.s]
        to = at.across if which == 1 else at.mate
        return remote(ref, ref, self.send.at[which], self.recv.at[which], (at.d, to))

    def start(self):
        self.copy(1).start()
        self.copy(0).start()

    def wait_mate(self):
        self.copy(0).wait_recv()

    def forward(self):
        self.copy(1).wait_recv()
        self.copy(2).start()

    def wait_corner(self):
        self.copy(2).wait_recv()

    def drain(self):
        for which in range(3):
            self.copy(which).wait_send()


class Fold:
    def __init__(self, at, parts, near, far, sems):
        self.at, self.parts, self.near, self.far = at, parts, near, far
        self.send, self.recv = sems

    def mate_copy(self, which):
        at = self.at
        src = self.parts.at[at.corner if which else at.mate]
        return remote(
            src, self.near.at[which], self.send.at[which], self.recv.at[which], (at.d, at.mate)
        )

    def x_copy(self):
        at = self.at
        return remote(
            self.parts.at[at.across], self.far, self.send.at[2], self.recv.at[2], (at.d, at.across)
        )

    def middle(self):
        at = self.at
        self.mate_copy(1).wait_recv()
        self.parts[at.across] = (
            self.parts[at.across].astype(f32) + self.near[1].astype(f32)
        ).astype(bf16)
        self.x_copy().start()

    def wait(self):
        self.mate_copy(0).wait_recv()
        self.x_copy().wait_recv()

    def total(self, rows):
        return (
            self.parts[self.at.s, rows, :].astype(f32)
            + self.near[0, rows, :].astype(f32)
            + self.far[rows, :].astype(f32)
        )

    def drain(self):
        self.mate_copy(0).wait_send()
        self.mate_copy(1).wait_send()
        self.x_copy().wait_send()


class Scatter:
    def __init__(self, at, src, from_y, from_z, sems):
        self.at, self.src, self.from_y, self.from_z = at, src, from_y, from_z
        (self.y_send, self.y_recv), (self.z_send, self.z_recv) = sems
        self.rows = src.shape[0] // at.dp

    def block(self, z, y):
        return rows_of(self.src, z * 2 + y, self.rows)

    def y_copy(self, k):
        at = self.at
        return remote(
            self.block(at.z_next(k), 1 - at.y),
            self.from_y.at[k],
            self.y_send.at[k],
            self.y_recv.at[k],
            (at.z * 2 + 1 - at.y, at.s),
        )

    def z_copy(self, k):
        at = self.at
        return remote(
            self.block(at.z_next(k), at.y),
            self.from_z.at[k - 1],
            self.z_send.at[k - 1],
            self.z_recv.at[k - 1],
            (at.z_next(k) * 2 + at.y, at.s),
        )

    def start(self):
        for k in (*range(1, self.at.lines), 0):
            self.y_copy(k).start()

    def middle(self, k):
        at = self.at
        self.y_copy(k).wait_recv()
        ref = self.block(at.z_next(k), at.y)
        ref[...] = (ref[...].astype(f32) + self.from_y[k].astype(f32)).astype(bf16)
        self.z_copy(k).start()

    def finish(self):
        at = self.at
        self.y_copy(0).wait_recv()
        total = self.block(at.z, at.y)[...].astype(f32) + self.from_y[0].astype(f32)
        for k in range(1, at.lines):
            self.z_copy(k).wait_recv()
            total = total + self.from_z[k - 1].astype(f32)
        return total

    def drain(self):
        for k in range(self.at.lines):
            self.y_copy(k).wait_send()
        for k in range(1, self.at.lines):
            self.z_copy(k).wait_send()


class Halves(Scatter):
    def partner(self, k):
        z = self.at.z
        return (3 - z, z + 1 - 2 * (z % 2), (z + 2) % 4, z)[k]

    def y_copy(self, k):
        at = self.at
        return remote(
            self.block(self.partner(k), 1 - at.y),
            self.from_y.at[k],
            self.y_send.at[k],
            self.y_recv.at[k],
            (at.z * 2 + 1 - at.y, at.s),
        )

    def z_copy(self, k):
        at = self.at
        return remote(
            self.block(self.partner(k), at.y),
            self.from_z.at[k],
            self.z_send.at[k],
            self.z_recv.at[k],
            (self.partner(max(k, 1)) * 2 + at.y, at.s),
        )

    def start(self):
        for k in range(4):
            self.y_copy(k).start()

    def middle(self, k):
        at, k = self.at, k - 1
        self.y_copy(k).wait_recv()
        ref = self.block(self.partner(k), at.y)
        total = ref[...].astype(f32) + self.from_y[k].astype(f32)
        if k == 2:
            self.z_copy(0).wait_recv()
            total = total + self.from_z[0].astype(f32)
        ref[...] = total.astype(bf16)
        self.z_copy(k).start()

    def finish(self):
        at = self.at
        self.y_copy(3).wait_recv()
        total = self.block(at.z, at.y)[...].astype(f32) + self.from_y[3].astype(f32)
        for k in (1, 2):
            self.z_copy(k).wait_recv()
            total = total + self.from_z[k].astype(f32)
        return total

    def drain(self):
        for k in range(4):
            self.y_copy(k).wait_send()
        for k in range(3):
            self.z_copy(k).wait_send()


class Exchange:
    def __init__(self, at, axis, slots, sems, block_for):
        self.at, self.axis, self.slots, self.block_for = at, axis, slots, block_for
        self.send, self.recv = sems
        self.count = at.dp if axis == "dp" else at.head
        self.me = at.d if axis == "dp" else at.s

    def copy(self, k):
        at = self.at
        peer = (self.me + k) % self.count
        device = (peer, at.s) if self.axis == "dp" else (at.d, peer)
        return remote(
            self.block_for(peer),
            self.slots.at[self.me],
            self.send.at[k - 1],
            self.recv.at[k - 1],
            device,
        )

    def start(self):
        for k in range(1, self.count):
            self.copy(k).start()

    def wait(self):
        for k in range(1, self.count):
            self.copy(k).wait_recv()

    def drain(self):
        for k in range(1, self.count):
            self.copy(k).wait_send()

    def total(self):
        total = self.slots[0]
        for k in range(1, self.count):
            total = total + self.slots[k]
        return total


class Doubling:
    def __init__(self, at, held, slots, sems, partners):
        self.at, self.held, self.slots, self.partners = at, held, slots, partners
        self.send, self.recv = sems

    def copy(self, k):
        return remote(
            self.held.at[k], self.slots.at[k], self.send.at[k], self.recv.at[k], self.partners[k]
        )

    def start(self):
        self.copy(0).start()

    def step(self, k):
        self.copy(k).wait_recv()
        total = self.held[k].astype(f32) + self.slots[k].astype(f32)
        if k + 1 == len(self.partners):
            return total
        self.held[k + 1] = total.astype(self.held.dtype)
        self.copy(k + 1).start()

    def drain(self):
        for k in range(len(self.partners)):
            self.copy(k).wait_send()


def norm_rows(x):
    center = jnp.mean(x, axis=-1, keepdims=True)
    centered = x - center
    spread = jnp.mean(centered * centered, axis=-1, keepdims=True)
    rs = lax.rsqrt(spread + epsilon)
    return centered * rs, rs


def norm_back_rows(grad, gain, xhat, rs):
    e = grad * gain
    return rs * (
        e
        - jnp.mean(e, axis=-1, keepdims=True)
        - xhat * jnp.mean(e * xhat, axis=-1, keepdims=True)
    )


def fold_rows(a):
    return jnp.sum(a.reshape(a.shape[0] // 8, 8, a.shape[1]), axis=0)


def block_kernel(sizes, names_in, names_out, names_scratch, *refs):
    seq, dp, head, scale = sizes
    n_in, n_out = len(names_in), len(names_out)
    i = types.SimpleNamespace(**dict(zip(names_in, refs[:n_in])))
    o = types.SimpleNamespace(**dict(zip(names_out, refs[n_in : n_in + n_out])))
    b = types.SimpleNamespace(**dict(zip(names_scratch, refs[n_in + n_out :])))
    at = Place(dp, head)
    images, padded, width = b.tok.shape
    b.bp, b.dq = b.actg, b.act.at[0]
    b.dk, b.mg = b.fi.at[:padded], b.wave.at[:padded]
    b.inp, b.out = b.n1, b.n2
    hops = range(1, at.lines)
    share = i.w_up.shape[0]
    own_rows = pl.ds(pl.multiple_of(at.d * share, share), share)
    loads = [
        pltpu.make_async_copy(src, dst, b.loads.at[n])
        for n, (src, dst) in enumerate(
            (
                (i.w_down, b.wd.at[own_rows]),
                (i.w_up, b.wu.at[own_rows]),
                (i.tokens, b.raw.at[0]),
                (i.out_grad, b.raw.at[1]),
            )
        )
    ]
    chunks = padded // 16
    wide = b.k.shape[0]
    slots = b.sc.shape[0]
    pairs = slots // 2
    units = b.wu.shape[1]
    bins = b.filt.shape[0] // 2

    def span(j, size):
        return pl.ds(j * size if isinstance(j, int) else pl.multiple_of(j * size, size), size)

    def chunk(j):
        return span(j, 16)

    def tile(p):
        return span(p, 128)

    def twice(body):
        def step(k, carry):
            body(1 - k)
            return carry

        lax.fori_loop(0, 2, step, 0)

    def each(steps, body):
        for j in range(steps) if isinstance(steps, int) else steps:
            body(j)

    def flip_block(a):
        return mm_nt(i.eye[: a.shape[1], : a.shape[1]], a)

    def halves(low, high):
        return (mm(low, i.eye[:64, :128]) + mm(high, i.eye[64:128, :128])).astype(bf16)

    at.call()
    for load in loads:
        load.start()
    w_q, w_k, w_v = i.w_qkv[0], i.w_qkv[1], i.w_qkv[2]
    b.wqk[at.s, own_rows, 0:128] = w_q[:, :128]
    b.wqk[at.s, own_rows, 128:256] = w_k[:, :128]
    b.wqk[at.s, own_rows, 256:384] = halves(w_q[:, 128:], w_k[:, 128:])
    own_gains, own_mixes = rows_of(b.gains, at.d, 8), b.mixes.at[at.s]
    own_gains[...] = jnp.zeros((8, 128), f32)
    own_mixes[...] = jnp.zeros((8, 128), f32)
    for r, gain in enumerate((i.ln1_gain, i.ln1_shift, i.ln2_gain, i.ln2_shift)):
        own_gains[r : r + 1, :share] = gain[...].astype(f32)
    local_heads, heads = i.mix_pre.shape
    own_mixes[:local_heads, :heads] = i.mix_pre[...]
    own_mixes[4 : 4 + local_heads, :heads] = i.mix_post[...]
    p_t = flip_block(i.w_proj[...]).astype(bf16)
    b.wv[at.s, own_rows, 0:128] = w_v[:, :128]
    b.wv[at.s, own_rows, 128:256] = halves(w_v[:, 128:], p_t[:, 128:])
    b.wp_two[at.s, own_rows, :] = p_t[:, :128]

    at.answer()
    loads[0].wait()
    loads[1].wait()

    def line(kind, buf, name, wide):
        sems = [(getattr(b, name + part + "_s"), getattr(b, name + part + "_r")) for part in ("zyxm" if wide else "zy")]
        return kind(at, buf, sems, wide)

    gains = line(Line, b.gains, "g", False)
    mixes = Share(at, b.mixes, (b.mi_s, b.mi_r))
    gq = line(Line, b.wqk, "q", True)
    gv = line(Line, b.wv, "v", True)
    gp = line(Line, b.wp_two, "p", True)
    cut = units // 3 * 2
    gu = line(Line, b.wu.at[:, :cut], "u", False)
    gr = line(Rows, b.wu.at[:, cut:], "r", False)
    gd = line(Line, b.wd, "d", False)
    ho = Share(at, b.ho, (b.ho_s, b.ho_r))
    ag = Share(at, b.ag, (b.ag_s, b.ag_r))
    out = Share(at, b.out, (b.ou_s, b.ou_r))
    inp = Share(at, b.inp, (b.in_s, b.in_r))
    fold_two = Fold(at, b.np, b.np_near, b.np_far, (b.np_s, b.np_r))
    fold_out = Fold(at, b.bp, b.bp_near, b.bp_far, (b.bp_s, b.bp_r))
    sc_up = Halves(at, b.g_up, b.up_y, b.up_z, ((b.uy2_s, b.uy2_r), (b.uz2_s, b.uz2_r)))
    sc_down = Halves(at, b.g_down, b.down_y, b.down_z, ((b.dy2_s, b.dy2_r), (b.dz2_s, b.dz2_r)))
    sc_qk = Scatter(at, b.g_qk, b.qk_y, b.qk_z, ((b.qy2_s, b.qy2_r), (b.qz2_s, b.qz2_r)))
    sc_pv = Scatter(at, b.g_pv, b.pv_y, b.pv_z, ((b.py2_s, b.py2_r), (b.pz2_s, b.pz2_r)))
    sc_v = Scatter(at, b.g_v, b.v_y, b.v_z, ((b.vy2_s, b.vy2_r), (b.vz2_s, b.vz2_r)))
    turn_v = Exchange(at, "head", b.turned_v, (b.tv_s, b.tv_r), lambda s: b.turn_v.at[s, :, pl.ds(0, 128)])
    turn_w = Exchange(at, "head", b.turned_w, (b.tw_s, b.tw_r), lambda s: b.turn_w.at[s])
    turn = Exchange(at, "head", b.turned, (b.tu_s, b.tu_r), lambda s: b.turn.at[s])
    over_dp = (
        ((at.z + 1 - 2 * (at.z % 2)) * 2 + at.y, at.s),
        ((at.z + 2) % 4 * 2 + at.y, at.s),
        (at.z * 2 + 1 - at.y, at.s),
    )
    taps = Doubling(at, b.taps, b.taps_in, (b.ta_s, b.ta_r), over_dp)
    small = Doubling(
        at, b.small, b.small_in, (b.sm_s, b.sm_r), ((at.d, at.across), (at.d, at.mate), *over_dp)
    )

    passed = ((0, False), (1, False), (0, True), (2, False), (1, True), (3, False), (2, True), (3, True))
    gq.begin()
    gq.over_y()
    gq.on(0, False)
    gains.begin()
    gains.over_y()
    mixes.start()
    gv.begin()
    gv.over_y()
    gv.on(0, False)
    gp.begin()
    gp.over_y()
    gp.on(0, False)
    gr.over_y()

    def norm_one(image):
        def body(j):
            xhat, _ = norm_rows(b.tok[image, chunk(j), :].astype(f32))
            b.n1[image, chunk(j), :] = (xhat * b.norms[0:1, :] + b.norms[1:2, :]).astype(bf16)

        each(chunks, body)

    ksize = i.taps.shape[0]
    b.edge[...] = jnp.zeros_like(b.edge)
    for p in range(ksize):
        b.edge[p * ksize : (p + 1) * ksize, :] = i.taps[p]
    b.filt[...] = exact(i.lag[...], b.edge[...])
    b.filt[:bins, :] += 1.0
    b.cross[...] = jnp.zeros_like(b.cross)
    b.mix_one[...] = jnp.zeros_like(b.mix_one)
    b.mix_two[...] = jnp.zeros_like(b.mix_two)
    b.k[padded:, :] = jnp.zeros((wide - padded, width), bf16)
    b.v[padded:, :] = jnp.zeros((wide - padded, width), bf16)

    for which, dst in enumerate((b.tok, b.og)):
        loads[2 + which].wait()
        for r in range(chunks):
            n = min(16, seq - r * 16)
            rows = b.raw[which, r * 16 : r * 16 + n].reshape(n * images, width)
            apart = mm(i.deal[:, : n * images], rows).astype(bf16)
            dst[:, chunk(r), :] = apart.reshape(images, 16, width)

    gains.from_z(1)
    gq.from_z(1)
    gq.on(1, False)
    gq.from_y(0)
    gq.on(0, True)
    gv.from_z(1)
    gp.from_z(1)
    gains.from_z(2)
    mixes.forward()
    gq.from_z(2)
    gq.on(2, False)
    gq.from_y(1)
    gq.on(1, True)
    gv.from_z(2)
    gp.from_z(2)
    gd.begin()
    gu.begin()
    gains.from_z(3)
    gq.from_z(3)
    gq.on(3, False)
    gd.over_y()
    gu.over_y()
    gr.from_y()
    gq.from_y(2)
    gq.on(2, True)
    gv.on(1, False)
    gv.from_y(0)
    gv.on(0, True)
    for k in range(at.lines):
        gains.from_y(k)
    spread = mm(b.gains[...].astype(bf16), i.comb[...])
    row = lax.broadcasted_iota(jnp.int32, spread.shape, 0)
    lane = lax.broadcasted_iota(jnp.int32, spread.shape, 1)
    first = (row >> 3) * share
    here = (lane >= first) & (lane < first + share)
    for r in range(4):
        b.norms[r : r + 1, :] = jnp.sum(
            jnp.where(here & ((row & 7) == r), spread, 0.0), axis=0, keepdims=True
        )
    norm_one(at.s)
    gv.from_z(3)
    gp.from_z(3)

    mixes.wait_mate()
    mixes.wait_corner()
    diagonal = i.diagonal[...]
    for part, piece in enumerate(split(b.mixes[...].reshape(head * 8, 128))):
        for which, pick in enumerate((i.pick_pre, i.pick_post)):
            picked = mm(pick[...], piece).astype(bf16)
            b.kron[which, part] = (mm_nt(picked, i.place[...]) * diagonal).astype(bf16)
            b.kron_t[which, part] = (mm_nt(i.place[...], picked) * diagonal).astype(bf16)

    gd.from_z(1)
    gq.from_y(3)
    gq.on(3, True)
    gv.on(2, False)
    gv.from_y(1)
    gv.on(1, True)
    gv.on(3, False)

    lo = (lax.broadcasted_iota(jnp.int32, (1, 128), 1) < 64).astype(f32)
    low_half = lax.broadcasted_iota(jnp.int32, (padded, 128), 1) < 64
    lo_b, hi_b = lo.astype(bf16), (1.0 - lo).astype(bf16)

    def project(g):
        t = mm(b.n1[at.s], b.wqk[g])
        b.q[:, tile(g)] = (t[:, :128] * scale).astype(bf16)
        b.k[:padded, tile(g)] = t[:, 128:256].astype(bf16)
        b.third_qk[g] = t[:, 256:]

    def project_v(g):
        t = mm(b.n1[at.s], b.wv[g])
        b.v[:padded, tile(g)] = t[:, :128].astype(bf16)
        b.third_v[g] = t[:, 128:]

    project(at.s)
    gv.from_y(2)
    gv.on(2, True)
    gq.from_mate(False)
    project(at.mate)
    gu.from_z(1)
    for block in passed:
        gq.from_x(*block)
    project(at.across)
    gv.from_y(3)
    gv.on(3, True)
    gq.from_mate(True)
    project(at.corner)
    for p in range(head // 2):
        one, two = b.third_qk[2 * p], b.third_qk[2 * p + 1]
        third = tile(head + p)
        b.q[:, third] = (jnp.where(low_half, one, pltpu.roll(two, 64, 1)) * scale).astype(bf16)
        b.k[:padded, third] = jnp.where(low_half, pltpu.roll(one, 64, 1), two).astype(bf16)

    def score(p):
        q, k = b.q[:, tile(p)], b.k[:, tile(p)]
        b.sc[2 * p] = mm_nt(q * lo_b, k).astype(bf16)
        b.sc[2 * p + 1] = mm_nt(q * hi_b, k).astype(bf16)

    each(pairs, score)
    gr.from_z(1)
    for block in passed[1:]:
        if block[1]:
            gp.from_y(block[0])
        gp.on(*block)
    gd.from_z(2)

    def mixed(table, which, block):
        return mm(table[which, 0], block) + mm(table[which, 1], block)

    def slab(ref, j):
        return ref[:, chunk(j), :].reshape(slots * 16, wide)

    def put(ref, j, value):
        ref[:, chunk(j), :] = value.reshape(slots, 16, wide)

    def soften(j):
        beyond = lax.broadcasted_iota(jnp.int32, (slots * 16, wide), 1) >= seq
        logits = jnp.where(beyond, -1e30, mixed(b.kron, 0, slab(b.sc, j)))
        top = jnp.max(logits, axis=-1, keepdims=True)
        power = jnp.exp(logits - top)
        probs = power / jnp.sum(power, axis=-1, keepdims=True)
        put(b.pr, j, probs)
        put(b.post, j, mixed(b.kron, 1, probs.astype(bf16)).astype(bf16))

    each(chunks, soften)
    gu.from_z(2)
    for block in passed:
        gv.from_x(*block)
    project_v(at.s)
    gv.from_mate(False)
    project_v(at.mate)
    project_v(at.across)
    gv.from_mate(True)
    project_v(at.corner)
    for p in range(head // 2):
        b.v[:padded, tile(head + p)] = jnp.where(
            low_half, b.third_v[2 * p], pltpu.roll(b.third_v[2 * p + 1], 64, 1)
        ).astype(bf16)

    def gather_heads(p):
        v = b.v[:, tile(p)]
        b.ho[at.s, :, tile(p)] = (mm(b.post[2 * p], v * lo_b) + mm(b.post[2 * p + 1], v * hi_b)).astype(bf16)

    each(pairs, gather_heads)
    ho.start()
    gr.from_z(2)
    gd.from_z(3)
    gu.from_z(3)

    def flip(src, dst):
        for r in range(width // 256):
            lanes = span(r, 256)
            block = src[:, :, lanes].reshape(images * padded, 256)
            dst[lanes, :] = mm_nt(i.eye[...], block).astype(bf16)

    def weight_grad(dst, left, right):
        for r in range(width // 256):
            rows = span(r, 256)
            dst[rows, :] = mm(left[rows, :], right()).astype(bf16)

    def flat(ref):
        return ref[...].reshape(images * padded, ref.shape[2])

    lax.fori_loop(1, images, lambda k, carry: (norm_one(at.head_next(k)), carry)[1], 0)
    flip(b.og, b.og_t)

    for block in passed:
        gp.from_x(*block)
    gp.from_mate(False)
    gp.from_mate(True)
    low_rows = lax.broadcasted_iota(jnp.int32, (width, 128), 1) < 64
    for g in range(head):
        b.wp[:, tile(g)] = b.wp_two[g]
    for p in range(head // 2):
        one, two = b.wv[2 * p, :, 128:].astype(f32), b.wv[2 * p + 1, :, 128:].astype(f32)
        b.wp[:, tile(head + p)] = jnp.where(low_rows, pltpu.roll(one, 64, 1), two).astype(bf16)

    def chip_images(step):
        return 2 * ((at.x + step) % 2)

    def two(ref, step):
        return ref[pl.ds(chip_images(step), 2)].reshape(2 * padded, ref.shape[2])

    def rows_in_two(step, body):
        for half in range(2):
            for r in range(chunks):
                body(chip_images(step) + half, chunk(r), chunk(half * chunks + r))

    def bins_of(body):
        for j in range(bins // 16):
            body(span(j, 16), pl.ds(bins + j * 16, 16))

    def conv_back(step):
        b.act[...] = mm(two(b.og, step), b.wd[...]).astype(bf16).reshape(2, padded, units)
        for half in range(2):
            image = chip_images(step) + half
            b.wave[...] = mm(i.fourier[...], b.act[half])

            def body(cos, sin):
                cos_g, sin_g = b.wave[cos, :], b.wave[sin, :]
                cos_k, sin_k = b.filt[cos, :], b.filt[sin, :]
                b.gf[image, cos, :] = cos_g.astype(bf16)
                b.gf[image, sin, :] = sin_g.astype(bf16)
                b.fi[cos, :] = (cos_k * cos_g - sin_k * sin_g).astype(bf16)
                b.fi[sin, :] = (cos_k * sin_g + sin_k * cos_g).astype(bf16)

            bins_of(body)
            b.actg[image] = mm(i.fourier_t[...], b.fi[...]).astype(bf16)

    def up(step, between):
        b.hid[...] = mm_nt(two(b.ho, step), b.wp[...])

        def norm_two(image, rows, both):
            middle = b.tok[image, rows, :].astype(f32) + b.hid[both, :]
            b.mid[jnp.minimum(jnp.abs(image - at.s), 1), rows, :] = middle
            xhat, _ = norm_rows(middle)
            b.n2[image, rows, :] = (xhat * b.norms[2:3, :] + b.norms[3:4, :]).astype(bf16)

        rows_in_two(step, norm_two)
        between()
        b.hid[...] = mm(two(b.n2, step), b.wu[...])

        def gelu(image, rows, both):
            h = b.hid[both, :]
            cdf = 0.5 * (1.0 + lax.erf(h * (0.5**0.5)))
            slope = cdf + h * jnp.exp(-0.5 * h * h) * 0.3989422804014327
            b.wid[image, rows, :] = (h * cdf).astype(bf16)
            b.hg[image, rows, :] = (b.actg[image, rows, :].astype(f32) * slope).astype(bf16)

        rows_in_two(step, gelu)
        b.np[pl.ds(chip_images(step), 2)] = (
            mm_nt(two(b.hg, step), b.wu[...]).astype(bf16).reshape(2, padded, width)
        )

    for k in range(at.lines):
        gd.from_y(k)

    def backward_part(step):
        conv_back(step)
        pl.when(step == 1)(ho.forward)

    def forward_part(step):
        pl.when(step == 0)(ho.wait_mate)
        up(step, lambda: pl.when(step == 0)(fold_two.middle))
        pl.when(step == 1)(lambda: fold_two.mate_copy(1).start())
        pl.when(step == 0)(lambda: fold_two.mate_copy(0).start())

    twice(backward_part)
    gr.from_z(3)
    for k in range(at.lines):
        gu.from_y(k)
    ho.wait_corner()
    twice(forward_part)
    flip(b.n2, b.flip)
    weight_grad(b.g_up, b.flip, lambda: flat(b.hg))
    sc_up.start()

    def down(step, between):
        for half in range(2):
            image = chip_images(step) + half
            if half:
                between()
            b.wave[...] = mm(i.fourier[...], b.wid[image])

            def body(cos, sin):
                cos_a, sin_a = b.wave[cos, :], b.wave[sin, :]
                cos_k, sin_k = b.filt[cos, :], b.filt[sin, :]
                cos_g, sin_g = b.gf[image, cos, :].astype(f32), b.gf[image, sin, :].astype(f32)
                b.fi[cos, :] = (cos_k * cos_a + sin_k * sin_a).astype(bf16)
                b.fi[sin, :] = (cos_k * sin_a - sin_k * cos_a).astype(bf16)
                b.cross[cos, :] += cos_a * cos_g + sin_a * sin_g
                b.cross[sin, :] += sin_a * cos_g - cos_a * sin_g

            bins_of(body)
            b.wid[image] = mm(i.fourier_t[...], b.fi[...]).astype(bf16)
        b.bp[pl.ds(chip_images(step), 2)] = (
            mm_nt(two(b.wid, step), b.wd[...]).astype(bf16).reshape(2, padded, width)
        )

    def down_part(step):
        down(step, lambda: pl.when(step == 0)(fold_out.middle))
        pl.when(step == 1)(lambda: fold_out.mate_copy(1).start())
        pl.when(step == 0)(lambda: fold_out.mate_copy(0).start())

    twice(down_part)
    weight_grad(b.g_down, b.og_t, lambda: flat(b.wid))
    sc_down.start()
    b.taps[0] = exact(i.lag_back[...], b.cross[...]).astype(bf16)
    taps.start()
    sc_up.middle(1)
    flip(b.n1, b.flip)

    fold_two.wait()
    zero = jnp.zeros((8, width), f32)
    gain_sum, shift_sum = zero, zero
    for j in range(chunks):
        grad = fold_two.total(chunk(j))
        xhat, rs = norm_rows(b.mid[0, chunk(j), :])
        inner = norm_back_rows(grad, b.norms[2:3, :], xhat, rs)
        total = b.og[at.s, chunk(j), :].astype(f32) + inner
        b.mg[chunk(j), :] = total
        b.ag[at.s, chunk(j), :] = total.astype(bf16)
        gain_sum += fold_rows(grad * xhat)
        shift_sum += fold_rows(grad)
    b.sums[2:3, :] = jnp.sum(gain_sum, axis=0, keepdims=True)
    b.sums[3:4, :] = jnp.sum(shift_sum, axis=0, keepdims=True)

    b.hgr[...] = mm(b.ag[at.s], b.wp[...]).astype(bf16)

    def flip_one(src, dst):
        for r in range(width // 256):
            dst[span(r, 256), :] = mm_nt(i.eye[...], src[:, span(r, 256)]).astype(bf16)

    flip_one(b.hgr, b.hgr_t)
    flip_one(b.q, b.q_t)

    def back_post(p):
        g, v = b.hgr[:, tile(p)], b.v[:, tile(p)]
        for half, mask in enumerate((lo_b, hi_b)):
            b.pg[2 * p + half] = mm_nt(g * mask, v).astype(bf16)
            rows = span(2 * p + half, 64)
            b.dv_t[rows, :] = mm(b.hgr_t[rows, :], b.post[2 * p + half]).astype(bf16)

    each(pairs, back_post)

    def unflip(src, dst):
        for r in range(width // 256):
            dst[:, span(r, 256)] = mm_nt(i.eye[:padded, :], src[span(r, 256), :]).astype(bf16)

    unflip(b.dv_t, b.dv)
    fold_at = b.turn_w.shape[1]
    for g in range(head):
        b.turn_v[g, :, 0:128] = b.dv[:, tile(g)]
        v3 = b.dv[:, tile(head + g // 2)].astype(f32)
        if g % 2:
            v3 = pltpu.roll(v3, 64, 1)
        b.turn_v[g, :, 128:256] = jnp.where(low_half, v3, 0.0).astype(bf16)
        b.turn_w[g] = jnp.where(low_half[:fold_at], v3[:fold_at], pltpu.roll(v3[-fold_at:], 64, 1)).astype(bf16)
    turn_v.start()
    turn_w.start()
    b.turned_v[at.s] = b.turn_v[at.s, :, 0:128]
    b.turned_w[at.s] = b.turn_w[at.s]
    sc_up.middle(2)

    def back_soften(j):
        grad = slab(b.pg, j)
        probs = slab(b.pr, j)
        b.mix_two[...] += mm_nt(grad, probs.astype(bf16))
        probs_grad = mixed(b.kron_t, 1, grad)
        inner = jnp.sum(probs_grad * probs, axis=-1, keepdims=True)
        mixed_grad = (probs * (probs_grad - inner)).astype(bf16)
        b.mix_one[...] += mm_nt(mixed_grad, slab(b.sc, j))
        put(b.pg, j, mixed(b.kron_t, 0, mixed_grad).astype(bf16))

    each(chunks, back_soften)

    def back_score(p):
        k = b.k[:, tile(p)]
        b.dq[:, tile(p)] = (
            (mm(b.pg[2 * p], k * lo_b) + mm(b.pg[2 * p + 1], k * hi_b)) * scale
        ).astype(bf16)
        for half in range(2):
            rows = span(2 * p + half, 64)
            b.dk_t[rows, :] = mm(b.q_t[rows, :], b.pg[2 * p + half]).astype(bf16)

    each(pairs, back_score)
    unflip(b.dk_t, b.dk)
    for g in range(head):
        b.turn[g, :, 0:128] = b.dq[:, tile(g)]
        b.turn[g, :, 128:256] = b.dk[:, tile(g)]
        third = tile(head + g // 2)
        q3, k3 = b.dq[:, third].astype(f32), b.dk[:, third].astype(f32)
        if g % 2:
            q3 = pltpu.roll(q3, 64, 1)
        else:
            k3 = pltpu.roll(k3, 64, 1)
        b.turn[g, :, 256:384] = jnp.where(low_half, q3, k3).astype(bf16)
    turn.start()
    b.turned[at.s] = b.turn[at.s]
    for k in range(3, at.lines):
        sc_up.middle(k)

    for g in range(head):
        part = mm_nt(b.turn[g], b.wqk[g]) + mm_nt(b.turn_v[g], b.wv[g])
        if g:
            b.hid[:padded, :] += part
        else:
            b.hid[:padded, :] = part
    gain_sum, shift_sum = zero, zero
    for j in range(chunks):
        grad = b.hid[chunk(j), :]
        xhat, rs = norm_rows(b.tok[at.s, chunk(j), :].astype(f32))
        inner = norm_back_rows(grad, b.norms[0:1, :], xhat, rs)
        b.inp[at.s, chunk(j), :] = (b.mg[chunk(j), :] + inner).astype(bf16)
        gain_sum += fold_rows(grad * xhat)
        shift_sum += fold_rows(grad)
    b.sums[0:1, :] = jnp.sum(gain_sum, axis=0, keepdims=True)
    b.sums[1:2, :] = jnp.sum(shift_sum, axis=0, keepdims=True)

    blocks = jnp.zeros((head * 8, 128), f32)
    for table, pick in ((b.mix_one, i.pick_pre_t), (b.mix_two, i.pick_post_t)):
        blocks += exact(exact(pick[...], table[...] * diagonal), i.place_f[...])
    b.sums[4:8, :] = jnp.zeros((4, width), f32)
    b.small[0, :, :width] = b.sums[...]
    for g in range(head):
        b.small[0, :, width + g * 128 : width + (g + 1) * 128] = blocks[g * 8 : (g + 1) * 8]
    small.start()
    ag.start()
    taps.step(0)

    turn_v.wait()
    turn_w.wait()
    inp.start()
    kept = []

    def keep(src, dst):
        kept.append(pltpu.make_async_copy(src, dst, b.saves.at[len(kept)]))
        kept[-1].start()

    def keep_image(src, dst, image):
        keep(src.at[image], dst.at[image])

    keep_image(b.inp, o.input, at.s)
    for image in range(images):
        b.thirds[image, :fold_at, :] = b.turned_w[image]
        rest = b.turned_w[image, 2 * fold_at - padded :, :].astype(f32)
        b.thirds[image, fold_at:, :] = pltpu.roll(rest, 64, 1).astype(bf16)
    for r in range(width // 256):
        rows = span(r, 256)
        b.g_v[rows, :] = mm(b.flip[rows, :], flat(b.turned_v)).astype(bf16)
        b.g_pv[rows, 0:128] = mm(b.flip[rows, :], flat(b.thirds)).astype(bf16)
    sc_v.start()
    sc_down.middle(1)
    fold_out.wait()
    for j in range(chunks):
        b.out[at.s, chunk(j), :] = (b.mid[0, chunk(j), :] + fold_out.total(chunk(j))).astype(bf16)
    out.start()
    keep_image(b.out, o.output, at.s)
    sc_down.middle(2)
    for item in (gains, mixes, gq, gv, gp, gu, gr, gd, ho, fold_two, turn_v, turn_w):
        item.drain()
    turn.wait()
    weight_grad(b.g_qk, b.flip, lambda: flat(b.turned))
    sc_qk.start()
    small.step(0)
    small.step(1)
    taps.step(1)
    sc_down.middle(3)
    for k in range(1, at.lines):
        sc_v.middle(k)
    small.step(2)
    ag.forward()
    sc_qk.middle(1)
    ag.wait_mate()
    ag.wait_corner()
    sc_qk.middle(2)
    flip(b.ag, b.og_t)
    mine = tile(at.s)
    third_tile = tile(head + at.s // 2)
    for r in range(width // 256):
        rows = span(r, 256)
        left = b.og_t[rows, :]
        proj = mm(left, b.ho[:, :, mine].reshape(images * padded, 128))
        third = pltpu.roll(mm(left, b.ho[:, :, third_tile].reshape(images * padded, 128)), 64 * (1 - at.c), 1)
        low = lax.broadcasted_iota(jnp.int32, third.shape, 1) < 64
        b.g_pv[rows, 0:128] = jnp.where(low, b.g_pv[rows, 0:128].astype(f32), third).astype(bf16)
        b.g_pv[rows, 128:256] = proj.astype(bf16)
    sc_pv.start()
    sc_qk.middle(3)
    small.step(3)
    b.s_up[...] = sc_up.finish()
    keep(b.s_up, o.w_up)
    for k in range(1, at.lines):
        sc_pv.middle(k)
    o.taps[...] = taps.step(2)
    b.s_down[...] = sc_down.finish()
    keep(b.s_down, o.w_down)
    inp.forward()
    keep_image(b.inp, o.input, at.across)
    inp.wait_mate()
    keep_image(b.inp, o.input, at.mate)
    o.w_v[:, 0:128] = sc_v.finish()
    small_total = small.step(4)
    o.mixes[...] = jnp.zeros((8, 128), f32)
    for g in range(head):

        @pl.when(at.s == g)
        def _():
            o.mixes[...] = small_total[:, width + g * 128 : width + (g + 1) * 128]

    columns = lax.broadcasted_iota(jnp.int32, (8, width), 1)
    own = (columns >= at.d * share) & (columns < (at.d + 1) * share)
    o.norms[...] = exact(jnp.where(own, small_total[:, :width], 0.0), i.comb_t[...])
    inp.wait_corner()
    keep_image(b.inp, o.input, at.corner)
    out.wait_mate()
    keep_image(b.out, o.output, at.mate)
    out.forward()
    keep_image(b.out, o.output, at.across)
    o.qk[...] = sc_qk.finish()
    out.wait_corner()
    keep_image(b.out, o.output, at.corner)
    pv = sc_pv.finish()
    o.w_v[:, 128:] = pv[:, :64]
    o.w_proj[:128, :] = pv[:, 128:].T
    o.w_proj[128:, :] = pv[:, :128].T[64:, :]
    for copy in kept:
        copy.wait()
    for item in (ag, out, inp, fold_out, sc_up, sc_down, sc_qk, sc_pv, sc_v, turn, taps, small):
        item.drain()


def finish_kernel(sizes, *refs):
    local_heads, heads, share = sizes
    (output, inputs, qk, w_v, w_proj, up, down, norms, mixes, taps, deal_t) = refs[:11]
    (o_output, o_input, o_one_g, o_one_s, o_qkv, o_proj, o_pre, o_post, o_two_g, o_two_s, o_up, o_taps, o_down) = refs[11:]
    images, rows, width = output.shape
    for src, dst in ((output, o_output), (inputs, o_input)):
        for r in range(rows // 16):
            some = pl.ds(r * 16, 16)
            mixed = mm(deal_t[...], src[:, some, :].reshape(images * 16, width))
            dst[some] = mixed.astype(bf16).reshape(16, images, width)

    @pl.when(pl.program_id(0) == 0)
    def _():
        thirds = qk[:, 256:]
        o_qkv[0, :, 0:128] = qk[:, 0:128]
        o_qkv[0, :, 128:] = thirds[:, :64]
        o_qkv[1, :, 0:128] = qk[:, 128:256]
        o_qkv[1, :, 128:] = pltpu.roll(thirds, 64, 1)[:, :64]
        o_qkv[2] = w_v[...]
        o_proj[...] = w_proj[...]
        o_up[...] = up[...]
        o_down[...] = down[...]
        o_pre[...] = mixes[:local_heads, :heads]
        o_post[...] = mixes[4 : 4 + local_heads, :heads]
        for r, ref in enumerate((o_one_g, o_one_s, o_two_g, o_two_s)):
            ref[...] = norms[r : r + 1, :share]
        ksize = o_taps.shape[0]
        for p in range(ksize):
            o_taps[p] = taps[p * ksize : (p + 1) * ksize, :]


def tables(seq, dp, head, heads, grid, ksize, share):
    cos, sin, cos_lag, sin_lag, back = spectrum(grid, ksize)
    used = cos.shape[0]
    bins = -(-used // 16) * 16
    padded = -(-seq // 16) * 16
    fourier = np.zeros((2 * bins, padded))
    fourier[:used, :seq] = cos
    fourier[bins : bins + used, :seq] = sin
    taps = ksize * ksize
    lag = np.zeros((2 * bins, -(-taps // 8) * 8))
    lag[:used, :taps] = cos_lag
    lag[bins : bins + used, :taps] = sin_lag
    lag_back = np.zeros((-(-taps // 16) * 16, 2 * bins))
    lag_back[:taps, :used] = (cos_lag * back[:, None]).T
    lag_back[:taps, bins : bins + used] = (sin_lag * back[:, None]).T
    comb = (np.arange(share * dp)[None, :] % share == np.arange(128)[:, None]) & (
        np.arange(128)[:, None] < share
    )
    group = heads // head
    slot = [group * g + l for g in range(head) for l in range(2)] + [group * g + 2 for g in range(head)]
    wide = heads * 16
    pick = np.zeros((2, wide, head * 8))
    place = np.zeros((wide, 128))
    for p, h in enumerate(slot):
        for row in range(16):
            for which in range(2):
                pick[which, p * 16 + row, (h // group) * 8 + which * 4 + h % group] = 1.0
            place[p * 16 + row, h] = 1.0
    deal = np.zeros((16 * head, 16 * head))
    for token in range(16):
        for image in range(head):
            deal[image * 16 + token, token * head + image] = 1.0
    diagonal = (np.arange(wide)[:, None] % 16) == (np.arange(wide)[None, :] % 16)
    return {
        "fourier": jnp.asarray(fourier, bf16),
        "fourier_t": jnp.asarray(fourier.T, bf16),
        "lag": jnp.asarray(lag, f32),
        "lag_back": jnp.asarray(lag_back, f32),
        "comb": jnp.asarray(comb, bf16),
        "comb_t": jnp.asarray(comb.T, f32),
        "pick_pre": jnp.asarray(pick[0], bf16),
        "pick_post": jnp.asarray(pick[1], bf16),
        "pick_pre_t": jnp.asarray(pick[0].T, f32),
        "pick_post_t": jnp.asarray(pick[1].T, f32),
        "place": jnp.asarray(place, bf16),
        "place_f": jnp.asarray(place, f32),
        "diagonal": jnp.asarray(diagonal, f32),
        "eye": jnp.asarray(np.eye(256), bf16),
        "eye_f": jnp.asarray(np.eye(256), f32),
        "deal": jnp.asarray(deal, bf16),
        "deal_t": jnp.asarray(deal.T, bf16),
    }


def whole_block(
    tokens,
    ln1_gain,
    ln1_shift,
    w_qkv,
    w_proj,
    mix_pre,
    mix_post,
    ln2_gain,
    ln2_shift,
    w_up,
    conv_kernel,
    w_down,
    out_grad,
):
    images, seq, width = tokens.shape
    dp, head = lax.axis_size("dp"), lax.axis_size("head")
    local_heads, heads = mix_pre.shape
    size = width // heads
    local = local_heads * size
    share = w_qkv.shape[0]
    ksize, units = conv_kernel.shape[0], conv_kernel.shape[2]
    grid = int(round((seq - 1) ** 0.5))
    padded = -(-seq // 16) * 16
    wide = -(-seq // 128) * 128
    lines = dp // 2
    const = tables(seq, dp, head, heads, grid, ksize, share)
    bins = const["fourier"].shape[0] // 2
    taps = const["lag_back"].shape[0]

    inputs = {
        "tokens": jnp.transpose(tokens, (1, 0, 2)),
        "out_grad": jnp.transpose(out_grad, (1, 0, 2)),
        "ln1_gain": ln1_gain.reshape(1, share),
        "ln1_shift": ln1_shift.reshape(1, share),
        "ln2_gain": ln2_gain.reshape(1, share),
        "ln2_shift": ln2_shift.reshape(1, share),
        "mix_pre": mix_pre,
        "mix_post": mix_post,
        "w_qkv": jnp.transpose(w_qkv, (1, 0, 2)),
        "w_proj": w_proj,
        "w_up": w_up,
        "w_down": w_down.T,
        "taps": conv_kernel,
        **{name: value for name, value in const.items() if name not in ("deal_t", "eye_f")},
    }
    outputs = {
        "output": ((images, padded, width), bf16),
        "input": ((images, padded, width), bf16),
        "qk": ((share, 384), f32),
        "w_v": ((share, local), f32),
        "w_proj": ((local, share), f32),
        "w_up": ((share, units), f32),
        "w_down": ((share, units), f32),
        "norms": ((8, 128), f32),
        "mixes": ((8, 128), f32),
        "taps": ((taps, units), f32),
    }
    finals = {
        "output": ((seq, images, width), bf16),
        "input": ((seq, images, width), bf16),
        "ln1_gain": ((1, share), f32),
        "ln1_shift": ((1, share), f32),
        "w_qkv": ((3, share, local), f32),
        "w_proj": ((local, share), f32),
        "mix_pre": ((local_heads, heads), f32),
        "mix_post": ((local_heads, heads), f32),
        "ln2_gain": ((1, share), f32),
        "ln2_shift": ((1, share), f32),
        "w_up": ((share, units), f32),
        "taps": ((ksize, ksize, units), f32),
        "w_down": ((share, units), f32),
    }
    one, every = (padded, width), (images, padded, width)
    square = (heads, padded, wide)
    table = (heads * 16, heads * 16)
    scratch = {
        "tok": (every, bf16),
        "og": (every, bf16),
        "raw": ((2, seq, images, width), bf16),
        "edge": ((const["lag"].shape[1], units), f32),
        "wqk": ((head, width, 384), bf16),
        "wv": ((head, width, 256), bf16),
        "wp_two": ((head, width, 128), bf16),
        "wp": ((width, width), bf16),
        "wu": ((width, units), bf16),
        "wd": ((width, units), bf16),
        "gains": ((dp * 8, 128), f32),
        "mixes": ((head, 8, 128), f32),
        "norms": ((8, width), f32),
        "filt": ((2 * bins, units), f32),
        "cross": ((2 * bins, units), f32),
        "wave": ((2 * bins, units), f32),
        "fi": ((2 * bins, units), bf16),
        "gf": ((images, 2 * bins, units), bf16),
        "actg": ((images, padded, units), bf16),
        "act": ((2, padded, units), bf16),
        "n1": (every, bf16),
        "n2": (every, bf16),
        "mid": ((2, *one), f32),
        "hid": ((2 * padded, width), f32),
        "wid": ((images, padded, units), bf16),
        "hg": ((images, padded, units), bf16),
        "np": (every, bf16),
        "np_near": ((2, *one), bf16),
        "np_far": (one, bf16),
        "bp_near": ((2, *one), bf16),
        "bp_far": (one, bf16),
        "flip": ((width, images * padded), bf16),
        "q": (one, bf16),
        "k": ((wide, width), bf16),
        "v": ((wide, width), bf16),
        "third_qk": ((head, padded, 128), f32),
        "third_v": ((head, padded, 128), f32),
        "kron": ((2, 2, *table), bf16),
        "kron_t": ((2, 2, *table), bf16),
        "mix_one": (table, f32),
        "mix_two": (table, f32),
        "sc": (square, bf16),
        "pr": (square, f32),
        "post": (square, bf16),
        "pg": (square, bf16),
        "ho": (every, bf16),
        "ag": (every, bf16),
        "hgr": (one, bf16),
        "hgr_t": ((width, padded), bf16),
        "q_t": ((width, padded), bf16),
        "dv_t": ((width, wide), bf16),
        "dk_t": ((width, wide), bf16),
        "dv": (one, bf16),
        "turn": ((head, padded, 384), bf16),
        "turned": ((head, padded, 384), bf16),
        "turn_v": ((head, padded, 256), bf16),
        "turned_v": ((head, padded, 128), bf16),
        "turn_w": ((head, (padded // 16 + 1) // 2 * 16, 128), bf16),
        "turned_w": ((head, (padded // 16 + 1) // 2 * 16, 128), bf16),
        "thirds": ((head, padded, 128), bf16),
        "og_t": ((width, images * padded), bf16),
        "sums": ((8, width), f32),
        "s_up": ((share, units), f32),
        "s_down": ((share, units), f32),
        "small": ((5, 8, width + head * 128), f32),
        "small_in": ((5, 8, width + head * 128), f32),
        "taps": ((3, taps, units), bf16),
        "taps_in": ((3, taps, units), bf16),
    }
    for name, columns in (("up", units), ("down", units), ("qk", 384), ("pv", 256), ("v", 128)):
        scratch["g_" + name] = ((width, columns), bf16)
        scratch[name + "_y"] = ((lines, share, columns), bf16)
        scratch[name + "_z"] = ((lines - 1, share, columns), bf16)
    sems = {"mi": 3, "ho": 3, "ag": 3, "ou": 3, "in": 3, "np": 3, "bp": 3}
    sems |= {"tv": head - 1, "tw": head - 1, "tu": head - 1, "ta": 3, "sm": 5}
    for name in "gqvpurd":
        sems |= {name + "z": 2 * (lines - 1), name + "y": lines}
    for name in "qvpud":
        sems |= {name + "y2": lines, name + "z2": lines - 1}
    for name in "qvp":
        sems |= {name + "x": dp, name + "m": 2 * dp}
    shapes = {name: pltpu.VMEM(*spec) for name, spec in scratch.items()}
    for name, number in sems.items():
        shapes[name + "_s"] = pltpu.SemaphoreType.DMA((number,))
        shapes[name + "_r"] = pltpu.SemaphoreType.DMA((number,))
    shapes["saves"] = pltpu.SemaphoreType.DMA((10,))
    shapes["loads"] = pltpu.SemaphoreType.DMA((4,))
    vmem = pl.BlockSpec(memory_space=pltpu.VMEM)
    left = pl.BlockSpec(memory_space=pl.ANY)
    results = pl.pallas_call(
        functools.partial(
            block_kernel,
            (seq, dp, head, size ** (-0.5)),
            tuple(inputs),
            tuple(outputs),
            tuple(shapes),
        ),
        out_shape=[jax.ShapeDtypeStruct(*spec) for spec in outputs.values()],
        in_specs=[left if n in ("tokens", "out_grad", "w_up", "w_down") else vmem for n in inputs],
        out_specs=[left if n in ("output", "input", "w_up", "w_down") else vmem for n in outputs],
        scratch_shapes=list(shapes.values()),
        compiler_params=pltpu.CompilerParams(
            collective_id=0, has_side_effects=True, vmem_limit_bytes=64 * 2**20
        ),
    )(*inputs.values())
    r = dict(zip(outputs, results))

    def kept(shape):
        return pl.BlockSpec(shape, lambda j: (0,) * len(shape))

    parts = [*r.values(), const["deal_t"]]
    step = -(-padded // (32)) * 16
    by_rows = pl.BlockSpec((images, step, width), lambda j: (0, j, 0))
    by_tokens = pl.BlockSpec((step, images, width), lambda j: (j, 0, 0))
    results = pl.pallas_call(
        functools.partial(finish_kernel, (local_heads, heads, share)),
        grid=(-(-padded // step),),
        out_shape=[jax.ShapeDtypeStruct(*spec) for spec in finals.values()],
        in_specs=[by_rows] * 2 + [kept(part.shape) for part in parts[2:]],
        out_specs=[by_tokens] * 2 + [kept(spec[0]) for spec in list(finals.values())[2:]],
    )(*parts)
    r = dict(zip(finals, results))
    for name in ("output", "input", "w_qkv"):
        r[name] = jnp.transpose(r[name], (1, 0, 2))
    for name in ("ln1_gain", "ln1_shift", "ln2_gain", "ln2_shift"):
        r[name] = r[name].reshape(share)
    r["w_down"] = r["w_down"].T
    return tuple(r.values())


def solution(mesh):
    in_specs = (
        P("dp", None, None),
        P("dp"),
        P("dp"),
        P("dp", None, "head"),
        P("head", "dp"),
        P("head", None),
        P("head", None),
        P("dp"),
        P("dp"),
        P("dp", "head"),
        P(None, None, "head"),
        P("head", "dp"),
        P("dp", None, None),
    )
    out_specs = (
        P("dp", None, None),
        P("dp", None, None),
        P("dp"),
        P("dp"),
        P("dp", None, "head"),
        P("head", "dp"),
        P("head", None),
        P("head", None),
        P("dp"),
        P("dp"),
        P("dp", "head"),
        P(None, None, "head"),
        P("head", "dp"),
    )
    dp, head = mesh.shape["dp"], mesh.shape["head"]

    def shards(*args):
        tokens, w_qkv, mix_pre = args[0], args[3], args[5]
        fits = head == 4 and dp == 8 and w_qkv.shape[0] % 32 == 0 and w_qkv.shape[0] <= 128
        fits = fits and tokens.shape[0] == head
        fits = fits and mix_pre.shape[0] == 3 and tokens.shape[2] == 64 * mix_pre.shape[1]
        return (whole_block if fits else plain)(*args)

    return jax.shard_map(shards, mesh=mesh, in_specs=in_specs, out_specs=out_specs, check_vma=False)
```

```python
import functools
import types

import jax
import jax.numpy as jnp
import numpy as np
from jax import lax
from jax.experimental import pallas as pl
from jax.experimental.pallas import tpu as pltpu
from jax.sharding import PartitionSpec as P

highest = lax.Precision.HIGHEST
epsilon = 1e-06
bf16 = jnp.bfloat16
f32 = jnp.float32


def spectrum(grid, ksize):
    margin = ksize // 2
    period = grid + margin
    pairs = [(0, 0)] + [(0, v) for v in range(1, period // 2 + 1)]
    pairs += [(u, v) for u in range(1, period // 2 + 1) for v in range(period)]
    freq = np.array(pairs, np.float64)
    place = np.array([(r, c) for r in range(grid) for c in range(grid)], np.float64)
    lags = np.array([(p - margin, q - margin) for p in range(ksize) for q in range(ksize)], np.float64)
    weight = np.sqrt(np.where(np.arange(len(pairs)) == 0, 1.0, 2.0)) / period
    angle = 2 * np.pi / period * freq @ place.T
    angle_lag = 2 * np.pi / period * freq @ lags.T
    count = len(pairs)
    cos = np.zeros((count + 1, grid * grid + 1))
    sin = np.zeros_like(cos)
    cos[:count, 1:] = weight[:, None] * np.cos(angle)
    sin[:count, 1:] = weight[:, None] * np.sin(angle)
    cos[count, 0] = 1.0
    cos_lag = np.zeros((count + 1, ksize * ksize))
    sin_lag = np.zeros_like(cos_lag)
    cos_lag[:count] = np.cos(angle_lag)
    sin_lag[:count] = np.sin(angle_lag)
    back = np.zeros(count + 1)
    back[:count] = 1.0
    return cos, sin, cos_lag, sin_lag, back


def layer_norm(values, gain, shift):
    center = jnp.mean(values, axis=-1, keepdims=True)
    centered = values - center
    spread = jnp.mean(centered * centered, axis=-1, keepdims=True)
    rs = lax.rsqrt(spread + epsilon)
    xhat = centered * rs
    return xhat * gain + shift, xhat, rs


def norm_back(grad, gain, xhat, rs):
    e = grad * gain
    inner = rs * (
        e
        - jnp.mean(e, axis=-1, keepdims=True)
        - xhat * jnp.mean(e * xhat, axis=-1, keepdims=True)
    )
    return inner, jnp.sum(grad * xhat, axis=(0, 1)), jnp.sum(grad, axis=(0, 1))


def dot(spec, a, b):
    return jnp.einsum(spec, a, b, preferred_element_type=f32)


def plain(
    tokens,
    ln1_gain,
    ln1_shift,
    w_qkv,
    w_proj,
    mix_pre,
    mix_post,
    ln2_gain,
    ln2_shift,
    w_up,
    conv_kernel,
    w_down,
    out_grad,
):
    images, seq, width = tokens.shape
    heads_local, heads = mix_pre.shape
    size = width // heads
    scale = size ** (-0.5)
    ksize = conv_kernel.shape[0]
    units = conv_kernel.shape[2]
    grid = int(round((seq - 1) ** 0.5))
    cos, sin, cos_lag, sin_lag, back = spectrum(grid, ksize)
    fourier = jnp.asarray(np.stack([cos, sin]), bf16)
    lagged = jnp.asarray(np.stack([cos_lag, sin_lag]), f32)
    lagged_back = jnp.asarray(np.stack([cos_lag, sin_lag]) * back[:, None], f32)
    mine = lax.axis_index("head")

    gains = jnp.stack([ln1_gain, ln1_shift, ln2_gain, ln2_shift])
    gains = lax.all_gather(gains, "dp", axis=1, tiled=True).astype(f32)
    gain_one, shift_one, gain_two, shift_two = gains[0], gains[1], gains[2], gains[3]
    qkv_w = lax.all_gather(w_qkv, "dp", axis=0, tiled=True)
    up_w = lax.all_gather(w_up, "dp", axis=0, tiled=True)
    down_w = lax.all_gather(w_down, "dp", axis=1, tiled=True)
    proj_w = lax.all_gather(w_proj, "head", axis=0, tiled=True)
    proj_w = lax.all_gather(proj_w, "dp", axis=1, tiled=True)
    mixes = lax.all_gather(jnp.stack([mix_pre, mix_post]), "head", axis=1, tiled=True)
    pre, post_mix = mixes[0], mixes[1]

    source = tokens.astype(f32)
    normed_one, xhat_one, rs_one = layer_norm(source, gain_one, shift_one)
    normed_one = normed_one.astype(bf16)
    qkv = dot("ind,dce->ince", normed_one, qkv_w).astype(bf16)
    qkv = lax.all_to_all(qkv, "head", split_axis=0, concat_axis=3, tiled=True)
    own = qkv.shape[0]
    query = qkv[:, :, 0].reshape(own, seq, heads, size)
    keys = qkv[:, :, 1].reshape(own, seq, heads, size)
    values = qkv[:, :, 2].reshape(own, seq, heads, size)
    scores = (dot("inhd,imhd->ihnm", query, keys) * scale).astype(bf16)
    mixed = jnp.einsum("hg,ignm->ihnm", pre, scores.astype(f32), precision=highest)
    probs = jax.nn.softmax(mixed, axis=-1)
    probs_low = probs.astype(bf16)
    post = jnp.einsum(
        "hg,ignm->ihnm", post_mix, probs_low.astype(f32), precision=highest
    ).astype(bf16)
    heads_own = dot("ihnm,imhd->inhd", post, values).reshape(own, seq, width).astype(bf16)
    heads_out = lax.all_gather(heads_own, "head", axis=0, tiled=True)
    middle = source + dot("ine,ed->ind", heads_out, proj_w)
    normed_two, xhat_two, rs_two = layer_norm(middle, gain_two, shift_two)
    normed_two = normed_two.astype(bf16)
    hidden = dot("ind,df->inf", normed_two, up_w)
    erf = lax.erf(hidden * (0.5**0.5))
    activ = 0.5 * hidden * (1.0 + erf)
    slope = 0.5 * (1.0 + erf) + hidden * jnp.exp(-0.5 * hidden * hidden) * 0.3989422804014327
    delta = np.zeros((ksize * ksize, 1), np.float32)
    delta[ksize * ksize // 2] = 1.0
    taps = conv_kernel.reshape(ksize * ksize, units)
    filters = jnp.einsum("zkl,lf->zkf", lagged, taps, precision=highest)
    cos_k, sin_k = filters[0] + 1.0, filters[1]
    wave = dot("zkn,inf->zikf", fourier, activ.astype(bf16))
    cos_a, sin_a = wave[0], wave[1]
    filtered = jnp.stack([cos_k * cos_a + sin_k * sin_a, cos_k * sin_a - sin_k * cos_a])
    widened = dot("zkn,zikf->inf", fourier, filtered.astype(bf16)).astype(bf16)
    branch = dot("inf,fd->ind", widened, down_w)
    branch = lax.psum(branch.astype(bf16), "head").astype(f32)
    output = (middle + branch).astype(bf16)

    down_grad = dot("inf,ind->fd", widened, out_grad)
    widened_grad = dot("ind,fd->inf", out_grad, down_w)
    wave_grad = dot("zkn,inf->zikf", fourier, widened_grad.astype(bf16))
    cos_g, sin_g = wave_grad[0], wave_grad[1]
    spread_grad = jnp.stack([cos_k * cos_g - sin_k * sin_g, cos_k * sin_g + sin_k * cos_g])
    activ_grad = dot("zkn,zikf->inf", fourier, spread_grad.astype(bf16))
    hidden_grad = (activ_grad * slope).astype(bf16)
    cross = jnp.stack(
        [
            jnp.sum(cos_a * cos_g + sin_a * sin_g, axis=0),
            jnp.sum(sin_a * cos_g - cos_a * sin_g, axis=0),
        ]
    )
    kernel_grad = jnp.einsum("zkl,zkf->lf", lagged_back, cross, precision=highest)
    up_grad = dot("ind,inf->df", normed_two, hidden_grad)
    two_grad = dot("inf,df->ind", hidden_grad, up_w).astype(bf16)
    two_grad = lax.psum_scatter(two_grad, "head", scatter_dimension=0, tiled=True).astype(f32)

    def pick(array):
        return lax.dynamic_slice_in_dim(array, mine * own, own, 0)

    middle_from, gain_two_grad, shift_two_grad = norm_back(
        two_grad, gain_two, pick(xhat_two), pick(rs_two)
    )
    middle_grad = pick(out_grad).astype(f32) + middle_from
    attention_own = middle_grad.astype(bf16)
    attention_grad = lax.all_gather(attention_own, "head", axis=0, tiled=True)
    local = width // lax.axis_size("head")
    heads_mine = lax.dynamic_slice_in_dim(heads_out, mine * local, local, 2)
    proj_grad = dot("ine,ind->ed", heads_mine, attention_grad)
    heads_grad = dot("ind,ed->ine", attention_own, proj_w).astype(bf16)
    heads_grad = heads_grad.reshape(own, seq, heads, size)
    values_grad = dot("ihnm,inhd->imhd", post, heads_grad)
    post_grad = dot("inhd,imhd->ihnm", heads_grad, values)
    probs_grad = jnp.einsum("hg,ihnm->ignm", post_mix, post_grad, precision=highest)
    mixed_grad = probs * (probs_grad - jnp.sum(probs_grad * probs, axis=-1, keepdims=True))
    scores_grad = jnp.einsum("hg,ihnm->ignm", pre, mixed_grad, precision=highest).astype(bf16)
    post_mix_grad = dot("ihnm,ignm->hg", post_grad.astype(bf16), probs_low)
    pre_mix_grad = dot("ihnm,ignm->hg", mixed_grad.astype(bf16), scores)
    query_grad = dot("ihnm,imhd->inhd", scores_grad, keys) * scale
    keys_grad = dot("ihnm,inhd->imhd", scores_grad, query) * scale
    qkv_grad = jnp.stack([query_grad, keys_grad, values_grad], axis=2)
    qkv_grad = qkv_grad.reshape(own, seq, 3, width).astype(bf16)
    qkv_grad = lax.all_to_all(qkv_grad, "head", split_axis=3, concat_axis=0, tiled=True)
    qkv_weight_grad = dot("ind,ince->dce", normed_one, qkv_grad)
    one_grad = dot("ince,dce->ind", qkv_grad, qkv_w).astype(bf16)
    one_grad = lax.psum_scatter(one_grad, "head", scatter_dimension=0, tiled=True).astype(f32)
    source_grad, gain_one_grad, shift_one_grad = norm_back(
        one_grad, gain_one, pick(xhat_one), pick(rs_one)
    )
    input_own = (middle_grad + source_grad).astype(bf16)
    input_grad = lax.all_gather(input_own, "head", axis=0, tiled=True)

    def share(grad, axis):
        return lax.psum_scatter(
            grad.astype(bf16), "dp", scatter_dimension=axis, tiled=True
        ).astype(f32)

    norm_grads = jnp.stack([gain_one_grad, shift_one_grad, gain_two_grad, shift_two_grad])
    norm_grads = lax.psum(norm_grads, "head")
    norm_grads = lax.psum_scatter(norm_grads, "dp", scatter_dimension=1, tiled=True)
    mix_grads = lax.psum_scatter(
        jnp.stack([pre_mix_grad, post_mix_grad]), "head", scatter_dimension=1, tiled=True
    )
    mix_grads, kernel_grad = lax.psum((mix_grads, kernel_grad), "dp")
    return (
        output,
        input_grad,
        norm_grads[0],
        norm_grads[1],
        share(qkv_weight_grad, 0),
        share(proj_grad, 1),
        mix_grads[0],
        mix_grads[1],
        norm_grads[2],
        norm_grads[3],
        share(up_grad, 0),
        kernel_grad.reshape(ksize, ksize, units),
        share(down_grad, 1),
    )


MESH = pl.DeviceIdType.MESH
NT = (((1,), (1,)), ((), ()))


def mm(a, b):
    return jnp.dot(a, b, preferred_element_type=f32)


def mm_nt(a, b):
    return lax.dot_general(a, b, NT, preferred_element_type=f32)


def exact(a, b):
    return jnp.dot(a, b, preferred_element_type=f32, precision=highest)


def split(a):
    high = a.astype(bf16)
    return high, (a - high.astype(f32)).astype(bf16)


def remote(src, dst, send, recv, device):
    return pltpu.make_async_remote_copy(
        src_ref=src,
        dst_ref=dst,
        send_sem=send,
        recv_sem=recv,
        device_id=device,
        device_id_type=MESH,
    )


class Place:
    def __init__(self, dp, head):
        self.dp, self.head = dp, head
        self.lines = dp // 2
        self.d, self.s = lax.axis_index("dp"), lax.axis_index("head")
        self.z, self.y = self.d // 2, self.d % 2
        self.x, self.c = self.s // 2, self.s % 2
        self.mate = self.x * 2 + 1 - self.c
        self.across = (1 - self.x) * 2 + self.c
        self.corner = (1 - self.x) * 2 + 1 - self.c

    def near(self, j):
        return ((self.x + j // 2) % 2) * 2 + (self.c + j % 2) % 2

    def z_next(self, k):
        return (self.z + k) % self.lines

    def z_prev(self, k):
        return (self.z + self.lines - k) % self.lines

    def head_next(self, k):
        return (self.s + k) % self.head

    def dp_next(self, k):
        return (self.d + k) % self.dp

    def call(self):
        barrier = pltpu.get_barrier_semaphore()

        def tell(d, s):
            pl.semaphore_signal(barrier, inc=1, device_id=(d, s), device_id_type=MESH)

        tell(self.d, self.mate)
        tell(self.d, self.across)
        tell(self.z * 2 + 1 - self.y, self.s)
        pl.when(self.z > 0)(lambda: tell((self.z - 1) * 2 + self.y, self.s))
        pl.when(self.z < self.lines - 1)(lambda: tell((self.z + 1) * 2 + self.y, self.s))

    def answer(self):
        inner = (self.z > 0) & (self.z < self.lines - 1)
        pl.semaphore_wait(pltpu.get_barrier_semaphore(), jnp.where(inner, 5, 4))


def rows_of(ref, index, count):
    return ref.at[pl.ds(pl.multiple_of(index * count, count), count)]


class Line:
    def __init__(self, at, buf, sems, wide):
        self.at, self.wide = at, wide
        self.groups = buf
        self.buf = buf.at[at.s] if wide else buf
        self.rows = self.buf.shape[0] // at.dp
        self.sems = sems

    def near(self, hops, body):
        at = self.at
        if hops == 0:
            body(at.z)
        else:
            pl.when(at.z >= hops)(lambda: body(at.z - hops))
            pl.when(at.z + hops < at.lines)(lambda: body(at.z + hops))

    def index(self, z, other):
        return z * 2 + (1 - self.at.y if other else self.at.y)

    def block(self, z, other, buf=None):
        return rows_of(self.buf if buf is None else buf, self.index(z, other), self.rows)

    def z_copy(self, up, hops):
        at, (send, recv) = self.at, self.sems[0]
        ref = self.block(at.z - hops if up else at.z + hops, False)
        slot = hops if up else at.lines - 1 + hops
        to = at.z_next(1) if up else at.z_prev(1)
        return remote(ref, ref, send.at[slot], recv.at[slot], (to * 2 + at.y, at.s))

    def pass_on(self, up, hops):
        at = self.at
        if up:
            there = (at.z >= hops) & (at.z < at.lines - 1)
        else:
            there = (at.z + hops < at.lines) & (at.z > 0)
        return pl.when(there)

    def y_copy(self, z):
        at, (send, recv) = self.at, self.sems[1]
        ref = self.block(z, False)
        return remote(ref, ref, send.at[z], recv.at[z], (at.z * 2 + 1 - at.y, at.s))

    def x_copy(self, z, other):
        at, (send, recv) = self.at, self.sems[2]
        ref, slot = self.block(z, other), self.index(z, other)
        return remote(ref, ref, send.at[slot], recv.at[slot], (at.d, at.across))

    def mate_copy(self, z, other, far):
        at, (send, recv) = self.at, self.sems[3]
        ref = self.block(z, other, self.groups.at[at.across if far else at.s])
        slot = self.index(z, other) + (at.dp if far else 0)
        return remote(ref, ref, send.at[slot], recv.at[slot], (at.d, at.mate))

    def begin(self):
        for up in (True, False):
            self.pass_on(up, 0)(lambda: self.z_copy(up, 0).start())

    def over_y(self):
        self.y_copy(self.at.z).start()

    def from_z(self, hops):
        at = self.at
        for up in (True, False):

            @pl.when(at.z >= hops if up else at.z + hops < at.lines)
            def _():
                source = at.z - hops if up else at.z + hops
                self.z_copy(up, hops - 1).wait_recv()
                if hops < at.lines - 1:
                    self.pass_on(up, hops)(lambda: self.z_copy(up, hops).start())
                self.y_copy(source).start()

    def on(self, hops, other):
        def body(z):
            self.x_copy(z, other).start()
            self.mate_copy(z, other, False).start()

        self.near(hops, body)

    def from_y(self, hops):
        self.near(hops, lambda z: self.y_copy(z).wait_recv())

    def from_x(self, hops, other):
        def body(z):
            self.x_copy(z, other).wait_recv()
            self.mate_copy(z, other, True).start()

        self.near(hops, body)

    def from_mate(self, far):
        for z in range(self.at.lines):
            for other in (False, True):
                self.mate_copy(z, other, far).wait_recv()

    def drain(self):
        at = self.at
        for hops in range(at.lines - 1):
            for up in (True, False):
                self.pass_on(up, hops)(lambda: self.z_copy(up, hops).wait_send())
        for z in range(at.lines):
            self.y_copy(z).wait_send()
            if self.wide:
                for other in (False, True):
                    self.x_copy(z, other).wait_send()
                    self.mate_copy(z, other, False).wait_send()
                    self.mate_copy(z, other, True).wait_send()


class Rows(Line):
    def both(self, z):
        return rows_of(self.buf, z, 2 * self.rows)

    def z_copy(self, up, hops):
        at, (send, recv) = self.at, self.sems[0]
        ref = self.both(at.z - hops if up else at.z + hops)
        slot = hops if up else at.lines - 1 + hops
        to = at.z_next(1) if up else at.z_prev(1)
        return remote(ref, ref, send.at[slot], recv.at[slot], (to * 2 + at.y, at.s))

    def from_y(self):
        self.y_copy(self.at.z).wait_recv()
        self.begin()

    def from_z(self, hops):
        at = self.at
        for up in (True, False):

            @pl.when(at.z >= hops if up else at.z + hops < at.lines)
            def _():
                self.z_copy(up, hops - 1).wait_recv()
                if hops < at.lines - 1:
                    self.pass_on(up, hops)(lambda: self.z_copy(up, hops).start())

    def drain(self):
        at = self.at
        self.y_copy(at.z).wait_send()
        for hops in range(at.lines - 1):
            for up in (True, False):
                self.pass_on(up, hops)(lambda: self.z_copy(up, hops).wait_send())


class Share:
    def __init__(self, at, buf, sems):
        self.at, self.buf = at, buf
        self.send, self.recv = sems

    def copy(self, which):
        at = self.at
        ref = self.buf.at[at.across if which == 2 else at.s]
        to = at.across if which == 1 else at.mate
        return remote(ref, ref, self.send.at[which], self.recv.at[which], (at.d, to))

    def start(self):
        self.copy(1).start()
        self.copy(0).start()

    def wait_mate(self):
        self.copy(0).wait_recv()

    def forward(self):
        self.copy(1).wait_recv()
        self.copy(2).start()

    def wait_corner(self):
        self.copy(2).wait_recv()

    def drain(self):
        for which in range(3):
            self.copy(which).wait_send()


class Fold:
    def __init__(self, at, parts, near, far, sems):
        self.at, self.parts, self.near, self.far = at, parts, near, far
        self.send, self.recv = sems

    def mate_copy(self, which):
        at = self.at
        src = self.parts.at[at.corner if which else at.mate]
        return remote(
            src, self.near.at[which], self.send.at[which], self.recv.at[which], (at.d, at.mate)
        )

    def x_copy(self):
        at = self.at
        return remote(
            self.parts.at[at.across], self.far, self.send.at[2], self.recv.at[2], (at.d, at.across)
        )

    def middle(self):
        at = self.at
        self.mate_copy(1).wait_recv()
        self.parts[at.across] = (
            self.parts[at.across].astype(f32) + self.near[1].astype(f32)
        ).astype(bf16)
        self.x_copy().start()

    def wait(self):
        self.mate_copy(0).wait_recv()
        self.x_copy().wait_recv()

    def total(self, rows):
        return (
            self.parts[self.at.s, rows, :].astype(f32)
            + self.near[0, rows, :].astype(f32)
            + self.far[rows, :].astype(f32)
        )

    def drain(self):
        self.mate_copy(0).wait_send()
        self.mate_copy(1).wait_send()
        self.x_copy().wait_send()


class Scatter:
    def __init__(self, at, src, from_y, from_z, sems):
        self.at, self.src, self.from_y, self.from_z = at, src, from_y, from_z
        (self.y_send, self.y_recv), (self.z_send, self.z_recv) = sems
        self.rows = src.shape[0] // at.dp

    def block(self, z, y):
        return rows_of(self.src, z * 2 + y, self.rows)

    def y_copy(self, k):
        at = self.at
        return remote(
            self.block(at.z_next(k), 1 - at.y),
            self.from_y.at[k],
            self.y_send.at[k],
            self.y_recv.at[k],
            (at.z * 2 + 1 - at.y, at.s),
        )

    def z_copy(self, k):
        at = self.at
        return remote(
            self.block(at.z_next(k), at.y),
            self.from_z.at[k - 1],
            self.z_send.at[k - 1],
            self.z_recv.at[k - 1],
            (at.z_next(k) * 2 + at.y, at.s),
        )

    def start(self):
        for k in (*range(1, self.at.lines), 0):
            self.y_copy(k).start()

    def middle(self, k):
        at = self.at
        self.y_copy(k).wait_recv()
        ref = self.block(at.z_next(k), at.y)
        ref[...] = (ref[...].astype(f32) + self.from_y[k].astype(f32)).astype(bf16)
        self.z_copy(k).start()

    def finish(self):
        at = self.at
        self.y_copy(0).wait_recv()
        total = self.block(at.z, at.y)[...].astype(f32) + self.from_y[0].astype(f32)
        for k in range(1, at.lines):
            self.z_copy(k).wait_recv()
            total = total + self.from_z[k - 1].astype(f32)
        return total

    def drain(self):
        for k in range(self.at.lines):
            self.y_copy(k).wait_send()
        for k in range(1, self.at.lines):
            self.z_copy(k).wait_send()


class Halves(Scatter):
    def partner(self, k):
        z = self.at.z
        return (3 - z, z + 1 - 2 * (z % 2), (z + 2) % 4, z)[k]

    def y_copy(self, k):
        at = self.at
        return remote(
            self.block(self.partner(k), 1 - at.y),
            self.from_y.at[k],
            self.y_send.at[k],
            self.y_recv.at[k],
            (at.z * 2 + 1 - at.y, at.s),
        )

    def z_copy(self, k):
        at = self.at
        return remote(
            self.block(self.partner(k), at.y),
            self.from_z.at[k],
            self.z_send.at[k],
            self.z_recv.at[k],
            (self.partner(max(k, 1)) * 2 + at.y, at.s),
        )

    def start(self):
        for k in range(4):
            self.y_copy(k).start()

    def middle(self, k):
        at, k = self.at, k - 1
        self.y_copy(k).wait_recv()
        ref = self.block(self.partner(k), at.y)
        total = ref[...].astype(f32) + self.from_y[k].astype(f32)
        if k == 2:
            self.z_copy(0).wait_recv()
            total = total + self.from_z[0].astype(f32)
        ref[...] = total.astype(bf16)
        self.z_copy(k).start()

    def finish(self):
        at = self.at
        self.y_copy(3).wait_recv()
        total = self.block(at.z, at.y)[...].astype(f32) + self.from_y[3].astype(f32)
        for k in (1, 2):
            self.z_copy(k).wait_recv()
            total = total + self.from_z[k].astype(f32)
        return total

    def drain(self):
        for k in range(4):
            self.y_copy(k).wait_send()
        for k in range(3):
            self.z_copy(k).wait_send()


class Exchange:
    def __init__(self, at, axis, slots, sems, block_for):
        self.at, self.axis, self.slots, self.block_for = at, axis, slots, block_for
        self.send, self.recv = sems
        self.count = at.dp if axis == "dp" else at.head
        self.me = at.d if axis == "dp" else at.s

    def copy(self, k):
        at = self.at
        peer = (self.me + k) % self.count
        device = (peer, at.s) if self.axis == "dp" else (at.d, peer)
        return remote(
            self.block_for(peer),
            self.slots.at[self.me],
            self.send.at[k - 1],
            self.recv.at[k - 1],
            device,
        )

    def start(self):
        for k in range(1, self.count):
            self.copy(k).start()

    def wait(self):
        for k in range(1, self.count):
            self.copy(k).wait_recv()

    def drain(self):
        for k in range(1, self.count):
            self.copy(k).wait_send()

    def total(self):
        total = self.slots[0]
        for k in range(1, self.count):
            total = total + self.slots[k]
        return total


class Doubling:
    def __init__(self, at, held, slots, sems, partners):
        self.at, self.held, self.slots, self.partners = at, held, slots, partners
        self.send, self.recv = sems

    def copy(self, k):
        return remote(
            self.held.at[k], self.slots.at[k], self.send.at[k], self.recv.at[k], self.partners[k]
        )

    def start(self):
        self.copy(0).start()

    def step(self, k):
        self.copy(k).wait_recv()
        total = self.held[k].astype(f32) + self.slots[k].astype(f32)
        if k + 1 == len(self.partners):
            return total
        self.held[k + 1] = total.astype(self.held.dtype)
        self.copy(k + 1).start()

    def drain(self):
        for k in range(len(self.partners)):
            self.copy(k).wait_send()


def norm_rows(x):
    center = jnp.mean(x, axis=-1, keepdims=True)
    centered = x - center
    spread = jnp.mean(centered * centered, axis=-1, keepdims=True)
    rs = lax.rsqrt(spread + epsilon)
    return centered * rs, rs


def norm_back_rows(grad, gain, xhat, rs):
    e = grad * gain
    return rs * (
        e
        - jnp.mean(e, axis=-1, keepdims=True)
        - xhat * jnp.mean(e * xhat, axis=-1, keepdims=True)
    )


def fold_rows(a):
    return jnp.sum(a.reshape(a.shape[0] // 8, 8, a.shape[1]), axis=0)


def block_kernel(sizes, names_in, names_out, names_scratch, *refs):
    seq, dp, head, scale = sizes
    n_in, n_out = len(names_in), len(names_out)
    i = types.SimpleNamespace(**dict(zip(names_in, refs[:n_in])))
    o = types.SimpleNamespace(**dict(zip(names_out, refs[n_in : n_in + n_out])))
    b = types.SimpleNamespace(**dict(zip(names_scratch, refs[n_in + n_out :])))
    at = Place(dp, head)
    images, padded, width = b.tok.shape
    b.bp, b.dq = b.actg, b.act.at[0]
    b.dk, b.mg = b.fi.at[:padded], b.wave.at[:padded]
    b.inp, b.out = b.n1, b.n2
    hops = range(1, at.lines)
    share = i.w_up.shape[0]
    own_rows = pl.ds(pl.multiple_of(at.d * share, share), share)
    loads = [
        pltpu.make_async_copy(src, dst, b.loads.at[n])
        for n, (src, dst) in enumerate(
            (
                (i.w_down, b.wd.at[own_rows]),
                (i.w_up, b.wu.at[own_rows]),
                (i.tokens, b.raw.at[0]),
                (i.out_grad, b.raw.at[1]),
            )
        )
    ]
    chunks = padded // 16
    wide = b.k.shape[0]
    slots = b.sc.shape[0]
    pairs = slots // 2
    units = b.wu.shape[1]
    bins = b.filt.shape[0] // 2

    def span(j, size):
        return pl.ds(j * size if isinstance(j, int) else pl.multiple_of(j * size, size), size)

    def chunk(j):
        return span(j, 16)

    def tile(p):
        return span(p, 128)

    def twice(body):
        def step(k, carry):
            body(1 - k)
            return carry

        lax.fori_loop(0, 2, step, 0)

    def each(steps, body):
        for j in range(steps) if isinstance(steps, int) else steps:
            body(j)

    def flip_block(a):
        return mm_nt(i.eye[: a.shape[1], : a.shape[1]], a)

    def halves(low, high):
        return (mm(low, i.eye[:64, :128]) + mm(high, i.eye[64:128, :128])).astype(bf16)

    at.call()
    for load in loads:
        load.start()
    w_q, w_k, w_v = i.w_qkv[0], i.w_qkv[1], i.w_qkv[2]
    b.wqk[at.s, own_rows, 0:128] = w_q[:, :128]
    b.wqk[at.s, own_rows, 128:256] = w_k[:, :128]
    b.wqk[at.s, own_rows, 256:384] = halves(w_q[:, 128:], w_k[:, 128:])
    own_gains, own_mixes = rows_of(b.gains, at.d, 8), b.mixes.at[at.s]
    own_gains[...] = jnp.zeros((8, 128), f32)
    own_mixes[...] = jnp.zeros((8, 128), f32)
    for r, gain in enumerate((i.ln1_gain, i.ln1_shift, i.ln2_gain, i.ln2_shift)):
        own_gains[r : r + 1, :share] = gain[...].astype(f32)
    local_heads, heads = i.mix_pre.shape
    own_mixes[:local_heads, :heads] = i.mix_pre[...]
    own_mixes[4 : 4 + local_heads, :heads] = i.mix_post[...]
    p_t = flip_block(i.w_proj[...]).astype(bf16)
    b.wv[at.s, own_rows, 0:128] = w_v[:, :128]
    b.wv[at.s, own_rows, 128:256] = halves(w_v[:, 128:], p_t[:, 128:])
    b.wp_two[at.s, own_rows, :] = p_t[:, :128]

    at.answer()
    loads[0].wait()
    loads[1].wait()

    def line(kind, buf, name, wide):
        sems = [(getattr(b, name + part + "_s"), getattr(b, name + part + "_r")) for part in ("zyxm" if wide else "zy")]
        return kind(at, buf, sems, wide)

    gains = line(Line, b.gains, "g", False)
    mixes = Share(at, b.mixes, (b.mi_s, b.mi_r))
    gq = line(Line, b.wqk, "q", True)
    gv = line(Line, b.wv, "v", True)
    gp = line(Line, b.wp_two, "p", True)
    cut = units // 3 * 2
    gu = line(Line, b.wu.at[:, :cut], "u", False)
    gr = line(Rows, b.wu.at[:, cut:], "r", False)
    gd = line(Line, b.wd, "d", False)
    ho = Share(at, b.ho, (b.ho_s, b.ho_r))
    ag = Share(at, b.ag, (b.ag_s, b.ag_r))
    out = Share(at, b.out, (b.ou_s, b.ou_r))
    inp = Share(at, b.inp, (b.in_s, b.in_r))
    fold_two = Fold(at, b.np, b.np_near, b.np_far, (b.np_s, b.np_r))
    fold_out = Fold(at, b.bp, b.bp_near, b.bp_far, (b.bp_s, b.bp_r))
    sc_up = Halves(at, b.g_up, b.up_y, b.up_z, ((b.uy2_s, b.uy2_r), (b.uz2_s, b.uz2_r)))
    sc_down = Halves(at, b.g_down, b.down_y, b.down_z, ((b.dy2_s, b.dy2_r), (b.dz2_s, b.dz2_r)))
    sc_qk = Scatter(at, b.g_qk, b.qk_y, b.qk_z, ((b.qy2_s, b.qy2_r), (b.qz2_s, b.qz2_r)))
    sc_pv = Scatter(at, b.g_pv, b.pv_y, b.pv_z, ((b.py2_s, b.py2_r), (b.pz2_s, b.pz2_r)))
    sc_v = Scatter(at, b.g_v, b.v_y, b.v_z, ((b.vy2_s, b.vy2_r), (b.vz2_s, b.vz2_r)))
    turn_v = Exchange(at, "head", b.turned_v, (b.tv_s, b.tv_r), lambda s: b.turn_v.at[s, :, pl.ds(0, 128)])
    turn_w = Exchange(at, "head", b.turned_w, (b.tw_s, b.tw_r), lambda s: b.turn_w.at[s])
    turn = Exchange(at, "head", b.turned, (b.tu_s, b.tu_r), lambda s: b.turn.at[s])
    over_dp = (
        ((at.z + 1 - 2 * (at.z % 2)) * 2 + at.y, at.s),
        ((at.z + 2) % 4 * 2 + at.y, at.s),
        (at.z * 2 + 1 - at.y, at.s),
    )
    taps = Doubling(at, b.taps, b.taps_in, (b.ta_s, b.ta_r), over_dp)
    small = Doubling(
        at, b.small, b.small_in, (b.sm_s, b.sm_r), ((at.d, at.across), (at.d, at.mate), *over_dp)
    )

    passed = ((0, False), (1, False), (0, True), (2, False), (1, True), (3, False), (2, True), (3, True))
    gq.begin()
    gq.over_y()
    gq.on(0, False)
    gains.begin()
    gains.over_y()
    mixes.start()
    gv.begin()
    gv.over_y()
    gv.on(0, False)
    gp.begin()
    gp.over_y()
    gp.on(0, False)
    gr.over_y()

    def norm_one(image):
        def body(j):
            xhat, _ = norm_rows(b.tok[image, chunk(j), :].astype(f32))
            b.n1[image, chunk(j), :] = (xhat * b.norms[0:1, :] + b.norms[1:2, :]).astype(bf16)

        each(chunks, body)

    ksize = i.taps.shape[0]
    b.edge[...] = jnp.zeros_like(b.edge)
    for p in range(ksize):
        b.edge[p * ksize : (p + 1) * ksize, :] = i.taps[p]
    b.filt[...] = exact(i.lag[...], b.edge[...])
    b.filt[:bins, :] += 1.0
    b.cross[...] = jnp.zeros_like(b.cross)
    b.mix_one[...] = jnp.zeros_like(b.mix_one)
    b.mix_two[...] = jnp.zeros_like(b.mix_two)
    b.k[padded:, :] = jnp.zeros((wide - padded, width), bf16)
    b.v[padded:, :] = jnp.zeros((wide - padded, width), bf16)

    for which, dst in enumerate((b.tok, b.og)):
        loads[2 + which].wait()
        for r in range(chunks):
            n = min(16, seq - r * 16)
            rows = b.raw[which, r * 16 : r * 16 + n].reshape(n * images, width)
            apart = mm(i.deal[:, : n * images], rows).astype(bf16)
            dst[:, chunk(r), :] = apart.reshape(images, 16, width)

    gq.from_z(1)
    gq.on(1, False)
    gains.from_z(1)
    gq.from_y(0)
    gq.on(0, True)
    gv.from_z(1)
    gp.from_z(1)
    gains.from_z(2)
    mixes.forward()
    gq.from_z(2)
    gq.on(2, False)
    gq.from_y(1)
    gq.on(1, True)
    gv.from_z(2)
    gp.from_z(2)
    gd.begin()
    gu.begin()
    gains.from_z(3)
    gq.from_z(3)
    gq.on(3, False)
    gd.over_y()
    gu.over_y()
    gr.from_y()
    gq.from_y(2)
    gq.on(2, True)
    gv.on(1, False)
    gv.from_y(0)
    gv.on(0, True)
    for k in range(at.lines):
        gains.from_y(k)
    spread = mm(b.gains[...].astype(bf16), i.comb[...])
    row = lax.broadcasted_iota(jnp.int32, spread.shape, 0)
    lane = lax.broadcasted_iota(jnp.int32, spread.shape, 1)
    first = (row >> 3) * share
    here = (lane >= first) & (lane < first + share)
    for r in range(4):
        b.norms[r : r + 1, :] = jnp.sum(
            jnp.where(here & ((row & 7) == r), spread, 0.0), axis=0, keepdims=True
        )
    norm_one(at.s)
    gv.from_z(3)
    gp.from_z(3)

    mixes.wait_mate()
    mixes.wait_corner()
    diagonal = i.diagonal[...]
    for part, piece in enumerate(split(b.mixes[...].reshape(head * 8, 128))):
        for which, pick in enumerate((i.pick_pre, i.pick_post)):
            picked = mm(pick[...], piece).astype(bf16)
            b.kron[which, part] = (mm_nt(picked, i.place[...]) * diagonal).astype(bf16)
            b.kron_t[which, part] = (mm_nt(i.place[...], picked) * diagonal).astype(bf16)

    gd.from_z(1)
    gq.from_y(3)
    gq.on(3, True)
    gv.on(2, False)
    gv.from_y(1)
    gv.on(1, True)
    gv.on(3, False)

    lo = (lax.broadcasted_iota(jnp.int32, (1, 128), 1) < 64).astype(f32)
    low_half = lax.broadcasted_iota(jnp.int32, (padded, 128), 1) < 64
    lo_b, hi_b = lo.astype(bf16), (1.0 - lo).astype(bf16)

    def project(g):
        t = mm(b.n1[at.s], b.wqk[g])
        b.q[:, tile(g)] = (t[:, :128] * scale).astype(bf16)
        b.k[:padded, tile(g)] = t[:, 128:256].astype(bf16)
        b.third_qk[g] = t[:, 256:]

    def project_v(g):
        t = mm(b.n1[at.s], b.wv[g])
        b.v[:padded, tile(g)] = t[:, :128].astype(bf16)
        b.third_v[g] = t[:, 128:]

    project(at.s)
    gv.from_y(2)
    gv.on(2, True)
    gq.from_mate(False)
    project(at.mate)
    gu.from_z(1)
    for block in passed:
        gq.from_x(*block)
    project(at.across)
    gv.from_y(3)
    gv.on(3, True)
    gq.from_mate(True)
    project(at.corner)
    for p in range(head // 2):
        one, two = b.third_qk[2 * p], b.third_qk[2 * p + 1]
        third = tile(head + p)
        b.q[:, third] = (jnp.where(low_half, one, pltpu.roll(two, 64, 1)) * scale).astype(bf16)
        b.k[:padded, third] = jnp.where(low_half, pltpu.roll(one, 64, 1), two).astype(bf16)

    def score(p):
        q, k = b.q[:, tile(p)], b.k[:, tile(p)]
        b.sc[2 * p] = mm_nt(q * lo_b, k).astype(bf16)
        b.sc[2 * p + 1] = mm_nt(q * hi_b, k).astype(bf16)

    each(pairs, score)
    gr.from_z(1)
    for block in passed[1:]:
        if block[1]:
            gp.from_y(block[0])
        gp.on(*block)
    gd.from_z(2)

    def mixed(table, which, block):
        return mm(table[which, 0], block) + mm(table[which, 1], block)

    def slab(ref, j):
        return ref[:, chunk(j), :].reshape(slots * 16, wide)

    def put(ref, j, value):
        ref[:, chunk(j), :] = value.reshape(slots, 16, wide)

    def soften(j):
        beyond = lax.broadcasted_iota(jnp.int32, (slots * 16, wide), 1) >= seq
        logits = jnp.where(beyond, -1e30, mixed(b.kron, 0, slab(b.sc, j)))
        top = jnp.max(logits, axis=-1, keepdims=True)
        power = jnp.exp(logits - top)
        probs = power / jnp.sum(power, axis=-1, keepdims=True)
        put(b.pr, j, probs)
        put(b.post, j, mixed(b.kron, 1, probs.astype(bf16)).astype(bf16))

    each(chunks, soften)
    gu.from_z(2)
    for block in passed:
        gv.from_x(*block)
    project_v(at.s)
    gv.from_mate(False)
    project_v(at.mate)
    project_v(at.across)
    gv.from_mate(True)
    project_v(at.corner)
    for p in range(head // 2):
        b.v[:padded, tile(head + p)] = jnp.where(
            low_half, b.third_v[2 * p], pltpu.roll(b.third_v[2 * p + 1], 64, 1)
        ).astype(bf16)

    def gather_heads(p):
        v = b.v[:, tile(p)]
        b.ho[at.s, :, tile(p)] = (mm(b.post[2 * p], v * lo_b) + mm(b.post[2 * p + 1], v * hi_b)).astype(bf16)

    each(pairs, gather_heads)
    ho.start()
    gr.from_z(2)
    gd.from_z(3)
    gu.from_z(3)

    def flip(src, dst):
        for r in range(width // 256):
            lanes = span(r, 256)
            block = src[:, :, lanes].reshape(images * padded, 256)
            dst[lanes, :] = mm_nt(i.eye[...], block).astype(bf16)

    def weight_grad(dst, left, right):
        for r in range(width // 256):
            rows = span(r, 256)
            dst[rows, :] = mm(left[rows, :], right()).astype(bf16)

    def flat(ref):
        return ref[...].reshape(images * padded, ref.shape[2])

    lax.fori_loop(1, images, lambda k, carry: (norm_one(at.head_next(k)), carry)[1], 0)
    flip(b.og, b.og_t)

    for block in passed:
        gp.from_x(*block)
    gp.from_mate(False)
    gp.from_mate(True)
    low_rows = lax.broadcasted_iota(jnp.int32, (width, 128), 1) < 64
    for g in range(head):
        b.wp[:, tile(g)] = b.wp_two[g]
    for p in range(head // 2):
        one, two = b.wv[2 * p, :, 128:].astype(f32), b.wv[2 * p + 1, :, 128:].astype(f32)
        b.wp[:, tile(head + p)] = jnp.where(low_rows, pltpu.roll(one, 64, 1), two).astype(bf16)

    def chip_images(step):
        return 2 * ((at.x + step) % 2)

    def two(ref, step):
        return ref[pl.ds(chip_images(step), 2)].reshape(2 * padded, ref.shape[2])

    def rows_in_two(step, body):
        for half in range(2):
            for r in range(chunks):
                body(chip_images(step) + half, chunk(r), chunk(half * chunks + r))

    def bins_of(body):
        for j in range(bins // 16):
            body(span(j, 16), pl.ds(bins + j * 16, 16))

    def conv_back(step):
        b.act[...] = mm(two(b.og, step), b.wd[...]).astype(bf16).reshape(2, padded, units)
        for half in range(2):
            image = chip_images(step) + half
            b.wave[...] = mm(i.fourier[...], b.act[half])

            def body(cos, sin):
                cos_g, sin_g = b.wave[cos, :], b.wave[sin, :]
                cos_k, sin_k = b.filt[cos, :], b.filt[sin, :]
                b.gf[image, cos, :] = cos_g.astype(bf16)
                b.gf[image, sin, :] = sin_g.astype(bf16)
                b.fi[cos, :] = (cos_k * cos_g - sin_k * sin_g).astype(bf16)
                b.fi[sin, :] = (cos_k * sin_g + sin_k * cos_g).astype(bf16)

            bins_of(body)
            b.actg[image] = mm(i.fourier_t[...], b.fi[...]).astype(bf16)

    def up(step, between):
        b.hid[...] = mm_nt(two(b.ho, step), b.wp[...])

        def norm_two(image, rows, both):
            middle = b.tok[image, rows, :].astype(f32) + b.hid[both, :]
            b.mid[jnp.minimum(jnp.abs(image - at.s), 1), rows, :] = middle
            xhat, _ = norm_rows(middle)
            b.n2[image, rows, :] = (xhat * b.norms[2:3, :] + b.norms[3:4, :]).astype(bf16)

        rows_in_two(step, norm_two)
        between()
        b.hid[...] = mm(two(b.n2, step), b.wu[...])

        def gelu(image, rows, both):
            h = b.hid[both, :]
            cdf = 0.5 * (1.0 + lax.erf(h * (0.5**0.5)))
            slope = cdf + h * jnp.exp(-0.5 * h * h) * 0.3989422804014327
            b.wid[image, rows, :] = (h * cdf).astype(bf16)
            b.hg[image, rows, :] = (b.actg[image, rows, :].astype(f32) * slope).astype(bf16)

        rows_in_two(step, gelu)
        b.np[pl.ds(chip_images(step), 2)] = (
            mm_nt(two(b.hg, step), b.wu[...]).astype(bf16).reshape(2, padded, width)
        )

    for k in range(at.lines):
        gd.from_y(k)

    def backward_part(step):
        conv_back(step)
        pl.when(step == 1)(ho.forward)

    def forward_part(step):
        pl.when(step == 0)(ho.wait_mate)
        up(step, lambda: pl.when(step == 0)(fold_two.middle))
        pl.when(step == 1)(lambda: fold_two.mate_copy(1).start())
        pl.when(step == 0)(lambda: fold_two.mate_copy(0).start())

    twice(backward_part)
    gr.from_z(3)
    for k in range(at.lines):
        gu.from_y(k)
    ho.wait_corner()
    twice(forward_part)
    flip(b.n2, b.flip)
    weight_grad(b.g_up, b.flip, lambda: flat(b.hg))
    sc_up.start()

    def down(step, between):
        for half in range(2):
            image = chip_images(step) + half
            if half:
                between()
            b.wave[...] = mm(i.fourier[...], b.wid[image])

            def body(cos, sin):
                cos_a, sin_a = b.wave[cos, :], b.wave[sin, :]
                cos_k, sin_k = b.filt[cos, :], b.filt[sin, :]
                cos_g, sin_g = b.gf[image, cos, :].astype(f32), b.gf[image, sin, :].astype(f32)
                b.fi[cos, :] = (cos_k * cos_a + sin_k * sin_a).astype(bf16)
                b.fi[sin, :] = (cos_k * sin_a - sin_k * cos_a).astype(bf16)
                b.cross[cos, :] += cos_a * cos_g + sin_a * sin_g
                b.cross[sin, :] += sin_a * cos_g - cos_a * sin_g

            bins_of(body)
            b.wid[image] = mm(i.fourier_t[...], b.fi[...]).astype(bf16)
        b.bp[pl.ds(chip_images(step), 2)] = (
            mm_nt(two(b.wid, step), b.wd[...]).astype(bf16).reshape(2, padded, width)
        )

    def down_part(step):
        down(step, lambda: pl.when(step == 0)(fold_out.middle))
        pl.when(step == 1)(lambda: fold_out.mate_copy(1).start())
        pl.when(step == 0)(lambda: fold_out.mate_copy(0).start())

    twice(down_part)
    weight_grad(b.g_down, b.og_t, lambda: flat(b.wid))
    sc_down.start()
    b.taps[0] = exact(i.lag_back[...], b.cross[...]).astype(bf16)
    taps.start()
    sc_up.middle(1)
    flip(b.n1, b.flip)

    fold_two.wait()
    zero = jnp.zeros((8, width), f32)
    gain_sum, shift_sum = zero, zero
    for j in range(chunks):
        grad = fold_two.total(chunk(j))
        xhat, rs = norm_rows(b.mid[0, chunk(j), :])
        inner = norm_back_rows(grad, b.norms[2:3, :], xhat, rs)
        total = b.og[at.s, chunk(j), :].astype(f32) + inner
        b.mg[chunk(j), :] = total
        b.ag[at.s, chunk(j), :] = total.astype(bf16)
        gain_sum += fold_rows(grad * xhat)
        shift_sum += fold_rows(grad)
    b.sums[2:3, :] = jnp.sum(gain_sum, axis=0, keepdims=True)
    b.sums[3:4, :] = jnp.sum(shift_sum, axis=0, keepdims=True)

    b.hgr[...] = mm(b.ag[at.s], b.wp[...]).astype(bf16)

    def flip_one(src, dst):
        for r in range(width // 256):
            dst[span(r, 256), :] = mm_nt(i.eye[...], src[:, span(r, 256)]).astype(bf16)

    flip_one(b.hgr, b.hgr_t)
    flip_one(b.q, b.q_t)

    def back_post(p):
        g, v = b.hgr[:, tile(p)], b.v[:, tile(p)]
        for half, mask in enumerate((lo_b, hi_b)):
            b.pg[2 * p + half] = mm_nt(g * mask, v).astype(bf16)
            rows = span(2 * p + half, 64)
            b.dv_t[rows, :] = mm(b.hgr_t[rows, :], b.post[2 * p + half]).astype(bf16)

    each(pairs, back_post)

    def unflip(src, dst):
        for r in range(width // 256):
            dst[:, span(r, 256)] = mm_nt(i.eye[:padded, :], src[span(r, 256), :]).astype(bf16)

    unflip(b.dv_t, b.dv)
    fold_at = b.turn_w.shape[1]
    for g in range(head):
        b.turn_v[g, :, 0:128] = b.dv[:, tile(g)]
        v3 = b.dv[:, tile(head + g // 2)].astype(f32)
        if g % 2:
            v3 = pltpu.roll(v3, 64, 1)
        b.turn_v[g, :, 128:256] = jnp.where(low_half, v3, 0.0).astype(bf16)
        b.turn_w[g] = jnp.where(low_half[:fold_at], v3[:fold_at], pltpu.roll(v3[-fold_at:], 64, 1)).astype(bf16)
    turn_v.start()
    turn_w.start()
    b.turned_v[at.s] = b.turn_v[at.s, :, 0:128]
    b.turned_w[at.s] = b.turn_w[at.s]
    sc_up.middle(2)

    def back_soften(j):
        grad = slab(b.pg, j)
        probs = slab(b.pr, j)
        b.mix_two[...] += mm_nt(grad, probs.astype(bf16))
        probs_grad = mixed(b.kron_t, 1, grad)
        inner = jnp.sum(probs_grad * probs, axis=-1, keepdims=True)
        mixed_grad = (probs * (probs_grad - inner)).astype(bf16)
        b.mix_one[...] += mm_nt(mixed_grad, slab(b.sc, j))
        put(b.pg, j, mixed(b.kron_t, 0, mixed_grad).astype(bf16))

    each(chunks, back_soften)

    def back_score(p):
        k = b.k[:, tile(p)]
        b.dq[:, tile(p)] = (
            (mm(b.pg[2 * p], k * lo_b) + mm(b.pg[2 * p + 1], k * hi_b)) * scale
        ).astype(bf16)
        for half in range(2):
            rows = span(2 * p + half, 64)
            b.dk_t[rows, :] = mm(b.q_t[rows, :], b.pg[2 * p + half]).astype(bf16)

    each(pairs, back_score)
    unflip(b.dk_t, b.dk)
    for g in range(head):
        b.turn[g, :, 0:128] = b.dq[:, tile(g)]
        b.turn[g, :, 128:256] = b.dk[:, tile(g)]
        third = tile(head + g // 2)
        q3, k3 = b.dq[:, third].astype(f32), b.dk[:, third].astype(f32)
        if g % 2:
            q3 = pltpu.roll(q3, 64, 1)
        else:
            k3 = pltpu.roll(k3, 64, 1)
        b.turn[g, :, 256:384] = jnp.where(low_half, q3, k3).astype(bf16)
    turn.start()
    b.turned[at.s] = b.turn[at.s]
    for k in range(3, at.lines):
        sc_up.middle(k)

    for g in range(head):
        part = mm_nt(b.turn[g], b.wqk[g]) + mm_nt(b.turn_v[g], b.wv[g])
        if g:
            b.hid[:padded, :] += part
        else:
            b.hid[:padded, :] = part
    gain_sum, shift_sum = zero, zero
    for j in range(chunks):
        grad = b.hid[chunk(j), :]
        xhat, rs = norm_rows(b.tok[at.s, chunk(j), :].astype(f32))
        inner = norm_back_rows(grad, b.norms[0:1, :], xhat, rs)
        b.inp[at.s, chunk(j), :] = (b.mg[chunk(j), :] + inner).astype(bf16)
        gain_sum += fold_rows(grad * xhat)
        shift_sum += fold_rows(grad)
    b.sums[0:1, :] = jnp.sum(gain_sum, axis=0, keepdims=True)
    b.sums[1:2, :] = jnp.sum(shift_sum, axis=0, keepdims=True)

    blocks = jnp.zeros((head * 8, 128), f32)
    for table, pick in ((b.mix_one, i.pick_pre_t), (b.mix_two, i.pick_post_t)):
        blocks += exact(exact(pick[...], table[...] * diagonal), i.place_f[...])
    b.sums[4:8, :] = jnp.zeros((4, width), f32)
    b.small[0, :, :width] = b.sums[...]
    for g in range(head):
        b.small[0, :, width + g * 128 : width + (g + 1) * 128] = blocks[g * 8 : (g + 1) * 8]
    small.start()
    ag.start()
    taps.step(0)

    turn_v.wait()
    turn_w.wait()
    inp.start()
    kept = []

    def keep(src, dst):
        kept.append(pltpu.make_async_copy(src, dst, b.saves.at[len(kept)]))
        kept[-1].start()

    def keep_image(src, dst, image):
        keep(src.at[image], dst.at[image])

    keep_image(b.inp, o.input, at.s)
    for image in range(images):
        b.thirds[image, :fold_at, :] = b.turned_w[image]
        rest = b.turned_w[image, 2 * fold_at - padded :, :].astype(f32)
        b.thirds[image, fold_at:, :] = pltpu.roll(rest, 64, 1).astype(bf16)
    for r in range(width // 256):
        rows = span(r, 256)
        b.g_v[rows, :] = mm(b.flip[rows, :], flat(b.turned_v)).astype(bf16)
        b.g_pv[rows, 0:128] = mm(b.flip[rows, :], flat(b.thirds)).astype(bf16)
    sc_v.start()
    sc_down.middle(1)
    fold_out.wait()
    for j in range(chunks):
        b.out[at.s, chunk(j), :] = (b.mid[0, chunk(j), :] + fold_out.total(chunk(j))).astype(bf16)
    out.start()
    keep_image(b.out, o.output, at.s)
    sc_down.middle(2)
    for item in (gains, mixes, gq, gv, gp, gu, gr, gd, ho, fold_two, turn_v, turn_w):
        item.drain()
    turn.wait()
    weight_grad(b.g_qk, b.flip, lambda: flat(b.turned))
    sc_qk.start()
    small.step(0)
    small.step(1)
    taps.step(1)
    sc_down.middle(3)
    for k in range(1, at.lines):
        sc_v.middle(k)
    small.step(2)
    ag.forward()
    sc_qk.middle(1)
    ag.wait_mate()
    ag.wait_corner()
    sc_qk.middle(2)
    flip(b.ag, b.og_t)
    mine = tile(at.s)
    third_tile = tile(head + at.s // 2)
    for r in range(width // 256):
        rows = span(r, 256)
        left = b.og_t[rows, :]
        proj = mm(left, b.ho[:, :, mine].reshape(images * padded, 128))
        third = pltpu.roll(mm(left, b.ho[:, :, third_tile].reshape(images * padded, 128)), 64 * (1 - at.c), 1)
        low = lax.broadcasted_iota(jnp.int32, third.shape, 1) < 64
        b.g_pv[rows, 0:128] = jnp.where(low, b.g_pv[rows, 0:128].astype(f32), third).astype(bf16)
        b.g_pv[rows, 128:256] = proj.astype(bf16)
    sc_pv.start()
    sc_qk.middle(3)
    small.step(3)
    b.s_up[...] = sc_up.finish()
    keep(b.s_up, o.w_up)
    for k in range(1, at.lines):
        sc_pv.middle(k)
    o.taps[...] = taps.step(2)
    b.s_down[...] = sc_down.finish()
    keep(b.s_down, o.w_down)
    inp.forward()
    keep_image(b.inp, o.input, at.across)
    inp.wait_mate()
    keep_image(b.inp, o.input, at.mate)
    o.w_v[:, 0:128] = sc_v.finish()
    small_total = small.step(4)
    o.mixes[...] = jnp.zeros((8, 128), f32)
    for g in range(head):

        @pl.when(at.s == g)
        def _():
            o.mixes[...] = small_total[:, width + g * 128 : width + (g + 1) * 128]

    columns = lax.broadcasted_iota(jnp.int32, (8, width), 1)
    own = (columns >= at.d * share) & (columns < (at.d + 1) * share)
    o.norms[...] = exact(jnp.where(own, small_total[:, :width], 0.0), i.comb_t[...])
    inp.wait_corner()
    keep_image(b.inp, o.input, at.corner)
    out.wait_mate()
    keep_image(b.out, o.output, at.mate)
    out.forward()
    keep_image(b.out, o.output, at.across)
    o.qk[...] = sc_qk.finish()
    out.wait_corner()
    keep_image(b.out, o.output, at.corner)
    pv = sc_pv.finish()
    o.w_v[:, 128:] = pv[:, :64]
    o.w_proj[:128, :] = pv[:, 128:].T
    o.w_proj[128:, :] = pv[:, :128].T[64:, :]
    for copy in kept:
        copy.wait()
    for item in (ag, out, inp, fold_out, sc_up, sc_down, sc_qk, sc_pv, sc_v, turn, taps, small):
        item.drain()


def finish_kernel(sizes, *refs):
    local_heads, heads, share = sizes
    (output, inputs, qk, w_v, w_proj, up, down, norms, mixes, taps, deal_t) = refs[:11]
    (o_output, o_input, o_one_g, o_one_s, o_qkv, o_proj, o_pre, o_post, o_two_g, o_two_s, o_up, o_taps, o_down) = refs[11:]
    images, rows, width = output.shape
    for src, dst in ((output, o_output), (inputs, o_input)):
        for r in range(rows // 16):
            some = pl.ds(r * 16, 16)
            mixed = mm(deal_t[...], src[:, some, :].reshape(images * 16, width))
            dst[some] = mixed.astype(bf16).reshape(16, images, width)

    @pl.when(pl.program_id(0) == 0)
    def _():
        thirds = qk[:, 256:]
        o_qkv[0, :, 0:128] = qk[:, 0:128]
        o_qkv[0, :, 128:] = thirds[:, :64]
        o_qkv[1, :, 0:128] = qk[:, 128:256]
        o_qkv[1, :, 128:] = pltpu.roll(thirds, 64, 1)[:, :64]
        o_qkv[2] = w_v[...]
        o_proj[...] = w_proj[...]
        o_up[...] = up[...]
        o_down[...] = down[...]
        o_pre[...] = mixes[:local_heads, :heads]
        o_post[...] = mixes[4 : 4 + local_heads, :heads]
        for r, ref in enumerate((o_one_g, o_one_s, o_two_g, o_two_s)):
            ref[...] = norms[r : r + 1, :share]
        ksize = o_taps.shape[0]
        for p in range(ksize):
            o_taps[p] = taps[p * ksize : (p + 1) * ksize, :]


def tables(seq, dp, head, heads, grid, ksize, share):
    cos, sin, cos_lag, sin_lag, back = spectrum(grid, ksize)
    used = cos.shape[0]
    bins = -(-used // 16) * 16
    padded = -(-seq // 16) * 16
    fourier = np.zeros((2 * bins, padded))
    fourier[:used, :seq] = cos
    fourier[bins : bins + used, :seq] = sin
    taps = ksize * ksize
    lag = np.zeros((2 * bins, -(-taps // 8) * 8))
    lag[:used, :taps] = cos_lag
    lag[bins : bins + used, :taps] = sin_lag
    lag_back = np.zeros((-(-taps // 16) * 16, 2 * bins))
    lag_back[:taps, :used] = (cos_lag * back[:, None]).T
    lag_back[:taps, bins : bins + used] = (sin_lag * back[:, None]).T
    comb = (np.arange(share * dp)[None, :] % share == np.arange(128)[:, None]) & (
        np.arange(128)[:, None] < share
    )
    group = heads // head
    slot = [group * g + l for g in range(head) for l in range(2)] + [group * g + 2 for g in range(head)]
    wide = heads * 16
    pick = np.zeros((2, wide, head * 8))
    place = np.zeros((wide, 128))
    for p, h in enumerate(slot):
        for row in range(16):
            for which in range(2):
                pick[which, p * 16 + row, (h // group) * 8 + which * 4 + h % group] = 1.0
            place[p * 16 + row, h] = 1.0
    deal = np.zeros((16 * head, 16 * head))
    for token in range(16):
        for image in range(head):
            deal[image * 16 + token, token * head + image] = 1.0
    diagonal = (np.arange(wide)[:, None] % 16) == (np.arange(wide)[None, :] % 16)
    return {
        "fourier": jnp.asarray(fourier, bf16),
        "fourier_t": jnp.asarray(fourier.T, bf16),
        "lag": jnp.asarray(lag, f32),
        "lag_back": jnp.asarray(lag_back, f32),
        "comb": jnp.asarray(comb, bf16),
        "comb_t": jnp.asarray(comb.T, f32),
        "pick_pre": jnp.asarray(pick[0], bf16),
        "pick_post": jnp.asarray(pick[1], bf16),
        "pick_pre_t": jnp.asarray(pick[0].T, f32),
        "pick_post_t": jnp.asarray(pick[1].T, f32),
        "place": jnp.asarray(place, bf16),
        "place_f": jnp.asarray(place, f32),
        "diagonal": jnp.asarray(diagonal, f32),
        "eye": jnp.asarray(np.eye(256), bf16),
        "eye_f": jnp.asarray(np.eye(256), f32),
        "deal": jnp.asarray(deal, bf16),
        "deal_t": jnp.asarray(deal.T, bf16),
    }


def whole_block(
    tokens,
    ln1_gain,
    ln1_shift,
    w_qkv,
    w_proj,
    mix_pre,
    mix_post,
    ln2_gain,
    ln2_shift,
    w_up,
    conv_kernel,
    w_down,
    out_grad,
):
    images, seq, width = tokens.shape
    dp, head = lax.axis_size("dp"), lax.axis_size("head")
    local_heads, heads = mix_pre.shape
    size = width // heads
    local = local_heads * size
    share = w_qkv.shape[0]
    ksize, units = conv_kernel.shape[0], conv_kernel.shape[2]
    grid = int(round((seq - 1) ** 0.5))
    padded = -(-seq // 16) * 16
    wide = -(-seq // 128) * 128
    lines = dp // 2
    const = tables(seq, dp, head, heads, grid, ksize, share)
    bins = const["fourier"].shape[0] // 2
    taps = const["lag_back"].shape[0]

    inputs = {
        "tokens": jnp.transpose(tokens, (1, 0, 2)),
        "out_grad": jnp.transpose(out_grad, (1, 0, 2)),
        "ln1_gain": ln1_gain.reshape(1, share),
        "ln1_shift": ln1_shift.reshape(1, share),
        "ln2_gain": ln2_gain.reshape(1, share),
        "ln2_shift": ln2_shift.reshape(1, share),
        "mix_pre": mix_pre,
        "mix_post": mix_post,
        "w_qkv": jnp.transpose(w_qkv, (1, 0, 2)),
        "w_proj": w_proj,
        "w_up": w_up,
        "w_down": w_down.T,
        "taps": conv_kernel,
        **{name: value for name, value in const.items() if name not in ("deal_t", "eye_f")},
    }
    outputs = {
        "output": ((images, padded, width), bf16),
        "input": ((images, padded, width), bf16),
        "qk": ((share, 384), f32),
        "w_v": ((share, local), f32),
        "w_proj": ((local, share), f32),
        "w_up": ((share, units), f32),
        "w_down": ((share, units), f32),
        "norms": ((8, 128), f32),
        "mixes": ((8, 128), f32),
        "taps": ((taps, units), f32),
    }
    finals = {
        "output": ((seq, images, width), bf16),
        "input": ((seq, images, width), bf16),
        "ln1_gain": ((1, share), f32),
        "ln1_shift": ((1, share), f32),
        "w_qkv": ((3, share, local), f32),
        "w_proj": ((local, share), f32),
        "mix_pre": ((local_heads, heads), f32),
        "mix_post": ((local_heads, heads), f32),
        "ln2_gain": ((1, share), f32),
        "ln2_shift": ((1, share), f32),
        "w_up": ((share, units), f32),
        "taps": ((ksize, ksize, units), f32),
        "w_down": ((share, units), f32),
    }
    one, every = (padded, width), (images, padded, width)
    square = (heads, padded, wide)
    table = (heads * 16, heads * 16)
    scratch = {
        "tok": (every, bf16),
        "og": (every, bf16),
        "raw": ((2, seq, images, width), bf16),
        "edge": ((const["lag"].shape[1], units), f32),
        "wqk": ((head, width, 384), bf16),
        "wv": ((head, width, 256), bf16),
        "wp_two": ((head, width, 128), bf16),
        "wp": ((width, width), bf16),
        "wu": ((width, units), bf16),
        "wd": ((width, units), bf16),
        "gains": ((dp * 8, 128), f32),
        "mixes": ((head, 8, 128), f32),
        "norms": ((8, width), f32),
        "filt": ((2 * bins, units), f32),
        "cross": ((2 * bins, units), f32),
        "wave": ((2 * bins, units), f32),
        "fi": ((2 * bins, units), bf16),
        "gf": ((images, 2 * bins, units), bf16),
        "actg": ((images, padded, units), bf16),
        "act": ((2, padded, units), bf16),
        "n1": (every, bf16),
        "n2": (every, bf16),
        "mid": ((2, *one), f32),
        "hid": ((2 * padded, width), f32),
        "wid": ((images, padded, units), bf16),
        "hg": ((images, padded, units), bf16),
        "np": (every, bf16),
        "np_near": ((2, *one), bf16),
        "np_far": (one, bf16),
        "bp_near": ((2, *one), bf16),
        "bp_far": (one, bf16),
        "flip": ((width, images * padded), bf16),
        "q": (one, bf16),
        "k": ((wide, width), bf16),
        "v": ((wide, width), bf16),
        "third_qk": ((head, padded, 128), f32),
        "third_v": ((head, padded, 128), f32),
        "kron": ((2, 2, *table), bf16),
        "kron_t": ((2, 2, *table), bf16),
        "mix_one": (table, f32),
        "mix_two": (table, f32),
        "sc": (square, bf16),
        "pr": (square, f32),
        "post": (square, bf16),
        "pg": (square, bf16),
        "ho": (every, bf16),
        "ag": (every, bf16),
        "hgr": (one, bf16),
        "hgr_t": ((width, padded), bf16),
        "q_t": ((width, padded), bf16),
        "dv_t": ((width, wide), bf16),
        "dk_t": ((width, wide), bf16),
        "dv": (one, bf16),
        "turn": ((head, padded, 384), bf16),
        "turned": ((head, padded, 384), bf16),
        "turn_v": ((head, padded, 256), bf16),
        "turned_v": ((head, padded, 128), bf16),
        "turn_w": ((head, (padded // 16 + 1) // 2 * 16, 128), bf16),
        "turned_w": ((head, (padded // 16 + 1) // 2 * 16, 128), bf16),
        "thirds": ((head, padded, 128), bf16),
        "og_t": ((width, images * padded), bf16),
        "sums": ((8, width), f32),
        "s_up": ((share, units), f32),
        "s_down": ((share, units), f32),
        "small": ((5, 8, width + head * 128), f32),
        "small_in": ((5, 8, width + head * 128), f32),
        "taps": ((3, taps, units), bf16),
        "taps_in": ((3, taps, units), bf16),
    }
    for name, columns in (("up", units), ("down", units), ("qk", 384), ("pv", 256), ("v", 128)):
        scratch["g_" + name] = ((width, columns), bf16)
        scratch[name + "_y"] = ((lines, share, columns), bf16)
        scratch[name + "_z"] = ((lines - 1, share, columns), bf16)
    sems = {"mi": 3, "ho": 3, "ag": 3, "ou": 3, "in": 3, "np": 3, "bp": 3}
    sems |= {"tv": head - 1, "tw": head - 1, "tu": head - 1, "ta": 3, "sm": 5}
    for name in "gqvpurd":
        sems |= {name + "z": 2 * (lines - 1), name + "y": lines}
    for name in "qvpud":
        sems |= {name + "y2": lines, name + "z2": lines - 1}
    for name in "qvp":
        sems |= {name + "x": dp, name + "m": 2 * dp}
    shapes = {name: pltpu.VMEM(*spec) for name, spec in scratch.items()}
    for name, number in sems.items():
        shapes[name + "_s"] = pltpu.SemaphoreType.DMA((number,))
        shapes[name + "_r"] = pltpu.SemaphoreType.DMA((number,))
    shapes["saves"] = pltpu.SemaphoreType.DMA((10,))
    shapes["loads"] = pltpu.SemaphoreType.DMA((4,))
    vmem = pl.BlockSpec(memory_space=pltpu.VMEM)
    left = pl.BlockSpec(memory_space=pl.ANY)
    results = pl.pallas_call(
        functools.partial(
            block_kernel,
            (seq, dp, head, size ** (-0.5)),
            tuple(inputs),
            tuple(outputs),
            tuple(shapes),
        ),
        out_shape=[jax.ShapeDtypeStruct(*spec) for spec in outputs.values()],
        in_specs=[left if n in ("tokens", "out_grad", "w_up", "w_down") else vmem for n in inputs],
        out_specs=[left if n in ("output", "input", "w_up", "w_down") else vmem for n in outputs],
        scratch_shapes=list(shapes.values()),
        compiler_params=pltpu.CompilerParams(
            collective_id=0, has_side_effects=True, vmem_limit_bytes=64 * 2**20
        ),
    )(*inputs.values())
    r = dict(zip(outputs, results))

    def kept(shape):
        return pl.BlockSpec(shape, lambda j: (0,) * len(shape))

    parts = [*r.values(), const["deal_t"]]
    step = -(-padded // (32)) * 16
    by_rows = pl.BlockSpec((images, step, width), lambda j: (0, j, 0))
    by_tokens = pl.BlockSpec((step, images, width), lambda j: (j, 0, 0))
    results = pl.pallas_call(
        functools.partial(finish_kernel, (local_heads, heads, share)),
        grid=(-(-padded // step),),
        out_shape=[jax.ShapeDtypeStruct(*spec) for spec in finals.values()],
        in_specs=[by_rows] * 2 + [kept(part.shape) for part in parts[2:]],
        out_specs=[by_tokens] * 2 + [kept(spec[0]) for spec in list(finals.values())[2:]],
    )(*parts)
    r = dict(zip(finals, results))
    for name in ("output", "input", "w_qkv"):
        r[name] = jnp.transpose(r[name], (1, 0, 2))
    for name in ("ln1_gain", "ln1_shift", "ln2_gain", "ln2_shift"):
        r[name] = r[name].reshape(share)
    r["w_down"] = r["w_down"].T
    return tuple(r.values())


def solution(mesh):
    in_specs = (
        P("dp", None, None),
        P("dp"),
        P("dp"),
        P("dp", None, "head"),
        P("head", "dp"),
        P("head", None),
        P("head", None),
        P("dp"),
        P("dp"),
        P("dp", "head"),
        P(None, None, "head"),
        P("head", "dp"),
        P("dp", None, None),
    )
    out_specs = (
        P("dp", None, None),
        P("dp", None, None),
        P("dp"),
        P("dp"),
        P("dp", None, "head"),
        P("head", "dp"),
        P("head", None),
        P("head", None),
        P("dp"),
        P("dp"),
        P("dp", "head"),
        P(None, None, "head"),
        P("head", "dp"),
    )
    dp, head = mesh.shape["dp"], mesh.shape["head"]

    def shards(*args):
        tokens, w_qkv, mix_pre = args[0], args[3], args[5]
        fits = head == 4 and dp == 8 and w_qkv.shape[0] % 32 == 0 and w_qkv.shape[0] <= 128
        fits = fits and tokens.shape[0] == head
        fits = fits and mix_pre.shape[0] == 3 and tokens.shape[2] == 64 * mix_pre.shape[1]
        return (whole_block if fits else plain)(*args)

    return jax.shard_map(shards, mesh=mesh, in_specs=in_specs, out_specs=out_specs, check_vma=False)
```
